32 devices in a mesh: seq: 32 (over z, y, x, core).
Axes of the slice: x: 2, y: 2, z: 4, core: 2. Of those that a mesh axis runs over, the one named last changes fastest.
Arguments:
- hidden_in: bfloat16 [2, 4096, 768], P(None, 'seq'), may hold values from -6 to 6
- norm_gain: float32 [2, 768], replicated, may hold values from 0.1 to 1.9
- in_weight: bfloat16 [2, 768, 3072], replicated, may hold values from -0.21875 to 0.21875
- conv_weight: float32 [2, 1536, 4], replicated, may hold values from -3 to 3
- conv_bias: float32 [2, 1536], replicated, may hold values from -3 to 3
- xproj_weight: bfloat16 [2, 1536, 80], replicated, may hold values from -0.15625 to 0.15625
- dtproj_weight: bfloat16 [2, 48, 1536], replicated, may hold values from -0.875 to 0.875
- dt_bias: float32 [2, 1536], replicated, may hold values from -4.5 to -2.5
- a_log: float32 [2, 1536, 16], replicated, as said below
- skip_gain: float32 [2, 1536], replicated, may hold values from 0.5 to 1.5
- out_weight: bfloat16 [2, 1536, 768], replicated, may hold values from -0.15625 to 0.15625
- hidden_grad: bfloat16 [2, 4096, 768], P(None, 'seq'), may hold values from -6 to 6
Outputs:
- hidden_out: bfloat16 [2, 4096, 768], P(None, 'seq')
- input_grad: bfloat16 [2, 4096, 768], P(None, 'seq')
- grad_norm_gain: float32 [2, 768], replicated
- grad_in_weight: float32 [2, 768, 3072], replicated
- grad_conv_weight: float32 [2, 1536, 4], replicated
- grad_conv_bias: float32 [2, 1536], replicated
- grad_xproj_weight: float32 [2, 1536, 80], replicated
- grad_dtproj_weight: float32 [2, 48, 1536], replicated
- grad_dt_bias: float32 [2, 1536], replicated
- grad_a_log: float32 [2, 1536, 16], replicated
- grad_skip_gain: float32 [2, 1536], replicated
- grad_out_weight: float32 [2, 1536, 768], replicated
The draws below stay inside these ranges and needn't reach their ends.
Inputs may be any that keep to these rules, and one draw needn't show every extreme that they name: `a_log`: logarithms of positive decay rates.
All inputs are finite; a program needn't handle non-finite values.
Results may differ from the reference program's by a relative error of at most 0.018.
The reference program's roundings to bfloat16 on the way count: a program that leaves them out, or rounds other values in their place, can miss the bound.
Values may be sent and summed in bfloat16 or wider, within the bound.
No kernel may reach another device: no remote copies, remote signals or barrier semaphores. Data moves between devices by JAX's collectives and lax.ppermute only.
A program may use at most 320 MiB of HBM per device.

```python
import math
import jax
import jax.numpy as jnp
from jax import lax

D = 768
DI = 1536
NSTATE = 16
DT_RANK = 48
KCONV = 4
LAYERS = 2
SEQS = 2
LENGTH = 4096


def draw_a_log(key, part):
    key_kind, key_slow, key_fast = jax.random.split(key, 3)
    shape_all = (LAYERS, DI, NSTATE)
    slow_share = 0.5
    slow_pick = jax.random.uniform(key_kind, shape_all) < slow_share
    slow_log = math.log(0.5 / LENGTH) + math.log(4.0) * jax.random.uniform(key_slow, shape_all)
    fast_log = math.log(0.3) + math.log(10.0) * jax.random.uniform(key_fast, shape_all)
    return jnp.where(slow_pick, slow_log, fast_log).astype(jnp.float32)


def shard_levels(own_key, extent, cuts, smallest, largest):
    def one(position, shards_of):
        steps = jax.random.uniform(jax.random.fold_in(jax.random.fold_in(own_key, 6), position), (shards_of,), jnp.float32, smallest / len(cuts), largest / len(cuts))
        return jnp.repeat(jnp.exp(steps), extent[position] // shards_of).reshape((-1,) + (1,) * (len(extent) - position - 1))

    factor_of = one(*cuts[0])
    for cut in cuts[1:]:
        factor_of = factor_of * one(*cut)
    return factor_of


def scatter_about(rng, dims, scale, bound, cuts=(), held_as=jnp.bfloat16):
    drawn = jax.random.normal(rng, dims, jnp.float32) * scale
    if len(cuts) > 0:
        drawn = shard_levels(rng, dims, cuts, -0.22, 0.18) * drawn
    return jnp.clip(drawn, min=-bound, max=bound).astype(held_as)


def setup_inputs(seed: int = 0) -> dict:
    seeds = jax.random.split(jax.random.key(seed), 13)
    return {
        "hidden_in": scatter_about(seeds[0], (SEQS, LENGTH, D), 1.0, 6.0, ((1, 32),)),
        "norm_gain": jnp.clip(1.0 + 0.18 * jax.random.normal(seeds[1], (LAYERS, D), jnp.float32), 0.1, 1.9),
        "in_weight": scatter_about(seeds[2], (LAYERS, D, 2 * DI), D ** -0.5, 0.21875),
        "conv_weight": scatter_about(seeds[3], (LAYERS, DI, KCONV), KCONV ** -0.5, 3.0, (), jnp.float32),
        "conv_bias": scatter_about(seeds[4], (LAYERS, DI), 0.5, 3.0, (), jnp.float32),
        "xproj_weight": scatter_about(seeds[5], (LAYERS, DI, DT_RANK + 2 * NSTATE), DI ** -0.5, 0.15625),
        "dtproj_weight": scatter_about(seeds[6], (LAYERS, DT_RANK, DI), DT_RANK ** -0.5, 0.875),
        "dt_bias": jnp.clip(jax.random.uniform(seeds[7], (LAYERS, DI), jnp.float32, -4.5, -2.5), -4.5, -2.5),
        "a_log": draw_a_log(jax.random.fold_in(seeds[12], 71), 0),
        "skip_gain": jnp.clip(jax.random.uniform(seeds[9], (LAYERS, DI), jnp.float32, 0.5, 1.5), 0.5, 1.5),
        "out_weight": scatter_about(seeds[10], (LAYERS, DI, D), DI ** -0.5, 0.15625),
        "hidden_grad": scatter_about(seeds[11], (SEQS, LENGTH, D), 1.0, 6.0, ((1, 32),)),
    }


@jax.custom_vjp
def low(v):
    return lax.optimization_barrier(v.astype(jnp.bfloat16)).astype(jnp.float32)

@jax.custom_vjp
def low_back(v):
    return v

def low_keep(v):
    return (low(v), None)

def low_pass(kept, grad):
    return (grad,)

def back_keep(v):
    return (v, None)

def back_low(kept, grad):
    return (low(grad),)
low.defvjp(low_keep, low_pass)
low_back.defvjp(back_keep, back_low)

def matmul(left, right):
    return jnp.dot(left, right, precision=lax.Precision.HIGHEST)

def selective(step_size, mixer, b_mat, c_mat, rate):
    row_count = step_size.shape[0]
    block_len = math.gcd(row_count, 64)

    def token(state, pieces):
        step_now, mixer_now, b_now, c_now = pieces
        state = jnp.exp(step_now[:, None] * rate) * state + (step_now * mixer_now)[:, None] * b_now[None, :]
        return (state, lax.optimization_barrier(jnp.sum(state * c_now[None, :], axis=1)))

    def advance(state, pieces):
        return lax.scan(token, state, pieces)

    def blocked(value):
        return value.reshape((row_count // block_len, block_len) + value.shape[1:])
    start = jnp.zeros((step_size.shape[1], rate.shape[1]), jnp.float32)
    _, outputs = lax.scan(jax.checkpoint(advance), start, (blocked(step_size), blocked(mixer), blocked(b_mat), blocked(c_mat)))
    return outputs.reshape(row_count, -1)

def layer(hidden, weights):
    norm_g, in_w, conv_w, conv_b, x_w, dt_w, dt_b, log_rate, skip_g, out_w = weights
    inner_dim = out_w.shape[0]
    rank_dt = dt_w.shape[0]
    state_count = log_rate.shape[1]
    tap_count = conv_w.shape[1]
    row_count = hidden.shape[0]
    rms_inv = lax.rsqrt(lax.optimization_barrier(jnp.mean(hidden * hidden, axis=-1, keepdims=True)) + 1e-05)
    normed = low(hidden * rms_inv * norm_g)
    proj = low(low_back(matmul(normed, in_w)))
    conv_in = proj[:, :inner_dim]
    gate_z = proj[:, inner_dim:]
    extended = jnp.concatenate([jnp.zeros((tap_count - 1, inner_dim), jnp.float32), conv_in], 0)
    conv_out = conv_b
    for tap_k in range(tap_count):
        conv_out = conv_out + conv_w[:, tap_k] * extended[tap_k:tap_k + row_count]
    mixer = low(jax.nn.silu(conv_out))
    x_dbl = low(low_back(matmul(mixer, x_w)))
    dt_low = x_dbl[:, :rank_dt]
    b_mat = x_dbl[:, rank_dt:rank_dt + state_count]
    c_mat = x_dbl[:, rank_dt + state_count:]
    dt_pre = low_back(matmul(dt_low, dt_w))
    step_size = jax.nn.softplus(dt_pre + dt_b)
    rate = -jnp.exp(log_rate)
    y_full = selective(step_size, mixer, b_mat, c_mat, rate) + skip_g * mixer
    gated = low(y_full * jax.nn.silu(gate_z))
    return hidden + low_back(matmul(gated, out_w))

def reference(hidden_in, norm_gain, in_weight, conv_weight, conv_bias, xproj_weight, dtproj_weight, dt_bias, a_log, skip_gain, out_weight, hidden_grad):
    params = tuple((v.astype(jnp.float32) for v in (norm_gain, in_weight, conv_weight, conv_bias, xproj_weight, dtproj_weight, dt_bias, a_log, skip_gain, out_weight)))

    def model(weights, inputs):

        def one_sequence(sequence):
            current = sequence
            for layer_i in range(LAYERS):
                current = layer(current, tuple((w[layer_i] for w in weights)))
            return current
        return lax.map(jax.checkpoint(one_sequence), inputs)
    output, pull = jax.vjp(model, params, hidden_in.astype(jnp.float32))
    grads, grad_input = pull(hidden_grad.astype(jnp.float32))
    return (output.astype(jnp.bfloat16), grad_input.astype(jnp.bfloat16), grads[0], grads[1], grads[2], grads[3], grads[4], grads[5], grads[6], grads[7], grads[8], grads[9])
```

```python
import functools
import math

import jax
import jax.numpy as jnp
from jax import lax
from jax.experimental import pallas as pl
from jax.experimental.pallas import tpu as pltpu
from jax.sharding import PartitionSpec as P

BF16 = jnp.bfloat16
F32 = jnp.float32
LOG2E = 1.4426950408889634
LN2 = 0.6931471805599453
AXIS = "seq"
XD = 128
EXTRA = 256
CHUNK = 256
UNROLL = 8
HALO = 8


def full(array):
    nd = len(array.shape)
    return pl.BlockSpec(array.shape, lambda i, nd=nd: (0,) * nd)


def part(shape, index):
    return pl.BlockSpec(shape, lambda i, index=index: index)


def run(kernel, outs, ins, scratch=(), flops=0, moved=None):
    arrays, specs = [], []
    for item in ins:
        if isinstance(item, tuple):
            arrays.append(item[0])
            specs.append(item[1])
        else:
            arrays.append(item)
            specs.append(full(item))
    if moved is None:
        moved = sum(math.prod(o.shape) * o.dtype.itemsize for o in outs) * 2
    return pl.pallas_call(
        kernel,
        grid=(1,),
        in_specs=specs,
        out_specs=[full(o) for o in outs],
        out_shape=outs,
        scratch_shapes=list(scratch),
        compiler_params=pltpu.CompilerParams(vmem_limit_bytes=58 * 1024 * 1024),
        cost_estimate=pl.CostEstimate(flops=flops, bytes_accessed=moved, transcendentals=0),
    )(*arrays)


def shape(dims, dtype):
    return jax.ShapeDtypeStruct(dims, dtype)


def dot(a, b):
    return jnp.dot(a, b, preferred_element_type=F32)


def dot_t(a, b):
    return lax.dot_general(a, b, (((1,), (1,)), ((), ())), preferred_element_type=F32)


def dot_rows(a, b):
    return lax.dot_general(a, b, (((0,), (0,)), ((), ())), preferred_element_type=F32)


def sigmoid(v):
    return 1.0 / (1.0 + jnp.exp(-v))


def softplus(v):
    return jnp.maximum(v, 0.0) + jnp.log1p(jnp.exp(-jnp.abs(v)))


def slope(v):
    s = sigmoid(v)
    return s * (1.0 + v * (1.0 - s))


def wide(block, lanes):
    return jnp.concatenate([block] * (lanes // block.shape[1]), axis=1)


def rows_of_sums(parts):
    row = lax.broadcasted_iota(jnp.int32, parts[0].shape, 0)
    m4, m2, m1 = row < 4, (row & 2) == 0, (row & 1) == 0
    q = []
    for i in range(4):
        first = jnp.where(m4, parts[i], parts[i + 4])
        other = jnp.where(m4, parts[i + 4], parts[i])
        q.append(first + pltpu.roll(other, 4, 0))
    s = []
    for i in range(2):
        s.append(
            jnp.where(
                m2, q[i] + pltpu.roll(q[i], 6, 0), q[i + 2] + pltpu.roll(q[i + 2], 2, 0)
            )
        )
    return jnp.where(m1, s[0] + pltpu.roll(s[0], 7, 0), s[1] + pltpu.roll(s[1], 1, 0))


def fold(block):
    out = block[0:8]
    for k in range(8, block.shape[0], 8):
        out = out + block[k : k + 8]
    return out


def fold_lanes(block):
    out = block[:, 0:128]
    for k in range(128, block.shape[1], 128):
        out = out + block[:, k : k + 128]
    return out


def normed_of(x, gain):
    rinv = lax.rsqrt(jnp.mean(x * x, axis=-1, keepdims=True) + 1e-05)
    return (x * rinv * gain).astype(BF16)


def fill_table(xdf_ref, lhs_ref, bc_ref, rank, states):
    rows = xdf_ref.shape[0]
    n_i = lax.broadcasted_iota(jnp.int32, (states, XD), 0)
    lane = lax.broadcasted_iota(jnp.int32, (states, XD), 1)
    mask = ((lane == rank + n_i) | (lane == rank + states + n_i)).astype(F32)

    def body(i, carry):
        for j in range(UNROLL):
            t = i * UNROLL + j
            line = xdf_ref[pl.ds(t, 1), :]
            lhs_ref[pl.ds(pl.multiple_of(t * states, states), states), :] = (
                line * mask
            ).astype(BF16)
        return carry

    lax.fori_loop(0, rows // UNROLL, body, 0)
    k_i = lax.broadcasted_iota(jnp.int32, (XD, 256), 0)
    c_i = lax.broadcasted_iota(jnp.int32, (XD, 256), 1)
    low = rank + jnp.where(c_i >= 128, states, 0)
    pick = ((k_i >= low) & (k_i < low + states)).astype(BF16)
    bc_ref[...] = dot(lhs_ref[...], pick)


def state_rows(t, states):
    return pl.ds(pl.multiple_of(t * states, states), states)


def scan_ends(dt_ref, dtu_ref, bc_ref, a2_ref, end_ref):
    rows, inner = dt_ref.shape
    states = a2_ref.shape[0]

    def chunk(c, carry):
        lanes = pl.ds(pl.multiple_of(c * CHUNK, CHUNK), CHUNK)
        a2 = a2_ref[:, lanes]

        def body(i, h):
            for j in range(UNROLL):
                t = i * UNROLL + j
                a = jnp.exp2(dt_ref[pl.ds(t, 1), lanes] * a2)
                b = wide(bc_ref[state_rows(t, states), 0:128], CHUNK)
                h = a * h + dtu_ref[pl.ds(t, 1), lanes] * b
            return h

        end_ref[:, lanes] = lax.fori_loop(
            0, rows // UNROLL, body, jnp.zeros((states, CHUNK), F32)
        )
        return carry

    lax.fori_loop(0, inner // CHUNK, chunk, 0)


def scan_back_ends(dt_ref, dy_ref, bc_ref, a2_ref, end_ref):
    rows, inner = dt_ref.shape
    states = a2_ref.shape[0]

    def chunk(c, carry):
        lanes = pl.ds(pl.multiple_of(c * CHUNK, CHUNK), CHUNK)
        a2 = a2_ref[:, lanes]

        def body(i, back):
            for j in range(UNROLL):
                t = rows - 1 - (i * UNROLL + j)
                a = jnp.exp2(dt_ref[pl.ds(t, 1), lanes] * a2)
                c_row = wide(bc_ref[state_rows(t, states), 128:256], CHUNK)
                back = a * (dy_ref[pl.ds(t, 1), lanes] * c_row + back)
            return back

        end_ref[:, lanes] = lax.fori_loop(
            0, rows // UNROLL, body, jnp.zeros((states, CHUNK), F32)
        )
        return carry

    lax.fori_loop(0, inner // CHUNK, chunk, 0)


def scan_forward(dt_ref, dtu_ref, bc_ref, a2_ref, h_in_ref, y_ref):
    rows, inner = dt_ref.shape
    states = a2_ref.shape[0]

    def chunk(c, carry):
        lanes = pl.ds(pl.multiple_of(c * CHUNK, CHUNK), CHUNK)
        a2 = a2_ref[:, lanes]

        def body(i, h):
            parts = []
            for j in range(UNROLL):
                t = i * UNROLL + j
                a = jnp.exp2(dt_ref[pl.ds(t, 1), lanes] * a2)
                both = bc_ref[state_rows(t, states), :]
                h = a * h + dtu_ref[pl.ds(t, 1), lanes] * wide(both[:, 0:128], CHUNK)
                parts.append(fold(h * wide(both[:, 128:256], CHUNK)))
            y_ref[pl.ds(pl.multiple_of(i * UNROLL, UNROLL), UNROLL), lanes] = rows_of_sums(
                parts
            )
            return h

        lax.fori_loop(0, rows // UNROLL, body, h_in_ref[:, lanes])
        return carry

    lax.fori_loop(0, inner // CHUNK, chunk, 0)


def scan_both(
    dt_ref,
    dtu_ref,
    dy_ref,
    bc_ref,
    a2_ref,
    h_in_ref,
    g_in_ref,
    y_ref,
    sgb_ref,
    sqa_ref,
    rate_ref,
    db_ref,
    dc_ref,
    a_s,
    ah_s,
):
    rows, inner = dt_ref.shape
    states = a2_ref.shape[0]
    db_ref[...] = jnp.zeros(db_ref.shape, F32)
    dc_ref[...] = jnp.zeros(dc_ref.shape, F32)

    def chunk(c, carry):
        lanes = pl.ds(pl.multiple_of(c * CHUNK, CHUNK), CHUNK)
        a2 = a2_ref[:, lanes]

        def ahead(i, h):
            parts = []
            for j in range(UNROLL):
                t = i * UNROLL + j
                at = state_rows(t, states)
                a = jnp.exp2(dt_ref[pl.ds(t, 1), lanes] * a2)
                both = bc_ref[at, :]
                ah = a * h
                a_s[at, :] = a
                ah_s[at, :] = ah
                h = ah + dtu_ref[pl.ds(t, 1), lanes] * wide(both[:, 0:128], CHUNK)
                dc_ref[at, :] += fold_lanes(h * dy_ref[pl.ds(t, 1), lanes])
                if y_ref is not None:
                    parts.append(fold(h * wide(both[:, 128:256], CHUNK)))
            if y_ref is not None:
                y_ref[pl.ds(pl.multiple_of(i * UNROLL, UNROLL), UNROLL), lanes] = (
                    rows_of_sums(parts)
                )
            return h

        lax.fori_loop(0, rows // UNROLL, ahead, h_in_ref[:, lanes])

        def retreat(i, carried):
            back, rate = carried
            block = rows // UNROLL - 1 - i
            gbs, qas = [None] * UNROLL, [None] * UNROLL
            for j in reversed(range(UNROLL)):
                t = block * UNROLL + j
                at = state_rows(t, states)
                both = bc_ref[at, :]
                g = dy_ref[pl.ds(t, 1), lanes] * wide(both[:, 128:256], CHUNK) + back
                q = g * ah_s[at, :]
                gbs[j] = fold(g * wide(both[:, 0:128], CHUNK))
                qas[j] = fold(q * a2)
                rate = rate + q * dt_ref[pl.ds(t, 1), lanes]
                db_ref[at, :] += fold_lanes(g * dtu_ref[pl.ds(t, 1), lanes])
                back = a_s[at, :] * g
            here = pl.ds(pl.multiple_of(block * UNROLL, UNROLL), UNROLL)
            sgb_ref[here, lanes] = rows_of_sums(gbs)
            sqa_ref[here, lanes] = rows_of_sums(qas)
            return back, rate

        _, rate = lax.fori_loop(
            0,
            rows // UNROLL,
            retreat,
            (g_in_ref[:, lanes], jnp.zeros((states, CHUNK), F32)),
        )
        rate_ref[:, lanes] = rate
        return carry

    lax.fori_loop(0, inner // CHUNK, chunk, 0)


def packed(state, total, wide_s):
    inner = total.shape[1]
    high = total.astype(BF16).astype(F32)
    rest = total - high
    wide_s[:, 0:inner] = state
    wide_s[:, inner:] = jnp.zeros((state.shape[0], EXTRA), F32)
    for k in range(inner // 128):
        wide_s[k : k + 1, inner : inner + 128] = high[:, k * 128 : (k + 1) * 128]
        wide_s[k : k + 1, inner + 128 : inner + 256] = rest[:, k * 128 : (k + 1) * 128]
    return wide_s[...].astype(BF16)


def unpack_total(wide_ref, m, total_ref, inner):
    for k in range(inner // 128):
        total_ref[m, 0:1, k * 128 : (k + 1) * 128] = (
            wide_ref[m, k : k + 1, inner : inner + 128]
            + wide_ref[m, k : k + 1, inner + 128 : inner + 256]
        )


def join_runs(states_ref, totals_ref, a2, digit, group, backward):
    inner = a2.shape[1]
    before = jnp.zeros(a2.shape, F32)
    entire = jnp.zeros(a2.shape, F32)
    sum_before = jnp.zeros((1, inner), F32)
    sum_entire = jnp.zeros((1, inner), F32)
    order = reversed(range(group)) if backward else range(group)
    for p in order:
        m = jnp.bitwise_xor(digit, p)
        state = states_ref[m, :, 0:inner]
        total = totals_ref[m, 0:1, :]
        through = jnp.exp2(total * a2)
        counts = (p > digit) if backward else (p < digit)
        before = jnp.where(counts, through * before + state, before)
        sum_before = jnp.where(counts, sum_before + total, sum_before)
        entire = through * entire + state
        sum_entire = sum_entire + total
    return before, sum_before, entire, sum_entire


def k_in(x_ref, g_ref, w_ref, n_ref, xc_ref, tail_ref):
    normed = normed_of(x_ref[...], g_ref[...])
    n_ref[...] = normed
    xc = dot(normed, w_ref[...]).astype(BF16)
    xc_ref[...] = xc
    tail_ref[...] = xc.astype(F32)[xc.shape[0] - HALO :, :]


def k_gate(n_ref, w_ref, z_ref):
    z_ref[...] = dot(n_ref[...], w_ref[...]).astype(BF16)


def k_dgated(e_ref, w_ref, out_ref):
    out_ref[...] = dot_t(e_ref[...], w_ref[...])


def conv_of(ext_s, halo_ref, xc_ref, cw_ref, cb_ref):
    rows = xc_ref.shape[0]
    taps = cw_ref.shape[0]
    ext_s[0:HALO, :] = halo_ref[...]
    ext_s[HALO:, :] = xc_ref[...].astype(F32)
    out = cb_ref[...]
    for k in range(taps):
        first = HALO - (taps - 1) + k
        out = out + cw_ref[k : k + 1, :] * ext_s[first : first + rows, :]
    return out


def k_local(
    rank, both, *refs
):
    refs = list(refs)
    halo, xc, cw, cb, xw, dw, db, a2 = refs[:8]
    refs = refs[8:]
    if both:
        dgated, z = refs[:2]
        refs = refs[2:]
    u_ref, xd_ref, v_ref, pay_ref = refs[:4]
    refs = refs[4:]
    if both:
        dy_ref = refs[0]
        refs = refs[1:]
    ext_s, dt_s, dtu_s, xdf_s, lhs_s, bc_s, end_s, wide_s = refs
    states = a2.shape[0]
    conv = conv_of(ext_s, halo, xc, cw, cb)
    u = (conv * sigmoid(conv)).astype(BF16)
    u_ref[...] = u
    xd = dot(u, xw[...]).astype(BF16)
    xd_ref[...] = xd
    xdf_s[...] = xd.astype(F32)
    v = dot(xd, dw[...]) + db[...]
    v_ref[...] = v
    dt = softplus(v)
    dt_s[...] = dt
    dtu_s[...] = dt * u.astype(F32)
    total = jnp.sum(dt, axis=0, keepdims=True)
    fill_table(xdf_s, lhs_s, bc_s, rank, states)
    scan_ends(dt_s, dtu_s, bc_s, a2, end_s)
    pay_ref[0:states, :] = packed(end_s[...], total, wide_s)
    if both:
        zf = z[...].astype(F32)
        dy_ref[...] = dgated[...] * (zf * sigmoid(zf))
        scan_back_ends(dt_s, dy_ref, bc_s, a2, end_s)
        pay_ref[states:, :] = packed(end_s[...], total, wide_s)


def k_join(group, nextgroup, mode, digits, *refs):
    refs = list(refs)
    received, refs = refs[:group], refs[group:]
    a2_ref, refs = refs[0], refs[1:]
    kinds = list(mode)
    n_pay = (nextgroup - 1) if (len(kinds) == 2 and nextgroup) else 1
    pays, refs = refs[:n_pay], refs[n_pay:]
    befores, refs = refs[: len(kinds)], refs[len(kinds) :]
    sums, refs = refs[: len(kinds)], refs[len(kinds) :]
    states_s, totals_s, wide_s = refs
    states, inner = a2_ref.shape
    digit = digits[0]
    nextdigit = digits[1]
    out = []
    for i in range(len(kinds)):
        for m in range(group):
            states_s[m] = received[m][i * states : (i + 1) * states, :].astype(F32)
            if i == 0:
                unpack_total(states_s, m, totals_s, inner)
        before, sum_before, entire, sum_entire = join_runs(
            states_s, totals_s, a2_ref[...], digit, group, kinds[i] == "b"
        )
        befores[i][...] = before
        sums[i][...] = sum_before
        out.append(packed(entire, sum_entire, wide_s))
    if len(kinds) == 2 and nextgroup:
        for m in range(1, nextgroup):
            ahead = jnp.bitwise_xor(nextdigit, m) > nextdigit
            pays[m - 1][...] = jnp.where(ahead, out[0].astype(F32), out[1].astype(F32)).astype(
                BF16
            )
    else:
        for i in range(len(kinds)):
            pays[0][i * states : (i + 1) * states, :] = out[i]


def entering(received, a2_ref, digit, befores, sums, states_s, totals_s, backward):
    states, inner = a2_ref.shape
    group = len(received) + 1
    states_s[0] = jnp.zeros(states_s.shape[1:], F32)
    for m in range(group):
        if m:
            states_s[m] = received[m - 1][...].astype(F32)
        unpack_total(states_s, m, totals_s, inner)
    value, _, _, _ = join_runs(states_s, totals_s, a2_ref[...], digit, group, backward)
    for before, total in reversed(list(zip(befores, sums))):
        value = jnp.exp2(total[...] * a2_ref[...]) * value + before[...]
    return value


def k_mix(rank, n_recv, n_low, digits, *refs):
    refs = list(refs)
    received, refs = refs[:n_recv], refs[n_recv:]
    befores, refs = refs[:n_low], refs[n_low:]
    sums, refs = refs[:n_low], refs[n_low:]
    a2, u_ref, v_ref, xd_ref, z_ref, x_ref, sk_ref, ow_ref, g_ref, iw_ref = refs[:10]
    refs = refs[10:]
    y_ref, gated_ref, x1_ref, n_ref, xc_ref, tail_ref, h_in_ref = refs[:7]
    dt_s, dtu_s, xdf_s, lhs_s, bc_s, states_s, totals_s = refs[7:]
    states = a2.shape[0]
    h_in_ref[...] = entering(received, a2, digits[0], befores, sums, states_s, totals_s, False)
    uf = u_ref[...].astype(F32)
    dt = softplus(v_ref[...])
    dt_s[...] = dt
    dtu_s[...] = dt * uf
    xdf_s[...] = xd_ref[...].astype(F32)
    fill_table(xdf_s, lhs_s, bc_s, rank, states)
    scan_forward(dt_s, dtu_s, bc_s, a2, h_in_ref, y_ref)
    y = y_ref[...] + sk_ref[...] * u_ref[...].astype(F32)
    y_ref[...] = y
    zf = z_ref[...].astype(F32)
    gated = (y * (zf * sigmoid(zf))).astype(BF16)
    gated_ref[...] = gated
    x1 = x_ref[...] + dot(gated, ow_ref[...])
    x1_ref[...] = x1
    normed = normed_of(x1, g_ref[...])
    n_ref[...] = normed
    xc = dot(normed, iw_ref[...]).astype(BF16)
    xc_ref[...] = xc
    tail_ref[...] = xc.astype(F32)[xc.shape[0] - HALO :, :]


def k_back(rank, n_recv, n_low, last, digits, *refs):
    refs = list(refs)
    received, refs = refs[:n_recv], refs[n_recv:]
    kinds = 2 if last else 1
    befores, refs = refs[: n_low * kinds], refs[n_low * kinds :]
    sums, refs = refs[: n_low * kinds], refs[n_low * kinds :]
    a2, u_ref, v_ref, xd_ref, dy_ref, halo, xc, cw, cb, xw, dw, sk_ref = refs[:12]
    refs = refs[12:]
    if last:
        y_ref = refs[0]
        refs = refs[1:]
    else:
        h_in_ref = refs[0]
        refs = refs[1:]
        y_ref = None
    dconv_ref, head_ref, small_ref = refs[:3]
    refs = refs[3:]
    (
        dt_s,
        dtu_s,
        xdf_s,
        lhs_s,
        bc_s,
        states_s,
        totals_s,
        ext_s,
        sgb_s,
        sqa_s,
        rate_s,
        db_s,
        dc_s,
        a_s,
        ah_s,
        g_s,
        h_s,
    ) = refs
    states = a2.shape[0]
    rows, inner = u_ref.shape
    low_f, low_b = befores[:n_low], befores[-n_low:]
    sum_f, sum_b = sums[:n_low], sums[-n_low:]
    if last:
        h_s[...] = entering(received, a2, digits[0], low_f, sum_f, states_s, totals_s, False)
        h_in_ref = h_s
    g_s[...] = entering(received, a2, digits[0], low_b, sum_b, states_s, totals_s, True)
    dt = softplus(v_ref[...])
    dt_s[...] = dt
    dtu_s[...] = dt * u_ref[...].astype(F32)
    xdf_s[...] = xd_ref[...].astype(F32)
    fill_table(xdf_s, lhs_s, bc_s, rank, states)
    scan_both(
        dt_s,
        dtu_s,
        dy_ref,
        bc_s,
        a2,
        h_in_ref,
        g_s,
        y_ref,
        sgb_s,
        sqa_s,
        rate_s,
        db_s,
        dc_s,
        a_s,
        ah_s,
    )
    u = u_ref[...]
    uf = u.astype(F32)
    dy = dy_ref[...]
    if last:
        y_ref[...] += sk_ref[...] * uf
    sgb = sgb_s[...]
    dpre = (LN2 * sqa_s[...] + uf * sgb) * sigmoid(v_ref[...])
    dpl = dpre.astype(BF16)

    ones = jnp.ones((128, 128), BF16)

    def lane_sums(block):
        high = block.astype(BF16)
        rest = (block - high.astype(F32)).astype(BF16)
        return dot(high, ones) + dot(rest, ones)

    n_i = lax.broadcasted_iota(jnp.int32, (states, XD), 0)
    lane = lax.broadcasted_iota(jnp.int32, (states, XD), 1)
    mask_b = (lane == rank + n_i).astype(F32)
    mask_c = (lane == rank + states + n_i).astype(F32)
    db_s[...] = lane_sums(db_s[...])
    dc_s[...] = lane_sums(dc_s[...])

    def gather(i, carry):
        parts = []
        for j in range(UNROLL):
            at = state_rows(i * UNROLL + j, states)
            parts.append(fold(db_s[at, :] * mask_b + dc_s[at, :] * mask_c))
        xdf_s[pl.ds(pl.multiple_of(i * UNROLL, UNROLL), UNROLL), :] = rows_of_sums(parts)
        return carry

    lax.fori_loop(0, rows // UNROLL, gather, 0)
    dxd = (dot_t(dpl, dw[...]) + xdf_s[...]).astype(BF16)
    du = dt_s[...] * sgb + sk_ref[...] * dy + dot_t(dxd, xw[...])
    conv = conv_of(ext_s, halo, xc, cw, cb)
    dconv = du * slope(conv)
    dconv_ref[...] = dconv
    head_ref[...] = dconv[0:HALO, :]
    taps = cw.shape[0]
    width = rank + 2 * states
    g_x = dot_rows(dxd, u)
    g_dt = dot_rows(xd_ref[...], dpl)
    at = 0
    small_ref[at : at + width, :] = g_x[0:width]
    at += width
    small_ref[at : at + rank, :] = g_dt[0:rank]
    at += rank
    small_ref[at : at + states, :] = rate_s[...] * (a2[...] * LN2)
    at += states
    for k in range(taps):
        first = HALO - (taps - 1) + k
        small_ref[at : at + 1, :] = jnp.sum(
            dconv * ext_s[first : first + rows, :], axis=0, keepdims=True
        )
        at += 1
    small_ref[at : at + 1, :] = jnp.sum(dconv, axis=0, keepdims=True)
    small_ref[at + 1 : at + 2, :] = jnp.sum(dpre, axis=0, keepdims=True)
    small_ref[at + 2 : at + 3, :] = jnp.sum(dy * uf, axis=0, keepdims=True)
    small_ref[at + 3 : at + 4, :] = jnp.zeros((1, inner), F32)


def k_out(x_ref, y_ref, z_ref, dgated_ref, ow_ref, iw_ref, hid_ref, gated_ref, dz_ref, dnz_ref):
    zf = z_ref[...].astype(F32)
    s = sigmoid(zf)
    y = y_ref[...]
    gated = (y * (zf * s)).astype(BF16)
    gated_ref[...] = gated
    dz = (dgated_ref[...] * y * (s * (1.0 + zf * (1.0 - s)))).astype(BF16)
    dz_ref[...] = dz
    dnz_ref[...] = dot_t(dz, iw_ref[...])
    hid_ref[...] = (x_ref[...] + dot(gated, ow_ref[...])).astype(BF16)


def conv_back(dce_s, dconv_ref, next_ref, cw_ref):
    rows = dconv_ref.shape[0]
    taps = cw_ref.shape[0]
    dce_s[0:rows, :] = dconv_ref[...]
    dce_s[rows:, :] = next_ref[...]
    out = cw_ref[taps - 1 : taps, :] * dce_s[0:rows, :]
    for k in range(taps - 1):
        first = taps - 1 - k
        out = out + cw_ref[k : k + 1, :] * dce_s[first : first + rows, :]
    return out.astype(BF16)


def norm_back(x, gain, e, dn):
    rinv = lax.rsqrt(jnp.mean(x * x, axis=-1, keepdims=True) + 1e-05)
    xhat = x * rinv
    dhat = dn * gain
    g_norm = jnp.sum(dn * xhat, axis=0, keepdims=True)
    return e + rinv * (dhat - xhat * jnp.mean(dhat * xhat, axis=-1, keepdims=True)), g_norm


def k_turn(
    rank,
    dconv_ref,
    next_ref,
    cw_ref,
    dnz_ref,
    iw_ref,
    x_ref,
    g_ref,
    e_ref,
    ow_ref,
    y_ref,
    z_ref,
    v_ref,
    xd_ref,
    a2,
    dxc_ref,
    gn_ref,
    e1_ref,
    de_ref,
    dy_ref,
    dz_ref,
    pay_ref,
    dce_s,
    dt_s,
    xdf_s,
    lhs_s,
    bc_s,
    end_s,
    wide_s,
):
    dxc = conv_back(dce_s, dconv_ref, next_ref, cw_ref)
    dxc_ref[...] = dxc
    dn = dnz_ref[...] + dot_t(dxc, iw_ref[...])
    e1, g_norm = norm_back(x_ref[...], g_ref[...], e_ref[...].astype(F32), dn)
    gn_ref[...] = g_norm
    e1_ref[...] = e1
    de = e1.astype(BF16)
    de_ref[...] = de
    dgated = dot_t(de, ow_ref[...])
    zf = z_ref[...].astype(F32)
    s = sigmoid(zf)
    dy_ref[...] = dgated * (zf * s)
    dz_ref[...] = (dgated * y_ref[...] * (s * (1.0 + zf * (1.0 - s)))).astype(BF16)
    states = a2.shape[0]
    dt = softplus(v_ref[...])
    dt_s[...] = dt
    total = jnp.sum(dt, axis=0, keepdims=True)
    xdf_s[...] = xd_ref[...].astype(F32)
    fill_table(xdf_s, lhs_s, bc_s, rank, states)
    scan_back_ends(dt_s, dy_ref, bc_s, a2, end_s)
    pay_ref[...] = packed(end_s[...], total, wide_s)


def k_end(
    dconv_ref, next_ref, cw_ref, dnz_ref, iw_ref, x_ref, g_ref, e_ref, dxc_ref, gn_ref, e0_ref, dce_s
):
    dxc = conv_back(dce_s, dconv_ref, next_ref, cw_ref)
    dxc_ref[...] = dxc
    dn = dnz_ref[...] + dot_t(dxc, iw_ref[...])
    e0, g_norm = norm_back(x_ref[...], g_ref[...], e_ref[...], dn)
    gn_ref[...] = g_norm
    e0_ref[...] = e0.astype(BF16)


def k_dnz(dz_ref, iw_ref, out_ref):
    out_ref[...] = dot_t(dz_ref[...], iw_ref[...])


def k_wgrad(a_ref, b_ref, out_ref):
    out_ref[...] = dot_rows(a_ref[...], b_ref[...]).astype(out_ref.dtype)


def shards(
    hidden_in,
    norm_gain,
    in_weight,
    conv_weight,
    conv_bias,
    xproj_weight,
    dtproj_weight,
    dt_bias,
    a_log,
    skip_gain,
    out_weight,
    hidden_grad,
):
    layers, width, _ = in_weight.shape
    inner, states = a_log.shape[1], a_log.shape[2]
    rank = dtproj_weight.shape[1]
    taps = conv_weight.shape[2]
    seqs, own, _ = hidden_in.shape
    ndev = lax.axis_size(AXIS)
    me = lax.axis_index(AXIS)
    core = me % 2
    chip = me // 2
    rows = seqs * own
    assert layers == 2 and seqs == 2 and ndev % 2 == 0
    assert inner % CHUNK == 0 and inner // 128 <= states and rank + 2 * states <= XD

    pairs = [(i, i ^ 1) for i in range(ndev)]

    def to_runs(block):
        mine = lax.dynamic_index_in_dim(block, core, 0, keepdims=False)
        other = lax.dynamic_index_in_dim(block, 1 - core, 0, keepdims=False)
        came = lax.ppermute(other, AXIS, pairs)
        first = jnp.where(core == 0, mine, came)
        second = jnp.where(core == 0, came, mine)
        return jnp.concatenate([first, second], axis=0)

    def from_runs(run_block):
        halves = run_block.reshape((2, own) + run_block.shape[1:])
        mine = lax.dynamic_index_in_dim(halves, core, 0, keepdims=False)
        other = lax.dynamic_index_in_dim(halves, 1 - core, 0, keepdims=False)
        came = lax.ppermute(other, AXIS, pairs)
        first = jnp.where(core == 0, mine, came)
        second = jnp.where(core == 0, came, mine)
        return jnp.stack([first, second], axis=0)

    def from_before(block):
        return lax.ppermute(block, AXIS, [(i, i + 2) for i in range(ndev - 2)])

    def from_after(block):
        return lax.ppermute(block, AXIS, [(i + 2, i) for i in range(ndev - 2)])

    bits = (ndev // 2).bit_length() - 1
    assert 2 << bits == ndev and bits > 2
    rounds = []
    low = 0
    while low < bits:
        n = 2 if bits - low >= 2 else 1
        rounds.append((low, 1 << n))
        low += n

    def digit_of(r):
        low, group = rounds[r]
        return (chip >> low) & (group - 1)

    def digits_of(r):
        nxt = digit_of(r + 1) if r + 1 < len(rounds) else jnp.zeros_like(chip)
        return jnp.stack([digit_of(r), nxt]).astype(jnp.int32)

    def send(block, r, m, which):
        low, group = rounds[r]
        flip = (m << low) << 1
        route = [(i, i ^ flip) for i in range(ndev)]
        if which == "up":
            route = [(i, j) for i, j in route if j > i]
        if which == "down":
            route = [(i, j) for i, j in route if j < i]
        return lax.ppermute(block, AXIS, route)

    smem = pl.BlockSpec(memory_space=pltpu.SMEM)
    pay = shape((states, inner + EXTRA), BF16)

    def exchange(payload, a2, mode):
        befores = [[] for _ in mode]
        sums = [[] for _ in mode]
        for r, (low, group) in enumerate(rounds[:-1]):
            received = [payload] + [send(payload, r, m, "all") for m in range(1, group)]
            final = r + 2 == len(rounds)
            split = len(mode) == 2 and final
            nextgroup = rounds[r + 1][1] if split else 0
            pays = (
                [pay] * (nextgroup - 1)
                if split
                else [shape((states * len(mode), inner + EXTRA), BF16)]
            )
            outs = run(
                functools.partial(k_join, group, nextgroup, mode),
                pays
                + [shape((states, inner), F32)] * len(mode)
                + [shape((1, inner), F32)] * len(mode),
                [(digits_of(r), smem)] + received + [a2],
                [
                    pltpu.VMEM((group, states, inner + EXTRA), F32),
                    pltpu.VMEM((group, 8, inner), F32),
                    pltpu.VMEM((states, inner + EXTRA), F32),
                ],
                flops=10**6,
            )
            sent, outs = outs[: len(pays)], outs[len(pays) :]
            for i in range(len(mode)):
                befores[i].append(outs[i])
                sums[i].append(outs[len(mode) + i])
            payload = sent if split else sent[0]
        r = len(rounds) - 1
        if len(mode) == 2:
            last = [send(payload[m - 1], r, m, "all") for m in range(1, rounds[r][1])]
        else:
            way = "up" if mode == "f" else "down"
            last = [send(payload, r, m, way) for m in range(1, rounds[r][1])]
        return last, sum(befores, []), sum(sums, []), digits_of(r)

    a2_all = -jnp.exp(jnp.swapaxes(a_log, 1, 2)) * LOG2E
    cw_all = jnp.swapaxes(conv_weight, 1, 2)
    xw_all = jnp.pad(xproj_weight, ((0, 0), (0, 0), (0, XD - xproj_weight.shape[2])))
    dw_all = jnp.pad(dtproj_weight, ((0, 0), (0, XD - rank), (0, 0)))

    def row(array, l):
        return array[l : l + 1, :]

    def w_in(l, half):
        return in_weight, part((None, width, inner), (l, 0, half))

    def w_out(l):
        return out_weight, part((None, inner, width), (l, 0, 0))

    def table_scratch():
        return [
            pltpu.VMEM((rows, XD), F32),
            pltpu.VMEM((rows * states, XD), BF16),
            pltpu.VMEM((rows * states, 256), F32),
        ]

    act = shape((rows, inner), F32)
    act_b = shape((rows, inner), BF16)
    res = shape((rows, width), F32)
    res_b = shape((rows, width), BF16)
    edge = shape((HALO, inner), F32)
    mm = 2 * rows * width * inner

    grad_out = to_runs(hidden_grad)
    x0 = to_runs(hidden_in).astype(F32)

    normed = [None, None]
    xc = [None, None]
    halo = [None, None]
    z = [None, None]
    u = [None, None]
    xd = [None, None]
    v = [None, None]

    normed[0], xc[0], tail = run(
        k_in, [res_b, act_b, edge], [x0, row(norm_gain, 0), w_in(0, 0)], flops=mm
    )

    def before_scan(l, tail, dgated=None):
        halo[l] = from_before(tail)
        (z[l],) = run(k_gate, [act_b], [normed[l], w_in(l, 1)], flops=mm)
        both = dgated is not None
        outs = run(
            functools.partial(k_local, rank, both),
            [
                act_b,
                shape((rows, XD), BF16),
                act,
                shape((states * (2 if both else 1), inner + EXTRA), BF16),
            ]
            + ([act] if both else []),
            [
                halo[l],
                xc[l],
                cw_all[l],
                row(conv_bias, l),
                xw_all[l],
                dw_all[l],
                row(dt_bias, l),
                a2_all[l],
            ]
            + ([dgated, z[l]] if both else []),
            [pltpu.VMEM((rows + HALO, inner), F32)]
            + [pltpu.VMEM((rows, inner), F32)] * 2
            + table_scratch()
            + [pltpu.VMEM((states, inner), F32), pltpu.VMEM((states, inner + EXTRA), F32)],
            flops=10**9,
        )
        u[l], xd[l], v[l] = outs[:3]
        return outs[3:]

    (dgated1,) = run(k_dgated, [act], [grad_out, w_out(1)], flops=mm)

    def join_scratch():
        group = rounds[-1][1]
        return [
            pltpu.VMEM((group, states, inner + EXTRA), F32),
            pltpu.VMEM((group, 8, inner), F32),
        ]

    (payload,) = before_scan(0, tail)
    last, befores, sums, digits = exchange(payload, a2_all[0], "f")
    y0, gated0, x1, normed[1], xc[1], tail, h0 = run(
        functools.partial(k_mix, rank, len(last), len(befores)),
        [act, act_b, res, res_b, act_b, edge, shape((states, inner), F32)],
        [(digits, smem)]
        + last
        + befores
        + sums
        + [
            a2_all[0],
            u[0],
            v[0],
            xd[0],
            z[0],
            x0,
            row(skip_gain, 0),
            w_out(0),
            row(norm_gain, 1),
            w_in(1, 0),
        ],
        [pltpu.VMEM((rows, inner), F32)] * 2 + table_scratch() + join_scratch(),
        flops=10**9,
    )
    payload, dy1 = before_scan(1, tail, dgated1)
    last, befores, sums, digits = exchange(payload, a2_all[1], "fb")

    small = shape((rank + 2 * states + rank + states + taps + 4, inner), F32)

    def backward(l, dy, last, befores, sums, digits, h_in):
        final = h_in is None
        n_low = len(rounds) - 1
        outs = run(
            functools.partial(k_back, rank, len(last), n_low, final),
            ([act] if final else []) + [act, edge, small],
            [(digits, smem)]
            + last
            + befores
            + sums
            + [
                a2_all[l],
                u[l],
                v[l],
                xd[l],
                dy,
                halo[l],
                xc[l],
                cw_all[l],
                row(conv_bias, l),
                xw_all[l],
                dw_all[l],
                row(skip_gain, l),
            ]
            + ([] if final else [h_in]),
            [pltpu.VMEM((rows, inner), F32)] * 2
            + table_scratch()
            + join_scratch()
            + [pltpu.VMEM((rows + HALO, inner), F32)]
            + [pltpu.VMEM((rows, inner), F32)] * 2
            + [pltpu.VMEM((states, inner), F32)]
            + [pltpu.VMEM((rows * states, 128), F32)] * 2
            + [pltpu.VMEM((rows * states, CHUNK), F32)] * 2
            + [pltpu.VMEM((states, inner), F32)] * 2,
            flops=2 * 10**9,
        )
        return outs

    y1, dconv1, head1, small1 = backward(1, dy1, last, befores, sums, digits, None)
    after1 = from_after(head1)
    hidden_out, gated1, dz1, dnz1 = run(
        k_out,
        [res_b, act_b, act_b, res],
        [x1, y1, z[1], dgated1, w_out(1), w_in(1, 1)],
        flops=2 * mm,
    )

    def wgrad(a, b):
        (out,) = run(
            k_wgrad, [shape((a.shape[1], b.shape[1]), F32)], [a, b], flops=mm
        )
        return out

    dxc1, gn1, e1, de0, dy0, dz0, payload = run(
        functools.partial(k_turn, rank),
        [act_b, shape((1, width), F32), res, res_b, act, act_b, pay],
        [
            dconv1,
            after1,
            cw_all[1],
            dnz1,
            w_in(1, 0),
            x1,
            row(norm_gain, 1),
            grad_out,
            w_out(0),
            y0,
            z[0],
            v[0],
            xd[0],
            a2_all[0],
        ],
        [pltpu.VMEM((rows + HALO, inner), F32), pltpu.VMEM((rows, inner), F32)]
        + table_scratch()
        + [pltpu.VMEM((states, inner), F32), pltpu.VMEM((states, inner + EXTRA), F32)],
        flops=10**9,
    )
    g_out1 = wgrad(gated1, grad_out)
    g_inz1 = wgrad(normed[1], dz1)
    last, befores, sums, digits = exchange(payload, a2_all[0], "b")
    g_inx1 = wgrad(normed[1], dxc1)
    layer1 = lax.psum((g_out1, g_inz1, g_inx1, small1, gn1), AXIS)
    (dnz0,) = run(k_dnz, [res], [dz0, w_in(0, 1)], flops=mm)
    g_out0 = wgrad(gated0, de0)
    g_inz0 = wgrad(normed[0], dz0)
    dconv0, head0, small0 = backward(0, dy0, last, befores, sums, digits, h0)
    after0 = from_after(head0)
    dxc0, gn0, e0 = run(
        k_end,
        [act_b, shape((1, width), F32), res_b],
        [dconv0, after0, cw_all[0], dnz0, w_in(0, 0), x0, row(norm_gain, 0), e1],
        [pltpu.VMEM((rows + HALO, inner), F32)],
        flops=mm,
    )
    g_inx0 = wgrad(normed[0], dxc0)
    layer0 = lax.psum((g_out0, g_inz0, g_inx0, small0, gn0), AXIS)

    def stacked(i):
        return jnp.stack([layer0[i], layer1[i]])

    g_in = jnp.concatenate([stacked(1), stacked(2)][::-1], axis=2)
    smalls = stacked(3)
    at = 0
    n_x = rank + 2 * states
    g_xw = jnp.swapaxes(smalls[:, 0:n_x], 1, 2)
    g_dw = smalls[:, n_x : n_x + rank]
    at = n_x + rank
    g_al = jnp.swapaxes(smalls[:, at : at + states], 1, 2)
    at += states
    g_cw = jnp.swapaxes(smalls[:, at : at + taps], 1, 2)
    at += taps
    return (
        from_runs(hidden_out),
        from_runs(e0),
        stacked(4)[:, 0],
        g_in,
        g_cw,
        smalls[:, at],
        g_xw,
        g_dw,
        smalls[:, at + 1],
        g_al,
        smalls[:, at + 2],
        stacked(0),
    )


def solution(mesh):
    split = P(None, AXIS, None)
    return jax.shard_map(
        shards,
        mesh=mesh,
        in_specs=(split,) + (P(),) * 10 + (split,),
        out_specs=(split, split) + (P(),) * 10,
        check_vma=False,
    )
```

```python
import functools
import math

import jax
import jax.numpy as jnp
from jax import lax
from jax.experimental import pallas as pl
from jax.experimental.pallas import tpu as pltpu
from jax.sharding import PartitionSpec as P

BF16 = jnp.bfloat16
F32 = jnp.float32
LOG2E = 1.4426950408889634
LN2 = 0.6931471805599453
AXIS = "seq"
XD = 128
EXTRA = 256
CHUNK = 256
UNROLL = 8
HALO = 8
COST = pl.CostEstimate(flops=1, bytes_accessed=1, transcendentals=0)
LONG = pl.CostEstimate(flops=1, bytes_accessed=10**8, transcendentals=0)
BLOCKS = 16


def full(array):
    nd = len(array.shape)
    return pl.BlockSpec(array.shape, lambda i, nd=nd: (0,) * nd)


def part(shape, index):
    return pl.BlockSpec(shape, lambda i, index=index: index)


def run(kernel, outs, ins, scratch=(), turn=None, cost=COST):
    out_specs = [o[1] if isinstance(o, tuple) else full(o) for o in outs]
    outs = [o[0] if isinstance(o, tuple) else o for o in outs]
    arrays, specs = [], []
    for item in ins:
        if isinstance(item, tuple):
            arrays.append(item[0])
            specs.append(item[1])
        else:
            arrays.append(item)
            specs.append(full(item))
    body = kernel
    if turn:
        n = len(arrays)
        arrays.append(turn[0])
        specs.append(pl.BlockSpec(memory_space=pl.ANY))

        def body(*refs):
            kernel(*refs[:n], *refs[n + 1 :])

    results = pl.pallas_call(
        body,
        grid=(1,),
        in_specs=specs,
        out_specs=out_specs,
        out_shape=outs,
        scratch_shapes=list(scratch),
        compiler_params=pltpu.CompilerParams(vmem_limit_bytes=58 * 1024 * 1024),
        cost_estimate=cost,
    )(*arrays)
    if turn is not None:
        turn[:] = [results[-1]]
    return results


def shape(dims, dtype):
    return jax.ShapeDtypeStruct(dims, dtype)


def dot(a, b):
    return jnp.dot(a, b, preferred_element_type=F32)


def dot_t(a, b):
    return lax.dot_general(a, b, (((1,), (1,)), ((), ())), preferred_element_type=F32)


def dot_rows(a, b):
    return lax.dot_general(a, b, (((0,), (0,)), ((), ())), preferred_element_type=F32)


def sigmoid(v):
    return 1.0 / (1.0 + jnp.exp(-v))


def softplus(v):
    return jnp.maximum(v, 0.0) + jnp.log1p(jnp.exp(-jnp.abs(v)))


def slope(v):
    s = sigmoid(v)
    return s * (1.0 + v * (1.0 - s))


def wide(block, lanes):
    return jnp.concatenate([block] * (lanes // block.shape[1]), axis=1)


def rows_of_sums(parts):
    row = lax.broadcasted_iota(jnp.int32, parts[0].shape, 0)
    m4, m2, m1 = row < 4, (row & 2) == 0, (row & 1) == 0
    q = []
    for i in range(4):
        first = jnp.where(m4, parts[i], parts[i + 4])
        other = jnp.where(m4, parts[i + 4], parts[i])
        q.append(first + pltpu.roll(other, 4, 0))
    s = []
    for i in range(2):
        s.append(
            jnp.where(
                m2, q[i] + pltpu.roll(q[i], 6, 0), q[i + 2] + pltpu.roll(q[i + 2], 2, 0)
            )
        )
    return jnp.where(m1, s[0] + pltpu.roll(s[0], 7, 0), s[1] + pltpu.roll(s[1], 1, 0))


def fold(block):
    out = block[0:8]
    for k in range(8, block.shape[0], 8):
        out = out + block[k : k + 8]
    return out


def fold_lanes(block):
    out = block[:, 0:128]
    for k in range(128, block.shape[1], 128):
        out = out + block[:, k : k + 128]
    return out


def normed_of(x, gain):
    rinv = lax.rsqrt(jnp.mean(x * x, axis=-1, keepdims=True) + 1e-05)
    return (x * rinv * gain).astype(BF16)


def fill_table(xdf_ref, lhs_ref, bc_ref, rank, states):
    rows = xdf_ref.shape[0]
    n_i = lax.broadcasted_iota(jnp.int32, (states, XD), 0)
    lane = lax.broadcasted_iota(jnp.int32, (states, XD), 1)
    mask = ((lane == rank + n_i) | (lane == rank + states + n_i)).astype(F32)

    def body(i, carry):
        for j in range(UNROLL):
            t = i * UNROLL + j
            line = xdf_ref[pl.ds(t, 1), :]
            lhs_ref[pl.ds(pl.multiple_of(t * states, states), states), :] = (
                line * mask
            ).astype(BF16)
        return carry

    lax.fori_loop(0, rows // UNROLL, body, 0)
    k_i = lax.broadcasted_iota(jnp.int32, (XD, 256), 0)
    c_i = lax.broadcasted_iota(jnp.int32, (XD, 256), 1)
    low = rank + jnp.where(c_i >= 128, states, 0)
    pick = ((k_i >= low) & (k_i < low + states)).astype(BF16)
    bc_ref[...] = dot(lhs_ref[...], pick)


def state_rows(t, states):
    return pl.ds(pl.multiple_of(t * states, states), states)


def scan_ends(dt_ref, dtu_ref, bc_ref, a2_ref, end_ref):
    rows, inner = dt_ref.shape
    states = a2_ref.shape[0]

    def chunk(c, carry):
        lanes = pl.ds(pl.multiple_of(c * CHUNK, CHUNK), CHUNK)
        a2 = a2_ref[:, lanes]

        def body(i, h):
            for j in range(UNROLL):
                t = i * UNROLL + j
                a = jnp.exp2(dt_ref[pl.ds(t, 1), lanes] * a2)
                b = wide(bc_ref[state_rows(t, states), 0:128], CHUNK)
                h = a * h + dtu_ref[pl.ds(t, 1), lanes] * b
            return h

        end_ref[:, lanes] = lax.fori_loop(
            0, rows // UNROLL, body, jnp.zeros((states, CHUNK), F32)
        )
        return carry

    lax.fori_loop(0, inner // CHUNK, chunk, 0)


def scan_back_ends(dt_ref, dy_ref, bc_ref, a2_ref, end_ref):
    rows, inner = dt_ref.shape
    states = a2_ref.shape[0]

    def chunk(c, carry):
        lanes = pl.ds(pl.multiple_of(c * CHUNK, CHUNK), CHUNK)
        a2 = a2_ref[:, lanes]

        def body(i, back):
            for j in range(UNROLL):
                t = rows - 1 - (i * UNROLL + j)
                a = jnp.exp2(dt_ref[pl.ds(t, 1), lanes] * a2)
                c_row = wide(bc_ref[state_rows(t, states), 128:256], CHUNK)
                back = a * (dy_ref[pl.ds(t, 1), lanes] * c_row + back)
            return back

        end_ref[:, lanes] = lax.fori_loop(
            0, rows // UNROLL, body, jnp.zeros((states, CHUNK), F32)
        )
        return carry

    lax.fori_loop(0, inner // CHUNK, chunk, 0)


def scan_forward(dt_ref, dtu_ref, bc_ref, a2_ref, h_in_ref, y_ref):
    rows, inner = dt_ref.shape
    states = a2_ref.shape[0]

    def chunk(c, carry):
        lanes = pl.ds(pl.multiple_of(c * CHUNK, CHUNK), CHUNK)
        a2 = a2_ref[:, lanes]

        def body(i, h):
            parts = []
            for j in range(UNROLL):
                t = i * UNROLL + j
                a = jnp.exp2(dt_ref[pl.ds(t, 1), lanes] * a2)
                both = bc_ref[state_rows(t, states), :]
                h = a * h + dtu_ref[pl.ds(t, 1), lanes] * wide(both[:, 0:128], CHUNK)
                parts.append(fold(h * wide(both[:, 128:256], CHUNK)))
            y_ref[pl.ds(pl.multiple_of(i * UNROLL, UNROLL), UNROLL), lanes] = rows_of_sums(
                parts
            )
            return h

        lax.fori_loop(0, rows // UNROLL, body, h_in_ref[:, lanes])
        return carry

    lax.fori_loop(0, inner // CHUNK, chunk, 0)


def scan_both(
    dt_ref,
    dtu_ref,
    dy_ref,
    bc_ref,
    a2_ref,
    h_in_ref,
    g_in_ref,
    sgb_ref,
    sqa_ref,
    rate_ref,
    db_ref,
    dc_ref,
    a_s,
    ah_s,
):
    rows, inner = dt_ref.shape
    states = a2_ref.shape[0]
    db_ref[...] = jnp.zeros(db_ref.shape, F32)
    dc_ref[...] = jnp.zeros(dc_ref.shape, F32)

    def chunk(c, carry):
        lanes = pl.ds(pl.multiple_of(c * CHUNK, CHUNK), CHUNK)
        a2 = a2_ref[:, lanes]

        def ahead(i, h):
            for j in range(UNROLL):
                t = i * UNROLL + j
                at = state_rows(t, states)
                a = jnp.exp2(dt_ref[pl.ds(t, 1), lanes] * a2)
                b_row = wide(bc_ref[at, 0:128], CHUNK)
                ah = a * h
                a_s[at, :] = a
                ah_s[at, :] = ah
                h = ah + dtu_ref[pl.ds(t, 1), lanes] * b_row
                dc_ref[at, :] += fold_lanes(h * dy_ref[pl.ds(t, 1), lanes])
            return h

        lax.fori_loop(0, rows // UNROLL, ahead, h_in_ref[:, lanes])

        def retreat(i, carried):
            back, rate = carried
            block = rows // UNROLL - 1 - i
            gbs, qas = [None] * UNROLL, [None] * UNROLL
            for j in reversed(range(UNROLL)):
                t = block * UNROLL + j
                at = state_rows(t, states)
                both = bc_ref[at, :]
                g = dy_ref[pl.ds(t, 1), lanes] * wide(both[:, 128:256], CHUNK) + back
                q = g * ah_s[at, :]
                gbs[j] = fold(g * wide(both[:, 0:128], CHUNK))
                qas[j] = fold(q * a2)
                rate = rate + q * dt_ref[pl.ds(t, 1), lanes]
                db_ref[at, :] += fold_lanes(g * dtu_ref[pl.ds(t, 1), lanes])
                back = a_s[at, :] * g
            here = pl.ds(pl.multiple_of(block * UNROLL, UNROLL), UNROLL)
            sgb_ref[here, lanes] = rows_of_sums(gbs)
            sqa_ref[here, lanes] = rows_of_sums(qas)
            return back, rate

        _, rate = lax.fori_loop(
            0,
            rows // UNROLL,
            retreat,
            (g_in_ref[:, lanes], jnp.zeros((states, CHUNK), F32)),
        )
        rate_ref[:, lanes] = rate
        return carry

    lax.fori_loop(0, inner // CHUNK, chunk, 0)


def packed(state, total, wide_s):
    inner = total.shape[1]
    high = total.astype(BF16).astype(F32)
    rest = total - high
    wide_s[:, 0:inner] = state
    wide_s[:, inner:] = jnp.zeros((state.shape[0], EXTRA), F32)
    for k in range(inner // 128):
        wide_s[k : k + 1, inner : inner + 128] = high[:, k * 128 : (k + 1) * 128]
        wide_s[k : k + 1, inner + 128 : inner + 256] = rest[:, k * 128 : (k + 1) * 128]
    return wide_s[...].astype(BF16)


def unpack_total(wide_ref, m, total_ref, inner):
    for k in range(inner // 128):
        total_ref[m, 0:1, k * 128 : (k + 1) * 128] = (
            wide_ref[m, k : k + 1, inner : inner + 128]
            + wide_ref[m, k : k + 1, inner + 128 : inner + 256]
        )


def join_runs(states_ref, totals_ref, a2, digit, group, backward):
    inner = a2.shape[1]
    before = jnp.zeros(a2.shape, F32)
    entire = jnp.zeros(a2.shape, F32)
    sum_before = jnp.zeros((1, inner), F32)
    sum_entire = jnp.zeros((1, inner), F32)
    order = reversed(range(group)) if backward else range(group)
    for p in order:
        m = jnp.bitwise_xor(digit, p)
        state = states_ref[m, :, 0:inner]
        total = totals_ref[m, 0:1, :]
        through = jnp.exp2(total * a2)
        counts = (p > digit) if backward else (p < digit)
        before = jnp.where(counts, through * before + state, before)
        sum_before = jnp.where(counts, sum_before + total, sum_before)
        entire = through * entire + state
        sum_entire = sum_entire + total
    return before, sum_before, entire, sum_entire


def k_in(x_ref, g_ref, w_ref, n_ref, xc_ref, tail_ref):
    normed = normed_of(x_ref[...], g_ref[...])
    n_ref[...] = normed
    xc = dot(normed, w_ref[...]).astype(BF16)
    xc_ref[...] = xc
    tail_ref[...] = xc.astype(F32)[xc.shape[0] - HALO :, :]


def k_gate(n_ref, w_ref, z_ref):
    z_ref[...] = dot(n_ref[...], w_ref[...]).astype(BF16)


def k_dgated(e_ref, w_ref, out_ref):
    out_ref[...] = dot_t(e_ref[...], w_ref[...])


def conv_of(ext_s, halo_ref, xc_ref, cw_ref, cb_ref):
    rows = xc_ref.shape[0]
    taps = cw_ref.shape[0]
    ext_s[0:HALO, :] = halo_ref[...]
    ext_s[HALO:, :] = xc_ref[...].astype(F32)
    out = cb_ref[...]
    for k in range(taps):
        first = HALO - (taps - 1) + k
        out = out + cw_ref[k : k + 1, :] * ext_s[first : first + rows, :]
    return out


def k_local(
    rank, both, *refs
):
    refs = list(refs)
    halo, xc, cw, cb, xw, dw, db, a2 = refs[:8]
    refs = refs[8:]
    if both:
        dgated, z = refs[:2]
        refs = refs[2:]
    u_ref, xd_ref, v_ref, pay_ref = refs[:4]
    refs = refs[4:]
    if both:
        dy_ref = refs[0]
        refs = refs[1:]
    ext_s, dt_s, dtu_s, xdf_s, lhs_s, bc_s, end_s, wide_s = refs
    states = a2.shape[0]
    conv = conv_of(ext_s, halo, xc, cw, cb)
    u = (conv * sigmoid(conv)).astype(BF16)
    u_ref[...] = u
    xd = dot(u, xw[...]).astype(BF16)
    xd_ref[...] = xd
    xdf_s[...] = xd.astype(F32)
    v = dot(xd, dw[...]) + db[...]
    v_ref[...] = v
    dt = softplus(v)
    dt_s[...] = dt
    dtu_s[...] = dt * u.astype(F32)
    total = jnp.sum(dt, axis=0, keepdims=True)
    fill_table(xdf_s, lhs_s, bc_s, rank, states)
    scan_ends(dt_s, dtu_s, bc_s, a2, end_s)
    pay_ref[0:states, :] = packed(end_s[...], total, wide_s)
    if both:
        zf = z[...].astype(F32)
        dy_ref[...] = dgated[...] * (zf * sigmoid(zf))
        scan_back_ends(dt_s, dy_ref, bc_s, a2, end_s)
        pay_ref[states:, :] = packed(end_s[...], total, wide_s)


def k_join(group, nextgroup, mode, digits, *refs):
    refs = list(refs)
    received, refs = refs[:group], refs[group:]
    a2_ref, refs = refs[0], refs[1:]
    kinds = list(mode)
    n_pay = (nextgroup - 1) if (len(kinds) == 2 and nextgroup) else 1
    pays, refs = refs[:n_pay], refs[n_pay:]
    befores, refs = refs[: len(kinds)], refs[len(kinds) :]
    sums, refs = refs[: len(kinds)], refs[len(kinds) :]
    states_s, totals_s, wide_s = refs
    states, inner = a2_ref.shape
    digit = digits[0]
    nextdigit = digits[1]
    out = []
    for i in range(len(kinds)):
        for m in range(group):
            states_s[m] = received[m][i * states : (i + 1) * states, :].astype(F32)
            if i == 0:
                unpack_total(states_s, m, totals_s, inner)
        before, sum_before, entire, sum_entire = join_runs(
            states_s, totals_s, a2_ref[...], digit, group, kinds[i] == "b"
        )
        befores[i][...] = before
        sums[i][...] = sum_before
        out.append(packed(entire, sum_entire, wide_s))
    if len(kinds) == 2 and nextgroup:
        for m in range(1, nextgroup):
            ahead = jnp.bitwise_xor(nextdigit, m) > nextdigit
            pays[m - 1][...] = jnp.where(ahead, out[0].astype(F32), out[1].astype(F32)).astype(
                BF16
            )
    else:
        for i in range(len(kinds)):
            pays[0][i * states : (i + 1) * states, :] = out[i]


def entering(received, a2_ref, digit, befores, sums, states_s, totals_s, backward, lane0=0):
    lanes = a2_ref.shape[1]
    inner = received[0].shape[1] - EXTRA
    here = slice(lane0, lane0 + lanes)
    group = len(received) + 1
    states_s[0] = jnp.zeros(states_s.shape[1:], F32)
    totals_s[0] = jnp.zeros(totals_s.shape[1:], F32)
    for m in range(1, group):
        states_s[m] = received[m - 1][:, here].astype(F32)
        sums_m = received[m - 1][:, inner:].astype(F32)
        for k in range(lanes // 128):
            row = lane0 // 128 + k
            totals_s[m, 0:1, k * 128 : (k + 1) * 128] = (
                sums_m[row : row + 1, 0:128] + sums_m[row : row + 1, 128:256]
            )
    value, _, _, _ = join_runs(states_s, totals_s, a2_ref[...], digit, group, backward)
    for before, total in reversed(list(zip(befores, sums))):
        value = jnp.exp2(total[:, here] * a2_ref[...]) * value + before[:, here]
    return value


def k_mix(rank, last, n_recv, n_low, digits, core, *refs):
    refs = list(refs)
    received, refs = refs[:n_recv], refs[n_recv:]
    befores, refs = refs[:n_low], refs[n_low:]
    sums, refs = refs[:n_low], refs[n_low:]
    a2, u_ref, v_ref, xd_ref, z_ref, x_ref, sk_ref, ow_ref = refs[:8]
    refs = refs[8:]
    if last:
        dgated_ref, hid_ref, dz_ref, dz_keep, dz_send, gated_keep, gated_send, h_in_ref = refs[:8]
        y_ref, refs = refs[8], refs[9:]
    else:
        g_ref, iw_ref, y_ref, x1_ref, n_ref, xc_ref, tail_ref = refs[:7]
        gated_keep, gated_send, h_in_ref = refs[7:10]
        refs = refs[10:]
    gated_s, dt_s, dtu_s, xdf_s, lhs_s, bc_s, states_s, totals_s = refs
    h_in_ref[...] = entering(received, a2, digits[0], befores, sums, states_s, totals_s, False)
    uf = u_ref[...].astype(F32)
    dt = softplus(v_ref[...])
    dt_s[...] = dt
    dtu_s[...] = dt * uf
    xdf_s[...] = xd_ref[...].astype(F32)
    fill_table(xdf_s, lhs_s, bc_s, rank, a2.shape[0])
    scan_forward(dt_s, dtu_s, bc_s, a2, h_in_ref, y_ref)
    y = y_ref[...] + sk_ref[...] * u_ref[...].astype(F32)
    zf = z_ref[...].astype(F32)
    s = sigmoid(zf)
    gated = (y * (zf * s)).astype(BF16)
    gated_s[...] = gated
    gated_keep[...] = lane_half(gated_s, core[0])
    gated_send[...] = lane_half(gated_s, 1 - core[0])
    x1 = x_ref[...] + dot(gated, ow_ref[...])
    if last:
        dz_ref[...] = (dgated_ref[...] * y * (s * (1.0 + zf * (1.0 - s)))).astype(BF16)
        dz_keep[...] = lane_half(dz_ref, core[0])
        dz_send[...] = lane_half(dz_ref, 1 - core[0])
        hid_ref[...] = x1.astype(BF16)
    else:
        y_ref[...] = y
        x1_ref[...] = x1
        normed = normed_of(x1, g_ref[...])
        n_ref[...] = normed
        xc = dot(normed, iw_ref[...]).astype(BF16)
        xc_ref[...] = xc
        tail_ref[...] = xc.astype(F32)[xc.shape[0] - HALO :, :]


def k_scan(rank, lane0, n_recv, n_low, digits, *refs):
    refs = list(refs)
    received, refs = refs[:n_recv], refs[n_recv:]
    befores, refs = refs[:n_low], refs[n_low:]
    sums, refs = refs[:n_low], refs[n_low:]
    a2, u_ref, v_ref, dy_ref, h_in_ref, xd_ref = refs[:6]
    sgb_ref, sqa_ref, rate_ref, dbc_ref = refs[6:10]
    dt_s, dtu_s, xdf_s, lhs_s, bc_s, states_s, totals_s, db_s, dc_s, a_s, ah_s, g_s = refs[10:]
    states = a2.shape[0]
    rows = u_ref.shape[0]
    g_s[...] = entering(
        received, a2, digits[0], befores, sums, states_s, totals_s, True, lane0
    )
    dt = softplus(v_ref[...])
    dt_s[...] = dt
    dtu_s[...] = dt * u_ref[...].astype(F32)
    xdf_s[...] = xd_ref[...].astype(F32)
    fill_table(xdf_s, lhs_s, bc_s, rank, states)
    scan_both(
        dt_s, dtu_s, dy_ref, bc_s, a2, h_in_ref, g_s, sgb_ref, sqa_ref, rate_ref, db_s, dc_s, a_s, ah_s
    )
    rate_ref[...] = rate_ref[...] * (a2[...] * LN2)

    ones = jnp.ones((128, 128), BF16)

    def lane_sums(block):
        high = block.astype(BF16)
        rest = (block - high.astype(F32)).astype(BF16)
        return dot(high, ones) + dot(rest, ones)

    n_i = lax.broadcasted_iota(jnp.int32, (states, XD), 0)
    lane = lax.broadcasted_iota(jnp.int32, (states, XD), 1)
    mask_b = (lane == rank + n_i).astype(F32)
    mask_c = (lane == rank + states + n_i).astype(F32)
    db_s[...] = lane_sums(db_s[...])
    dc_s[...] = lane_sums(dc_s[...])

    def gather(i, carry):
        parts = []
        for j in range(UNROLL):
            at = state_rows(i * UNROLL + j, states)
            parts.append(fold(db_s[at, :] * mask_b + dc_s[at, :] * mask_c))
        dbc_ref[pl.ds(pl.multiple_of(i * UNROLL, UNROLL), UNROLL), :] = rows_of_sums(parts)
        return carry

    lax.fori_loop(0, rows // UNROLL, gather, 0)


def k_post(rank, n_parts, *refs):
    refs = list(refs)
    sgbs, refs = refs[:n_parts], refs[n_parts:]
    sqas, refs = refs[:n_parts], refs[n_parts:]
    rates, refs = refs[:n_parts], refs[n_parts:]
    dbcs, refs = refs[:n_parts], refs[n_parts:]
    u_ref, v_ref, xd_ref, dy_ref, halo, xc, cw, cb, xw, dw, sk_ref = refs[:11]
    dconv_ref, head_ref, small_ref, ext_s = refs[11:]
    states = rates[0].shape[0]
    rows, inner = u_ref.shape
    sgb = jnp.concatenate([ref[...] for ref in sgbs], axis=1)
    sqa = jnp.concatenate([ref[...] for ref in sqas], axis=1)
    dbc = dbcs[0][...]
    for ref in dbcs[1:]:
        dbc = dbc + ref[...]
    u = u_ref[...]
    uf = u.astype(F32)
    dy = dy_ref[...]
    v = v_ref[...]
    dpre = (LN2 * sqa + uf * sgb) * sigmoid(v)
    dpl = dpre.astype(BF16)
    dxd = (dot_t(dpl, dw[...]) + dbc).astype(BF16)
    du = softplus(v) * sgb + sk_ref[...] * dy + dot_t(dxd, xw[...])
    conv = conv_of(ext_s, halo, xc, cw, cb)
    dconv = du * slope(conv)
    dconv_ref[...] = dconv
    head_ref[...] = dconv[0:HALO, :]
    taps = cw.shape[0]
    width = rank + 2 * states
    g_x = dot_rows(dxd, u)
    g_dt = dot_rows(xd_ref[...], dpl)
    at = 0
    small_ref[at : at + width, :] = g_x[0:width]
    at += width
    small_ref[at : at + rank, :] = g_dt[0:rank]
    at += rank
    small_ref[at : at + states, :] = jnp.concatenate([ref[...] for ref in rates], axis=1)
    at += states
    for k in range(taps):
        first = HALO - (taps - 1) + k
        small_ref[at : at + 1, :] = jnp.sum(
            dconv * ext_s[first : first + rows, :], axis=0, keepdims=True
        )
        at += 1
    small_ref[at : at + 1, :] = jnp.sum(dconv, axis=0, keepdims=True)
    small_ref[at + 1 : at + 2, :] = jnp.sum(dpre, axis=0, keepdims=True)
    small_ref[at + 2 : at + 3, :] = jnp.sum(dy * uf, axis=0, keepdims=True)
    small_ref[at + 3 : at + 4, :] = jnp.zeros((1, inner), F32)


def lane_half(ref, which):
    half = ref.shape[1] // 2
    return ref[:, pl.ds(pl.multiple_of(which * half, 128), half)]


def conv_back(dce_s, dconv_ref, next_ref, cw_ref):
    rows = dconv_ref.shape[0]
    taps = cw_ref.shape[0]
    dce_s[0:rows, :] = dconv_ref[...]
    dce_s[rows:, :] = next_ref[...]
    out = cw_ref[taps - 1 : taps, :] * dce_s[0:rows, :]
    for k in range(taps - 1):
        first = taps - 1 - k
        out = out + cw_ref[k : k + 1, :] * dce_s[first : first + rows, :]
    return out.astype(BF16)


def norm_back(x, gain, e, dn):
    rinv = lax.rsqrt(jnp.mean(x * x, axis=-1, keepdims=True) + 1e-05)
    xhat = x * rinv
    dhat = dn * gain
    g_norm = jnp.sum(dn * xhat, axis=0, keepdims=True)
    return e + rinv * (dhat - xhat * jnp.mean(dhat * xhat, axis=-1, keepdims=True)), g_norm


def small_out(core, small_ref, g_norm, keep_ref, send_ref):
    rows, inner = small_ref.shape
    width = g_norm.shape[1]
    small_ref[rows - 1 : rows, 0:width] = g_norm
    for which, ref in ((core[0], keep_ref), (1 - core[0], send_ref)):
        ref[0:rows, :] = lane_half(small_ref, which)
        ref[rows:, :] = jnp.zeros((ref.shape[0] - rows, ref.shape[1]), F32)


def k_turn(
    rank,
    core,
    small_ref,
    dconv_ref,
    next_ref,
    cw_ref,
    dnz_ref,
    iw_ref,
    x_ref,
    g_ref,
    e_ref,
    ow_ref,
    y_ref,
    z_ref,
    v_ref,
    xd_ref,
    a2,
    dxc_keep,
    dxc_send,
    small_keep,
    small_send,
    e1_ref,
    de_ref,
    dy_ref,
    dz_ref,
    dz_keep,
    dz_send,
    pay_ref,
    small_s,
    dxc_s,
    dce_s,
    dt_s,
    xdf_s,
    lhs_s,
    bc_s,
    end_s,
    wide_s,
):
    dxc = conv_back(dce_s, dconv_ref, next_ref, cw_ref)
    dxc_s[...] = dxc
    dxc_keep[...] = lane_half(dxc_s, core[0])
    dxc_send[...] = lane_half(dxc_s, 1 - core[0])
    dn = dnz_ref[...] + dot_t(dxc, iw_ref[...])
    e1, g_norm = norm_back(x_ref[...], g_ref[...], e_ref[...].astype(F32), dn)
    small_s[...] = small_ref[...]
    small_out(core, small_s, g_norm, small_keep, small_send)
    e1_ref[...] = e1
    de = e1.astype(BF16)
    de_ref[...] = de
    dgated = dot_t(de, ow_ref[...])
    zf = z_ref[...].astype(F32)
    s = sigmoid(zf)
    dy_ref[...] = dgated * (zf * s)
    dz_ref[...] = (dgated * y_ref[...] * (s * (1.0 + zf * (1.0 - s)))).astype(BF16)
    dz_keep[...] = lane_half(dz_ref, core[0])
    dz_send[...] = lane_half(dz_ref, 1 - core[0])
    states = a2.shape[0]
    dt = softplus(v_ref[...])
    dt_s[...] = dt
    total = jnp.sum(dt, axis=0, keepdims=True)
    xdf_s[...] = xd_ref[...].astype(F32)
    fill_table(xdf_s, lhs_s, bc_s, rank, states)
    scan_back_ends(dt_s, dy_ref, bc_s, a2, end_s)
    pay_ref[...] = packed(end_s[...], total, wide_s)


def k_end(
    core,
    small_ref,
    dconv_ref,
    next_ref,
    cw_ref,
    dnz_ref,
    iw_ref,
    x_ref,
    g_ref,
    e_ref,
    dxc_keep,
    dxc_send,
    small_keep,
    small_send,
    e0_ref,
    small_s,
    dxc_s,
    dce_s,
):
    dxc = conv_back(dce_s, dconv_ref, next_ref, cw_ref)
    dxc_s[...] = dxc
    dxc_keep[...] = lane_half(dxc_s, core[0])
    dxc_send[...] = lane_half(dxc_s, 1 - core[0])
    dn = dnz_ref[...] + dot_t(dxc, iw_ref[...])
    e0, g_norm = norm_back(x_ref[...], g_ref[...], e_ref[...], dn)
    small_s[...] = small_ref[...]
    small_out(core, small_s, g_norm, small_keep, small_send)
    e0_ref[...] = e0.astype(BF16)


def k_dnz(dz_ref, iw_ref, out_ref):
    out_ref[...] = dot_t(dz_ref[...], iw_ref[...])


def k_chip_sum(n_pairs, has_small, *refs):
    refs = list(refs)
    pairs, refs = [refs[4 * i : 4 * i + 4] for i in range(n_pairs)], refs[4 * n_pairs :]
    if has_small:
        (small_a, small_b), refs = refs[:2], refs[2:]
    (s_ref,) = refs
    blocks = s_ref.shape[0]
    rows = pairs[0][0].shape[1] // blocks
    for i, (a, a_came, b, b_came) in enumerate(pairs):
        total = dot_rows(
            jnp.concatenate([a[...], a_came[...]], axis=0),
            jnp.concatenate([b[...], b_came[...]], axis=0),
        )
        s_ref[:, i * rows : (i + 1) * rows, :] = total.reshape(blocks, rows, total.shape[1])
    if has_small:
        n = small_a.shape[0] // blocks
        top = n_pairs * rows
        s_ref[:, top:, :] = jnp.zeros((blocks, s_ref.shape[1] - top, s_ref.shape[2]), F32)
        for k in range(blocks):
            here = slice(k * n, (k + 1) * n)
            s_ref[k, top : top + n, :] = small_a[here, :] + small_b[here, :]


def k_first(n_pairs, has_small, place, *refs):
    keep_a, keep_b, send_a, send_b, s_ref = refs[-5:]
    k_chip_sum(n_pairs, has_small, *refs[:-5], s_ref)
    blocks = s_ref.shape[0]
    half = s_ref.shape[2] // 2
    x, y = place[0] & 1, (place[0] >> 1) & 1
    for i in range(blocks // 2):
        at = (i >> 1) * 4 + (i & 1) * 2
        keep_a[i] = s_ref[at + x, :, 0:half]
        send_a[i] = s_ref[at + 1 - x, :, 0:half].astype(BF16)
        at = (i >> 1) * 4 + (i & 1)
        keep_b[i] = s_ref[at + 2 * y, :, half:]
        send_b[i] = s_ref[at + 2 * (1 - y), :, half:].astype(BF16)


def k_second(place, keep_a, keep_b, came_a, came_b, stay_a, stay_b, send_a, send_b):
    x, y = place[0] & 1, (place[0] >> 1) & 1
    for i in range(stay_a.shape[0]):
        for keep, came, stay, send, bit in (
            (keep_a, came_a, stay_a, send_a, y),
            (keep_b, came_b, stay_b, send_b, x),
        ):
            at = 2 * i + bit
            stay[i] = keep[at] + came[at].astype(F32)
            at = 2 * i + 1 - bit
            send[i] = (keep[at] + came[at].astype(F32)).astype(BF16)


def k_third(place, stay_a, stay_b, came_a, came_b, keep, send1, send2, send3):
    z = (place[0] >> 2) & 3
    half = stay_a.shape[2]
    for m, ref in enumerate((keep, send1, send2, send3)):
        at = jnp.bitwise_xor(z, m)
        ref[:, 0:half] = (stay_a[at] + came_a[at].astype(F32)).astype(ref.dtype)
        ref[:, half:] = (stay_b[at] + came_b[at].astype(F32)).astype(ref.dtype)


def k_fourth(keep, came1, came2, came3, out):
    out[...] = (
        keep[...] + came1[...].astype(F32) + came2[...].astype(F32) + came3[...].astype(F32)
    ).astype(BF16)


def k_stack(mine, came1, came2, came3, out_a, out_b):
    half = out_a.shape[2]
    for m, ref in enumerate((mine, came1, came2, came3)):
        out_a[m] = ref[:, 0:half]
        out_b[m] = ref[:, half:]


def k_chip(place, *refs):
    left, right, out = refs[0:4], refs[4:8], refs[8]
    half = left[0].shape[2]
    xy, z = place[0] & 3, (place[0] >> 2) & 3
    for d in range(4):
        for m in range(4):
            at = jnp.bitwise_xor(z, m) * 4 + jnp.bitwise_xor(xy, d)
            out[at, :, 0:half] = left[d][m]
            out[at, :, half:] = right[d][m]


def k_place(split_rows, core, mine, came, *refs):
    out, done = refs[-2:]
    done[...] = jnp.zeros(done.shape, F32)
    blocks, rows, lanes = mine.shape
    own = core[0] == 0
    a = mine[...].astype(F32).reshape(blocks * rows, lanes)
    b = came[...].astype(F32).reshape(blocks * rows, lanes)
    low, high = jnp.where(own, a, b), jnp.where(own, b, a)
    if split_rows:
        out[0], out[1] = low, high
    else:
        out[:, 0:lanes] = low
        out[:, lanes:] = high


def k_place_small(row0, core, mine, came, out):
    blocks, _, lanes = mine.shape
    n = out.shape[0] // blocks
    first = jnp.where(core[0] == 0, 0, 1)
    for src, half in ((mine, first), (came, 1 - first)):
        for k in range(blocks):
            out[k * n : (k + 1) * n, pl.ds(pl.multiple_of(half * lanes, 128), lanes)] = src[
                k, row0 : row0 + 16, :
            ].astype(F32)[0:n]


def shards(
    hidden_in,
    norm_gain,
    in_weight,
    conv_weight,
    conv_bias,
    xproj_weight,
    dtproj_weight,
    dt_bias,
    a_log,
    skip_gain,
    out_weight,
    hidden_grad,
):
    layers, width, _ = in_weight.shape
    inner, states = a_log.shape[1], a_log.shape[2]
    rank = dtproj_weight.shape[1]
    taps = conv_weight.shape[2]
    seqs, own, _ = hidden_in.shape
    ndev = lax.axis_size(AXIS)
    me = lax.axis_index(AXIS)
    core = me % 2
    chip = me // 2
    rows = seqs * own
    assert layers == 2 and seqs == 2 and ndev % 2 == 0
    assert inner % CHUNK == 0 and inner // 128 <= states and rank + 2 * states <= XD

    pairs = [(i, i ^ 1) for i in range(ndev)]
    turn = []
    call = functools.partial(run, turn=turn)

    def to_runs(block):
        mine = lax.dynamic_index_in_dim(block, core, 0, keepdims=False)
        other = lax.dynamic_index_in_dim(block, 1 - core, 0, keepdims=False)
        came = lax.ppermute(other, AXIS, pairs)
        first = jnp.where(core == 0, mine, came)
        second = jnp.where(core == 0, came, mine)
        return jnp.concatenate([first, second], axis=0)

    def from_runs(run_block):
        halves = run_block.reshape((2, own) + run_block.shape[1:])
        mine = lax.dynamic_index_in_dim(halves, core, 0, keepdims=False)
        other = lax.dynamic_index_in_dim(halves, 1 - core, 0, keepdims=False)
        came = lax.ppermute(other, AXIS, pairs)
        first = jnp.where(core == 0, mine, came)
        second = jnp.where(core == 0, came, mine)
        return jnp.stack([first, second], axis=0)

    def from_before(block):
        return lax.ppermute(block, AXIS, [(i, i + 2) for i in range(ndev - 2)])

    def from_after(block):
        return lax.ppermute(block, AXIS, [(i + 2, i) for i in range(ndev - 2)])

    bits = (ndev // 2).bit_length() - 1
    assert 2 << bits == ndev and bits > 2
    rounds = []
    low = 0
    while low < bits:
        n = 2 if bits - low >= 2 else 1
        rounds.append((low, 1 << n))
        low += n

    def digit_of(r):
        low, group = rounds[r]
        return (chip >> low) & (group - 1)

    def digits_of(r):
        nxt = digit_of(r + 1) if r + 1 < len(rounds) else jnp.zeros_like(chip)
        return jnp.stack([digit_of(r), nxt]).astype(jnp.int32)

    def send(block, r, m, which):
        low, group = rounds[r]
        flip = (m << low) << 1
        route = [(i, i ^ flip) for i in range(ndev)]
        if which == "up":
            route = [(i, j) for i, j in route if j > i]
        if which == "down":
            route = [(i, j) for i, j in route if j < i]
        return lax.ppermute(block, AXIS, route)

    smem = pl.BlockSpec(memory_space=pltpu.SMEM)
    core_s = (core[None].astype(jnp.int32), smem)

    def swap(block):
        return lax.ppermute(block, AXIS, pairs)

    pay = shape((states, inner + EXTRA), BF16)

    def exchange(payload, a2, mode, meanwhile=()):
        meanwhile = dict(enumerate(meanwhile))
        befores = [[] for _ in mode]
        sums = [[] for _ in mode]
        for r, (low, group) in enumerate(rounds[:-1]):
            received = [payload] + [send(payload, r, m, "all") for m in range(1, group)]
            if r in meanwhile:
                meanwhile[r]()
            final = r + 2 == len(rounds)
            split = len(mode) == 2 and final
            nextgroup = rounds[r + 1][1] if split else 0
            pays = (
                [pay] * (nextgroup - 1)
                if split
                else [shape((states * len(mode), inner + EXTRA), BF16)]
            )
            outs = call(
                functools.partial(k_join, group, nextgroup, mode),
                pays
                + [shape((states, inner), F32)] * len(mode)
                + [shape((1, inner), F32)] * len(mode),
                [(digits_of(r), smem)] + received + [a2],
                [
                    pltpu.VMEM((group, states, inner + EXTRA), F32),
                    pltpu.VMEM((group, 8, inner), F32),
                    pltpu.VMEM((states, inner + EXTRA), F32),
                ],
            )
            sent, outs = outs[: len(pays)], outs[len(pays) :]
            for i in range(len(mode)):
                befores[i].append(outs[i])
                sums[i].append(outs[len(mode) + i])
            payload = sent if split else sent[0]
        r = len(rounds) - 1
        if len(mode) == 2:
            last = [send(payload[m - 1], r, m, "all") for m in range(1, rounds[r][1])]
        else:
            way = "up" if mode == "f" else "down"
            last = [send(payload, r, m, way) for m in range(1, rounds[r][1])]
        for step in sorted(meanwhile):
            if step >= r:
                meanwhile[step]()
        return last, sum(befores, []), sum(sums, []), digits_of(r)

    a2_all = -jnp.exp(jnp.swapaxes(a_log, 1, 2)) * LOG2E
    cw_all = jnp.swapaxes(conv_weight, 1, 2)
    xw_all = jnp.pad(xproj_weight, ((0, 0), (0, 0), (0, XD - xproj_weight.shape[2])))
    dw_all = jnp.pad(dtproj_weight, ((0, 0), (0, XD - rank), (0, 0)))

    def row(array, l):
        return array[l : l + 1, :]

    def w_in(l, half):
        return in_weight, part((None, width, inner), (l, 0, half))

    def w_out(l):
        return out_weight, part((None, inner, width), (l, 0, 0))

    def table_scratch():
        return [
            pltpu.VMEM((rows, XD), F32),
            pltpu.VMEM((rows * states, XD), BF16),
            pltpu.VMEM((rows * states, 256), F32),
        ]

    act = shape((rows, inner), F32)
    act_b = shape((rows, inner), BF16)
    res = shape((rows, width), F32)
    res_b = shape((rows, width), BF16)
    edge = shape((HALO, inner), F32)
    mm = 2 * rows * width * inner

    grad_out = to_runs(hidden_grad)
    x0 = to_runs(hidden_in).astype(F32)

    normed = [None, None]
    xc = [None, None]
    halo = [None, None]
    z = [None, None]
    u = [None, None]
    xd = [None, None]
    v = [None, None]

    normed[0], xc[0], tail = call(
        k_in, [res_b, act_b, edge], [x0, row(norm_gain, 0), w_in(0, 0)]
    )

    def before_scan(l, tail, dgated=None):
        halo[l] = from_before(tail)
        (z[l],) = call(k_gate, [act_b], [normed[l], w_in(l, 1)])
        if l == 0:
            (dgated1,) = call(k_dgated, [act], [grad_out, w_out(1)])
        both = dgated is not None
        outs = call(
            functools.partial(k_local, rank, both),
            [
                act_b,
                shape((rows, XD), BF16),
                act,
                shape((states * (2 if both else 1), inner + EXTRA), BF16),
            ]
            + ([act] if both else []),
            [
                halo[l],
                xc[l],
                cw_all[l],
                row(conv_bias, l),
                xw_all[l],
                dw_all[l],
                row(dt_bias, l),
                a2_all[l],
            ]
            + ([dgated, z[l]] if both else []),
            [pltpu.VMEM((rows + HALO, inner), F32)]
            + [pltpu.VMEM((rows, inner), F32)] * 2
            + table_scratch()
            + [pltpu.VMEM((states, inner), F32), pltpu.VMEM((states, inner + EXTRA), F32)],
            cost=LONG,
        )
        u[l], xd[l], v[l] = outs[:3]
        return (outs[3], dgated1) if l == 0 else outs[3:]

    def join_scratch():
        group = rounds[-1][1]
        return [
            pltpu.VMEM((group, states, inner), F32),
            pltpu.VMEM((group, 8, inner), F32),
        ]

    def mix(l, parts, extra, outs):
        final = l == layers - 1
        last, befores, sums, digits = parts
        befores, sums = befores[: len(rounds) - 1], sums[: len(rounds) - 1]
        return call(
            functools.partial(k_mix, rank, final, len(last), len(befores)),
            outs,
            [(digits, smem), core_s]
            + last
            + befores
            + sums
            + [a2_all[l], u[l], v[l], xd[l], z[l], residual[l], row(skip_gain, l), w_out(l)]
            + extra,
            ([act_scratch] if final else [])
            + [pltpu.VMEM((rows, inner), BF16)]
            + [act_scratch] * 2
            + table_scratch()
            + join_scratch(),
            cost=LONG,
        )

    half_b = shape((rows, width), BF16)
    entry = shape((states, inner), F32)
    act_scratch = pltpu.VMEM((rows, inner), F32)
    residual = [x0, None]
    payload, dgated1 = before_scan(0, tail)
    parts = exchange(payload, a2_all[0], "f")
    y0, x1, normed[1], xc[1], tail, gated_keep, gated_send, h0 = mix(
        0,
        parts,
        [row(norm_gain, 1), w_in(1, 0)],
        [act, res, res_b, act_b, edge, half_b, half_b, entry],
    )
    residual[1] = x1
    gated0_pair = (gated_keep, swap(gated_send))
    payload, dy1 = before_scan(1, tail, dgated1)
    parts = exchange(payload, a2_all[1], "fb")
    n_small = rank + 2 * states + rank + states + taps + 4
    small = shape((n_small, inner), F32)
    small_pad = -(-n_small // (BLOCKS * 2)) * BLOCKS * 2 if n_small % BLOCKS else n_small

    n_parts = 2
    lanes = inner // n_parts

    def scan(l, i, dy, parts, h_in):
        last, befores, sums, digits = parts
        n_low = len(rounds) - 1
        cut = part((rows, lanes), (0, i))
        cut_s = part((states, lanes), (0, i))
        return call(
            functools.partial(k_scan, rank, i * lanes, len(last), n_low),
            [shape((rows, lanes), F32)] * 2 + [shape((states, lanes), F32), shape((rows, XD), F32)],
            [(digits, smem)]
            + last
            + befores[-n_low:]
            + sums[-n_low:]
            + [(a2_all[l], cut_s), (u[l], cut), (v[l], cut), (dy, cut), (h_in, cut_s), xd[l]],
            [pltpu.VMEM((rows, lanes), F32)] * 2
            + table_scratch()
            + [
                pltpu.VMEM((rounds[-1][1], states, lanes), F32),
                pltpu.VMEM((rounds[-1][1], 8, lanes), F32),
            ]
            + [pltpu.VMEM((rows * states, 128), F32)] * 2
            + [pltpu.VMEM((rows * states, CHUNK), F32)] * 2
            + [pltpu.VMEM((states, lanes), F32)],
            cost=LONG,
        )

    def post(l, scans, dy):
        return call(
            functools.partial(k_post, rank, n_parts),
            [act, edge, small],
            [outs[k] for k in range(4) for outs in scans]
            + [
                u[l],
                v[l],
                xd[l],
                dy,
                halo[l],
                xc[l],
                cw_all[l],
                row(conv_bias, l),
                xw_all[l],
                dw_all[l],
                row(skip_gain, l),
            ],
            [pltpu.VMEM((rows + HALO, inner), F32)],
            cost=LONG,
        )


    def over(block, flip):
        return lax.ppermute(block, AXIS, [(i, i ^ (flip << 1)) for i in range(ndev)])

    place_s = (chip[None].astype(jnp.int32), smem)

    def summed(matrices, smalls):
        ins = []
        each = width // BLOCKS
        for (a, a_came), (b, b_came) in matrices:
            ins += [a, a_came, b, b_came]
        r = each * len(matrices)
        if smalls is not None:
            ins += list(smalls)
            r += 16
        has_small = smalls is not None
        half = width // 2
        if ndev != 2 * BLOCKS:
            (mine,) = call(
                functools.partial(k_chip_sum, len(matrices), has_small),
                [shape((BLOCKS, r, width), F32)],
                ins,
            )
            empty = jnp.zeros((2,) + mine.shape, F32)
            total = lax.psum(lax.dynamic_update_index_in_dim(empty, mine, core, 0), AXIS)
            total = total.astype(BF16)
            for _ in range(5):
                yield None
            yield (
                lax.dynamic_index_in_dim(total, core, 0, keepdims=False),
                lax.dynamic_index_in_dim(total, 1 - core, 0, keepdims=False),
            )
            return
        n = BLOCKS // 2
        keep_a, keep_b, send_a, send_b = call(
            functools.partial(k_first, len(matrices), has_small),
            [shape((n, r, half), F32)] * 2 + [shape((n, r, half), BF16)] * 2,
            [place_s] + ins,
            [pltpu.VMEM((BLOCKS, r, width), F32)],
        )
        came_a, came_b = over(send_a, 1), over(send_b, 2)
        yield None
        n = BLOCKS // 4
        stay_a, stay_b, send_a, send_b = call(
            k_second,
            [shape((n, r, half), F32)] * 2 + [shape((n, r, half), BF16)] * 2,
            [place_s, keep_a, keep_b, came_a, came_b],
        )
        came_a, came_b = over(send_a, 2), over(send_b, 1)
        yield None
        keep, *sends = call(
            k_third,
            [shape((r, width), F32)] + [shape((r, width), BF16)] * 3,
            [place_s, stay_a, stay_b, came_a, came_b],
        )
        came = [over(send_m, 4 * (m + 1)) for m, send_m in enumerate(sends)]
        yield None
        (done,) = call(k_fourth, [shape((r, width), BF16)], [keep] + came)
        came = [over(done, 4 * m) for m in (1, 2, 3)]
        yield None
        left, right = call(k_stack, [shape((4, r, half), BF16)] * 2, [done] + came)
        left_y, right_x = over(left, 2), over(right, 1)
        lefts = [left, over(left, 1), left_y, over(left_y, 1)]
        rights = [right, right_x, over(right, 2), over(right_x, 2)]
        yield None
        (mine,) = call(
            k_chip, [shape((BLOCKS, r, width), BF16)], [place_s] + lefts + rights
        )
        yield mine, swap(mine)

    def placed(halves, i, whole, block, index, split_rows, before):
        each = width // BLOCKS
        steps = 4
        per = BLOCKS // steps
        source = pl.BlockSpec((per, each, width), lambda g: (g, i, 0))
        anywhere = pl.BlockSpec(memory_space=pl.ANY)
        ins = [core_s[0], halves[0], halves[1], turn[0]]
        specs = [smem, source, source, anywhere]
        aliases = {}
        if before is not None:
            ins.append(before)
            specs.append(anywhere)
            aliases = {4: 0}
        out, turn[0] = pl.pallas_call(
            functools.partial(k_place, split_rows),
            grid=(steps,),
            in_specs=specs,
            out_specs=[pl.BlockSpec(block, index), pl.BlockSpec((8, 128), lambda g: (0, 0))],
            out_shape=[whole, shape((8, 128), F32)],
            input_output_aliases=aliases,
            compiler_params=pltpu.CompilerParams(vmem_limit_bytes=58 * 1024 * 1024),
            cost_estimate=COST,
        )(*ins)
        return out

    g_out_shape = shape((layers, 2, width, width), F32)
    g_in_shape = shape((layers, width, 2 * inner), F32)
    quarter = width // 4
    out_block = (None, 2, quarter, width)
    in_block = (None, quarter, inner)

    def out_at(l):
        return lambda g: (l, 0, g, 0)

    def in_at(l, half):
        return lambda g: (l, g, half)

    def placed_small(halves, i):
        each = width // BLOCKS
        (out,) = call(
            functools.partial(k_place_small, i * each),
            [shape((small_pad, inner), F32)],
            [core_s, halves[0], halves[1]],
        )
        return out

    half_small = shape((small_pad, width), F32)
    n1_pair = (normed[1], swap(normed[1]))
    n0_pair = (normed[0], swap(normed[0]))
    e1_pair = (grad_out, swap(grad_out))

    hidden_out, dz1, dz_keep, dz_send, gated_keep, gated_send, h1 = mix(
        1, parts, [dgated1], [res_b, act_b] + [half_b] * 4 + [entry]
    )
    a_sum = summed(
        [((gated_keep, swap(gated_send)), e1_pair), (n1_pair, (dz_keep, swap(dz_send)))], None
    )
    scans = [scan(1, 0, dy1, parts, h1)]
    next(a_sum)
    scans.append(scan(1, 1, dy1, parts, h1))
    next(a_sum)
    dconv1, head1, small1 = post(1, scans, dy1)
    after1 = from_after(head1)
    (dnz1,) = call(k_dnz, [res], [dz1, w_in(1, 1)])
    next(a_sum)
    (
        dxc_keep,
        dxc_send,
        small_keep,
        small_send,
        e1,
        de0,
        dy0,
        dz0,
        dz_keep,
        dz_send,
        payload,
    ) = call(
        functools.partial(k_turn, rank),
        [half_b, half_b, half_small, half_small, res, res_b, act, act_b, half_b, half_b, pay],
        [
            core_s,
            small1,
            dconv1,
            after1,
            cw_all[1],
            dnz1,
            w_in(1, 0),
            x1,
            row(norm_gain, 1),
            grad_out,
            w_out(0),
            y0,
            z[0],
            v[0],
            xd[0],
            a2_all[0],
        ],
        [
            pltpu.VMEM((n_small, inner), F32),
            pltpu.VMEM((rows, inner), BF16),
            pltpu.VMEM((rows + HALO, inner), F32),
            pltpu.VMEM((rows, inner), F32),
        ]
        + table_scratch()
        + [pltpu.VMEM((states, inner), F32), pltpu.VMEM((states, inner + EXTRA), F32)],
        cost=LONG,
    )
    b_sum = summed(
        [
            (n1_pair, (dxc_keep, swap(dxc_send))),
            (gated0_pair, (de0, swap(de0))),
            (n0_pair, (dz_keep, swap(dz_send))),
        ],
        (small_keep, swap(small_send)),
    )
    kept = {}

    def first_shadow():
        (kept["dnz0"],) = call(k_dnz, [res], [dz0, w_in(0, 1)])

    def second_shadow():
        next(b_sum)

    parts = exchange(payload, a2_all[0], "b", (first_shadow, second_shadow))
    dnz0 = kept["dnz0"]
    next(a_sum)
    scans = [scan(0, 0, dy0, parts, h0)]
    next(a_sum)
    next(b_sum)
    scans.append(scan(0, 1, dy0, parts, h0))
    next(b_sum)
    dconv0, head0, small0 = post(0, scans, dy0)
    after0 = from_after(head0)
    sum_a1 = next(a_sum)
    dxc_keep, dxc_send, small_keep, small_send, e0 = call(
        k_end,
        [half_b, half_b, half_small, half_small, res_b],
        [core_s, small0, dconv0, after0, cw_all[0], dnz0, w_in(0, 0), x0, row(norm_gain, 0), e1],
        [
            pltpu.VMEM((n_small, inner), F32),
            pltpu.VMEM((rows, inner), BF16),
            pltpu.VMEM((rows + HALO, inner), F32),
        ],
        cost=LONG,
    )
    c_sum = summed([(n0_pair, (dxc_keep, swap(dxc_send)))], (small_keep, swap(small_send)))
    next(c_sum)
    g_out = placed(sum_a1, 0, g_out_shape, out_block, out_at(1), True, None)
    next(b_sum)
    next(c_sum)
    g_in = placed(sum_a1, 1, g_in_shape, in_block, in_at(1, 1), False, None)
    next(c_sum)
    next(b_sum)
    next(c_sum)
    next(c_sum)
    sum_b = next(b_sum)
    small1 = placed_small(sum_b, 3)
    g_in = placed(sum_b, 0, g_in_shape, in_block, in_at(1, 0), False, g_in)
    g_out = placed(sum_b, 1, g_out_shape, out_block, out_at(0), True, g_out)
    sum_c = next(c_sum)
    g_in = placed(sum_b, 2, g_in_shape, in_block, in_at(0, 1), False, g_in)
    g_in = placed(sum_c, 0, g_in_shape, in_block, in_at(0, 0), False, g_in)
    small0 = placed_small(sum_c, 1)

    smalls = jnp.stack([small0, small1])
    n_x = rank + 2 * states
    g_xw = jnp.swapaxes(smalls[:, 0:n_x], 1, 2)
    g_dw = smalls[:, n_x : n_x + rank]
    at = n_x + rank
    g_al = jnp.swapaxes(smalls[:, at : at + states], 1, 2)
    at += states
    g_cw = jnp.swapaxes(smalls[:, at : at + taps], 1, 2)
    at += taps
    return (
        from_runs(hidden_out),
        from_runs(e0),
        smalls[:, n_small - 1, 0:width],
        g_in,
        g_cw,
        smalls[:, at],
        g_xw,
        g_dw,
        smalls[:, at + 1],
        g_al,
        smalls[:, at + 2],
        g_out.reshape(layers, inner, width),
    )


def solution(mesh):
    split = P(None, AXIS, None)
    return jax.shard_map(
        shards,
        mesh=mesh,
        in_specs=(split,) + (P(),) * 10 + (split,),
        out_specs=(split, split) + (P(),) * 10,
        check_vma=False,
    )
```

```python
import functools
import math

import jax
import jax.numpy as jnp
from jax import lax
from jax.experimental import pallas as pl
from jax.experimental.pallas import tpu as pltpu
from jax.sharding import PartitionSpec as P

BF16 = jnp.bfloat16
F32 = jnp.float32
LOG2E = 1.4426950408889634
LN2 = 0.6931471805599453
AXIS = "seq"
XD = 128
EXTRA = 256
CHUNK = 512
UNROLL = 8
HALO = 8
COST = pl.CostEstimate(flops=1, bytes_accessed=1, transcendentals=0)
LONG = pl.CostEstimate(flops=1, bytes_accessed=10**8, transcendentals=0)
BLOCKS = 16


def full(array):
    nd = len(array.shape)
    return pl.BlockSpec(array.shape, lambda i, nd=nd: (0,) * nd)


def part(shape, index):
    return pl.BlockSpec(shape, lambda i, index=index: index)


class Row:
    def __init__(self, array, index):
        self.array, self.index = array, index


def run(kernel, outs, ins, scratch=(), turn=None, cost=COST):
    out_specs = [o[1] if isinstance(o, tuple) else full(o) for o in outs]
    outs = [o[0] if isinstance(o, tuple) else o for o in outs]
    arrays, specs, picks = [], [], {}
    for item in ins:
        if isinstance(item, Row):
            picks[len(arrays)] = item.index
            item = item.array
        if isinstance(item, tuple):
            arrays.append(item[0])
            specs.append(item[1])
        else:
            arrays.append(item)
            specs.append(full(item))
    n = len(arrays)
    if turn:
        arrays.append(turn[0])
        specs.append(pl.BlockSpec(memory_space=pl.ANY))
    after = len(arrays)

    def body(*refs):
        given = list(refs[:n])
        for k, index in picks.items():
            given[k] = given[k].at[index : index + 1, :]
        kernel(*given, *refs[after:])

    results = pl.pallas_call(
        body,
        grid=(1,),
        in_specs=specs,
        out_specs=out_specs,
        out_shape=outs,
        scratch_shapes=list(scratch),
        compiler_params=pltpu.CompilerParams(vmem_limit_bytes=58 * 1024 * 1024),
        cost_estimate=cost,
    )(*arrays)
    if turn is not None:
        turn[:] = [results[-1]]
    return results


def shape(dims, dtype):
    return jax.ShapeDtypeStruct(dims, dtype)


def dot(a, b):
    return jnp.dot(a, b, preferred_element_type=F32)


def dot_t(a, b):
    return lax.dot_general(a, b, (((1,), (1,)), ((), ())), preferred_element_type=F32)


def dot_rows(a, b):
    return lax.dot_general(a, b, (((0,), (0,)), ((), ())), preferred_element_type=F32)


def sigmoid(v):
    return 1.0 / (1.0 + jnp.exp(-v))


def softplus(v):
    return jnp.maximum(v, 0.0) + jnp.log1p(jnp.exp(-jnp.abs(v)))


def slope(v):
    s = sigmoid(v)
    return s * (1.0 + v * (1.0 - s))


def wide(block, lanes):
    return jnp.concatenate([block] * (lanes // block.shape[1]), axis=1)


def rows_of_sums(parts):
    row = lax.broadcasted_iota(jnp.int32, parts[0].shape, 0)
    m4, m2, m1 = row < 4, (row & 2) == 0, (row & 1) == 0
    q = []
    for i in range(4):
        first = jnp.where(m4, parts[i], parts[i + 4])
        other = jnp.where(m4, parts[i + 4], parts[i])
        q.append(first + pltpu.roll(other, 4, 0))
    s = []
    for i in range(2):
        s.append(
            jnp.where(
                m2, q[i] + pltpu.roll(q[i], 6, 0), q[i + 2] + pltpu.roll(q[i + 2], 2, 0)
            )
        )
    return jnp.where(m1, s[0] + pltpu.roll(s[0], 7, 0), s[1] + pltpu.roll(s[1], 1, 0))


def fold(block):
    out = block[0:8]
    for k in range(8, block.shape[0], 8):
        out = out + block[k : k + 8]
    return out


def fold_lanes(block):
    out = block[:, 0:128]
    for k in range(128, block.shape[1], 128):
        out = out + block[:, k : k + 128]
    return out


def normed_of(x, gain):
    rinv = lax.rsqrt(jnp.mean(x * x, axis=-1, keepdims=True) + 1e-05)
    return (x * rinv * gain).astype(BF16)


def fill_table(xdf_ref, lhs_ref, bc_ref, rank, states):
    rows = xdf_ref.shape[0]
    n_i = lax.broadcasted_iota(jnp.int32, (states, XD), 0)
    lane = lax.broadcasted_iota(jnp.int32, (states, XD), 1)
    mask = ((lane == rank + n_i) | (lane == rank + states + n_i)).astype(F32)

    def body(i, carry):
        for j in range(UNROLL):
            t = i * UNROLL + j
            line = xdf_ref[pl.ds(t, 1), :]
            lhs_ref[pl.ds(pl.multiple_of(t * states, states), states), :] = (
                line * mask
            ).astype(BF16)
        return carry

    lax.fori_loop(0, rows // UNROLL, body, 0)
    k_i = lax.broadcasted_iota(jnp.int32, (XD, 256), 0)
    c_i = lax.broadcasted_iota(jnp.int32, (XD, 256), 1)
    low = rank + jnp.where(c_i >= 128, states, 0)
    pick = ((k_i >= low) & (k_i < low + states)).astype(BF16)
    bc_ref[...] = dot(lhs_ref[...], pick)


def state_rows(t, states):
    return pl.ds(pl.multiple_of(t * states, states), states)


def scan_ends(dt_ref, dtu_ref, bc_ref, a2_ref, end_ref):
    rows, inner = dt_ref.shape
    states = a2_ref.shape[0]

    def chunk(c, carry):
        lanes = pl.ds(pl.multiple_of(c * CHUNK, CHUNK), CHUNK)
        a2 = a2_ref[:, lanes]

        def body(i, h):
            for j in range(UNROLL):
                t = i * UNROLL + j
                a = jnp.exp2(dt_ref[pl.ds(t, 1), lanes] * a2)
                b = wide(bc_ref[state_rows(t, states), 0:128], CHUNK)
                h = a * h + dtu_ref[pl.ds(t, 1), lanes] * b
            return h

        end_ref[:, lanes] = lax.fori_loop(
            0, rows // UNROLL, body, jnp.zeros((states, CHUNK), F32)
        )
        return carry

    lax.fori_loop(0, inner // CHUNK, chunk, 0)


def scan_back_ends(dt_ref, dy_ref, bc_ref, a2_ref, end_ref):
    rows, inner = dt_ref.shape
    states = a2_ref.shape[0]

    def chunk(c, carry):
        lanes = pl.ds(pl.multiple_of(c * CHUNK, CHUNK), CHUNK)
        a2 = a2_ref[:, lanes]

        def body(i, back):
            for j in range(UNROLL):
                t = rows - 1 - (i * UNROLL + j)
                a = jnp.exp2(dt_ref[pl.ds(t, 1), lanes] * a2)
                c_row = wide(bc_ref[state_rows(t, states), 128:256], CHUNK)
                back = a * (dy_ref[pl.ds(t, 1), lanes] * c_row + back)
            return back

        end_ref[:, lanes] = lax.fori_loop(
            0, rows // UNROLL, body, jnp.zeros((states, CHUNK), F32)
        )
        return carry

    lax.fori_loop(0, inner // CHUNK, chunk, 0)


def scan_forward(dt_ref, dtu_ref, bc_ref, a2_ref, h_in_ref, y_ref):
    rows, inner = dt_ref.shape
    states = a2_ref.shape[0]

    def chunk(c, carry):
        lanes = pl.ds(pl.multiple_of(c * CHUNK, CHUNK), CHUNK)
        a2 = a2_ref[:, lanes]

        def body(i, h):
            parts = []
            for j in range(UNROLL):
                t = i * UNROLL + j
                a = jnp.exp2(dt_ref[pl.ds(t, 1), lanes] * a2)
                both = bc_ref[state_rows(t, states), :]
                h = a * h + dtu_ref[pl.ds(t, 1), lanes] * wide(both[:, 0:128], CHUNK)
                parts.append(fold(h * wide(both[:, 128:256], CHUNK)))
            y_ref[pl.ds(pl.multiple_of(i * UNROLL, UNROLL), UNROLL), lanes] = rows_of_sums(
                parts
            )
            return h

        lax.fori_loop(0, rows // UNROLL, body, h_in_ref[:, lanes])
        return carry

    lax.fori_loop(0, inner // CHUNK, chunk, 0)


def scan_both(
    dt_ref,
    dtu_ref,
    dy_ref,
    bc_ref,
    a2_ref,
    h_in_ref,
    g_in_ref,
    sgb_ref,
    sqa_ref,
    rate_ref,
    db_ref,
    dc_ref,
    a_s,
    ah_s,
):
    rows, inner = dt_ref.shape
    states = a2_ref.shape[0]
    db_ref[...] = jnp.zeros(db_ref.shape, F32)
    dc_ref[...] = jnp.zeros(dc_ref.shape, F32)

    def chunk(c, carry):
        lanes = pl.ds(pl.multiple_of(c * CHUNK, CHUNK), CHUNK)
        a2 = a2_ref[:, lanes]

        def ahead(i, h):
            for j in range(UNROLL):
                t = i * UNROLL + j
                at = state_rows(t, states)
                a = jnp.exp2(dt_ref[pl.ds(t, 1), lanes] * a2)
                b_row = wide(bc_ref[at, 0:128], CHUNK)
                ah = a * h
                a_s[at, :] = a
                ah_s[at, :] = ah
                h = ah + dtu_ref[pl.ds(t, 1), lanes] * b_row
                dc_ref[at, :] += fold_lanes(h * dy_ref[pl.ds(t, 1), lanes])
            return h

        lax.fori_loop(0, rows // UNROLL, ahead, h_in_ref[:, lanes])

        def retreat(i, carried):
            back, rate = carried
            block = rows // UNROLL - 1 - i
            gbs, qas = [None] * UNROLL, [None] * UNROLL
            for j in reversed(range(UNROLL)):
                t = block * UNROLL + j
                at = state_rows(t, states)
                both = bc_ref[at, :]
                g = dy_ref[pl.ds(t, 1), lanes] * wide(both[:, 128:256], CHUNK) + back
                q = g * ah_s[at, :]
                gbs[j] = fold(g * wide(both[:, 0:128], CHUNK))
                qas[j] = fold(q * a2)
                rate = rate + q * dt_ref[pl.ds(t, 1), lanes]
                db_ref[at, :] += fold_lanes(g * dtu_ref[pl.ds(t, 1), lanes])
                back = a_s[at, :] * g
            here = pl.ds(pl.multiple_of(block * UNROLL, UNROLL), UNROLL)
            sgb_ref[here, lanes] = rows_of_sums(gbs)
            sqa_ref[here, lanes] = rows_of_sums(qas)
            return back, rate

        _, rate = lax.fori_loop(
            0,
            rows // UNROLL,
            retreat,
            (g_in_ref[:, lanes], jnp.zeros((states, CHUNK), F32)),
        )
        rate_ref[:, lanes] = rate
        return carry

    lax.fori_loop(0, inner // CHUNK, chunk, 0)


def packed(state, total, wide_s):
    inner = total.shape[1]
    high = total.astype(BF16).astype(F32)
    rest = total - high
    wide_s[:, 0:inner] = state
    wide_s[:, inner:] = jnp.zeros((state.shape[0], EXTRA), F32)
    for k in range(inner // 128):
        wide_s[k : k + 1, inner : inner + 128] = high[:, k * 128 : (k + 1) * 128]
        wide_s[k : k + 1, inner + 128 : inner + 256] = rest[:, k * 128 : (k + 1) * 128]
    return wide_s[...].astype(BF16)


def unpack_total(wide_ref, m, total_ref, inner):
    for k in range(inner // 128):
        total_ref[m, 0:1, k * 128 : (k + 1) * 128] = (
            wide_ref[m, k : k + 1, inner : inner + 128]
            + wide_ref[m, k : k + 1, inner + 128 : inner + 256]
        )


def join_runs(states_ref, totals_ref, a2, digit, group, backward):
    inner = a2.shape[1]
    before = jnp.zeros(a2.shape, F32)
    entire = jnp.zeros(a2.shape, F32)
    sum_before = jnp.zeros((1, inner), F32)
    sum_entire = jnp.zeros((1, inner), F32)
    order = reversed(range(group)) if backward else range(group)
    for p in order:
        m = jnp.bitwise_xor(digit, p)
        state = states_ref[m, :, 0:inner]
        total = totals_ref[m, 0:1, :]
        through = jnp.exp2(total * a2)
        counts = (p > digit) if backward else (p < digit)
        before = jnp.where(counts, through * before + state, before)
        sum_before = jnp.where(counts, sum_before + total, sum_before)
        entire = through * entire + state
        sum_entire = sum_entire + total
    return before, sum_before, entire, sum_entire


def k_in(x_ref, g_ref, w_ref, n_ref, xc_ref, tail_ref):
    normed = normed_of(x_ref[...], g_ref[...])
    n_ref[...] = normed
    xc = dot(normed, w_ref[...]).astype(BF16)
    xc_ref[...] = xc
    tail_ref[...] = xc.astype(F32)[xc.shape[0] - HALO :, :]


def k_gate(n_ref, w_ref, z_ref):
    z_ref[...] = dot(n_ref[...], w_ref[...]).astype(BF16)


def k_dgated(e_ref, w_ref, out_ref):
    out_ref[...] = dot_t(e_ref[...], w_ref[...])


def conv_of(ext_s, halo_ref, xc_ref, cw_ref, cb_ref):
    rows = xc_ref.shape[0]
    taps = cw_ref.shape[0]
    ext_s[0:HALO, :] = halo_ref[...]
    ext_s[HALO:, :] = xc_ref[...].astype(F32)
    out = cb_ref[...]
    for k in range(taps):
        first = HALO - (taps - 1) + k
        out = out + cw_ref[k : k + 1, :] * ext_s[first : first + rows, :]
    return out


def k_local(
    rank, both, *refs
):
    refs = list(refs)
    halo, xc, cw, cb, xw, dw, db, a2 = refs[:8]
    refs = refs[8:]
    if both:
        dgated, z = refs[:2]
        refs = refs[2:]
    u_ref, xd_ref, v_ref, pay_ref = refs[:4]
    refs = refs[4:]
    if both:
        dy_ref = refs[0]
        refs = refs[1:]
    ext_s, dt_s, dtu_s, xdf_s, lhs_s, bc_s, end_s, wide_s = refs
    states = a2.shape[0]
    conv = conv_of(ext_s, halo, xc, cw, cb)
    u = (conv * sigmoid(conv)).astype(BF16)
    u_ref[...] = u
    xd = dot(u, xw[...]).astype(BF16)
    xd_ref[...] = xd
    xdf_s[...] = xd.astype(F32)
    v = dot(xd, dw[...]) + db[...]
    v_ref[...] = v
    dt = softplus(v)
    dt_s[...] = dt
    dtu_s[...] = dt * u.astype(F32)
    total = jnp.sum(dt, axis=0, keepdims=True)
    fill_table(xdf_s, lhs_s, bc_s, rank, states)
    scan_ends(dt_s, dtu_s, bc_s, a2, end_s)
    pay_ref[0:states, :] = packed(end_s[...], total, wide_s)
    if both:
        zf = z[...].astype(F32)
        dy_ref[...] = dgated[...] * (zf * sigmoid(zf))
        scan_back_ends(dt_s, dy_ref, bc_s, a2, end_s)
        pay_ref[states:, :] = packed(end_s[...], total, wide_s)


def k_join(group, nextgroup, mode, digits, *refs):
    refs = list(refs)
    received, refs = refs[:group], refs[group:]
    a2_ref, refs = refs[0], refs[1:]
    kinds = list(mode)
    n_pay = (nextgroup - 1) if (len(kinds) == 2 and nextgroup) else 1
    pays, refs = refs[:n_pay], refs[n_pay:]
    befores, refs = refs[: len(kinds)], refs[len(kinds) :]
    sums, refs = refs[: len(kinds)], refs[len(kinds) :]
    states_s, totals_s, wide_s = refs
    states, inner = a2_ref.shape
    digit = digits[0]
    nextdigit = digits[1]
    out = []
    for i in range(len(kinds)):
        for m in range(group):
            states_s[m] = received[m][i * states : (i + 1) * states, :].astype(F32)
            if i == 0:
                unpack_total(states_s, m, totals_s, inner)
        before, sum_before, entire, sum_entire = join_runs(
            states_s, totals_s, a2_ref[...], digit, group, kinds[i] == "b"
        )
        befores[i][...] = before
        sums[i][...] = sum_before
        out.append(packed(entire, sum_entire, wide_s))
    if len(kinds) == 2 and nextgroup:
        for m in range(1, nextgroup):
            ahead = jnp.bitwise_xor(nextdigit, m) > nextdigit
            pays[m - 1][...] = jnp.where(ahead, out[0].astype(F32), out[1].astype(F32)).astype(
                BF16
            )
    else:
        for i in range(len(kinds)):
            pays[0][i * states : (i + 1) * states, :] = out[i]


def entering(received, a2_ref, digit, befores, sums, states_s, totals_s, backward, lane0=0):
    lanes = a2_ref.shape[1]
    inner = received[0].shape[1] - EXTRA
    here = slice(lane0, lane0 + lanes)
    group = len(received) + 1
    states_s[0] = jnp.zeros(states_s.shape[1:], F32)
    totals_s[0] = jnp.zeros(totals_s.shape[1:], F32)
    for m in range(1, group):
        states_s[m] = received[m - 1][:, here].astype(F32)
        sums_m = received[m - 1][:, inner:].astype(F32)
        for k in range(lanes // 128):
            row = lane0 // 128 + k
            totals_s[m, 0:1, k * 128 : (k + 1) * 128] = (
                sums_m[row : row + 1, 0:128] + sums_m[row : row + 1, 128:256]
            )
    value, _, _, _ = join_runs(states_s, totals_s, a2_ref[...], digit, group, backward)
    for before, total in reversed(list(zip(befores, sums))):
        value = jnp.exp2(total[:, here] * a2_ref[...]) * value + before[:, here]
    return value


def k_mix(rank, last, n_recv, n_low, digits, core, *refs):
    refs = list(refs)
    received, refs = refs[:n_recv], refs[n_recv:]
    befores, refs = refs[:n_low], refs[n_low:]
    sums, refs = refs[:n_low], refs[n_low:]
    a2, u_ref, v_ref, xd_ref, z_ref, x_ref, sk_ref, ow_ref = refs[:8]
    refs = refs[8:]
    if last:
        dgated_ref, hid_mine, hid_other, dz_ref, dz_keep, gated_keep, sends, h_in_ref = refs[:8]
        y_ref, hid_s, refs = refs[8], refs[9], refs[10:]
    else:
        g_ref, iw_ref, y_ref, x1_ref, n_ref, xc_ref, tail_ref = refs[:7]
        gated_keep, sends, h_in_ref = refs[7:10]
        refs = refs[10:]
    gated_s, dt_s, dtu_s, xdf_s, lhs_s, bc_s, states_s, totals_s = refs
    h_in_ref[...] = entering(received, a2, digits[0], befores, sums, states_s, totals_s, False)
    uf = u_ref[...].astype(F32)
    dt = softplus(v_ref[...])
    dt_s[...] = dt
    dtu_s[...] = dt * uf
    xdf_s[...] = xd_ref[...].astype(F32)
    fill_table(xdf_s, lhs_s, bc_s, rank, a2.shape[0])
    scan_forward(dt_s, dtu_s, bc_s, a2, h_in_ref, y_ref)
    y = y_ref[...] + sk_ref[...] * u_ref[...].astype(F32)
    zf = z_ref[...].astype(F32)
    s = sigmoid(zf)
    gated = (y * (zf * s)).astype(BF16)
    gated_s[...] = gated
    rows = gated.shape[0]
    gated_keep[...] = lane_half(gated_s, core[0])
    sends[0:rows, :] = lane_half(gated_s, 1 - core[0])
    x1 = x_ref[...] + dot(gated, ow_ref[...])
    if last:
        dz_ref[...] = (dgated_ref[...] * y * (s * (1.0 + zf * (1.0 - s)))).astype(BF16)
        dz_keep[...] = lane_half(dz_ref, core[0])
        sends[rows:, :] = lane_half(dz_ref, 1 - core[0])
        hid_s[...] = x1
        hid_mine[...] = row_half(hid_s, core[0]).astype(BF16)
        hid_other[...] = row_half(hid_s, 1 - core[0]).astype(BF16)
    else:
        y_ref[...] = y
        x1_ref[...] = x1
        normed = normed_of(x1, g_ref[...])
        n_ref[...] = normed
        sends[rows:, :] = normed
        xc = dot(normed, iw_ref[...]).astype(BF16)
        xc_ref[...] = xc
        tail_ref[...] = xc.astype(F32)[xc.shape[0] - HALO :, :]


def k_scan(rank, lane0, n_recv, n_low, digits, *refs):
    refs = list(refs)
    received, refs = refs[:n_recv], refs[n_recv:]
    befores, refs = refs[:n_low], refs[n_low:]
    sums, refs = refs[:n_low], refs[n_low:]
    a2, u_ref, v_ref, dy_ref, h_in_ref, xd_ref = refs[:6]
    sgb_ref, sqa_ref, rate_ref, dbc_ref = refs[6:10]
    dt_s, dtu_s, xdf_s, lhs_s, bc_s, states_s, totals_s, db_s, dc_s, a_s, ah_s, g_s = refs[10:]
    states = a2.shape[0]
    rows = u_ref.shape[0]
    g_s[...] = entering(
        received, a2, digits[0], befores, sums, states_s, totals_s, True, lane0
    )
    dt = softplus(v_ref[...])
    dt_s[...] = dt
    dtu_s[...] = dt * u_ref[...].astype(F32)
    xdf_s[...] = xd_ref[...].astype(F32)
    fill_table(xdf_s, lhs_s, bc_s, rank, states)
    scan_both(
        dt_s, dtu_s, dy_ref, bc_s, a2, h_in_ref, g_s, sgb_ref, sqa_ref, rate_ref, db_s, dc_s, a_s, ah_s
    )
    rate_ref[...] = rate_ref[...] * (a2[...] * LN2)

    ones = jnp.ones((128, 128), BF16)

    def lane_sums(block):
        high = block.astype(BF16)
        rest = (block - high.astype(F32)).astype(BF16)
        return dot(high, ones) + dot(rest, ones)

    n_i = lax.broadcasted_iota(jnp.int32, (states, XD), 0)
    lane = lax.broadcasted_iota(jnp.int32, (states, XD), 1)
    mask_b = (lane == rank + n_i).astype(F32)
    mask_c = (lane == rank + states + n_i).astype(F32)
    db_s[...] = lane_sums(db_s[...])
    dc_s[...] = lane_sums(dc_s[...])

    def gather(i, carry):
        parts = []
        for j in range(UNROLL):
            at = state_rows(i * UNROLL + j, states)
            parts.append(fold(db_s[at, :] * mask_b + dc_s[at, :] * mask_c))
        dbc_ref[pl.ds(pl.multiple_of(i * UNROLL, UNROLL), UNROLL), :] = rows_of_sums(parts)
        return carry

    lax.fori_loop(0, rows // UNROLL, gather, 0)


def k_post(rank, n_parts, *refs):
    refs = list(refs)
    sgbs, refs = refs[:n_parts], refs[n_parts:]
    sqas, refs = refs[:n_parts], refs[n_parts:]
    rates, refs = refs[:n_parts], refs[n_parts:]
    dbcs, refs = refs[:n_parts], refs[n_parts:]
    u_ref, v_ref, xd_ref, dy_ref, halo, xc, cw, cb, xw, dw, sk_ref = refs[:11]
    dconv_ref, head_ref, small_ref, ext_s = refs[11:]
    states = rates[0].shape[0]
    rows, inner = u_ref.shape
    sgb = jnp.concatenate([ref[...] for ref in sgbs], axis=1)
    sqa = jnp.concatenate([ref[...] for ref in sqas], axis=1)
    dbc = dbcs[0][...]
    for ref in dbcs[1:]:
        dbc = dbc + ref[...]
    u = u_ref[...]
    uf = u.astype(F32)
    dy = dy_ref[...]
    v = v_ref[...]
    dpre = (LN2 * sqa + uf * sgb) * sigmoid(v)
    dpl = dpre.astype(BF16)
    dxd = (dot_t(dpl, dw[...]) + dbc).astype(BF16)
    du = softplus(v) * sgb + sk_ref[...] * dy + dot_t(dxd, xw[...])
    conv = conv_of(ext_s, halo, xc, cw, cb)
    dconv = du * slope(conv)
    dconv_ref[...] = dconv
    head_ref[...] = dconv[0:HALO, :]
    taps = cw.shape[0]
    width = rank + 2 * states
    g_x = dot_rows(dxd, u)
    g_dt = dot_rows(xd_ref[...], dpl)
    at = 0
    small_ref[at : at + width, :] = g_x[0:width]
    at += width
    small_ref[at : at + rank, :] = g_dt[0:rank]
    at += rank
    small_ref[at : at + states, :] = jnp.concatenate([ref[...] for ref in rates], axis=1)
    at += states
    for k in range(taps):
        first = HALO - (taps - 1) + k
        small_ref[at : at + 1, :] = jnp.sum(
            dconv * ext_s[first : first + rows, :], axis=0, keepdims=True
        )
        at += 1
    small_ref[at : at + 1, :] = jnp.sum(dconv, axis=0, keepdims=True)
    small_ref[at + 1 : at + 2, :] = jnp.sum(dpre, axis=0, keepdims=True)
    small_ref[at + 2 : at + 3, :] = jnp.sum(dy * uf, axis=0, keepdims=True)
    small_ref[at + 3 : at + 4, :] = jnp.zeros((1, inner), F32)


def row_half(ref, which):
    half = ref.shape[0] // 2
    return ref[pl.ds(pl.multiple_of(which * half, 16), half), :]


def lane_half(ref, which):
    half = ref.shape[1] // 2
    return ref[:, pl.ds(pl.multiple_of(which * half, 128), half)]


def conv_back(dce_s, dconv_ref, next_ref, cw_ref):
    rows = dconv_ref.shape[0]
    taps = cw_ref.shape[0]
    dce_s[0:rows, :] = dconv_ref[...]
    dce_s[rows:, :] = next_ref[...]
    out = cw_ref[taps - 1 : taps, :] * dce_s[0:rows, :]
    for k in range(taps - 1):
        first = taps - 1 - k
        out = out + cw_ref[k : k + 1, :] * dce_s[first : first + rows, :]
    return out.astype(BF16)


def norm_back(x, gain, e, dn):
    rinv = lax.rsqrt(jnp.mean(x * x, axis=-1, keepdims=True) + 1e-05)
    xhat = x * rinv
    dhat = dn * gain
    g_norm = jnp.sum(dn * xhat, axis=0, keepdims=True)
    return e + rinv * (dhat - xhat * jnp.mean(dhat * xhat, axis=-1, keepdims=True)), g_norm


def small_out(core, small_ref, g_norm, keep_ref, sends, at):
    rows, inner = small_ref.shape
    width = g_norm.shape[1]
    small_ref[rows - 1 : rows, 0:width] = g_norm
    pad = keep_ref.shape[0] - rows
    for which, ref, first in ((core[0], keep_ref, 0), (1 - core[0], sends, at)):
        block = lane_half(small_ref, which)
        block = jnp.concatenate([block, jnp.zeros((pad, block.shape[1]), F32)], axis=0)
        ref[first : first + rows + pad, :] = block.astype(ref.dtype)
    sends[at + rows + pad :, :] = jnp.zeros((sends.shape[0] - at - rows - pad, inner // 2), BF16)


def k_turn(
    rank,
    core,
    small_ref,
    dconv_ref,
    next_ref,
    cw_ref,
    dnz_ref,
    iw_ref,
    x_ref,
    g_ref,
    e_ref,
    ow_ref,
    y_ref,
    z_ref,
    v_ref,
    xd_ref,
    a2,
    dxc_keep,
    small_keep,
    e1_ref,
    de_ref,
    dy_ref,
    dz_ref,
    dz_keep,
    sends,
    pay_ref,
    small_s,
    dxc_s,
    dce_s,
    dt_s,
    xdf_s,
    lhs_s,
    bc_s,
    end_s,
    wide_s,
):
    dxc = conv_back(dce_s, dconv_ref, next_ref, cw_ref)
    rows = dxc.shape[0]
    dxc_s[...] = dxc
    dxc_keep[...] = lane_half(dxc_s, core[0])
    sends[0:rows, :] = lane_half(dxc_s, 1 - core[0])
    dn = dnz_ref[...] + dot_t(dxc, iw_ref[...])
    e1, g_norm = norm_back(x_ref[...], g_ref[...], e_ref[...].astype(F32), dn)
    small_s[...] = small_ref[...]
    small_out(core, small_s, g_norm, small_keep, sends, 3 * rows)
    e1_ref[...] = e1
    de = e1.astype(BF16)
    de_ref[...] = de
    sends[2 * rows : 3 * rows, :] = de
    dgated = dot_t(de, ow_ref[...])
    zf = z_ref[...].astype(F32)
    s = sigmoid(zf)
    dy_ref[...] = dgated * (zf * s)
    dz_ref[...] = (dgated * y_ref[...] * (s * (1.0 + zf * (1.0 - s)))).astype(BF16)
    dz_keep[...] = lane_half(dz_ref, core[0])
    sends[rows : 2 * rows, :] = lane_half(dz_ref, 1 - core[0])
    states = a2.shape[0]
    dt = softplus(v_ref[...])
    dt_s[...] = dt
    total = jnp.sum(dt, axis=0, keepdims=True)
    xdf_s[...] = xd_ref[...].astype(F32)
    fill_table(xdf_s, lhs_s, bc_s, rank, states)
    scan_back_ends(dt_s, dy_ref, bc_s, a2, end_s)
    pay_ref[...] = packed(end_s[...], total, wide_s)


def k_end(
    core,
    small_ref,
    dconv_ref,
    next_ref,
    cw_ref,
    dnz_ref,
    iw_ref,
    x_ref,
    g_ref,
    e_ref,
    dxc_keep,
    small_keep,
    sends,
    e0_mine,
    e0_other,
    small_s,
    dxc_s,
    dce_s,
    e0_s,
):
    dxc = conv_back(dce_s, dconv_ref, next_ref, cw_ref)
    rows = dxc.shape[0]
    dxc_s[...] = dxc
    dxc_keep[...] = lane_half(dxc_s, core[0])
    sends[0:rows, :] = lane_half(dxc_s, 1 - core[0])
    dn = dnz_ref[...] + dot_t(dxc, iw_ref[...])
    e0, g_norm = norm_back(x_ref[...], g_ref[...], e_ref[...], dn)
    small_s[...] = small_ref[...]
    small_out(core, small_s, g_norm, small_keep, sends, rows)
    e0_s[...] = e0
    e0_mine[...] = row_half(e0_s, core[0]).astype(BF16)
    e0_other[...] = row_half(e0_s, 1 - core[0]).astype(BF16)


def k_dnz(dz_ref, iw_ref, out_ref):
    out_ref[...] = dot_t(dz_ref[...], iw_ref[...])


def k_chip_sum(n_pairs, has_small, *refs):
    refs = list(refs)
    pairs, refs = [refs[4 * i : 4 * i + 4] for i in range(n_pairs)], refs[4 * n_pairs :]
    if has_small:
        (small_a, small_b), refs = refs[:2], refs[2:]
    (s_ref,) = refs
    blocks = s_ref.shape[0]
    rows = pairs[0][0].shape[1] // blocks
    for i, (a, a_came, b, b_came) in enumerate(pairs):
        total = dot_rows(
            jnp.concatenate([a[...], a_came[...]], axis=0),
            jnp.concatenate([b[...], b_came[...]], axis=0),
        )
        s_ref[:, i * rows : (i + 1) * rows, :] = total.reshape(blocks, rows, total.shape[1])
    if has_small:
        n = small_a.shape[0] // blocks
        top = n_pairs * rows
        s_ref[:, top:, :] = jnp.zeros((blocks, s_ref.shape[1] - top, s_ref.shape[2]), F32)
        small = small_a[...] + small_b[...].astype(F32)[0 : small_a.shape[0]]
        for k in range(blocks):
            s_ref[k, top : top + n, :] = small[k * n : (k + 1) * n]


def k_first(n_pairs, has_small, place, *refs):
    keep_a, keep_b, send_a, send_b, s_ref = refs[-5:]
    k_chip_sum(n_pairs, has_small, *refs[:-5], s_ref)
    blocks = s_ref.shape[0]
    half = s_ref.shape[2] // 2
    x, y = place[0] & 1, (place[0] >> 1) & 1
    for i in range(blocks // 2):
        at = (i >> 1) * 4 + (i & 1) * 2
        keep_a[i] = s_ref[at + x, :, 0:half]
        send_a[i] = s_ref[at + 1 - x, :, 0:half].astype(BF16)
        at = (i >> 1) * 4 + (i & 1)
        keep_b[i] = s_ref[at + 2 * y, :, half:]
        send_b[i] = s_ref[at + 2 * (1 - y), :, half:].astype(BF16)


def k_second(place, keep_a, keep_b, came_a, came_b, stay_a, stay_b, send_a, send_b):
    x, y = place[0] & 1, (place[0] >> 1) & 1
    for i in range(stay_a.shape[0]):
        for keep, came, stay, send, bit in (
            (keep_a, came_a, stay_a, send_a, y),
            (keep_b, came_b, stay_b, send_b, x),
        ):
            at = 2 * i + bit
            stay[i] = keep[at] + came[at].astype(F32)
            at = 2 * i + 1 - bit
            send[i] = (keep[at] + came[at].astype(F32)).astype(BF16)


def k_third(place, stay_a, stay_b, came_a, came_b, keep, send1, send2, send3):
    z = (place[0] >> 2) & 3
    half = stay_a.shape[2]
    for m, ref in enumerate((keep, send1, send2, send3)):
        at = jnp.bitwise_xor(z, m)
        ref[:, 0:half] = (stay_a[at] + came_a[at].astype(F32)).astype(ref.dtype)
        ref[:, half:] = (stay_b[at] + came_b[at].astype(F32)).astype(ref.dtype)


def k_fourth(keep, came1, came2, came3, out):
    out[...] = (
        keep[...] + came1[...].astype(F32) + came2[...].astype(F32) + came3[...].astype(F32)
    ).astype(BF16)


def k_stack(mine, came1, came2, came3, out_a, out_b):
    half = out_a.shape[2]
    for m, ref in enumerate((mine, came1, came2, came3)):
        out_a[m] = ref[:, 0:half]
        out_b[m] = ref[:, half:]


def k_chip(place, *refs):
    left, right, out = refs[0:4], refs[4:8], refs[8]
    half = left[0].shape[2]
    xy, z = place[0] & 3, (place[0] >> 2) & 3
    for d in range(4):
        for m in range(4):
            at = jnp.bitwise_xor(z, m) * 4 + jnp.bitwise_xor(xy, d)
            out[at, :, 0:half] = left[d][m]
            out[at, :, half:] = right[d][m]


def in_order(core, sources):
    if len(sources) == 1:
        return sources[0][:, 0].astype(F32), sources[0][:, 1].astype(F32)
    own = core[0] == 0
    a, b = sources[0][...].astype(F32), sources[1][...].astype(F32)
    return jnp.where(own, a, b), jnp.where(own, b, a)


def k_place(n_sources, split_rows, core, *refs):
    out, done = refs[-2:]
    done[...] = jnp.zeros(done.shape, F32)
    low, high = in_order(core, refs[:n_sources])
    blocks, rows, lanes = low.shape
    low, high = low.reshape(blocks * rows, lanes), high.reshape(blocks * rows, lanes)
    if split_rows:
        out[0], out[1] = low, high
    else:
        out[:, 0:lanes] = low
        out[:, lanes:] = high


def k_place_small(rank, taps, counts, core, *refs):
    refs = list(refs)
    given, refs = refs[: sum(counts)], refs[sum(counts) :]
    norm, cw, cb, xw, dw, db, al, sk, all_s = refs
    states = al.shape[1]
    n_x = rank + 2 * states
    all_s[...] = jnp.zeros(all_s.shape, F32)
    at = 0
    for l, count in enumerate(counts):
        low, high = in_order(core, given[at : at + count])
        at += count
        blocks, _, lanes = low.shape
        n = -(-(n_x + rank + states + taps + 4) // blocks)
        for k in range(blocks):
            all_s[k * n : (k + 1) * n, 0:lanes] = low[k, 0:n]
            all_s[k * n : (k + 1) * n, lanes:] = high[k, 0:n]
        dw[l] = all_s[n_x : n_x + rank, :]
        first = n_x + rank
        xw[l] = all_s[0:n_x, :]
        al[l] = all_s[first : first + states, :]
        cw[l] = all_s[first + states : first + states + taps, :]
        first += states + taps
        cb[l : l + 1, :] = all_s[first : first + 1, :]
        db[l : l + 1, :] = all_s[first + 1 : first + 2, :]
        sk[l : l + 1, :] = all_s[first + 2 : first + 3, :]
        norm[l : l + 1, :] = all_s[first + 3 : first + 4, 0 : norm.shape[1]]


def shards(
    hidden_in,
    norm_gain,
    in_weight,
    conv_weight,
    conv_bias,
    xproj_weight,
    dtproj_weight,
    dt_bias,
    a_log,
    skip_gain,
    out_weight,
    hidden_grad,
):
    layers, width, _ = in_weight.shape
    inner, states = a_log.shape[1], a_log.shape[2]
    rank = dtproj_weight.shape[1]
    taps = conv_weight.shape[2]
    seqs, own, _ = hidden_in.shape
    ndev = lax.axis_size(AXIS)
    me = lax.axis_index(AXIS)
    core = me % 2
    chip = me // 2
    rows = seqs * own
    assert layers == 2 and seqs == 2 and ndev % 2 == 0
    assert inner % CHUNK == 0 and inner // 128 <= states and rank + 2 * states <= XD

    pairs = [(i, i ^ 1) for i in range(ndev)]
    turn = []
    call = functools.partial(run, turn=turn)

    def to_runs(block):
        mine = lax.dynamic_index_in_dim(block, core, 0, keepdims=False)
        other = lax.dynamic_index_in_dim(block, 1 - core, 0, keepdims=False)
        came = lax.ppermute(other, AXIS, pairs)
        first = jnp.where(core == 0, mine, came)
        second = jnp.where(core == 0, came, mine)
        return jnp.concatenate([first, second], axis=0)

    def from_runs(mine, other):
        came = lax.ppermute(other, AXIS, pairs)
        first = jnp.where(core == 0, mine, came)
        second = jnp.where(core == 0, came, mine)
        return jnp.stack([first, second], axis=0)

    def done_by_now(array):
        array, turn[0] = lax.optimization_barrier((array, turn[0]))
        return array

    def not_before(*arrays):
        return lax.optimization_barrier(arrays + (turn[0],))[:-1]

    def from_before(block):
        return lax.ppermute(block, AXIS, [(i, i + 2) for i in range(ndev - 2)])

    def from_after(block):
        return lax.ppermute(block, AXIS, [(i + 2, i) for i in range(ndev - 2)])

    bits = (ndev // 2).bit_length() - 1
    assert 2 << bits == ndev and bits > 2
    rounds = []
    low = 0
    while low < bits:
        n = 2 if bits - low >= 2 else 1
        rounds.append((low, 1 << n))
        low += n

    def digit_of(r):
        low, group = rounds[r]
        return (chip >> low) & (group - 1)

    def digits_of(r):
        nxt = digit_of(r + 1) if r + 1 < len(rounds) else jnp.zeros_like(chip)
        return jnp.stack([digit_of(r), nxt]).astype(jnp.int32)

    def send(block, r, m, which):
        low, group = rounds[r]
        flip = (m << low) << 1
        route = [(i, i ^ flip) for i in range(ndev)]
        if which == "up":
            route = [(i, j) for i, j in route if j > i]
        if which == "down":
            route = [(i, j) for i, j in route if j < i]
        return lax.ppermute(block, AXIS, route)

    smem = pl.BlockSpec(memory_space=pltpu.SMEM)
    core_s = (core[None].astype(jnp.int32), smem)

    def swap(block):
        return lax.ppermute(block, AXIS, pairs)

    pay = shape((states, inner + EXTRA), BF16)

    kept = {}

    def exchange(payload, a2, mode, meanwhile=()):
        meanwhile = dict(enumerate(meanwhile))
        befores = [[] for _ in mode]
        sums = [[] for _ in mode]
        for r, (low, group) in enumerate(rounds[:-1]):
            received = [payload] + [send(payload, r, m, "all") for m in range(1, group)]
            if r in meanwhile:
                meanwhile[r]()
            final = r + 2 == len(rounds)
            split = len(mode) == 2 and final
            nextgroup = rounds[r + 1][1] if split else 0
            pays = (
                [pay] * (nextgroup - 1)
                if split
                else [shape((states * len(mode), inner + EXTRA), BF16)]
            )
            outs = call(
                functools.partial(k_join, group, nextgroup, mode),
                pays
                + [shape((states, inner), F32)] * len(mode)
                + [shape((1, inner), F32)] * len(mode),
                [(digits_of(r), smem)] + received + [a2],
                [
                    pltpu.VMEM((group, states, inner + EXTRA), F32),
                    pltpu.VMEM((group, 8, inner), F32),
                    pltpu.VMEM((states, inner + EXTRA), F32),
                ],
            )
            sent, outs = outs[: len(pays)], outs[len(pays) :]
            for i in range(len(mode)):
                befores[i].append(outs[i])
                sums[i].append(outs[len(mode) + i])
            payload = sent if split else sent[0]
        r = len(rounds) - 1
        if len(mode) == 2:
            last = [send(payload[m - 1], r, m, "all") for m in range(1, rounds[r][1])]
        else:
            way = "up" if mode == "f" else "down"
            last = [send(payload, r, m, way) for m in range(1, rounds[r][1])]
        kept["last"] = last
        for step in sorted(meanwhile):
            if step >= r:
                meanwhile[step]()
        return last, sum(befores, []), sum(sums, []), digits_of(r)

    def row(array, l):
        return Row(array, l)

    def layer_of(array, l):
        return array, part((None,) + array.shape[1:], (l, 0, 0))

    def w_in(l, half):
        return in_weight, part((None, width, inner), (l, 0, half))

    def w_out(l):
        return out_weight, part((None, inner, width), (l, 0, 0))

    def table_scratch():
        return [
            pltpu.VMEM((rows, XD), F32),
            pltpu.VMEM((rows * states, XD), BF16),
            pltpu.VMEM((rows * states, 256), F32),
        ]

    act = shape((rows, inner), F32)
    act_b = shape((rows, inner), BF16)
    res = shape((rows, width), F32)
    res_b = shape((rows, width), BF16)
    edge = shape((HALO, inner), F32)
    mm = 2 * rows * width * inner

    x0 = to_runs(hidden_in).astype(F32)

    normed = [None, None]
    xc = [None, None]
    halo = [None, None]
    z = [None, None]
    u = [None, None]
    xd = [None, None]
    v = [None, None]

    normed[0], xc[0], tail = call(
        k_in, [res_b, act_b, edge], [x0, row(norm_gain, 0), w_in(0, 0)]
    )

    a_log, conv_weight, xproj_weight, dtproj_weight, hidden_grad = not_before(
        a_log, conv_weight, xproj_weight, dtproj_weight, hidden_grad
    )
    a2_all = -jnp.exp(jnp.swapaxes(a_log, 1, 2)) * LOG2E
    cw_all = jnp.swapaxes(conv_weight, 1, 2)
    xw_all = jnp.pad(xproj_weight, ((0, 0), (0, 0), (0, XD - xproj_weight.shape[2])))
    dw_all = jnp.pad(dtproj_weight, ((0, 0), (0, XD - rank), (0, 0)))
    grad_out = to_runs(hidden_grad)

    def before_scan(l, tail, dgated=None):
        halo[l] = from_before(tail)
        (z[l],) = call(k_gate, [act_b], [normed[l], w_in(l, 1)], cost=LONG)
        both = dgated is not None
        outs = call(
            functools.partial(k_local, rank, both),
            [
                act_b,
                shape((rows, XD), BF16),
                act,
                shape((states * (2 if both else 1), inner + EXTRA), BF16),
            ]
            + ([act] if both else []),
            [
                halo[l],
                xc[l],
                layer_of(cw_all, l),
                row(conv_bias, l),
                layer_of(xw_all, l),
                layer_of(dw_all, l),
                row(dt_bias, l),
                layer_of(a2_all, l),
            ]
            + ([dgated, z[l]] if both else []),
            [pltpu.VMEM((rows + HALO, inner), F32)]
            + [pltpu.VMEM((rows, inner), F32)] * 2
            + table_scratch()
            + [pltpu.VMEM((states, inner), F32), pltpu.VMEM((states, inner + EXTRA), F32)],
            cost=LONG,
        )
        u[l], xd[l], v[l] = outs[:3]
        return outs[3:]

    def join_scratch():
        group = rounds[-1][1]
        return [
            pltpu.VMEM((group, states, inner), F32),
            pltpu.VMEM((group, 8, inner), F32),
        ]

    def piece(array, i):
        return array, part((rows, array.shape[1]), (i, 0))

    def mix(l, parts, extra, outs):
        final = l == layers - 1
        last, befores, sums, digits = parts
        befores, sums = befores[: len(rounds) - 1], sums[: len(rounds) - 1]
        return call(
            functools.partial(k_mix, rank, final, len(last), len(befores)),
            outs,
            [(digits, smem), core_s]
            + last
            + befores
            + sums
            + [layer_of(a2_all, l), u[l], v[l], xd[l], z[l], residual[l], row(skip_gain, l), w_out(l)]
            + extra,
            ([act_scratch, pltpu.VMEM((rows, width), F32)] if final else [])
            + [pltpu.VMEM((rows, inner), BF16)]
            + [act_scratch] * 2
            + table_scratch()
            + join_scratch(),
            cost=LONG,
        )

    half_b = shape((rows, width), BF16)
    entry = shape((states, inner), F32)
    act_scratch = pltpu.VMEM((rows, inner), F32)
    residual = [x0, None]
    def shadow_0():
        (kept["dgated1"],) = call(k_dgated, [act], [grad_out, w_out(1)], cost=LONG)

    (payload,) = before_scan(0, tail)
    parts = exchange(payload, layer_of(a2_all, 0), "f", (shadow_0,))
    dgated1 = kept["dgated1"]
    y0, x1, normed[1], xc[1], tail, gated_keep, sends, h0 = mix(
        0,
        parts,
        [row(norm_gain, 1), w_in(1, 0)],
        [act, res, res_b, act_b, edge, half_b, shape((2 * rows, width), BF16), entry],
    )
    residual[1] = x1
    came = swap(sends)
    n1_pair = (normed[1], piece(came, 1))
    gated0_pair = (gated_keep, piece(came, 0))
    n0_pair = (normed[0], swap(normed[0]))
    e1_pair = (grad_out, swap(grad_out))
    payload, dy1 = before_scan(1, tail, dgated1)
    parts = exchange(payload, layer_of(a2_all, 1), "fb")
    n_small = rank + 2 * states + rank + states + taps + 4
    small = shape((n_small, inner), F32)
    small_pad = -(-n_small // (BLOCKS * 2)) * BLOCKS * 2 if n_small % BLOCKS else n_small

    n_chunks = inner // CHUNK
    cuts = [(0, (n_chunks + 1) // 2 * CHUNK), ((n_chunks + 1) // 2 * CHUNK, n_chunks // 2 * CHUNK)]
    n_parts = len(cuts)
    assert all(first % lanes == 0 for first, lanes in cuts)

    def scan(l, i, dy, parts, h_in):
        lane0, lanes = cuts[i]
        last, befores, sums, digits = parts
        n_low = len(rounds) - 1
        cut = part((rows, lanes), (0, lane0 // lanes))
        cut_s = part((states, lanes), (0, lane0 // lanes))
        cut_a = part((None, states, lanes), (l, 0, lane0 // lanes))
        return call(
            functools.partial(k_scan, rank, lane0, len(last), n_low),
            [shape((rows, lanes), F32)] * 2 + [shape((states, lanes), F32), shape((rows, XD), F32)],
            [(digits, smem)]
            + last
            + befores[-n_low:]
            + sums[-n_low:]
            + [(a2_all, cut_a), (u[l], cut), (v[l], cut), (dy, cut), (h_in, cut_s), xd[l]],
            [pltpu.VMEM((rows, lanes), F32)] * 2
            + table_scratch()
            + [
                pltpu.VMEM((rounds[-1][1], states, lanes), F32),
                pltpu.VMEM((rounds[-1][1], 8, lanes), F32),
            ]
            + [pltpu.VMEM((rows * states, 128), F32)] * 2
            + [pltpu.VMEM((rows * states, CHUNK), F32)] * 2
            + [pltpu.VMEM((states, lanes), F32)],
            cost=LONG,
        )

    def post(l, scans, dy):
        return call(
            functools.partial(k_post, rank, n_parts),
            [act, edge, small],
            [outs[k] for k in range(4) for outs in scans]
            + [
                u[l],
                v[l],
                xd[l],
                dy,
                halo[l],
                xc[l],
                layer_of(cw_all, l),
                row(conv_bias, l),
                layer_of(xw_all, l),
                layer_of(dw_all, l),
                row(skip_gain, l),
            ],
            [pltpu.VMEM((rows + HALO, inner), F32)],
            cost=LONG,
        )


    def over(block, flip):
        return lax.ppermute(block, AXIS, [(i, i ^ (flip << 1)) for i in range(ndev)])

    place_s = (chip[None].astype(jnp.int32), smem)

    def held(arrays, gate):
        if gate is None:
            return arrays
        return lax.optimization_barrier(tuple(arrays) + tuple(gate()))[: len(arrays)]

    def summed(matrices, smalls, aside=False, gates=(None, None, None)):
        ins = []
        each = width // BLOCKS
        for (a, a_came), (b, b_came) in matrices:
            ins += [a, a_came, b, b_came]
        r = each * len(matrices)
        if smalls is not None:
            ins += list(smalls)
            r += 16
        has_small = smalls is not None
        half = width // 2
        if ndev != 2 * BLOCKS:
            (mine,) = call(
                functools.partial(k_chip_sum, len(matrices), has_small),
                [shape((BLOCKS, r, width), F32)],
                ins,
            )
            empty = jnp.zeros((2,) + mine.shape, F32)
            total = lax.psum(lax.dynamic_update_index_in_dim(empty, mine, core, 0), AXIS)
            total = total.astype(BF16)
            for _ in range(3 if aside else 5):
                yield None
            if aside:
                yield jnp.swapaxes(total, 0, 1)
                return
            yield (
                lax.dynamic_index_in_dim(total, core, 0, keepdims=False),
                lax.dynamic_index_in_dim(total, 1 - core, 0, keepdims=False),
            )
            return
        n = BLOCKS // 2
        keep_a, keep_b, send_a, send_b = call(
            functools.partial(k_first, len(matrices), has_small),
            [shape((n, r, half), F32)] * 2 + [shape((n, r, half), BF16)] * 2,
            [place_s] + ins,
            [pltpu.VMEM((BLOCKS, r, width), F32)],
            cost=LONG,
        )
        send_a, send_b = held([send_a, send_b], gates[0])
        came_a, came_b = over(send_a, 1), over(send_b, 2)
        yield None
        n = BLOCKS // 4
        stay_a, stay_b, send_a, send_b = call(
            k_second,
            [shape((n, r, half), F32)] * 2 + [shape((n, r, half), BF16)] * 2,
            [place_s, keep_a, keep_b, came_a, came_b],
        )
        send_a, send_b = held([send_a, send_b], gates[1])
        came_a, came_b = over(send_a, 2), over(send_b, 1)
        yield None
        keep, *sends = call(
            k_third,
            [shape((r, width), F32)] + [shape((r, width), BF16)] * 3,
            [place_s, stay_a, stay_b, came_a, came_b],
        )
        sends = held(sends, gates[2])
        came = [over(send_m, 4 * (m + 1)) for m, send_m in enumerate(sends)]
        yield None
        (done,) = call(k_fourth, [shape((r, width), BF16)], [keep] + came)
        if aside:
            every = lax.all_gather(done, AXIS)
            yield every.reshape(BLOCKS, 2, r, width)
            return
        came = [over(done, 4 * m) for m in (1, 2, 3)]
        yield None
        left, right = call(k_stack, [shape((4, r, half), BF16)] * 2, [done] + came)
        left_y, right_x = over(left, 2), over(right, 1)
        lefts = [left, over(left, 1), left_y, over(left_y, 1)]
        rights = [right, right_x, over(right, 2), over(right_x, 2)]
        yield None
        (mine,) = call(
            k_chip, [shape((BLOCKS, r, width), BF16)], [place_s] + lefts + rights
        )
        yield mine, swap(mine)

    def sources(halves, i, per, each, place):
        if not isinstance(halves, tuple):
            spec = pl.BlockSpec((per, 2, each, width), lambda g: (place(g), 0, i, 0))
            return [halves], [spec]
        spec = pl.BlockSpec((per, each, width), lambda g: (place(g), i, 0))
        return list(halves), [spec, spec]

    def placed(halves, i, whole, block, index, split_rows, before):
        each = width // BLOCKS
        steps = 4
        anywhere = pl.BlockSpec(memory_space=pl.ANY)
        arrays, specs = sources(halves, i, BLOCKS // steps, each, lambda g: g)
        ins = [core_s[0]] + arrays + [turn[0]]
        specs = [smem] + specs + [anywhere]
        aliases = {}
        if before is not None:
            aliases = {len(ins): 0}
            ins.append(before)
            specs.append(anywhere)
        out, turn[0] = pl.pallas_call(
            functools.partial(k_place, len(arrays), split_rows),
            grid=(steps,),
            in_specs=specs,
            out_specs=[pl.BlockSpec(block, index), pl.BlockSpec((8, 128), lambda g: (0, 0))],
            out_shape=[whole, shape((8, 128), F32)],
            input_output_aliases=aliases,
            compiler_params=pltpu.CompilerParams(vmem_limit_bytes=58 * 1024 * 1024),
            cost_estimate=COST,
        )(*ins)
        return out

    g_out_shape = shape((layers, 2, width, width), F32)
    g_in_shape = shape((layers, width, 2 * inner), F32)
    quarter = width // 4
    out_block = (None, 2, quarter, width)
    in_block = (None, quarter, inner)

    def out_at(l):
        return lambda g: (l, 0, g, 0)

    def in_at(l, half):
        return lambda g: (l, g, half)

    def placed_small(layer_sums):
        each = width // BLOCKS
        ins, counts = [core_s], []
        for halves, i in layer_sums:
            arrays, specs = sources(halves, i * each // 16, BLOCKS, 16, lambda g: 0)
            ins += list(zip(arrays, specs))
            counts.append(len(arrays))
        n_x = rank + 2 * states
        return call(
            functools.partial(k_place_small, rank, taps, tuple(counts)),
            [
                shape((layers, width), F32),
                shape((layers, taps, inner), F32),
                shape((layers, inner), F32),
                shape((layers, n_x, inner), F32),
                shape((layers, rank, inner), F32),
                shape((layers, inner), F32),
                shape((layers, states, inner), F32),
                shape((layers, inner), F32),
            ],
            ins,
            [pltpu.VMEM((small_pad, inner), F32)],
        )

    half_small = shape((small_pad, width), F32)

    hid_mine, hid_other, dz1, dz_keep, gated_keep, sends, h1 = mix(
        1,
        parts,
        [dgated1],
        [shape((own, width), BF16)] * 2
        + [act_b, half_b, half_b, shape((2 * rows, width), BF16), entry],
    )
    came = swap(sends)
    hidden_out = from_runs(hid_mine, hid_other)
    a_sum = summed(
        [((gated_keep, piece(came, 0)), e1_pair), (n1_pair, (dz_keep, piece(came, 1)))],
        None,
        True,
        (None, None, lambda: [after1]),
    )
    scans = [scan(1, 0, dy1, parts, h1)]
    next(a_sum)
    scans.append(scan(1, 1, dy1, parts, h1))
    hidden_out = done_by_now(hidden_out)
    next(a_sum)
    dconv1, head1, small1 = post(1, scans, dy1)
    after1 = from_after(head1)
    (dnz1,) = call(k_dnz, [res], [dz1, w_in(1, 1)], cost=LONG)
    next(a_sum)
    turn_back = functools.partial(
        call,
        functools.partial(k_turn, rank),
        [half_b, half_small, res, res_b, act, act_b, half_b, shape((4 * rows, width), BF16), pay],
        [
            core_s,
            small1,
            dconv1,
            after1,
            layer_of(cw_all, 1),
            dnz1,
            w_in(1, 0),
            x1,
            row(norm_gain, 1),
            grad_out,
            w_out(0),
            y0,
            z[0],
            v[0],
            xd[0],
            layer_of(a2_all, 0),
        ],
        [
            pltpu.VMEM((n_small, inner), F32),
            pltpu.VMEM((rows, inner), BF16),
            pltpu.VMEM((rows + HALO, inner), F32),
            pltpu.VMEM((rows, inner), F32),
        ]
        + table_scratch()
        + [pltpu.VMEM((states, inner), F32), pltpu.VMEM((states, inner + EXTRA), F32)],
        cost=LONG,
    )
    dxc_keep, small_keep, e1, de0, dy0, dz0, dz_keep, sends, payload = turn_back()
    came = swap(sends)
    b_sum = summed(
        [
            (n1_pair, (dxc_keep, piece(came, 0))),
            (gated0_pair, (de0, piece(came, 2))),
            (n0_pair, (dz_keep, piece(came, 1))),
        ],
        (small_keep, piece(came, 3)),
        True,
        (lambda: kept["last"], None, None),
    )

    def shadow_1():
        kept["sum_a"] = next(a_sum)
        (kept["dnz0"],) = call(k_dnz, [res], [dz0, w_in(0, 1)], cost=LONG)

    def shadow_2():
        next(b_sum)

    parts = exchange(payload, layer_of(a2_all, 0), "b", (shadow_1, shadow_2))
    dnz0 = kept["dnz0"]
    sum_a = kept["sum_a"]
    scans = [scan(0, 0, dy0, parts, h0)]
    next(b_sum)
    scans.append(scan(0, 1, dy0, parts, h0))
    next(b_sum)
    dconv0, head0, small0 = post(0, scans, dy0)
    after0 = from_after(head0)
    dxc_keep, small_keep, sends, e0_mine, e0_other = call(
        k_end,
        [half_b, half_small, shape((2 * rows, width), BF16)] + [shape((own, width), BF16)] * 2,
        [
            core_s,
            small0,
            dconv0,
            after0,
            layer_of(cw_all, 0),
            dnz0,
            w_in(0, 0),
            x0,
            row(norm_gain, 0),
            e1,
        ],
        [
            pltpu.VMEM((n_small, inner), F32),
            pltpu.VMEM((rows, inner), BF16),
            pltpu.VMEM((rows + HALO, inner), F32),
            pltpu.VMEM((rows, width), F32),
        ],
        cost=LONG,
    )
    came = swap(sends)
    c_sum = summed(
        [(n0_pair, (dxc_keep, piece(came, 0)))], (small_keep, piece(came, 1))
    )
    sum_b = next(b_sum)
    next(c_sum)
    g_out = placed(sum_a, 0, g_out_shape, out_block, out_at(1), True, None)
    input_grad = done_by_now(from_runs(e0_mine, e0_other))
    next(c_sum)
    next(c_sum)
    g_in = placed(sum_a, 1, g_in_shape, in_block, in_at(1, 1), False, None)
    next(c_sum)
    next(c_sum)
    sum_c = next(c_sum)
    g_in = placed(sum_b, 0, g_in_shape, in_block, in_at(1, 0), False, g_in)
    g_out = placed(sum_b, 1, g_out_shape, out_block, out_at(0), True, g_out)
    g_in = placed(sum_b, 2, g_in_shape, in_block, in_at(0, 1), False, g_in)
    g_in = placed(sum_c, 0, g_in_shape, in_block, in_at(0, 0), False, g_in)
    g_norm, g_cw, g_cb, g_xw, g_dw, g_db, g_al, g_sk = placed_small([(sum_c, 1), (sum_b, 3)])
    return (
        hidden_out,
        input_grad,
        g_norm,
        g_in,
        jnp.swapaxes(g_cw, 1, 2),
        g_cb,
        jnp.swapaxes(g_xw, 1, 2),
        g_dw,
        g_db,
        jnp.swapaxes(g_al, 1, 2),
        g_sk,
        g_out.reshape(layers, inner, width),
    )


def solution(mesh):
    split = P(None, AXIS, None)
    return jax.shard_map(
        shards,
        mesh=mesh,
        in_specs=(split,) + (P(),) * 10 + (split,),
        out_specs=(split, split) + (P(),) * 10,
        check_vma=False,
    )
```

```python
import functools
import math

import jax
import jax.numpy as jnp
from jax import lax
from jax.experimental import pallas as pl
from jax.experimental.pallas import tpu as pltpu
from jax.sharding import PartitionSpec as P

BF16 = jnp.bfloat16
F32 = jnp.float32
LOG2E = 1.4426950408889634
LN2 = 0.6931471805599453
AXIS = "seq"
XD = 128
EXTRA = 256
CHUNK = 512
UNROLL = 8
HALO = 8
COST = pl.CostEstimate(flops=1, bytes_accessed=1, transcendentals=0)
LONG = pl.CostEstimate(flops=1, bytes_accessed=10**8, transcendentals=0)
SPARE = 6
BLOCKS = 16


def full(array):
    nd = len(array.shape)
    return pl.BlockSpec(array.shape, lambda i, nd=nd: (0,) * nd)


def part(shape, index):
    return pl.BlockSpec(shape, lambda i, index=index: index)


def room(specs, dtypes, out_specs, out_dtypes, scratch, spare):
    total = spare << 20
    for spec, dtype in list(zip(specs, dtypes)) + list(zip(out_specs, out_dtypes)):
        if spec.block_shape is not None:
            total += math.prod(d or 1 for d in spec.block_shape) * jnp.dtype(dtype).itemsize
    for item in scratch:
        if not hasattr(item, "shape"):
            continue
        total += math.prod(item.shape) * jnp.dtype(item.dtype).itemsize
    return min(total, 58 << 20)


class Late:
    def __init__(self, array, index, dims):
        self.array, self.index, self.dims = array, index, dims


class Fetched:
    def __init__(self, source, target, sem):
        self.copy, self.ref = pltpu.make_async_copy(source, target, sem), target
        self.copy.start()

    def __getitem__(self, where):
        if self.copy is not None:
            self.copy.wait()
            self.copy = None
        return self.ref[where]


class Row:
    def __init__(self, array, index):
        self.array, self.index = array, index


def run(kernel, outs, ins, scratch=(), turn=None, cost=COST, spare=SPARE):
    out_specs = [o[1] if isinstance(o, tuple) else full(o) for o in outs]
    outs = [o[0] if isinstance(o, tuple) else o for o in outs]
    arrays, specs, picks, late = [], [], {}, {}
    scratch = list(scratch)
    for item in ins:
        if isinstance(item, Late):
            late[len(arrays)] = item.index
            scratch += [pltpu.VMEM(item.dims, item.array.dtype), pltpu.SemaphoreType.DMA]
            item = (item.array, pl.BlockSpec(memory_space=pltpu.HBM))
        if isinstance(item, Row):
            picks[len(arrays)] = item.index
            item = item.array
        if isinstance(item, tuple):
            arrays.append(item[0])
            specs.append(item[1])
        else:
            arrays.append(item)
            specs.append(full(item))
    n = len(arrays)
    limit = room(specs, [a.dtype for a in arrays], out_specs, [o.dtype for o in outs], scratch, spare)
    if turn:
        arrays.append(turn[0])
        specs.append(pl.BlockSpec(memory_space=pl.ANY))
    after = len(arrays)

    def body(*refs):
        given = list(refs[:n])
        for k, index in picks.items():
            given[k] = given[k].at[index : index + 1, :]
        rest, buffers = refs[after:], ()
        if late:
            rest, buffers = rest[: -2 * len(late)], rest[-2 * len(late) :]
        for i, (k, index) in enumerate(late.items()):
            given[k] = Fetched(given[k].at[index], buffers[2 * i], buffers[2 * i + 1])
        kernel(*given, *rest)

    results = pl.pallas_call(
        body,
        grid=(1,),
        in_specs=specs,
        out_specs=out_specs,
        out_shape=outs,
        scratch_shapes=list(scratch),
        compiler_params=pltpu.CompilerParams(vmem_limit_bytes=limit),
        cost_estimate=cost,
    )(*arrays)
    if turn is not None:
        turn[:] = [results[-1]]
    return results


def shape(dims, dtype):
    return jax.ShapeDtypeStruct(dims, dtype)


def dot(a, b):
    return jnp.dot(a, b, preferred_element_type=F32)


def dot_t(a, b):
    return lax.dot_general(a, b, (((1,), (1,)), ((), ())), preferred_element_type=F32)


def dot_rows(a, b):
    return lax.dot_general(a, b, (((0,), (0,)), ((), ())), preferred_element_type=F32)


def sigmoid(v):
    return 1.0 / (1.0 + jnp.exp(-v))


def softplus(v):
    return jnp.maximum(v, 0.0) + jnp.log1p(jnp.exp(-jnp.abs(v)))


def slope(v):
    s = sigmoid(v)
    return s * (1.0 + v * (1.0 - s))


def wide(block, lanes):
    return jnp.concatenate([block] * (lanes // block.shape[1]), axis=1)


def rows_of_sums(parts):
    row = lax.broadcasted_iota(jnp.int32, parts[0].shape, 0)
    m4, m2, m1 = row < 4, (row & 2) == 0, (row & 1) == 0
    q = []
    for i in range(4):
        first = jnp.where(m4, parts[i], parts[i + 4])
        other = jnp.where(m4, parts[i + 4], parts[i])
        q.append(first + pltpu.roll(other, 4, 0))
    s = []
    for i in range(2):
        s.append(
            jnp.where(
                m2, q[i] + pltpu.roll(q[i], 6, 0), q[i + 2] + pltpu.roll(q[i + 2], 2, 0)
            )
        )
    return jnp.where(m1, s[0] + pltpu.roll(s[0], 7, 0), s[1] + pltpu.roll(s[1], 1, 0))


def fold(block):
    out = block[0:8]
    for k in range(8, block.shape[0], 8):
        out = out + block[k : k + 8]
    return out


def fold_lanes(block):
    out = block[:, 0:128]
    for k in range(128, block.shape[1], 128):
        out = out + block[:, k : k + 128]
    return out


def normed_of(x, gain):
    rinv = lax.rsqrt(jnp.mean(x * x, axis=-1, keepdims=True) + 1e-05)
    return (x * rinv * gain).astype(BF16)


def fill_table(xdf_ref, lhs_ref, bc_ref, rank, states):
    rows = xdf_ref.shape[0]
    n_i = lax.broadcasted_iota(jnp.int32, (states, XD), 0)
    lane = lax.broadcasted_iota(jnp.int32, (states, XD), 1)
    mask = ((lane == rank + n_i) | (lane == rank + states + n_i)).astype(F32)

    def body(i, carry):
        for j in range(UNROLL):
            t = i * UNROLL + j
            line = xdf_ref[pl.ds(t, 1), :]
            lhs_ref[pl.ds(pl.multiple_of(t * states, states), states), :] = (
                line * mask
            ).astype(BF16)
        return carry

    lax.fori_loop(0, rows // UNROLL, body, 0)
    k_i = lax.broadcasted_iota(jnp.int32, (XD, 256), 0)
    c_i = lax.broadcasted_iota(jnp.int32, (XD, 256), 1)
    low = rank + jnp.where(c_i >= 128, states, 0)
    pick = ((k_i >= low) & (k_i < low + states)).astype(BF16)
    bc_ref[...] = dot(lhs_ref[...], pick)


def state_rows(t, states):
    return pl.ds(pl.multiple_of(t * states, states), states)


def scan_ends(dt_ref, dtu_ref, bc_ref, a2_ref, end_ref):
    rows, inner = dt_ref.shape
    states = a2_ref.shape[0]

    def chunk(c, carry):
        lanes = pl.ds(pl.multiple_of(c * CHUNK, CHUNK), CHUNK)
        a2 = a2_ref[:, lanes]

        def body(i, h):
            for j in range(UNROLL):
                t = i * UNROLL + j
                a = jnp.exp2(dt_ref[pl.ds(t, 1), lanes] * a2)
                b = wide(bc_ref[state_rows(t, states), 0:128], CHUNK)
                h = a * h + dtu_ref[pl.ds(t, 1), lanes] * b
            return h

        end_ref[:, lanes] = lax.fori_loop(
            0, rows // UNROLL, body, jnp.zeros((states, CHUNK), F32)
        )
        return carry

    lax.fori_loop(0, inner // CHUNK, chunk, 0)


def scan_back_ends(dt_ref, dy_ref, bc_ref, a2_ref, end_ref):
    rows, inner = dt_ref.shape
    states = a2_ref.shape[0]

    def chunk(c, carry):
        lanes = pl.ds(pl.multiple_of(c * CHUNK, CHUNK), CHUNK)
        a2 = a2_ref[:, lanes]

        def body(i, back):
            for j in range(UNROLL):
                t = rows - 1 - (i * UNROLL + j)
                a = jnp.exp2(dt_ref[pl.ds(t, 1), lanes] * a2)
                c_row = wide(bc_ref[state_rows(t, states), 128:256], CHUNK)
                back = a * (dy_ref[pl.ds(t, 1), lanes] * c_row + back)
            return back

        end_ref[:, lanes] = lax.fori_loop(
            0, rows // UNROLL, body, jnp.zeros((states, CHUNK), F32)
        )
        return carry

    lax.fori_loop(0, inner // CHUNK, chunk, 0)


def scan_forward(dt_ref, dtu_ref, bc_ref, a2_ref, h_in_ref, y_ref):
    rows, inner = dt_ref.shape
    states = a2_ref.shape[0]

    def chunk(c, carry):
        lanes = pl.ds(pl.multiple_of(c * CHUNK, CHUNK), CHUNK)
        a2 = a2_ref[:, lanes]

        def body(i, h):
            parts = []
            for j in range(UNROLL):
                t = i * UNROLL + j
                a = jnp.exp2(dt_ref[pl.ds(t, 1), lanes] * a2)
                both = bc_ref[state_rows(t, states), :]
                h = a * h + dtu_ref[pl.ds(t, 1), lanes] * wide(both[:, 0:128], CHUNK)
                parts.append(fold(h * wide(both[:, 128:256], CHUNK)))
            y_ref[pl.ds(pl.multiple_of(i * UNROLL, UNROLL), UNROLL), lanes] = rows_of_sums(
                parts
            )
            return h

        lax.fori_loop(0, rows // UNROLL, body, h_in_ref[:, lanes])
        return carry

    lax.fori_loop(0, inner // CHUNK, chunk, 0)


def scan_both(
    dt_ref,
    dtu_ref,
    dy_ref,
    bc_ref,
    a2_ref,
    h_in_ref,
    g_in_ref,
    sgb_ref,
    sqa_ref,
    rate_ref,
    db_ref,
    dc_ref,
    a_s,
    ah_s,
):
    rows, inner = dt_ref.shape
    states = a2_ref.shape[0]
    db_ref[...] = jnp.zeros(db_ref.shape, F32)
    dc_ref[...] = jnp.zeros(dc_ref.shape, F32)

    def chunk(c, carry):
        lanes = pl.ds(pl.multiple_of(c * CHUNK, CHUNK), CHUNK)
        a2 = a2_ref[:, lanes]

        def ahead(i, h):
            for j in range(UNROLL):
                t = i * UNROLL + j
                at = state_rows(t, states)
                a = jnp.exp2(dt_ref[pl.ds(t, 1), lanes] * a2)
                b_row = wide(bc_ref[at, 0:128], CHUNK)
                ah = a * h
                a_s[at, :] = a
                ah_s[at, :] = ah
                h = ah + dtu_ref[pl.ds(t, 1), lanes] * b_row
                dc_ref[at, :] += fold_lanes(h * dy_ref[pl.ds(t, 1), lanes])
            return h

        lax.fori_loop(0, rows // UNROLL, ahead, h_in_ref[:, lanes])

        def retreat(i, carried):
            back, rate = carried
            block = rows // UNROLL - 1 - i
            gbs, qas = [None] * UNROLL, [None] * UNROLL
            for j in reversed(range(UNROLL)):
                t = block * UNROLL + j
                at = state_rows(t, states)
                both = bc_ref[at, :]
                g = dy_ref[pl.ds(t, 1), lanes] * wide(both[:, 128:256], CHUNK) + back
                q = g * ah_s[at, :]
                gbs[j] = fold(g * wide(both[:, 0:128], CHUNK))
                qas[j] = fold(q * a2)
                rate = rate + q * dt_ref[pl.ds(t, 1), lanes]
                db_ref[at, :] += fold_lanes(g * dtu_ref[pl.ds(t, 1), lanes])
                back = a_s[at, :] * g
            here = pl.ds(pl.multiple_of(block * UNROLL, UNROLL), UNROLL)
            sgb_ref[here, lanes] = rows_of_sums(gbs)
            sqa_ref[here, lanes] = rows_of_sums(qas)
            return back, rate

        _, rate = lax.fori_loop(
            0,
            rows // UNROLL,
            retreat,
            (g_in_ref[:, lanes], jnp.zeros((states, CHUNK), F32)),
        )
        rate_ref[:, lanes] = rate
        return carry

    lax.fori_loop(0, inner // CHUNK, chunk, 0)


def packed(state, total, wide_s):
    inner = total.shape[1]
    high = total.astype(BF16).astype(F32)
    rest = total - high
    wide_s[:, 0:inner] = state
    wide_s[:, inner:] = jnp.zeros((state.shape[0], EXTRA), F32)
    for k in range(inner // 128):
        wide_s[k : k + 1, inner : inner + 128] = high[:, k * 128 : (k + 1) * 128]
        wide_s[k : k + 1, inner + 128 : inner + 256] = rest[:, k * 128 : (k + 1) * 128]
    return wide_s[...].astype(BF16)


def unpack_total(wide_ref, m, total_ref, inner):
    for k in range(inner // 128):
        total_ref[m, 0:1, k * 128 : (k + 1) * 128] = (
            wide_ref[m, k : k + 1, inner : inner + 128]
            + wide_ref[m, k : k + 1, inner + 128 : inner + 256]
        )


def join_runs(states_ref, totals_ref, a2, digit, group, backward):
    inner = a2.shape[1]
    before = jnp.zeros(a2.shape, F32)
    entire = jnp.zeros(a2.shape, F32)
    sum_before = jnp.zeros((1, inner), F32)
    sum_entire = jnp.zeros((1, inner), F32)
    order = reversed(range(group)) if backward else range(group)
    for p in order:
        m = jnp.bitwise_xor(digit, p)
        state = states_ref[m, :, 0:inner]
        total = totals_ref[m, 0:1, :]
        through = jnp.exp2(total * a2)
        counts = (p > digit) if backward else (p < digit)
        before = jnp.where(counts, through * before + state, before)
        sum_before = jnp.where(counts, sum_before + total, sum_before)
        entire = through * entire + state
        sum_entire = sum_entire + total
    return before, sum_before, entire, sum_entire


def k_in(x_ref, g_ref, w_ref, n_ref, xc_ref, tail_ref):
    normed = normed_of(x_ref[...], g_ref[...])
    n_ref[...] = normed
    xc = dot(normed, w_ref[...]).astype(BF16)
    xc_ref[...] = xc
    tail_ref[...] = xc.astype(F32)[xc.shape[0] - HALO :, :]


def k_gate(n_ref, w_ref, z_ref):
    z_ref[...] = dot(n_ref[...], w_ref[...]).astype(BF16)


def k_dgated(e_ref, w_ref, out_ref):
    out_ref[...] = dot_t(e_ref[...], w_ref[...])


def conv_of(ext_s, halo_ref, xc_ref, cw_ref, cb_ref):
    rows = xc_ref.shape[0]
    taps = cw_ref.shape[0]
    ext_s[0:HALO, :] = halo_ref[...]
    ext_s[HALO:, :] = xc_ref[...].astype(F32)
    out = cb_ref[...]
    for k in range(taps):
        first = HALO - (taps - 1) + k
        out = out + cw_ref[k : k + 1, :] * ext_s[first : first + rows, :]
    return out


def k_local(
    rank, both, *refs
):
    refs = list(refs)
    halo, xc, cw, cb, xw, dw, db, a2 = refs[:8]
    refs = refs[8:]
    if both:
        dgated, z = refs[:2]
        refs = refs[2:]
    u_ref, xd_ref, v_ref, dt_s, pay_ref = refs[:5]
    refs = refs[5:]
    if both:
        dy_ref = refs[0]
        refs = refs[1:]
    ext_s, dtu_s, xdf_s, lhs_s, bc_s, end_s, wide_s = refs
    states = a2.shape[0]
    conv = conv_of(ext_s, halo, xc, cw, cb)
    u = (conv * sigmoid(conv)).astype(BF16)
    u_ref[...] = u
    xd = dot(u, xw[...]).astype(BF16)
    xd_ref[...] = xd
    xdf_s[...] = xd.astype(F32)
    v = dot(xd, dw[...]) + db[...]
    v_ref[...] = v
    dt = softplus(v)
    dt_s[...] = dt
    dtu_s[...] = dt * u.astype(F32)
    total = jnp.sum(dt, axis=0, keepdims=True)
    fill_table(xdf_s, lhs_s, bc_s, rank, states)
    scan_ends(dt_s, dtu_s, bc_s, a2, end_s)
    pay_ref[0:states, :] = packed(end_s[...], total, wide_s)
    if both:
        zf = z[...].astype(F32)
        dy_ref[...] = dgated[...] * (zf * sigmoid(zf))
        scan_back_ends(dt_s, dy_ref, bc_s, a2, end_s)
        pay_ref[states:, :] = packed(end_s[...], total, wide_s)


def k_join(group, nextgroup, mode, digits, *refs):
    refs = list(refs)
    received, refs = refs[:group], refs[group:]
    a2_ref, refs = refs[0], refs[1:]
    kinds = list(mode)
    n_pay = (nextgroup - 1) if (len(kinds) == 2 and nextgroup) else 1
    pays, refs = refs[:n_pay], refs[n_pay:]
    befores, refs = refs[: len(kinds)], refs[len(kinds) :]
    sums, refs = refs[: len(kinds)], refs[len(kinds) :]
    states_s, totals_s, wide_s = refs
    states, inner = a2_ref.shape
    digit = digits[0]
    nextdigit = digits[1]
    out = []
    for i in range(len(kinds)):
        for m in range(group):
            states_s[m] = received[m][i * states : (i + 1) * states, :].astype(F32)
            if i == 0:
                unpack_total(states_s, m, totals_s, inner)
        before, sum_before, entire, sum_entire = join_runs(
            states_s, totals_s, a2_ref[...], digit, group, kinds[i] == "b"
        )
        befores[i][...] = before
        sums[i][...] = sum_before
        out.append(packed(entire, sum_entire, wide_s))
    if len(kinds) == 2 and nextgroup:
        for m in range(1, nextgroup):
            ahead = jnp.bitwise_xor(nextdigit, m) > nextdigit
            pays[m - 1][...] = jnp.where(ahead, out[0].astype(F32), out[1].astype(F32)).astype(
                BF16
            )
    else:
        for i in range(len(kinds)):
            pays[0][i * states : (i + 1) * states, :] = out[i]


def entering(received, a2_ref, digit, befores, sums, states_s, totals_s, backward, lane0=0):
    lanes = a2_ref.shape[1]
    inner = received[0].shape[1] - EXTRA
    here = slice(lane0, lane0 + lanes)
    group = len(received) + 1
    states_s[0] = jnp.zeros(states_s.shape[1:], F32)
    totals_s[0] = jnp.zeros(totals_s.shape[1:], F32)
    for m in range(1, group):
        states_s[m] = received[m - 1][:, here].astype(F32)
        sums_m = received[m - 1][:, inner:].astype(F32)
        for k in range(lanes // 128):
            row = lane0 // 128 + k
            totals_s[m, 0:1, k * 128 : (k + 1) * 128] = (
                sums_m[row : row + 1, 0:128] + sums_m[row : row + 1, 128:256]
            )
    value, _, _, _ = join_runs(states_s, totals_s, a2_ref[...], digit, group, backward)
    for before, total in reversed(list(zip(befores, sums))):
        value = jnp.exp2(total[:, here] * a2_ref[...]) * value + before[:, here]
    return value


def k_mix(rank, last, n_recv, n_low, digits, core, *refs):
    refs = list(refs)
    received, refs = refs[:n_recv], refs[n_recv:]
    befores, refs = refs[:n_low], refs[n_low:]
    sums, refs = refs[:n_low], refs[n_low:]
    a2, u_ref, dt_ref, xd_ref, z_ref, x_ref, sk_ref, ow_ref = refs[:8]
    refs = refs[8:]
    if last:
        dgated_ref, hid_mine, hid_other, dz_ref, dz_keep, gated_keep, sends, h_in_ref = refs[:8]
        y_ref, hid_s, refs = refs[8], refs[9], refs[10:]
    else:
        g_ref, iw_ref, y_ref, x1_ref, n_ref, xc_ref, tail_ref = refs[:7]
        gated_keep, sends, h_in_ref = refs[7:10]
        refs = refs[10:]
    gated_s, dtu_s, xdf_s, lhs_s, bc_s, states_s, totals_s = refs
    h_in_ref[...] = entering(received, a2, digits[0], befores, sums, states_s, totals_s, False)
    uf = u_ref[...].astype(F32)
    dtu_s[...] = dt_ref[...] * uf
    xdf_s[...] = xd_ref[...].astype(F32)
    fill_table(xdf_s, lhs_s, bc_s, rank, a2.shape[0])
    scan_forward(dt_ref, dtu_s, bc_s, a2, h_in_ref, y_ref)
    y = y_ref[...] + sk_ref[...] * u_ref[...].astype(F32)
    zf = z_ref[...].astype(F32)
    s = sigmoid(zf)
    gated = (y * (zf * s)).astype(BF16)
    gated_s[...] = gated
    rows = gated.shape[0]
    gated_keep[...] = lane_half(gated_s, core[0])
    sends[0:rows, :] = lane_half(gated_s, 1 - core[0])
    x1 = x_ref[...] + dot(gated, ow_ref[...])
    if last:
        dz_ref[...] = (dgated_ref[...] * y * (s * (1.0 + zf * (1.0 - s)))).astype(BF16)
        dz_keep[...] = lane_half(dz_ref, core[0])
        sends[rows:, :] = lane_half(dz_ref, 1 - core[0])
        hid_s[...] = x1
        hid_mine[...] = row_half(hid_s, core[0]).astype(BF16)
        hid_other[...] = row_half(hid_s, 1 - core[0]).astype(BF16)
    else:
        y_ref[...] = y
        x1_ref[...] = x1
        normed = normed_of(x1, g_ref[...])
        n_ref[...] = normed
        sends[rows:, :] = normed
        xc = dot(normed, iw_ref[...]).astype(BF16)
        xc_ref[...] = xc
        tail_ref[...] = xc.astype(F32)[xc.shape[0] - HALO :, :]


def k_scan(rank, lane0, n_recv, n_low, digits, *refs):
    refs = list(refs)
    received, refs = refs[:n_recv], refs[n_recv:]
    befores, refs = refs[:n_low], refs[n_low:]
    sums, refs = refs[:n_low], refs[n_low:]
    a2, u_ref, dt_ref, dy_ref, h_in_ref, xd_ref = refs[:6]
    sgb_ref, sqa_ref, rate_ref, dbc_ref = refs[6:10]
    dtu_s, xdf_s, lhs_s, bc_s, states_s, totals_s, db_s, dc_s, a_s, ah_s, g_s = refs[10:]
    states = a2.shape[0]
    rows = u_ref.shape[0]
    g_s[...] = entering(
        received, a2, digits[0], befores, sums, states_s, totals_s, True, lane0
    )
    dtu_s[...] = dt_ref[...] * u_ref[...].astype(F32)
    xdf_s[...] = xd_ref[...].astype(F32)
    fill_table(xdf_s, lhs_s, bc_s, rank, states)
    scan_both(
        dt_ref, dtu_s, dy_ref, bc_s, a2, h_in_ref, g_s, sgb_ref, sqa_ref, rate_ref, db_s, dc_s, a_s, ah_s
    )
    rate_ref[...] = rate_ref[...] * (a2[...] * LN2)

    ones = jnp.ones((128, 128), BF16)

    def lane_sums(block):
        high = block.astype(BF16)
        rest = (block - high.astype(F32)).astype(BF16)
        return dot(high, ones) + dot(rest, ones)

    n_i = lax.broadcasted_iota(jnp.int32, (states, XD), 0)
    lane = lax.broadcasted_iota(jnp.int32, (states, XD), 1)
    mask_b = (lane == rank + n_i).astype(F32)
    mask_c = (lane == rank + states + n_i).astype(F32)
    db_s[...] = lane_sums(db_s[...])
    dc_s[...] = lane_sums(dc_s[...])

    def gather(i, carry):
        parts = []
        for j in range(UNROLL):
            at = state_rows(i * UNROLL + j, states)
            parts.append(fold(db_s[at, :] * mask_b + dc_s[at, :] * mask_c))
        dbc_ref[pl.ds(pl.multiple_of(i * UNROLL, UNROLL), UNROLL), :] = rows_of_sums(parts)
        return carry

    lax.fori_loop(0, rows // UNROLL, gather, 0)


def k_post(rank, n_parts, *refs):
    refs = list(refs)
    sgbs, refs = refs[:n_parts], refs[n_parts:]
    sqas, refs = refs[:n_parts], refs[n_parts:]
    rates, refs = refs[:n_parts], refs[n_parts:]
    dbcs, refs = refs[:n_parts], refs[n_parts:]
    u_ref, v_ref, dt_ref, xd_ref, dy_ref, halo, xc, cw, cb, xw, dw, sk_ref = refs[:12]
    dconv_ref, head_ref, small_ref, ext_s = refs[12:]
    states = rates[0].shape[0]
    rows, inner = u_ref.shape
    sgb = jnp.concatenate([ref[...] for ref in sgbs], axis=1)
    sqa = jnp.concatenate([ref[...] for ref in sqas], axis=1)
    dbc = dbcs[0][...]
    for ref in dbcs[1:]:
        dbc = dbc + ref[...]
    u = u_ref[...]
    uf = u.astype(F32)
    dy = dy_ref[...]
    v = v_ref[...]
    dpre = (LN2 * sqa + uf * sgb) * sigmoid(v)
    dpl = dpre.astype(BF16)
    dxd = (dot_t(dpl, dw[...]) + dbc).astype(BF16)
    du = dt_ref[...] * sgb + sk_ref[...] * dy + dot_t(dxd, xw[...])
    conv = conv_of(ext_s, halo, xc, cw, cb)
    dconv = du * slope(conv)
    dconv_ref[...] = dconv
    head_ref[...] = dconv[0:HALO, :]
    taps = cw.shape[0]
    width = rank + 2 * states
    g_x = dot_rows(dxd, u)
    g_dt = dot_rows(xd_ref[...], dpl)
    at = 0
    small_ref[at : at + width, :] = g_x[0:width]
    at += width
    small_ref[at : at + rank, :] = g_dt[0:rank]
    at += rank
    small_ref[at : at + states, :] = jnp.concatenate([ref[...] for ref in rates], axis=1)
    at += states
    for k in range(taps):
        first = HALO - (taps - 1) + k
        small_ref[at : at + 1, :] = jnp.sum(
            dconv * ext_s[first : first + rows, :], axis=0, keepdims=True
        )
        at += 1
    small_ref[at : at + 1, :] = jnp.sum(dconv, axis=0, keepdims=True)
    small_ref[at + 1 : at + 2, :] = jnp.sum(dpre, axis=0, keepdims=True)
    small_ref[at + 2 : at + 3, :] = jnp.sum(dy * uf, axis=0, keepdims=True)
    small_ref[at + 3 : at + 4, :] = jnp.zeros((1, inner), F32)


def row_half(ref, which):
    half = ref.shape[0] // 2
    return ref[pl.ds(pl.multiple_of(which * half, 16), half), :]


def lane_half(ref, which):
    half = ref.shape[1] // 2
    return ref[:, pl.ds(pl.multiple_of(which * half, 128), half)]


def conv_back(dce_s, dconv_ref, next_ref, cw_ref):
    rows = dconv_ref.shape[0]
    taps = cw_ref.shape[0]
    dce_s[0:rows, :] = dconv_ref[...]
    dce_s[rows:, :] = next_ref[...]
    out = cw_ref[taps - 1 : taps, :] * dce_s[0:rows, :]
    for k in range(taps - 1):
        first = taps - 1 - k
        out = out + cw_ref[k : k + 1, :] * dce_s[first : first + rows, :]
    return out.astype(BF16)


def norm_back(x, gain, e, dn):
    rinv = lax.rsqrt(jnp.mean(x * x, axis=-1, keepdims=True) + 1e-05)
    xhat = x * rinv
    dhat = dn * gain
    g_norm = jnp.sum(dn * xhat, axis=0, keepdims=True)
    return e + rinv * (dhat - xhat * jnp.mean(dhat * xhat, axis=-1, keepdims=True)), g_norm


def small_out(core, small_ref, g_norm, keep_ref, sends, at):
    rows, inner = small_ref.shape
    width = g_norm.shape[1]
    small_ref[rows - 1 : rows, 0:width] = g_norm
    pad = keep_ref.shape[0] - rows
    for which, ref, first in ((core[0], keep_ref, 0), (1 - core[0], sends, at)):
        block = lane_half(small_ref, which)
        block = jnp.concatenate([block, jnp.zeros((pad, block.shape[1]), F32)], axis=0)
        ref[first : first + rows + pad, :] = block.astype(ref.dtype)
    sends[at + rows + pad :, :] = jnp.zeros((sends.shape[0] - at - rows - pad, inner // 2), BF16)


def k_turn(
    rank,
    core,
    small_ref,
    dconv_ref,
    next_ref,
    cw_ref,
    dnz_ref,
    iw_ref,
    x_ref,
    g_ref,
    e_ref,
    ow_ref,
    y_ref,
    z_ref,
    dt_ref,
    xd_ref,
    a2,
    iz_ref,
    dxc_keep,
    small_keep,
    e1_ref,
    de_ref,
    dy_ref,
    dz_ref,
    dz_keep,
    sends,
    dnz0_ref,
    pay_ref,
    small_s,
    dxc_s,
    dce_s,
    xdf_s,
    lhs_s,
    bc_s,
    end_s,
    wide_s,
):
    dxc = conv_back(dce_s, dconv_ref, next_ref, cw_ref)
    rows = dxc.shape[0]
    dxc_s[...] = dxc
    dxc_keep[...] = lane_half(dxc_s, core[0])
    sends[0:rows, :] = lane_half(dxc_s, 1 - core[0])
    dn = dnz_ref[...] + dot_t(dxc, iw_ref[...])
    e1, g_norm = norm_back(x_ref[...], g_ref[...], e_ref[...].astype(F32), dn)
    small_s[...] = small_ref[...]
    small_out(core, small_s, g_norm, small_keep, sends, 3 * rows)
    e1_ref[...] = e1
    de = e1.astype(BF16)
    de_ref[...] = de
    sends[2 * rows : 3 * rows, :] = de
    dgated = dot_t(de, ow_ref[...])
    zf = z_ref[...].astype(F32)
    s = sigmoid(zf)
    dy_ref[...] = dgated * (zf * s)
    dz_ref[...] = (dgated * y_ref[...] * (s * (1.0 + zf * (1.0 - s)))).astype(BF16)
    dz_keep[...] = lane_half(dz_ref, core[0])
    sends[rows : 2 * rows, :] = lane_half(dz_ref, 1 - core[0])
    dnz0_ref[...] = dot_t(dz_ref[...], iz_ref[...])
    states = a2.shape[0]
    total = jnp.sum(dt_ref[...], axis=0, keepdims=True)
    xdf_s[...] = xd_ref[...].astype(F32)
    fill_table(xdf_s, lhs_s, bc_s, rank, states)
    scan_back_ends(dt_ref, dy_ref, bc_s, a2, end_s)
    pay_ref[...] = packed(end_s[...], total, wide_s)


def k_end(
    core,
    small_ref,
    dconv_ref,
    next_ref,
    cw_ref,
    dnz_ref,
    iw_ref,
    x_ref,
    g_ref,
    e_ref,
    dxc_keep,
    small_keep,
    sends,
    e0_mine,
    e0_other,
    small_s,
    dxc_s,
    dce_s,
    e0_s,
):
    dxc = conv_back(dce_s, dconv_ref, next_ref, cw_ref)
    rows = dxc.shape[0]
    dxc_s[...] = dxc
    dxc_keep[...] = lane_half(dxc_s, core[0])
    sends[0:rows, :] = lane_half(dxc_s, 1 - core[0])
    dn = dnz_ref[...] + dot_t(dxc, iw_ref[...])
    e0, g_norm = norm_back(x_ref[...], g_ref[...], e_ref[...], dn)
    small_s[...] = small_ref[...]
    small_out(core, small_s, g_norm, small_keep, sends, rows)
    e0_s[...] = e0
    e0_mine[...] = row_half(e0_s, core[0]).astype(BF16)
    e0_other[...] = row_half(e0_s, 1 - core[0]).astype(BF16)


def k_dnz(dz_ref, iw_ref, out_ref):
    out_ref[...] = dot_t(dz_ref[...], iw_ref[...])


def k_chip_sum(n_pairs, has_small, *refs):
    refs = list(refs)
    pairs, refs = [refs[4 * i : 4 * i + 4] for i in range(n_pairs)], refs[4 * n_pairs :]
    if has_small:
        (small_a, small_b), refs = refs[:2], refs[2:]
    (s_ref,) = refs
    blocks = s_ref.shape[0]
    rows = pairs[0][0].shape[1] // blocks
    for i, (a, a_came, b, b_came) in enumerate(pairs):
        total = dot_rows(
            jnp.concatenate([a[...], a_came[...]], axis=0),
            jnp.concatenate([b[...], b_came[...]], axis=0),
        )
        s_ref[:, i * rows : (i + 1) * rows, :] = total.reshape(blocks, rows, total.shape[1])
    if has_small:
        n = small_a.shape[0] // blocks
        top = n_pairs * rows
        s_ref[:, top:, :] = jnp.zeros((blocks, s_ref.shape[1] - top, s_ref.shape[2]), F32)
        small = small_a[...] + small_b[...].astype(F32)[0 : small_a.shape[0]]
        for k in range(blocks):
            s_ref[k, top : top + n, :] = small[k * n : (k + 1) * n]


def k_first(n_pairs, has_small, place, *refs):
    keep_a, keep_b, send_a, send_b, s_ref = refs[-5:]
    k_chip_sum(n_pairs, has_small, *refs[:-5], s_ref)
    blocks = s_ref.shape[0]
    half = s_ref.shape[2] // 2
    x, y = place[0] & 1, (place[0] >> 1) & 1
    for i in range(blocks // 2):
        at = (i >> 1) * 4 + (i & 1) * 2
        keep_a[i] = s_ref[at + x, :, 0:half]
        send_a[i] = s_ref[at + 1 - x, :, 0:half].astype(BF16)
        at = (i >> 1) * 4 + (i & 1)
        keep_b[i] = s_ref[at + 2 * y, :, half:]
        send_b[i] = s_ref[at + 2 * (1 - y), :, half:].astype(BF16)


def k_second(place, keep_a, keep_b, came_a, came_b, stay_a, stay_b, send_a, send_b):
    x, y = place[0] & 1, (place[0] >> 1) & 1
    for i in range(stay_a.shape[0]):
        for keep, came, stay, send, bit in (
            (keep_a, came_a, stay_a, send_a, y),
            (keep_b, came_b, stay_b, send_b, x),
        ):
            at = 2 * i + bit
            stay[i] = keep[at] + came[at].astype(F32)
            at = 2 * i + 1 - bit
            send[i] = (keep[at] + came[at].astype(F32)).astype(BF16)


def k_third(place, stay_a, stay_b, came_a, came_b, keep, send1, send2, send3):
    z = (place[0] >> 2) & 3
    half = stay_a.shape[2]
    for m, ref in enumerate((keep, send1, send2, send3)):
        at = jnp.bitwise_xor(z, m)
        ref[:, 0:half] = (stay_a[at] + came_a[at].astype(F32)).astype(ref.dtype)
        ref[:, half:] = (stay_b[at] + came_b[at].astype(F32)).astype(ref.dtype)


def k_fourth(keep, came1, came2, came3, out):
    out[...] = (
        keep[...] + came1[...].astype(F32) + came2[...].astype(F32) + came3[...].astype(F32)
    ).astype(BF16)


def k_stack(mine, came1, came2, came3, out_a, out_b):
    half = out_a.shape[2]
    for m, ref in enumerate((mine, came1, came2, came3)):
        out_a[m] = ref[:, 0:half]
        out_b[m] = ref[:, half:]


def k_chip(place, *refs):
    left, right, out = refs[0:4], refs[4:8], refs[8]
    half = left[0].shape[2]
    xy, z = place[0] & 3, (place[0] >> 2) & 3
    for d in range(4):
        for m in range(4):
            at = jnp.bitwise_xor(z, m) * 4 + jnp.bitwise_xor(xy, d)
            out[at, :, 0:half] = left[d][m]
            out[at, :, half:] = right[d][m]


def in_order(core, sources):
    if len(sources) == 1:
        return sources[0][:, 0].astype(F32), sources[0][:, 1].astype(F32)
    own = core[0] == 0
    a, b = sources[0][...].astype(F32), sources[1][...].astype(F32)
    return jnp.where(own, a, b), jnp.where(own, b, a)


def k_place(n_sources, split_rows, core, *refs):
    out, done = refs[-2:]
    done[...] = jnp.zeros(done.shape, F32)
    low, high = in_order(core, refs[:n_sources])
    blocks, rows, lanes = low.shape
    low, high = low.reshape(blocks * rows, lanes), high.reshape(blocks * rows, lanes)
    if split_rows:
        out[0], out[1] = low, high
    else:
        out[:, 0:lanes] = low
        out[:, lanes:] = high


def k_place_small(rank, taps, counts, core, *refs):
    refs = list(refs)
    given, refs = refs[: sum(counts)], refs[sum(counts) :]
    norm, cw, cb, xw, dw, db, al, sk, all_s = refs
    states = al.shape[1]
    n_x = rank + 2 * states
    all_s[...] = jnp.zeros(all_s.shape, F32)
    at = 0
    for l, count in enumerate(counts):
        low, high = in_order(core, given[at : at + count])
        at += count
        blocks, _, lanes = low.shape
        n = -(-(n_x + rank + states + taps + 4) // blocks)
        for k in range(blocks):
            all_s[k * n : (k + 1) * n, 0:lanes] = low[k, 0:n]
            all_s[k * n : (k + 1) * n, lanes:] = high[k, 0:n]
        dw[l] = all_s[n_x : n_x + rank, :]
        first = n_x + rank
        xw[l] = all_s[0:n_x, :]
        al[l] = all_s[first : first + states, :]
        cw[l] = all_s[first + states : first + states + taps, :]
        first += states + taps
        cb[l : l + 1, :] = all_s[first : first + 1, :]
        db[l : l + 1, :] = all_s[first + 1 : first + 2, :]
        sk[l : l + 1, :] = all_s[first + 2 : first + 3, :]
        norm[l : l + 1, :] = all_s[first + 3 : first + 4, 0 : norm.shape[1]]


def shards(
    hidden_in,
    norm_gain,
    in_weight,
    conv_weight,
    conv_bias,
    xproj_weight,
    dtproj_weight,
    dt_bias,
    a_log,
    skip_gain,
    out_weight,
    hidden_grad,
):
    layers, width, _ = in_weight.shape
    inner, states = a_log.shape[1], a_log.shape[2]
    rank = dtproj_weight.shape[1]
    taps = conv_weight.shape[2]
    seqs, own, _ = hidden_in.shape
    ndev = lax.axis_size(AXIS)
    me = lax.axis_index(AXIS)
    core = me % 2
    chip = me // 2
    rows = seqs * own
    assert layers == 2 and seqs == 2 and ndev % 2 == 0
    assert inner % CHUNK == 0 and inner // 128 <= states and rank + 2 * states <= XD

    pairs = [(i, i ^ 1) for i in range(ndev)]
    turn = []
    call = functools.partial(run, turn=turn)

    def to_runs(block):
        mine = lax.dynamic_index_in_dim(block, core, 0, keepdims=False)
        other = lax.dynamic_index_in_dim(block, 1 - core, 0, keepdims=False)
        came = lax.ppermute(other, AXIS, pairs)
        first = jnp.where(core == 0, mine, came)
        second = jnp.where(core == 0, came, mine)
        return jnp.concatenate([first, second], axis=0)

    def from_runs(mine, other):
        came = lax.ppermute(other, AXIS, pairs)
        first = jnp.where(core == 0, mine, came)
        second = jnp.where(core == 0, came, mine)
        return jnp.stack([first, second], axis=0)

    def done_by_now(array):
        array, turn[0] = lax.optimization_barrier((array, turn[0]))
        return array

    def not_before(*arrays):
        return lax.optimization_barrier(arrays + (turn[0],))[:-1]

    def from_before(block):
        return lax.ppermute(block, AXIS, [(i, i + 2) for i in range(ndev - 2)])

    def from_after(block):
        return lax.ppermute(block, AXIS, [(i + 2, i) for i in range(ndev - 2)])

    bits = (ndev // 2).bit_length() - 1
    assert 2 << bits == ndev and bits > 2
    rounds = []
    low = 0
    while low < bits:
        n = 2 if bits - low >= 2 else 1
        rounds.append((low, 1 << n))
        low += n

    def digit_of(r):
        low, group = rounds[r]
        return (chip >> low) & (group - 1)

    def digits_of(r):
        nxt = digit_of(r + 1) if r + 1 < len(rounds) else jnp.zeros_like(chip)
        return jnp.stack([digit_of(r), nxt]).astype(jnp.int32)

    def send(block, r, m, which):
        low, group = rounds[r]
        flip = (m << low) << 1
        route = [(i, i ^ flip) for i in range(ndev)]
        if which == "up":
            route = [(i, j) for i, j in route if j > i]
        if which == "down":
            route = [(i, j) for i, j in route if j < i]
        return lax.ppermute(block, AXIS, route)

    smem = pl.BlockSpec(memory_space=pltpu.SMEM)
    core_s = (core[None].astype(jnp.int32), smem)

    def swap(block):
        return lax.ppermute(block, AXIS, pairs)

    pay = shape((states, inner + EXTRA), BF16)

    kept = {}

    def exchange(payload, a2, mode, meanwhile=()):
        meanwhile = dict(enumerate(meanwhile))
        befores = [[] for _ in mode]
        sums = [[] for _ in mode]
        for r, (low, group) in enumerate(rounds[:-1]):
            received = [payload] + [send(payload, r, m, "all") for m in range(1, group)]
            kept["first"] = received[1:]
            if r in meanwhile:
                meanwhile[r]()
            final = r + 2 == len(rounds)
            split = len(mode) == 2 and final
            nextgroup = rounds[r + 1][1] if split else 0
            pays = (
                [pay] * (nextgroup - 1)
                if split
                else [shape((states * len(mode), inner + EXTRA), BF16)]
            )
            outs = call(
                functools.partial(k_join, group, nextgroup, mode),
                pays
                + [shape((states, inner), F32)] * len(mode)
                + [shape((1, inner), F32)] * len(mode),
                [(digits_of(r), smem)] + received + [a2],
                [
                    pltpu.VMEM((group, states, inner + EXTRA), F32),
                    pltpu.VMEM((group, 8, inner), F32),
                    pltpu.VMEM((states, inner + EXTRA), F32),
                ],
            )
            sent, outs = outs[: len(pays)], outs[len(pays) :]
            for i in range(len(mode)):
                befores[i].append(outs[i])
                sums[i].append(outs[len(mode) + i])
            payload = sent if split else sent[0]
        r = len(rounds) - 1
        if len(mode) == 2:
            last = [send(payload[m - 1], r, m, "all") for m in range(1, rounds[r][1])]
        else:
            way = "up" if mode == "f" else "down"
            last = [send(payload, r, m, way) for m in range(1, rounds[r][1])]
        for step in sorted(meanwhile):
            if step >= r:
                meanwhile[step]()
        return last, sum(befores, []), sum(sums, []), digits_of(r)

    def row(array, l):
        return Row(array, l)

    def layer_of(array, l):
        return array, part((None,) + array.shape[1:], (l, 0, 0))

    def w_in(l, half):
        columns = slice(half * inner, (half + 1) * inner)
        return Late(in_weight, (l, slice(None), columns), (width, inner))

    def w_out(l):
        return Late(out_weight, (l,), (inner, width))

    def table_scratch():
        return [
            pltpu.VMEM((rows, XD), F32),
            pltpu.VMEM((rows * states, XD), BF16),
            pltpu.VMEM((rows * states, 256), F32),
        ]

    act = shape((rows, inner), F32)
    act_b = shape((rows, inner), BF16)
    res = shape((rows, width), F32)
    res_b = shape((rows, width), BF16)
    edge = shape((HALO, inner), F32)
    mm = 2 * rows * width * inner

    x0 = to_runs(hidden_in).astype(F32)

    normed = [None, None]
    xc = [None, None]
    halo = [None, None]
    z = [None, None]
    u = [None, None]
    xd = [None, None]
    v = [None, None]
    step = [None, None]

    normed[0], xc[0], tail = call(
        k_in, [res_b, act_b, edge], [x0, row(norm_gain, 0), in_weight[0, :, 0:inner]]
    )

    a_log, conv_weight, xproj_weight, dtproj_weight, hidden_grad = not_before(
        a_log, conv_weight, xproj_weight, dtproj_weight, hidden_grad
    )
    a2_all = -jnp.exp(jnp.swapaxes(a_log, 1, 2)) * LOG2E
    cw_all = jnp.swapaxes(conv_weight, 1, 2)
    xw_all = jnp.pad(xproj_weight, ((0, 0), (0, 0), (0, XD - xproj_weight.shape[2])))
    dw_all = jnp.pad(dtproj_weight, ((0, 0), (0, XD - rank), (0, 0)))
    grad_out = to_runs(hidden_grad)

    def gate(l):
        (z[l],) = call(k_gate, [act_b], [normed[l], w_in(l, 1)], cost=LONG)

    def before_scan(l, tail, dgated=None):
        halo[l] = from_before(tail)
        if l:
            gate(l)
        both = dgated is not None
        outs = call(
            functools.partial(k_local, rank, both),
            [
                act_b,
                shape((rows, XD), BF16),
                act,
                act,
                shape((states * (2 if both else 1), inner + EXTRA), BF16),
            ]
            + ([act] if both else []),
            [
                halo[l],
                xc[l],
                layer_of(cw_all, l),
                row(conv_bias, l),
                layer_of(xw_all, l),
                layer_of(dw_all, l),
                row(dt_bias, l),
                layer_of(a2_all, l),
            ]
            + ([dgated, z[l]] if both else []),
            [pltpu.VMEM((rows + HALO, inner), F32)]
            + [pltpu.VMEM((rows, inner), F32)]
            + table_scratch()
            + [pltpu.VMEM((states, inner), F32), pltpu.VMEM((states, inner + EXTRA), F32)],
            cost=LONG,
        )
        u[l], xd[l], v[l], step[l] = outs[:4]
        return outs[4:]

    def join_scratch():
        group = rounds[-1][1]
        return [
            pltpu.VMEM((group, states, inner), F32),
            pltpu.VMEM((group, 8, inner), F32),
        ]

    def piece(array, i):
        return array, part((rows, array.shape[1]), (i, 0))

    def mix(l, parts, extra, outs):
        final = l == layers - 1
        last, befores, sums, digits = parts
        befores, sums = befores[: len(rounds) - 1], sums[: len(rounds) - 1]
        return call(
            functools.partial(k_mix, rank, final, len(last), len(befores)),
            outs,
            [(digits, smem), core_s]
            + last
            + befores
            + sums
            + [layer_of(a2_all, l), u[l], step[l], xd[l], z[l], residual[l], row(skip_gain, l), w_out(l)]
            + extra,
            ([act_scratch, pltpu.VMEM((rows, width), F32)] if final else [])
            + [pltpu.VMEM((rows, inner), BF16)]
            + [act_scratch]
            + table_scratch()
            + join_scratch(),
            cost=LONG,
        )

    half_b = shape((rows, width), BF16)
    entry = shape((states, inner), F32)
    act_scratch = pltpu.VMEM((rows, inner), F32)
    residual = [x0, None]
    def shadow_00():
        gate(0)

    def shadow_0():
        (kept["dgated1"],) = call(k_dgated, [act], [grad_out, w_out(1)], cost=LONG)

    (payload,) = before_scan(0, tail)
    parts = exchange(payload, layer_of(a2_all, 0), "f", (shadow_00, shadow_0))
    dgated1 = kept["dgated1"]
    y0, x1, normed[1], xc[1], tail, gated_keep, sends, h0 = mix(
        0,
        parts,
        [row(norm_gain, 1), w_in(1, 0)],
        [act, res, res_b, act_b, edge, half_b, shape((2 * rows, width), BF16), entry],
    )
    residual[1] = x1
    came = swap(sends)
    n1_pair = (normed[1], piece(came, 1))
    gated0_pair = (gated_keep, piece(came, 0))
    n0_pair = (normed[0], swap(normed[0]))
    e1_pair = (grad_out, swap(grad_out))
    payload, dy1 = before_scan(1, tail, dgated1)
    parts = exchange(payload, layer_of(a2_all, 1), "fb")
    n_small = rank + 2 * states + rank + states + taps + 4
    small = shape((n_small, inner), F32)
    small_pad = -(-n_small // (BLOCKS * 2)) * BLOCKS * 2 if n_small % BLOCKS else n_small

    n_chunks = inner // CHUNK
    cuts = [(0, (n_chunks + 1) // 2 * CHUNK), ((n_chunks + 1) // 2 * CHUNK, n_chunks // 2 * CHUNK)]
    n_parts = len(cuts)
    assert all(first % lanes == 0 for first, lanes in cuts)

    def scan(l, i, dy, parts, h_in):
        lane0, lanes = cuts[i]
        last, befores, sums, digits = parts
        n_low = len(rounds) - 1
        cut = part((rows, lanes), (0, lane0 // lanes))
        cut_s = part((states, lanes), (0, lane0 // lanes))
        cut_a = part((None, states, lanes), (l, 0, lane0 // lanes))
        return call(
            functools.partial(k_scan, rank, lane0, len(last), n_low),
            [shape((rows, lanes), F32)] * 2 + [shape((states, lanes), F32), shape((rows, XD), F32)],
            [(digits, smem)]
            + last
            + befores[-n_low:]
            + sums[-n_low:]
            + [(a2_all, cut_a), (u[l], cut), (step[l], cut), (dy, cut), (h_in, cut_s), xd[l]],
            [pltpu.VMEM((rows, lanes), F32)]
            + table_scratch()
            + [
                pltpu.VMEM((rounds[-1][1], states, lanes), F32),
                pltpu.VMEM((rounds[-1][1], 8, lanes), F32),
            ]
            + [pltpu.VMEM((rows * states, 128), F32)] * 2
            + [pltpu.VMEM((rows * states, CHUNK), F32)] * 2
            + [pltpu.VMEM((states, lanes), F32)],
            cost=LONG,
        )

    def post(l, scans, dy):
        return call(
            functools.partial(k_post, rank, n_parts),
            [act, edge, small],
            [outs[k] for k in range(4) for outs in scans]
            + [
                u[l],
                v[l],
                step[l],
                xd[l],
                dy,
                halo[l],
                xc[l],
                layer_of(cw_all, l),
                row(conv_bias, l),
                layer_of(xw_all, l),
                layer_of(dw_all, l),
                row(skip_gain, l),
            ],
            [pltpu.VMEM((rows + HALO, inner), F32)],
            cost=LONG,
        )


    def over(block, flip):
        return lax.ppermute(block, AXIS, [(i, i ^ (flip << 1)) for i in range(ndev)])

    place_s = (chip[None].astype(jnp.int32), smem)

    def held(arrays, gate):
        if gate is None:
            return arrays
        return lax.optimization_barrier(tuple(arrays) + tuple(gate()))[: len(arrays)]

    def summed(matrices, smalls, aside=False, gates=(None, None, None)):
        ins = []
        each = width // BLOCKS
        for (a, a_came), (b, b_came) in matrices:
            ins += [a, a_came, b, b_came]
        r = each * len(matrices)
        if smalls is not None:
            ins += list(smalls)
            r += 16
        has_small = smalls is not None
        half = width // 2
        if ndev != 2 * BLOCKS:
            (mine,) = call(
                functools.partial(k_chip_sum, len(matrices), has_small),
                [shape((BLOCKS, r, width), F32)],
                ins,
            )
            empty = jnp.zeros((2,) + mine.shape, F32)
            total = lax.psum(lax.dynamic_update_index_in_dim(empty, mine, core, 0), AXIS)
            total = total.astype(BF16)
            for _ in range(3 if aside else 5):
                yield None
            if aside:
                yield jnp.swapaxes(total, 0, 1)
                return
            yield (
                lax.dynamic_index_in_dim(total, core, 0, keepdims=False),
                lax.dynamic_index_in_dim(total, 1 - core, 0, keepdims=False),
            )
            return
        n = BLOCKS // 2
        keep_a, keep_b, send_a, send_b = call(
            functools.partial(k_first, len(matrices), has_small),
            [shape((n, r, half), F32)] * 2 + [shape((n, r, half), BF16)] * 2,
            [place_s] + ins,
            [pltpu.VMEM((BLOCKS, r, width), F32)],
            cost=LONG,
        )
        send_a, send_b = held([send_a, send_b], gates[0])
        came_a, came_b = over(send_a, 1), over(send_b, 2)
        yield None
        n = BLOCKS // 4
        stay_a, stay_b, send_a, send_b = call(
            k_second,
            [shape((n, r, half), F32)] * 2 + [shape((n, r, half), BF16)] * 2,
            [place_s, keep_a, keep_b, came_a, came_b],
        )
        send_a, send_b = held([send_a, send_b], gates[1])
        came_a, came_b = over(send_a, 2), over(send_b, 1)
        yield None
        keep, *sends = call(
            k_third,
            [shape((r, width), F32)] + [shape((r, width), BF16)] * 3,
            [place_s, stay_a, stay_b, came_a, came_b],
        )
        sends = held(sends, gates[2])
        came = [over(send_m, 4 * (m + 1)) for m, send_m in enumerate(sends)]
        yield None
        (done,) = call(k_fourth, [shape((r, width), BF16)], [keep] + came)
        if aside:
            every = lax.all_gather(done, AXIS)
            yield every.reshape(BLOCKS, 2, r, width)
            return
        came = [over(done, 4 * m) for m in (1, 2, 3)]
        yield None
        left, right = call(k_stack, [shape((4, r, half), BF16)] * 2, [done] + came)
        left_y, right_x = over(left, 2), over(right, 1)
        lefts = [left, over(left, 1), left_y, over(left_y, 1)]
        rights = [right, right_x, over(right, 2), over(right_x, 2)]
        yield None
        (mine,) = call(
            k_chip, [shape((BLOCKS, r, width), BF16)], [place_s] + lefts + rights
        )
        yield mine, swap(mine)

    def sources(halves, i, per, each, place):
        if not isinstance(halves, tuple):
            spec = pl.BlockSpec((per, 2, each, width), lambda g: (place(g), 0, i, 0))
            return [halves], [spec]
        spec = pl.BlockSpec((per, each, width), lambda g: (place(g), i, 0))
        return list(halves), [spec, spec]

    def placed(halves, i, whole, block, index, split_rows, before):
        each = width // BLOCKS
        steps = 2
        anywhere = pl.BlockSpec(memory_space=pl.ANY)
        arrays, specs = sources(halves, i, BLOCKS // steps, each, lambda g: g)
        ins = [core_s[0]] + arrays + [turn[0]]
        specs = [smem] + specs + [anywhere]
        aliases = {}
        if before is not None:
            aliases = {len(ins): 0}
            ins.append(before)
            specs.append(anywhere)
        out, turn[0] = pl.pallas_call(
            functools.partial(k_place, len(arrays), split_rows),
            grid=(steps,),
            in_specs=specs,
            out_specs=[pl.BlockSpec(block, index), pl.BlockSpec((8, 128), lambda g: (0, 0))],
            out_shape=[whole, shape((8, 128), F32)],
            input_output_aliases=aliases,
            compiler_params=pltpu.CompilerParams(vmem_limit_bytes=58 * 1024 * 1024),
            cost_estimate=COST,
        )(*ins)
        return out

    g_out_shape = shape((layers, 2, width, width), F32)
    g_in_shape = shape((layers, width, 2 * inner), F32)
    several = width // 2
    out_block = (None, 2, several, width)
    in_block = (None, several, inner)

    def out_at(l):
        return lambda g: (l, 0, g, 0)

    def in_at(l, half):
        return lambda g: (l, g, half)

    def placed_small(layer_sums):
        each = width // BLOCKS
        ins, counts = [core_s], []
        for halves, i in layer_sums:
            arrays, specs = sources(halves, i * each // 16, BLOCKS, 16, lambda g: 0)
            ins += list(zip(arrays, specs))
            counts.append(len(arrays))
        n_x = rank + 2 * states
        return call(
            functools.partial(k_place_small, rank, taps, tuple(counts)),
            [
                shape((layers, width), F32),
                shape((layers, taps, inner), F32),
                shape((layers, inner), F32),
                shape((layers, n_x, inner), F32),
                shape((layers, rank, inner), F32),
                shape((layers, inner), F32),
                shape((layers, states, inner), F32),
                shape((layers, inner), F32),
            ],
            ins,
            [pltpu.VMEM((small_pad, inner), F32)],
            spare=58,
        )

    half_small = shape((small_pad, width), F32)

    hid_mine, hid_other, dz1, dz_keep, gated_keep, sends, h1 = mix(
        1,
        parts,
        [dgated1],
        [shape((own, width), BF16)] * 2
        + [act_b, half_b, half_b, shape((2 * rows, width), BF16), entry],
    )
    came = swap(sends)
    hidden_out = from_runs(hid_mine, hid_other)
    a_sum = summed(
        [((gated_keep, piece(came, 0)), e1_pair), (n1_pair, (dz_keep, piece(came, 1)))],
        None,
        True,
        (None, None, lambda: [after1]),
    )
    scans = [scan(1, 0, dy1, parts, h1)]
    next(a_sum)
    scans.append(scan(1, 1, dy1, parts, h1))
    hidden_out = done_by_now(hidden_out)
    next(a_sum)
    dconv1, head1, small1 = post(1, scans, dy1)
    after1 = from_after(head1)
    (dnz1,) = call(k_dnz, [res], [dz1, w_in(1, 1)], cost=LONG)
    next(a_sum)
    turn_back = functools.partial(
        call,
        functools.partial(k_turn, rank),
        [half_b, half_small, res, res_b, act, act_b, half_b]
        + [shape((4 * rows, width), BF16), res, pay],
        [
            core_s,
            small1,
            dconv1,
            after1,
            layer_of(cw_all, 1),
            dnz1,
            w_in(1, 0),
            x1,
            row(norm_gain, 1),
            grad_out,
            w_out(0),
            y0,
            z[0],
            step[0],
            xd[0],
            layer_of(a2_all, 0),
            w_in(0, 1),
        ],
        [
            pltpu.VMEM((n_small, inner), F32),
            pltpu.VMEM((rows, inner), BF16),
            pltpu.VMEM((rows + HALO, inner), F32),
        ]
        + table_scratch()
        + [pltpu.VMEM((states, inner), F32), pltpu.VMEM((states, inner + EXTRA), F32)],
        cost=LONG,
    )
    dxc_keep, small_keep, e1, de0, dy0, _, dz_keep, sends, dnz0, payload = turn_back()
    came = swap(sends)
    b_sum = summed(
        [
            (n1_pair, (dxc_keep, piece(came, 0))),
            (gated0_pair, (de0, piece(came, 2))),
            (n0_pair, (dz_keep, piece(came, 1))),
        ],
        (small_keep, piece(came, 3)),
        True,
        (lambda: kept["first"], None, None),
    )

    def shadow_1():
        kept["sum_a"] = next(a_sum)
        next(b_sum)

    parts = exchange(payload, layer_of(a2_all, 0), "b", (shadow_1,))
    sum_a = kept["sum_a"]
    scans = [scan(0, 0, dy0, parts, h0)]
    next(b_sum)
    scans.append(scan(0, 1, dy0, parts, h0))
    next(b_sum)
    dconv0, head0, small0 = post(0, scans, dy0)
    after0 = from_after(head0)
    dxc_keep, small_keep, sends, e0_mine, e0_other = call(
        k_end,
        [half_b, half_small, shape((2 * rows, width), BF16)] + [shape((own, width), BF16)] * 2,
        [
            core_s,
            small0,
            dconv0,
            after0,
            layer_of(cw_all, 0),
            dnz0,
            w_in(0, 0),
            x0,
            row(norm_gain, 0),
            e1,
        ],
        [
            pltpu.VMEM((n_small, inner), F32),
            pltpu.VMEM((rows, inner), BF16),
            pltpu.VMEM((rows + HALO, inner), F32),
            pltpu.VMEM((rows, width), F32),
        ],
        cost=LONG,
    )
    came = swap(sends)
    c_sum = summed(
        [(n0_pair, (dxc_keep, piece(came, 0)))], (small_keep, piece(came, 1))
    )
    sum_b = next(b_sum)
    next(c_sum)
    g_out = placed(sum_a, 0, g_out_shape, out_block, out_at(1), True, None)
    input_grad = done_by_now(from_runs(e0_mine, e0_other))
    next(c_sum)
    next(c_sum)
    g_in = placed(sum_a, 1, g_in_shape, in_block, in_at(1, 1), False, None)
    next(c_sum)
    next(c_sum)
    sum_c = next(c_sum)
    g_in = placed(sum_b, 0, g_in_shape, in_block, in_at(1, 0), False, g_in)
    g_out = placed(sum_b, 1, g_out_shape, out_block, out_at(0), True, g_out)
    g_in = placed(sum_b, 2, g_in_shape, in_block, in_at(0, 1), False, g_in)
    g_in = placed(sum_c, 0, g_in_shape, in_block, in_at(0, 0), False, g_in)
    g_norm, g_cw, g_cb, g_xw, g_dw, g_db, g_al, g_sk = placed_small([(sum_c, 1), (sum_b, 3)])
    return (
        hidden_out,
        input_grad,
        g_norm,
        g_in,
        jnp.swapaxes(g_cw, 1, 2),
        g_cb,
        jnp.swapaxes(g_xw, 1, 2),
        g_dw,
        g_db,
        jnp.swapaxes(g_al, 1, 2),
        g_sk,
        g_out.reshape(layers, inner, width),
    )


def solution(mesh):
    split = P(None, AXIS, None)
    return jax.shard_map(
        shards,
        mesh=mesh,
        in_specs=(split,) + (P(),) * 10 + (split,),
        out_specs=(split, split) + (P(),) * 10,
        check_vma=False,
    )
```

```python
import functools
import math

import jax
import jax.numpy as jnp
from jax import lax
from jax.experimental import pallas as pl
from jax.experimental.pallas import tpu as pltpu
from jax.sharding import PartitionSpec as P

BF16 = jnp.bfloat16
F32 = jnp.float32
LOG2E = 1.4426950408889634
LN2 = 0.6931471805599453
AXIS = "seq"
XD = 128
EXTRA = 256
CHUNK = 512
UNROLL = 8
HALO = 8
COST = pl.CostEstimate(flops=1, bytes_accessed=1, transcendentals=0)
LONG = pl.CostEstimate(flops=1, bytes_accessed=10**8, transcendentals=0)
SPARE = 6
BLOCKS = 16


def full(array):
    nd = len(array.shape)
    return pl.BlockSpec(array.shape, lambda i, nd=nd: (0,) * nd)


def part(shape, index):
    return pl.BlockSpec(shape, lambda i, index=index: index)


def room(specs, dtypes, out_specs, out_dtypes, scratch, spare):
    total = spare << 20
    for spec, dtype in list(zip(specs, dtypes)) + list(zip(out_specs, out_dtypes)):
        if spec.block_shape is not None:
            total += math.prod(d or 1 for d in spec.block_shape) * jnp.dtype(dtype).itemsize
    for item in scratch:
        if not hasattr(item, "shape"):
            continue
        total += math.prod(item.shape) * jnp.dtype(item.dtype).itemsize
    return min(total, 58 << 20)


class Late:
    def __init__(self, array, index, dims):
        self.array, self.index, self.dims = array, index, dims


class Fetched:
    def __init__(self, source, target, sem):
        self.copy, self.ref = pltpu.make_async_copy(source, target, sem), target
        self.copy.start()

    def __getitem__(self, where):
        if self.copy is not None:
            self.copy.wait()
            self.copy = None
        return self.ref[where]


class Row:
    def __init__(self, array, index):
        self.array, self.index = array, index


def run(kernel, outs, ins, scratch=(), turn=None, cost=COST, spare=SPARE):
    out_specs = [o[1] if isinstance(o, tuple) else full(o) for o in outs]
    outs = [o[0] if isinstance(o, tuple) else o for o in outs]
    arrays, specs, picks, late = [], [], {}, {}
    scratch = list(scratch)
    for item in ins:
        if isinstance(item, Late):
            late[len(arrays)] = item.index
            scratch += [pltpu.VMEM(item.dims, item.array.dtype), pltpu.SemaphoreType.DMA]
            item = (item.array, pl.BlockSpec(memory_space=pltpu.HBM))
        if isinstance(item, Row):
            picks[len(arrays)] = item.index
            item = item.array
        if isinstance(item, tuple):
            arrays.append(item[0])
            specs.append(item[1])
        else:
            arrays.append(item)
            specs.append(full(item))
    n = len(arrays)
    limit = room(specs, [a.dtype for a in arrays], out_specs, [o.dtype for o in outs], scratch, spare)
    if turn:
        arrays.append(turn[0])
        specs.append(pl.BlockSpec(memory_space=pl.ANY))
    after = len(arrays)

    def body(*refs):
        given = list(refs[:n])
        for k, index in picks.items():
            given[k] = given[k].at[index : index + 1, :]
        rest, buffers = refs[after:], ()
        if late:
            rest, buffers = rest[: -2 * len(late)], rest[-2 * len(late) :]
        for i, (k, index) in enumerate(late.items()):
            given[k] = Fetched(given[k].at[index], buffers[2 * i], buffers[2 * i + 1])
        kernel(*given, *rest)

    results = pl.pallas_call(
        body,
        grid=(1,),
        in_specs=specs,
        out_specs=out_specs,
        out_shape=outs,
        scratch_shapes=list(scratch),
        compiler_params=pltpu.CompilerParams(vmem_limit_bytes=limit),
        cost_estimate=cost,
    )(*arrays)
    if turn is not None:
        turn[:] = [results[-1]]
    return results


def shape(dims, dtype):
    return jax.ShapeDtypeStruct(dims, dtype)


def dot(a, b):
    return jnp.dot(a, b, preferred_element_type=F32)


def dot_t(a, b):
    return lax.dot_general(a, b, (((1,), (1,)), ((), ())), preferred_element_type=F32)


def dot_rows(a, b):
    return lax.dot_general(a, b, (((0,), (0,)), ((), ())), preferred_element_type=F32)


def sigmoid(v):
    return 1.0 / (1.0 + jnp.exp(-v))


def softplus(v):
    return jnp.maximum(v, 0.0) + jnp.log1p(jnp.exp(-jnp.abs(v)))


def slope(v):
    s = sigmoid(v)
    return s * (1.0 + v * (1.0 - s))


def wide(block, lanes):
    return jnp.concatenate([block] * (lanes // block.shape[1]), axis=1)


def rows_of_sums(parts):
    row = lax.broadcasted_iota(jnp.int32, parts[0].shape, 0)
    m4, m2, m1 = row < 4, (row & 2) == 0, (row & 1) == 0
    q = []
    for i in range(4):
        first = jnp.where(m4, parts[i], parts[i + 4])
        other = jnp.where(m4, parts[i + 4], parts[i])
        q.append(first + pltpu.roll(other, 4, 0))
    s = []
    for i in range(2):
        s.append(
            jnp.where(
                m2, q[i] + pltpu.roll(q[i], 6, 0), q[i + 2] + pltpu.roll(q[i + 2], 2, 0)
            )
        )
    return jnp.where(m1, s[0] + pltpu.roll(s[0], 7, 0), s[1] + pltpu.roll(s[1], 1, 0))


def fold(block):
    out = block[0:8]
    for k in range(8, block.shape[0], 8):
        out = out + block[k : k + 8]
    return out


def fold_lanes(block):
    out = block[:, 0:128]
    for k in range(128, block.shape[1], 128):
        out = out + block[:, k : k + 128]
    return out


def normed_of(x, gain):
    rinv = lax.rsqrt(jnp.mean(x * x, axis=-1, keepdims=True) + 1e-05)
    return (x * rinv * gain).astype(BF16)


def fill_table(xdf_ref, lhs_ref, bc_ref, rank, states):
    rows = xdf_ref.shape[0]
    n_i = lax.broadcasted_iota(jnp.int32, (states, XD), 0)
    lane = lax.broadcasted_iota(jnp.int32, (states, XD), 1)
    mask = ((lane == rank + n_i) | (lane == rank + states + n_i)).astype(F32)

    def body(i, carry):
        for j in range(UNROLL):
            t = i * UNROLL + j
            line = xdf_ref[pl.ds(t, 1), :]
            lhs_ref[pl.ds(pl.multiple_of(t * states, states), states), :] = (
                line * mask
            ).astype(BF16)
        return carry

    lax.fori_loop(0, rows // UNROLL, body, 0)
    k_i = lax.broadcasted_iota(jnp.int32, (XD, 256), 0)
    c_i = lax.broadcasted_iota(jnp.int32, (XD, 256), 1)
    low = rank + jnp.where(c_i >= 128, states, 0)
    pick = ((k_i >= low) & (k_i < low + states)).astype(BF16)
    bc_ref[...] = dot(lhs_ref[...], pick)


def state_rows(t, states):
    return pl.ds(pl.multiple_of(t * states, states), states)


def scan_ends(dt_ref, dtu_ref, bc_ref, a2_ref, end_ref):
    rows, inner = dt_ref.shape
    states = a2_ref.shape[0]

    def chunk(c, carry):
        lanes = pl.ds(pl.multiple_of(c * CHUNK, CHUNK), CHUNK)
        a2 = a2_ref[:, lanes]

        def body(i, h):
            for j in range(UNROLL):
                t = i * UNROLL + j
                a = jnp.exp2(dt_ref[pl.ds(t, 1), lanes] * a2)
                b = wide(bc_ref[state_rows(t, states), 0:128], CHUNK)
                h = a * h + dtu_ref[pl.ds(t, 1), lanes] * b
            return h

        end_ref[:, lanes] = lax.fori_loop(
            0, rows // UNROLL, body, jnp.zeros((states, CHUNK), F32)
        )
        return carry

    lax.fori_loop(0, inner // CHUNK, chunk, 0)


def scan_back_ends(dt_ref, dy_ref, bc_ref, a2_ref, end_ref):
    rows, inner = dt_ref.shape
    states = a2_ref.shape[0]

    def chunk(c, carry):
        lanes = pl.ds(pl.multiple_of(c * CHUNK, CHUNK), CHUNK)
        a2 = a2_ref[:, lanes]

        def body(i, back):
            for j in range(UNROLL):
                t = rows - 1 - (i * UNROLL + j)
                a = jnp.exp2(dt_ref[pl.ds(t, 1), lanes] * a2)
                c_row = wide(bc_ref[state_rows(t, states), 128:256], CHUNK)
                back = a * (dy_ref[pl.ds(t, 1), lanes] * c_row + back)
            return back

        end_ref[:, lanes] = lax.fori_loop(
            0, rows // UNROLL, body, jnp.zeros((states, CHUNK), F32)
        )
        return carry

    lax.fori_loop(0, inner // CHUNK, chunk, 0)


def scan_forward(dt_ref, dtu_ref, bc_ref, a2_ref, h_in_ref, y_ref):
    rows, inner = dt_ref.shape
    states = a2_ref.shape[0]

    def chunk(c, carry):
        lanes = pl.ds(pl.multiple_of(c * CHUNK, CHUNK), CHUNK)
        a2 = a2_ref[:, lanes]

        def body(i, h):
            parts = []
            for j in range(UNROLL):
                t = i * UNROLL + j
                a = jnp.exp2(dt_ref[pl.ds(t, 1), lanes] * a2)
                both = bc_ref[state_rows(t, states), :]
                h = a * h + dtu_ref[pl.ds(t, 1), lanes] * wide(both[:, 0:128], CHUNK)
                parts.append(fold(h * wide(both[:, 128:256], CHUNK)))
            y_ref[pl.ds(pl.multiple_of(i * UNROLL, UNROLL), UNROLL), lanes] = rows_of_sums(
                parts
            )
            return h

        lax.fori_loop(0, rows // UNROLL, body, h_in_ref[:, lanes])
        return carry

    lax.fori_loop(0, inner // CHUNK, chunk, 0)


def scan_both(
    dt_ref,
    dtu_ref,
    dy_ref,
    bc_ref,
    a2_ref,
    h_in_ref,
    g_in_ref,
    sgb_ref,
    sqa_ref,
    rate_ref,
    db_ref,
    dc_ref,
    a_s,
    ah_s,
):
    rows, inner = dt_ref.shape
    states = a2_ref.shape[0]
    db_ref[...] = jnp.zeros(db_ref.shape, F32)
    dc_ref[...] = jnp.zeros(dc_ref.shape, F32)

    def chunk(c, carry):
        lanes = pl.ds(pl.multiple_of(c * CHUNK, CHUNK), CHUNK)
        a2 = a2_ref[:, lanes]

        def ahead(i, h):
            for j in range(UNROLL):
                t = i * UNROLL + j
                at = state_rows(t, states)
                a = jnp.exp2(dt_ref[pl.ds(t, 1), lanes] * a2)
                b_row = wide(bc_ref[at, 0:128], CHUNK)
                ah = a * h
                a_s[at, :] = a
                ah_s[at, :] = ah
                h = ah + dtu_ref[pl.ds(t, 1), lanes] * b_row
                dc_ref[at, :] += fold_lanes(h * dy_ref[pl.ds(t, 1), lanes])
            return h

        lax.fori_loop(0, rows // UNROLL, ahead, h_in_ref[:, lanes])

        def retreat(i, carried):
            back, rate = carried
            block = rows // UNROLL - 1 - i
            gbs, qas = [None] * UNROLL, [None] * UNROLL
            for j in reversed(range(UNROLL)):
                t = block * UNROLL + j
                at = state_rows(t, states)
                both = bc_ref[at, :]
                g = dy_ref[pl.ds(t, 1), lanes] * wide(both[:, 128:256], CHUNK) + back
                q = g * ah_s[at, :]
                gbs[j] = fold(g * wide(both[:, 0:128], CHUNK))
                qas[j] = fold(q * a2)
                rate = rate + q * dt_ref[pl.ds(t, 1), lanes]
                db_ref[at, :] += fold_lanes(g * dtu_ref[pl.ds(t, 1), lanes])
                back = a_s[at, :] * g
            here = pl.ds(pl.multiple_of(block * UNROLL, UNROLL), UNROLL)
            sgb_ref[here, lanes] = rows_of_sums(gbs)
            sqa_ref[here, lanes] = rows_of_sums(qas)
            return back, rate

        _, rate = lax.fori_loop(
            0,
            rows // UNROLL,
            retreat,
            (g_in_ref[:, lanes], jnp.zeros((states, CHUNK), F32)),
        )
        rate_ref[:, lanes] = rate
        return carry

    lax.fori_loop(0, inner // CHUNK, chunk, 0)


def packed(state, total, wide_s):
    inner = total.shape[1]
    high = total.astype(BF16).astype(F32)
    rest = total - high
    wide_s[:, 0:inner] = state
    wide_s[:, inner:] = jnp.zeros((state.shape[0], EXTRA), F32)
    for k in range(inner // 128):
        wide_s[k : k + 1, inner : inner + 128] = high[:, k * 128 : (k + 1) * 128]
        wide_s[k : k + 1, inner + 128 : inner + 256] = rest[:, k * 128 : (k + 1) * 128]
    return wide_s[...].astype(BF16)


def unpack_total(wide_ref, m, total_ref, inner):
    for k in range(inner // 128):
        total_ref[m, 0:1, k * 128 : (k + 1) * 128] = (
            wide_ref[m, k : k + 1, inner : inner + 128]
            + wide_ref[m, k : k + 1, inner + 128 : inner + 256]
        )


def join_runs(states_ref, totals_ref, a2, digit, group, backward):
    inner = a2.shape[1]
    before = jnp.zeros(a2.shape, F32)
    entire = jnp.zeros(a2.shape, F32)
    sum_before = jnp.zeros((1, inner), F32)
    sum_entire = jnp.zeros((1, inner), F32)
    order = reversed(range(group)) if backward else range(group)
    for p in order:
        m = jnp.bitwise_xor(digit, p)
        state = states_ref[m, :, 0:inner]
        total = totals_ref[m, 0:1, :]
        through = jnp.exp2(total * a2)
        counts = (p > digit) if backward else (p < digit)
        before = jnp.where(counts, through * before + state, before)
        sum_before = jnp.where(counts, sum_before + total, sum_before)
        entire = through * entire + state
        sum_entire = sum_entire + total
    return before, sum_before, entire, sum_entire


def k_in(x_ref, g_ref, w_ref, n_ref, xc_ref, tail_ref):
    normed = normed_of(x_ref[...], g_ref[...])
    n_ref[...] = normed
    xc = dot(normed, w_ref[...]).astype(BF16)
    xc_ref[...] = xc
    tail_ref[...] = xc.astype(F32)[xc.shape[0] - HALO :, :]


def k_gate(n_ref, w_ref, z_ref):
    z_ref[...] = dot(n_ref[...], w_ref[...]).astype(BF16)


def k_dgated(e_ref, w_ref, out_ref):
    out_ref[...] = dot_t(e_ref[...], w_ref[...])


def conv_of(ext_s, halo_ref, xc_ref, cw_ref, cb_ref):
    rows = xc_ref.shape[0]
    taps = cw_ref.shape[0]
    ext_s[0:HALO, :] = halo_ref[...]
    ext_s[HALO:, :] = xc_ref[...].astype(F32)
    out = cb_ref[...]
    for k in range(taps):
        first = HALO - (taps - 1) + k
        out = out + cw_ref[k : k + 1, :] * ext_s[first : first + rows, :]
    return out


def k_local(
    rank, both, *refs
):
    refs = list(refs)
    halo, xc, cw, cb, xw, dw, db, a2 = refs[:8]
    refs = refs[8:]
    if both:
        dgated, z = refs[:2]
        refs = refs[2:]
    u_ref, xd_ref, v_ref, dt_s, pay_ref = refs[:5]
    refs = refs[5:]
    if both:
        dy_ref = refs[0]
        refs = refs[1:]
    ext_s, dtu_s, xdf_s, lhs_s, bc_s, end_s, wide_s = refs
    states = a2.shape[0]
    conv = conv_of(ext_s, halo, xc, cw, cb)
    u = (conv * sigmoid(conv)).astype(BF16)
    u_ref[...] = u
    xd = dot(u, xw[...]).astype(BF16)
    xd_ref[...] = xd
    xdf_s[...] = xd.astype(F32)
    v = dot(xd, dw[...]) + db[...]
    v_ref[...] = v
    dt = softplus(v)
    dt_s[...] = dt
    dtu_s[...] = dt * u.astype(F32)
    total = jnp.sum(dt, axis=0, keepdims=True)
    fill_table(xdf_s, lhs_s, bc_s, rank, states)
    scan_ends(dt_s, dtu_s, bc_s, a2, end_s)
    pay_ref[0:states, :] = packed(end_s[...], total, wide_s)
    if both:
        zf = z[...].astype(F32)
        dy_ref[...] = dgated[...] * (zf * sigmoid(zf))
        scan_back_ends(dt_s, dy_ref, bc_s, a2, end_s)
        pay_ref[states:, :] = packed(end_s[...], total, wide_s)


def k_join(group, nextgroup, mode, digits, *refs):
    refs = list(refs)
    received, refs = refs[:group], refs[group:]
    a2_ref, refs = refs[0], refs[1:]
    kinds = list(mode)
    n_pay = (nextgroup - 1) if (len(kinds) == 2 and nextgroup) else 1
    pays, refs = refs[:n_pay], refs[n_pay:]
    befores, refs = refs[: len(kinds)], refs[len(kinds) :]
    sums, refs = refs[: len(kinds)], refs[len(kinds) :]
    states_s, totals_s, wide_s = refs
    states, inner = a2_ref.shape
    digit = digits[0]
    nextdigit = digits[1]
    out = []
    for i in range(len(kinds)):
        for m in range(group):
            states_s[m] = received[m][i * states : (i + 1) * states, :].astype(F32)
            if i == 0:
                unpack_total(states_s, m, totals_s, inner)
        before, sum_before, entire, sum_entire = join_runs(
            states_s, totals_s, a2_ref[...], digit, group, kinds[i] == "b"
        )
        befores[i][...] = before
        sums[i][...] = sum_before
        out.append(packed(entire, sum_entire, wide_s))
    if len(kinds) == 2 and nextgroup:
        for m in range(1, nextgroup):
            ahead = jnp.bitwise_xor(nextdigit, m) > nextdigit
            pays[m - 1][...] = jnp.where(ahead, out[0].astype(F32), out[1].astype(F32)).astype(
                BF16
            )
    else:
        for i in range(len(kinds)):
            pays[0][i * states : (i + 1) * states, :] = out[i]


def entering(received, a2_ref, digit, befores, sums, states_s, totals_s, backward, lane0=0):
    lanes = a2_ref.shape[1]
    inner = received[0].shape[1] - EXTRA
    here = slice(lane0, lane0 + lanes)
    group = len(received) + 1
    states_s[0] = jnp.zeros(states_s.shape[1:], F32)
    totals_s[0] = jnp.zeros(totals_s.shape[1:], F32)
    for m in range(1, group):
        states_s[m] = received[m - 1][:, here].astype(F32)
        sums_m = received[m - 1][:, inner:].astype(F32)
        for k in range(lanes // 128):
            row = lane0 // 128 + k
            totals_s[m, 0:1, k * 128 : (k + 1) * 128] = (
                sums_m[row : row + 1, 0:128] + sums_m[row : row + 1, 128:256]
            )
    value, _, _, _ = join_runs(states_s, totals_s, a2_ref[...], digit, group, backward)
    for before, total in reversed(list(zip(befores, sums))):
        value = jnp.exp2(total[:, here] * a2_ref[...]) * value + before[:, here]
    return value


def k_mix(rank, last, n_recv, n_low, digits, core, *refs):
    refs = list(refs)
    received, refs = refs[:n_recv], refs[n_recv:]
    befores, refs = refs[:n_low], refs[n_low:]
    sums, refs = refs[:n_low], refs[n_low:]
    a2, u_ref, dt_ref, xd_ref, z_ref, x_ref, sk_ref, ow_ref = refs[:8]
    refs = refs[8:]
    if last:
        dgated_ref, hid_mine, hid_other, dz_ref, dz_keep, gated_keep, sends, h_in_ref = refs[:8]
        y_ref, hid_s, refs = refs[8], refs[9], refs[10:]
    else:
        g_ref, iw_ref, y_ref, x1_ref, n_ref, xc_ref, tail_ref = refs[:7]
        gated_keep, sends, h_in_ref = refs[7:10]
        refs = refs[10:]
    gated_s, dtu_s, xdf_s, lhs_s, bc_s, states_s, totals_s = refs
    h_in_ref[...] = entering(received, a2, digits[0], befores, sums, states_s, totals_s, False)
    uf = u_ref[...].astype(F32)
    dtu_s[...] = dt_ref[...] * uf
    xdf_s[...] = xd_ref[...].astype(F32)
    fill_table(xdf_s, lhs_s, bc_s, rank, a2.shape[0])
    scan_forward(dt_ref, dtu_s, bc_s, a2, h_in_ref, y_ref)
    y = y_ref[...] + sk_ref[...] * u_ref[...].astype(F32)
    zf = z_ref[...].astype(F32)
    s = sigmoid(zf)
    gated = (y * (zf * s)).astype(BF16)
    gated_s[...] = gated
    rows = gated.shape[0]
    gated_keep[...] = lane_half(gated_s, core[0])
    sends[0:rows, :] = lane_half(gated_s, 1 - core[0])
    x1 = x_ref[...] + dot(gated, ow_ref[...])
    if last:
        dz_ref[...] = (dgated_ref[...] * y * (s * (1.0 + zf * (1.0 - s)))).astype(BF16)
        dz_keep[...] = lane_half(dz_ref, core[0])
        sends[rows:, :] = lane_half(dz_ref, 1 - core[0])
        hid_s[...] = x1
        hid_mine[...] = row_half(hid_s, core[0]).astype(BF16)
        hid_other[...] = row_half(hid_s, 1 - core[0]).astype(BF16)
    else:
        y_ref[...] = y
        x1_ref[...] = x1
        normed = normed_of(x1, g_ref[...])
        n_ref[...] = normed
        sends[rows:, :] = normed
        xc = dot(normed, iw_ref[...]).astype(BF16)
        xc_ref[...] = xc
        tail_ref[...] = xc.astype(F32)[xc.shape[0] - HALO :, :]


def k_scan(rank, lane0, n_recv, n_low, digits, *refs):
    refs = list(refs)
    received, refs = refs[:n_recv], refs[n_recv:]
    befores, refs = refs[:n_low], refs[n_low:]
    sums, refs = refs[:n_low], refs[n_low:]
    a2, u_ref, dt_ref, dy_ref, h_in_ref, xd_ref = refs[:6]
    sgb_ref, sqa_ref, rate_ref, dbc_ref = refs[6:10]
    dtu_s, xdf_s, lhs_s, bc_s, states_s, totals_s, db_s, dc_s, a_s, ah_s, g_s = refs[10:]
    states = a2.shape[0]
    rows = u_ref.shape[0]
    g_s[...] = entering(
        received, a2, digits[0], befores, sums, states_s, totals_s, True, lane0
    )
    dtu_s[...] = dt_ref[...] * u_ref[...].astype(F32)
    xdf_s[...] = xd_ref[...].astype(F32)
    fill_table(xdf_s, lhs_s, bc_s, rank, states)
    scan_both(
        dt_ref, dtu_s, dy_ref, bc_s, a2, h_in_ref, g_s, sgb_ref, sqa_ref, rate_ref, db_s, dc_s, a_s, ah_s
    )
    rate_ref[...] = rate_ref[...] * (a2[...] * LN2)

    ones = jnp.ones((128, 128), BF16)

    def lane_sums(block):
        high = block.astype(BF16)
        rest = (block - high.astype(F32)).astype(BF16)
        return dot(high, ones) + dot(rest, ones)

    n_i = lax.broadcasted_iota(jnp.int32, (states, XD), 0)
    lane = lax.broadcasted_iota(jnp.int32, (states, XD), 1)
    mask_b = (lane == rank + n_i).astype(F32)
    mask_c = (lane == rank + states + n_i).astype(F32)
    db_s[...] = lane_sums(db_s[...])
    dc_s[...] = lane_sums(dc_s[...])

    def gather(i, carry):
        parts = []
        for j in range(UNROLL):
            at = state_rows(i * UNROLL + j, states)
            parts.append(fold(db_s[at, :] * mask_b + dc_s[at, :] * mask_c))
        dbc_ref[pl.ds(pl.multiple_of(i * UNROLL, UNROLL), UNROLL), :] = rows_of_sums(parts)
        return carry

    lax.fori_loop(0, rows // UNROLL, gather, 0)


def k_post(rank, n_parts, *refs):
    refs = list(refs)
    sgbs, refs = refs[:n_parts], refs[n_parts:]
    sqas, refs = refs[:n_parts], refs[n_parts:]
    rates, refs = refs[:n_parts], refs[n_parts:]
    dbcs, refs = refs[:n_parts], refs[n_parts:]
    u_ref, v_ref, dt_ref, xd_ref, dy_ref, halo, xc, cw, cb, xw, dw, sk_ref = refs[:12]
    dconv_ref, head_ref, small_ref, ext_s = refs[12:]
    states = rates[0].shape[0]
    rows, inner = u_ref.shape
    sgb = jnp.concatenate([ref[...] for ref in sgbs], axis=1)
    sqa = jnp.concatenate([ref[...] for ref in sqas], axis=1)
    dbc = dbcs[0][...]
    for ref in dbcs[1:]:
        dbc = dbc + ref[...]
    u = u_ref[...]
    uf = u.astype(F32)
    dy = dy_ref[...]
    v = v_ref[...]
    dpre = (LN2 * sqa + uf * sgb) * sigmoid(v)
    dpl = dpre.astype(BF16)
    dxd = (dot_t(dpl, dw[...]) + dbc).astype(BF16)
    du = dt_ref[...] * sgb + sk_ref[...] * dy + dot_t(dxd, xw[...])
    conv = conv_of(ext_s, halo, xc, cw, cb)
    dconv = du * slope(conv)
    dconv_ref[...] = dconv
    head_ref[...] = dconv[0:HALO, :]
    taps = cw.shape[0]
    width = rank + 2 * states
    g_x = dot_rows(dxd, u)
    g_dt = dot_rows(xd_ref[...], dpl)
    at = 0
    small_ref[at : at + width, :] = g_x[0:width]
    at += width
    small_ref[at : at + rank, :] = g_dt[0:rank]
    at += rank
    small_ref[at : at + states, :] = jnp.concatenate([ref[...] for ref in rates], axis=1)
    at += states
    for k in range(taps):
        first = HALO - (taps - 1) + k
        small_ref[at : at + 1, :] = jnp.sum(
            dconv * ext_s[first : first + rows, :], axis=0, keepdims=True
        )
        at += 1
    small_ref[at : at + 1, :] = jnp.sum(dconv, axis=0, keepdims=True)
    small_ref[at + 1 : at + 2, :] = jnp.sum(dpre, axis=0, keepdims=True)
    small_ref[at + 2 : at + 3, :] = jnp.sum(dy * uf, axis=0, keepdims=True)
    small_ref[at + 3 : at + 4, :] = jnp.zeros((1, inner), F32)


def row_half(ref, which):
    half = ref.shape[0] // 2
    return ref[pl.ds(pl.multiple_of(which * half, 16), half), :]


def lane_half(ref, which):
    half = ref.shape[1] // 2
    return ref[:, pl.ds(pl.multiple_of(which * half, 128), half)]


def conv_back(dce_s, dconv_ref, next_ref, cw_ref):
    rows = dconv_ref.shape[0]
    taps = cw_ref.shape[0]
    dce_s[0:rows, :] = dconv_ref[...]
    dce_s[rows:, :] = next_ref[...]
    out = cw_ref[taps - 1 : taps, :] * dce_s[0:rows, :]
    for k in range(taps - 1):
        first = taps - 1 - k
        out = out + cw_ref[k : k + 1, :] * dce_s[first : first + rows, :]
    return out.astype(BF16)


def norm_back(x, gain, e, dn):
    rinv = lax.rsqrt(jnp.mean(x * x, axis=-1, keepdims=True) + 1e-05)
    xhat = x * rinv
    dhat = dn * gain
    g_norm = jnp.sum(dn * xhat, axis=0, keepdims=True)
    return e + rinv * (dhat - xhat * jnp.mean(dhat * xhat, axis=-1, keepdims=True)), g_norm


def small_out(core, small_ref, g_norm, keep_ref, sends, at):
    rows, inner = small_ref.shape
    width = g_norm.shape[1]
    small_ref[rows - 1 : rows, 0:width] = g_norm
    pad = keep_ref.shape[0] - rows
    for which, ref, first in ((core[0], keep_ref, 0), (1 - core[0], sends, at)):
        block = lane_half(small_ref, which)
        block = jnp.concatenate([block, jnp.zeros((pad, block.shape[1]), F32)], axis=0)
        ref[first : first + rows + pad, :] = block.astype(ref.dtype)
    sends[at + rows + pad :, :] = jnp.zeros((sends.shape[0] - at - rows - pad, inner // 2), BF16)


def k_turn(
    rank,
    core,
    small_ref,
    dconv_ref,
    next_ref,
    cw_ref,
    dnz_ref,
    iw_ref,
    x_ref,
    g_ref,
    e_ref,
    ow_ref,
    y_ref,
    z_ref,
    dt_ref,
    xd_ref,
    a2,
    iz_ref,
    dxc_keep,
    small_keep,
    e1_ref,
    de_ref,
    dy_ref,
    dz_ref,
    dz_keep,
    sends,
    dnz0_ref,
    pay_ref,
    small_s,
    dxc_s,
    dce_s,
    xdf_s,
    lhs_s,
    bc_s,
    end_s,
    wide_s,
):
    dxc = conv_back(dce_s, dconv_ref, next_ref, cw_ref)
    rows = dxc.shape[0]
    dxc_s[...] = dxc
    dxc_keep[...] = lane_half(dxc_s, core[0])
    sends[0:rows, :] = lane_half(dxc_s, 1 - core[0])
    dn = dnz_ref[...] + dot_t(dxc, iw_ref[...])
    e1, g_norm = norm_back(x_ref[...], g_ref[...], e_ref[...].astype(F32), dn)
    small_s[...] = small_ref[...]
    small_out(core, small_s, g_norm, small_keep, sends, 3 * rows)
    e1_ref[...] = e1
    de = e1.astype(BF16)
    de_ref[...] = de
    sends[2 * rows : 3 * rows, :] = de
    dgated = dot_t(de, ow_ref[...])
    zf = z_ref[...].astype(F32)
    s = sigmoid(zf)
    dy_ref[...] = dgated * (zf * s)
    dz_ref[...] = (dgated * y_ref[...] * (s * (1.0 + zf * (1.0 - s)))).astype(BF16)
    dz_keep[...] = lane_half(dz_ref, core[0])
    sends[rows : 2 * rows, :] = lane_half(dz_ref, 1 - core[0])
    dnz0_ref[...] = dot_t(dz_ref[...], iz_ref[...])
    states = a2.shape[0]
    total = jnp.sum(dt_ref[...], axis=0, keepdims=True)
    xdf_s[...] = xd_ref[...].astype(F32)
    fill_table(xdf_s, lhs_s, bc_s, rank, states)
    scan_back_ends(dt_ref, dy_ref, bc_s, a2, end_s)
    pay_ref[...] = packed(end_s[...], total, wide_s)


def k_end(
    core,
    small_ref,
    dconv_ref,
    next_ref,
    cw_ref,
    dnz_ref,
    iw_ref,
    x_ref,
    g_ref,
    e_ref,
    dxc_keep,
    small_keep,
    sends,
    e0_mine,
    e0_other,
    small_s,
    dxc_s,
    dce_s,
    e0_s,
):
    dxc = conv_back(dce_s, dconv_ref, next_ref, cw_ref)
    rows = dxc.shape[0]
    dxc_s[...] = dxc
    dxc_keep[...] = lane_half(dxc_s, core[0])
    sends[0:rows, :] = lane_half(dxc_s, 1 - core[0])
    dn = dnz_ref[...] + dot_t(dxc, iw_ref[...])
    e0, g_norm = norm_back(x_ref[...], g_ref[...], e_ref[...], dn)
    small_s[...] = small_ref[...]
    small_out(core, small_s, g_norm, small_keep, sends, rows)
    e0_s[...] = e0
    e0_mine[...] = row_half(e0_s, core[0]).astype(BF16)
    e0_other[...] = row_half(e0_s, 1 - core[0]).astype(BF16)


def k_dnz(dz_ref, iw_ref, out_ref):
    out_ref[...] = dot_t(dz_ref[...], iw_ref[...])


def chip_sums(n_pairs, has_small, refs, s_ref):
    refs = list(refs)
    pairs, refs = [refs[4 * i : 4 * i + 4] for i in range(n_pairs)], refs[4 * n_pairs :]
    blocks = s_ref.shape[0]
    rows = pairs[0][0].shape[1] // blocks
    for i, (a, a_came, b, b_came) in enumerate(pairs):
        total = dot_rows(
            jnp.concatenate([a[...], a_came[...]], axis=0),
            jnp.concatenate([b[...], b_came[...]], axis=0),
        )
        s_ref[:, 0:rows, :] = total.reshape(blocks, rows, total.shape[1])
        yield i * rows, rows
    if has_small:
        small_a, small_b = refs
        n = small_a.shape[0] // blocks
        s_ref[:, 0:16, :] = jnp.zeros((blocks, 16, s_ref.shape[2]), F32)
        small = small_a[...] + small_b[...].astype(F32)[0 : small_a.shape[0]]
        for k in range(blocks):
            s_ref[k, 0:n, :] = small[k * n : (k + 1) * n]
        yield n_pairs * rows, 16


def k_chip_sum(n_pairs, has_small, *refs):
    out, s_ref = refs[-2:]
    for top, rows in chip_sums(n_pairs, has_small, refs[:-2], s_ref):
        out[:, top : top + rows, :] = s_ref[:, 0:rows, :]


def k_first(n_pairs, has_small, place, *refs):
    keep_a, keep_b, send_a, send_b, s_ref = refs[-5:]
    blocks = s_ref.shape[0]
    half = s_ref.shape[2] // 2
    x, y = place[0] & 1, (place[0] >> 1) & 1
    for top, rows in chip_sums(n_pairs, has_small, refs[:-5], s_ref):
        to, take = slice(top, top + rows), slice(0, rows)
        for i in range(blocks // 2):
            at = (i >> 1) * 4 + (i & 1) * 2
            keep_a[i, to, :] = s_ref[at + x, take, 0:half]
            send_a[i, to, :] = s_ref[at + 1 - x, take, 0:half].astype(BF16)
            at = (i >> 1) * 4 + (i & 1)
            keep_b[i, to, :] = s_ref[at + 2 * y, take, half:]
            send_b[i, to, :] = s_ref[at + 2 * (1 - y), take, half:].astype(BF16)


def k_second(place, keep_a, keep_b, came_a, came_b, stay_a, stay_b, send_a, send_b):
    x, y = place[0] & 1, (place[0] >> 1) & 1
    for i in range(stay_a.shape[0]):
        for keep, came, stay, send, bit in (
            (keep_a, came_a, stay_a, send_a, y),
            (keep_b, came_b, stay_b, send_b, x),
        ):
            at = 2 * i + bit
            stay[i] = keep[at] + came[at].astype(F32)
            at = 2 * i + 1 - bit
            send[i] = (keep[at] + came[at].astype(F32)).astype(BF16)


def k_third(place, stay_a, stay_b, came_a, came_b, keep, send1, send2, send3):
    z = (place[0] >> 2) & 3
    half = stay_a.shape[2]
    for m, ref in enumerate((keep, send1, send2, send3)):
        at = jnp.bitwise_xor(z, m)
        ref[:, 0:half] = (stay_a[at] + came_a[at].astype(F32)).astype(ref.dtype)
        ref[:, half:] = (stay_b[at] + came_b[at].astype(F32)).astype(ref.dtype)


def k_fourth(keep, came1, came2, came3, out):
    out[...] = (
        keep[...] + came1[...].astype(F32) + came2[...].astype(F32) + came3[...].astype(F32)
    ).astype(BF16)


def k_stack(mine, came1, came2, came3, out_a, out_b):
    half = out_a.shape[2]
    for m, ref in enumerate((mine, came1, came2, came3)):
        out_a[m] = ref[:, 0:half]
        out_b[m] = ref[:, half:]


def k_chip(place, *refs):
    left, right, out = refs[0:4], refs[4:8], refs[8]
    half = left[0].shape[2]
    xy, z = place[0] & 3, (place[0] >> 2) & 3
    for d in range(4):
        for m in range(4):
            at = jnp.bitwise_xor(z, m) * 4 + jnp.bitwise_xor(xy, d)
            out[at, :, 0:half] = left[d][m]
            out[at, :, half:] = right[d][m]


def in_order(core, sources):
    if len(sources) == 1:
        return sources[0][:, 0].astype(F32), sources[0][:, 1].astype(F32)
    own = core[0] == 0
    a, b = sources[0][...].astype(F32), sources[1][...].astype(F32)
    return jnp.where(own, a, b), jnp.where(own, b, a)


def k_place(n_sources, split_rows, core, *refs):
    out, done = refs[-2:]
    done[...] = jnp.zeros(done.shape, F32)
    low, high = in_order(core, refs[:n_sources])
    blocks, rows, lanes = low.shape
    low, high = low.reshape(blocks * rows, lanes), high.reshape(blocks * rows, lanes)
    if split_rows:
        out[0], out[1] = low, high
    else:
        out[:, 0:lanes] = low
        out[:, lanes:] = high


def k_place_small(rank, taps, counts, core, *refs):
    refs = list(refs)
    given, refs = refs[: sum(counts)], refs[sum(counts) :]
    norm, cw, cb, xw, dw, db, al, sk, all_s = refs
    states = al.shape[1]
    n_x = rank + 2 * states
    all_s[...] = jnp.zeros(all_s.shape, F32)
    at = 0
    for l, count in enumerate(counts):
        low, high = in_order(core, given[at : at + count])
        at += count
        blocks, _, lanes = low.shape
        n = -(-(n_x + rank + states + taps + 4) // blocks)
        for k in range(blocks):
            all_s[k * n : (k + 1) * n, 0:lanes] = low[k, 0:n]
            all_s[k * n : (k + 1) * n, lanes:] = high[k, 0:n]
        dw[l] = all_s[n_x : n_x + rank, :]
        first = n_x + rank
        xw[l] = all_s[0:n_x, :]
        al[l] = all_s[first : first + states, :]
        cw[l] = all_s[first + states : first + states + taps, :]
        first += states + taps
        cb[l : l + 1, :] = all_s[first : first + 1, :]
        db[l : l + 1, :] = all_s[first + 1 : first + 2, :]
        sk[l : l + 1, :] = all_s[first + 2 : first + 3, :]
        norm[l : l + 1, :] = all_s[first + 3 : first + 4, 0 : norm.shape[1]]


def shards(
    hidden_in,
    norm_gain,
    in_weight,
    conv_weight,
    conv_bias,
    xproj_weight,
    dtproj_weight,
    dt_bias,
    a_log,
    skip_gain,
    out_weight,
    hidden_grad,
):
    layers, width, _ = in_weight.shape
    inner, states = a_log.shape[1], a_log.shape[2]
    rank = dtproj_weight.shape[1]
    taps = conv_weight.shape[2]
    seqs, own, _ = hidden_in.shape
    ndev = lax.axis_size(AXIS)
    me = lax.axis_index(AXIS)
    core = me % 2
    chip = me // 2
    rows = seqs * own
    assert layers == 2 and seqs == 2 and ndev % 2 == 0
    assert inner % CHUNK == 0 and inner // 128 <= states and rank + 2 * states <= XD

    pairs = [(i, i ^ 1) for i in range(ndev)]
    turn = []
    call = functools.partial(run, turn=turn)

    def to_runs(block):
        mine = lax.dynamic_index_in_dim(block, core, 0, keepdims=False)
        other = lax.dynamic_index_in_dim(block, 1 - core, 0, keepdims=False)
        came = lax.ppermute(other, AXIS, pairs)
        first = jnp.where(core == 0, mine, came)
        second = jnp.where(core == 0, came, mine)
        return jnp.concatenate([first, second], axis=0)

    def from_runs(mine, other):
        came = lax.ppermute(other, AXIS, pairs)
        first = jnp.where(core == 0, mine, came)
        second = jnp.where(core == 0, came, mine)
        return jnp.stack([first, second], axis=0)

    def done_by_now(array):
        array, turn[0] = lax.optimization_barrier((array, turn[0]))
        return array

    def not_before(*arrays):
        return lax.optimization_barrier(arrays + (turn[0],))[:-1]

    def from_before(block):
        return lax.ppermute(block, AXIS, [(i, i + 2) for i in range(ndev - 2)])

    def from_after(block):
        return lax.ppermute(block, AXIS, [(i + 2, i) for i in range(ndev - 2)])

    bits = (ndev // 2).bit_length() - 1
    assert 2 << bits == ndev and bits > 2
    rounds = []
    low = 0
    while low < bits:
        n = 2 if bits - low >= 2 else 1
        rounds.append((low, 1 << n))
        low += n

    def digit_of(r):
        low, group = rounds[r]
        return (chip >> low) & (group - 1)

    def digits_of(r):
        nxt = digit_of(r + 1) if r + 1 < len(rounds) else jnp.zeros_like(chip)
        return jnp.stack([digit_of(r), nxt]).astype(jnp.int32)

    def send(block, r, m, which):
        low, group = rounds[r]
        flip = (m << low) << 1
        route = [(i, i ^ flip) for i in range(ndev)]
        if which == "up":
            route = [(i, j) for i, j in route if j > i]
        if which == "down":
            route = [(i, j) for i, j in route if j < i]
        return lax.ppermute(block, AXIS, route)

    smem = pl.BlockSpec(memory_space=pltpu.SMEM)
    core_s = (core[None].astype(jnp.int32), smem)

    def swap(block):
        return lax.ppermute(block, AXIS, pairs)

    pay = shape((states, inner + EXTRA), BF16)

    kept = {}

    def exchange(payload, a2, mode, meanwhile=()):
        meanwhile = dict(enumerate(meanwhile))
        befores = [[] for _ in mode]
        sums = [[] for _ in mode]
        for r, (low, group) in enumerate(rounds[:-1]):
            received = [payload] + [send(payload, r, m, "all") for m in range(1, group)]
            kept["first"] = received[1:]
            if r in meanwhile:
                meanwhile[r]()
            final = r + 2 == len(rounds)
            split = len(mode) == 2 and final
            nextgroup = rounds[r + 1][1] if split else 0
            pays = (
                [pay] * (nextgroup - 1)
                if split
                else [shape((states * len(mode), inner + EXTRA), BF16)]
            )
            outs = call(
                functools.partial(k_join, group, nextgroup, mode),
                pays
                + [shape((states, inner), F32)] * len(mode)
                + [shape((1, inner), F32)] * len(mode),
                [(digits_of(r), smem)] + received + [a2],
                [
                    pltpu.VMEM((group, states, inner + EXTRA), F32),
                    pltpu.VMEM((group, 8, inner), F32),
                    pltpu.VMEM((states, inner + EXTRA), F32),
                ],
            )
            sent, outs = outs[: len(pays)], outs[len(pays) :]
            for i in range(len(mode)):
                befores[i].append(outs[i])
                sums[i].append(outs[len(mode) + i])
            payload = sent if split else sent[0]
        r = len(rounds) - 1
        if len(mode) == 2:
            last = [send(payload[m - 1], r, m, "all") for m in range(1, rounds[r][1])]
        else:
            way = "all"
            last = [send(payload, r, m, way) for m in range(1, rounds[r][1])]
        for step in sorted(meanwhile):
            if step >= r:
                meanwhile[step]()
        return last, sum(befores, []), sum(sums, []), digits_of(r)

    def row(array, l):
        return Row(array, l)

    def layer_of(array, l):
        return array, part((None,) + array.shape[1:], (l, 0, 0))

    def w_in(l, half):
        columns = slice(half * inner, (half + 1) * inner)
        return Late(in_weight, (l, slice(None), columns), (width, inner))

    def w_out(l):
        return Late(out_weight, (l,), (inner, width))

    def table_scratch():
        return [
            pltpu.VMEM((rows, XD), F32),
            pltpu.VMEM((rows * states, XD), BF16),
            pltpu.VMEM((rows * states, 256), F32),
        ]

    act = shape((rows, inner), F32)
    act_b = shape((rows, inner), BF16)
    res = shape((rows, width), F32)
    res_b = shape((rows, width), BF16)
    edge = shape((HALO, inner), F32)
    mm = 2 * rows * width * inner

    x0 = to_runs(hidden_in).astype(F32)

    normed = [None, None]
    xc = [None, None]
    halo = [None, None]
    z = [None, None]
    u = [None, None]
    xd = [None, None]
    v = [None, None]
    step = [None, None]

    normed[0], xc[0], tail = call(
        k_in, [res_b, act_b, edge], [x0, row(norm_gain, 0), in_weight[0, :, 0:inner]]
    )

    a_log, conv_weight, xproj_weight, dtproj_weight, hidden_grad = not_before(
        a_log, conv_weight, xproj_weight, dtproj_weight, hidden_grad
    )
    a2_all = -jnp.exp(jnp.swapaxes(a_log, 1, 2)) * LOG2E
    cw_all = jnp.swapaxes(conv_weight, 1, 2)
    xw_all = jnp.pad(xproj_weight, ((0, 0), (0, 0), (0, XD - xproj_weight.shape[2])))
    dw_all = jnp.pad(dtproj_weight, ((0, 0), (0, XD - rank), (0, 0)))
    grad_out = to_runs(hidden_grad)

    def gate(l):
        (z[l],) = call(k_gate, [act_b], [normed[l], w_in(l, 1)], cost=LONG)

    def before_scan(l, tail, dgated=None):
        halo[l] = from_before(tail)
        if l:
            gate(l)
        both = dgated is not None
        outs = call(
            functools.partial(k_local, rank, both),
            [
                act_b,
                shape((rows, XD), BF16),
                act,
                act,
                shape((states * (2 if both else 1), inner + EXTRA), BF16),
            ]
            + ([act] if both else []),
            [
                halo[l],
                xc[l],
                layer_of(cw_all, l),
                row(conv_bias, l),
                layer_of(xw_all, l),
                layer_of(dw_all, l),
                row(dt_bias, l),
                layer_of(a2_all, l),
            ]
            + ([dgated, z[l]] if both else []),
            [pltpu.VMEM((rows + HALO, inner), F32)]
            + [pltpu.VMEM((rows, inner), F32)]
            + table_scratch()
            + [pltpu.VMEM((states, inner), F32), pltpu.VMEM((states, inner + EXTRA), F32)],
            cost=LONG,
        )
        u[l], xd[l], v[l], step[l] = outs[:4]
        return outs[4:]

    def join_scratch():
        group = rounds[-1][1]
        return [
            pltpu.VMEM((group, states, inner), F32),
            pltpu.VMEM((group, 8, inner), F32),
        ]

    def piece(array, i):
        return array, part((rows, array.shape[1]), (i, 0))

    def mix(l, parts, extra, outs):
        final = l == layers - 1
        last, befores, sums, digits = parts
        befores, sums = befores[: len(rounds) - 1], sums[: len(rounds) - 1]
        return call(
            functools.partial(k_mix, rank, final, len(last), len(befores)),
            outs,
            [(digits, smem), core_s]
            + last
            + befores
            + sums
            + [layer_of(a2_all, l), u[l], step[l], xd[l], z[l], residual[l], row(skip_gain, l), w_out(l)]
            + extra,
            ([act_scratch, pltpu.VMEM((rows, width), F32)] if final else [])
            + [pltpu.VMEM((rows, inner), BF16)]
            + [act_scratch]
            + table_scratch()
            + join_scratch(),
            cost=LONG,
        )

    half_b = shape((rows, width), BF16)
    entry = shape((states, inner), F32)
    act_scratch = pltpu.VMEM((rows, inner), F32)
    residual = [x0, None]
    def shadow_00():
        gate(0)

    def shadow_0():
        (kept["dgated1"],) = call(k_dgated, [act], [grad_out, w_out(1)], cost=LONG)

    (payload,) = before_scan(0, tail)
    parts = exchange(payload, layer_of(a2_all, 0), "f", (shadow_00, shadow_0))
    dgated1 = kept["dgated1"]
    y0, x1, normed[1], xc[1], tail, gated_keep, sends, h0 = mix(
        0,
        parts,
        [row(norm_gain, 1), w_in(1, 0)],
        [act, res, res_b, act_b, edge, half_b, shape((2 * rows, width), BF16), entry],
    )
    residual[1] = x1
    came = swap(sends)
    n1_pair = (normed[1], piece(came, 1))
    gated0_pair = (gated_keep, piece(came, 0))
    n0_pair = (normed[0], swap(normed[0]))
    e1_pair = (grad_out, swap(grad_out))
    payload, dy1 = before_scan(1, tail, dgated1)
    parts = exchange(payload, layer_of(a2_all, 1), "fb")
    n_small = rank + 2 * states + rank + states + taps + 4
    small = shape((n_small, inner), F32)
    small_pad = -(-n_small // (BLOCKS * 2)) * BLOCKS * 2 if n_small % BLOCKS else n_small

    n_chunks = inner // CHUNK
    cuts = [(0, (n_chunks + 1) // 2 * CHUNK), ((n_chunks + 1) // 2 * CHUNK, n_chunks // 2 * CHUNK)]
    n_parts = len(cuts)
    assert all(first % lanes == 0 for first, lanes in cuts)

    def scan(l, i, dy, parts, h_in):
        lane0, lanes = cuts[i]
        last, befores, sums, digits = parts
        n_low = len(rounds) - 1
        cut = part((rows, lanes), (0, lane0 // lanes))
        cut_s = part((states, lanes), (0, lane0 // lanes))
        cut_a = part((None, states, lanes), (l, 0, lane0 // lanes))
        return call(
            functools.partial(k_scan, rank, lane0, len(last), n_low),
            [shape((rows, lanes), F32)] * 2 + [shape((states, lanes), F32), shape((rows, XD), F32)],
            [(digits, smem)]
            + last
            + befores[-n_low:]
            + sums[-n_low:]
            + [(a2_all, cut_a), (u[l], cut), (step[l], cut), (dy, cut), (h_in, cut_s), xd[l]],
            [pltpu.VMEM((rows, lanes), F32)]
            + table_scratch()
            + [
                pltpu.VMEM((rounds[-1][1], states, lanes), F32),
                pltpu.VMEM((rounds[-1][1], 8, lanes), F32),
            ]
            + [pltpu.VMEM((rows * states, 128), F32)] * 2
            + [pltpu.VMEM((rows * states, CHUNK), F32)] * 2
            + [pltpu.VMEM((states, lanes), F32)],
            cost=LONG,
        )

    def post(l, scans, dy):
        return call(
            functools.partial(k_post, rank, n_parts),
            [act, edge, small],
            [outs[k] for k in range(4) for outs in scans]
            + [
                u[l],
                v[l],
                step[l],
                xd[l],
                dy,
                halo[l],
                xc[l],
                layer_of(cw_all, l),
                row(conv_bias, l),
                layer_of(xw_all, l),
                layer_of(dw_all, l),
                row(skip_gain, l),
            ],
            [pltpu.VMEM((rows + HALO, inner), F32)],
            cost=LONG,
        )


    def over(block, flip):
        return lax.ppermute(block, AXIS, [(i, i ^ (flip << 1)) for i in range(ndev)])

    place_s = (chip[None].astype(jnp.int32), smem)

    def held(arrays, gate):
        if gate is None:
            return arrays
        return lax.optimization_barrier(tuple(arrays) + tuple(gate()))[: len(arrays)]

    def summed(matrices, smalls, aside=False, gates=(None, None, None)):
        ins = []
        each = width // BLOCKS
        for (a, a_came), (b, b_came) in matrices:
            ins += [a, a_came, b, b_came]
        r = each * len(matrices)
        if smalls is not None:
            ins += list(smalls)
            r += 16
        has_small = smalls is not None
        half = width // 2
        if ndev != 2 * BLOCKS:
            (mine,) = call(
                functools.partial(k_chip_sum, len(matrices), has_small),
                [shape((BLOCKS, r, width), F32)],
                ins,
                [pltpu.VMEM((BLOCKS, each, width), F32)],
            )
            empty = jnp.zeros((2,) + mine.shape, F32)
            total = lax.psum(lax.dynamic_update_index_in_dim(empty, mine, core, 0), AXIS)
            total = total.astype(BF16)
            for _ in range(3 if aside else 5):
                yield None
            if aside:
                yield jnp.swapaxes(total, 0, 1)
                return
            yield (
                lax.dynamic_index_in_dim(total, core, 0, keepdims=False),
                lax.dynamic_index_in_dim(total, 1 - core, 0, keepdims=False),
            )
            return
        n = BLOCKS // 2
        keep_a, keep_b, send_a, send_b = call(
            functools.partial(k_first, len(matrices), has_small),
            [shape((n, r, half), F32)] * 2 + [shape((n, r, half), BF16)] * 2,
            [place_s] + ins,
            [pltpu.VMEM((BLOCKS, each, width), F32)],
            cost=LONG,
        )
        send_a, send_b = held([send_a, send_b], gates[0])
        came_a, came_b = over(send_a, 1), over(send_b, 2)
        yield None
        n = BLOCKS // 4
        stay_a, stay_b, send_a, send_b = call(
            k_second,
            [shape((n, r, half), F32)] * 2 + [shape((n, r, half), BF16)] * 2,
            [place_s, keep_a, keep_b, came_a, came_b],
        )
        send_a, send_b = held([send_a, send_b], gates[1])
        came_a, came_b = over(send_a, 2), over(send_b, 1)
        yield None
        keep, *sends = call(
            k_third,
            [shape((r, width), F32)] + [shape((r, width), BF16)] * 3,
            [place_s, stay_a, stay_b, came_a, came_b],
        )
        sends = held(sends, gates[2])
        came = [over(send_m, 4 * (m + 1)) for m, send_m in enumerate(sends)]
        yield None
        (done,) = call(k_fourth, [shape((r, width), BF16)], [keep] + came)
        if aside:
            every = lax.all_gather(done, AXIS)
            yield every.reshape(BLOCKS, 2, r, width)
            return
        came = [over(done, 4 * m) for m in (1, 2, 3)]
        yield None
        left, right = call(k_stack, [shape((4, r, half), BF16)] * 2, [done] + came)
        left_y, right_x = over(left, 2), over(right, 1)
        lefts = [left, over(left, 1), left_y, over(left_y, 1)]
        rights = [right, right_x, over(right, 2), over(right_x, 2)]
        yield None
        (mine,) = call(
            k_chip, [shape((BLOCKS, r, width), BF16)], [place_s] + lefts + rights
        )
        yield mine, swap(mine)

    def sources(halves, i, per, each, place):
        if not isinstance(halves, tuple):
            spec = pl.BlockSpec((per, 2, each, width), lambda g: (place(g), 0, i, 0))
            return [halves], [spec]
        spec = pl.BlockSpec((per, each, width), lambda g: (place(g), i, 0))
        return list(halves), [spec, spec]

    def placed(halves, i, whole, block, index, split_rows, before):
        each = width // BLOCKS
        steps = 2
        anywhere = pl.BlockSpec(memory_space=pl.ANY)
        arrays, specs = sources(halves, i, BLOCKS // steps, each, lambda g: g)
        ins = [core_s[0]] + arrays + [turn[0]]
        specs = [smem] + specs + [anywhere]
        aliases = {}
        if before is not None:
            aliases = {len(ins): 0}
            ins.append(before)
            specs.append(anywhere)
        out, turn[0] = pl.pallas_call(
            functools.partial(k_place, len(arrays), split_rows),
            grid=(steps,),
            in_specs=specs,
            out_specs=[pl.BlockSpec(block, index), pl.BlockSpec((8, 128), lambda g: (0, 0))],
            out_shape=[whole, shape((8, 128), F32)],
            input_output_aliases=aliases,
            compiler_params=pltpu.CompilerParams(vmem_limit_bytes=58 * 1024 * 1024),
            cost_estimate=COST,
        )(*ins)
        return out

    g_out_shape = shape((layers, 2, width, width), F32)
    g_in_shape = shape((layers, width, 2 * inner), F32)
    several = width // 2
    out_block = (None, 2, several, width)
    in_block = (None, several, inner)

    def out_at(l):
        return lambda g: (l, 0, g, 0)

    def in_at(l, half):
        return lambda g: (l, g, half)

    def placed_small(layer_sums):
        each = width // BLOCKS
        ins, counts = [core_s], []
        for halves, i in layer_sums:
            arrays, specs = sources(halves, i * each // 16, BLOCKS, 16, lambda g: 0)
            ins += list(zip(arrays, specs))
            counts.append(len(arrays))
        n_x = rank + 2 * states
        return call(
            functools.partial(k_place_small, rank, taps, tuple(counts)),
            [
                shape((layers, width), F32),
                shape((layers, taps, inner), F32),
                shape((layers, inner), F32),
                shape((layers, n_x, inner), F32),
                shape((layers, rank, inner), F32),
                shape((layers, inner), F32),
                shape((layers, states, inner), F32),
                shape((layers, inner), F32),
            ],
            ins,
            [pltpu.VMEM((small_pad, inner), F32)],
            spare=58,
        )

    half_small = shape((small_pad, width), F32)

    hid_mine, hid_other, dz1, dz_keep, gated_keep, sends, h1 = mix(
        1,
        parts,
        [dgated1],
        [shape((own, width), BF16)] * 2
        + [act_b, half_b, half_b, shape((2 * rows, width), BF16), entry],
    )
    came = swap(sends)
    hidden_out = from_runs(hid_mine, hid_other)
    a_sum = summed(
        [((gated_keep, piece(came, 0)), e1_pair), (n1_pair, (dz_keep, piece(came, 1)))],
        None,
        True,
        (None, None, lambda: [after1]),
    )
    scans = [scan(1, 0, dy1, parts, h1)]
    next(a_sum)
    scans.append(scan(1, 1, dy1, parts, h1))
    hidden_out = done_by_now(hidden_out)
    next(a_sum)
    dconv1, head1, small1 = post(1, scans, dy1)
    after1 = from_after(head1)
    (dnz1,) = call(k_dnz, [res], [dz1, w_in(1, 1)], cost=LONG)
    next(a_sum)
    turn_back = functools.partial(
        call,
        functools.partial(k_turn, rank),
        [half_b, half_small, res, res_b, act, act_b, half_b]
        + [shape((4 * rows, width), BF16), res, pay],
        [
            core_s,
            small1,
            dconv1,
            after1,
            layer_of(cw_all, 1),
            dnz1,
            w_in(1, 0),
            x1,
            row(norm_gain, 1),
            grad_out,
            w_out(0),
            y0,
            z[0],
            step[0],
            xd[0],
            layer_of(a2_all, 0),
            w_in(0, 1),
        ],
        [
            pltpu.VMEM((n_small, inner), F32),
            pltpu.VMEM((rows, inner), BF16),
            pltpu.VMEM((rows + HALO, inner), F32),
        ]
        + table_scratch()
        + [pltpu.VMEM((states, inner), F32), pltpu.VMEM((states, inner + EXTRA), F32)],
        cost=LONG,
    )
    dxc_keep, small_keep, e1, de0, dy0, _, dz_keep, sends, dnz0, payload = turn_back()
    came = swap(sends)
    b_sum = summed(
        [
            (n1_pair, (dxc_keep, piece(came, 0))),
            (gated0_pair, (de0, piece(came, 2))),
            (n0_pair, (dz_keep, piece(came, 1))),
        ],
        (small_keep, piece(came, 3)),
        True,
        (lambda: kept["first"], None, None),
    )

    def shadow_1():
        next(b_sum)

    def shadow_2():
        kept["sum_a"] = next(a_sum)

    parts = exchange(payload, layer_of(a2_all, 0), "b", (shadow_1, shadow_2))
    sum_a = kept["sum_a"]
    scans = [scan(0, 0, dy0, parts, h0)]
    next(b_sum)
    scans.append(scan(0, 1, dy0, parts, h0))
    dconv0, head0, small0 = post(0, scans, dy0)
    after0 = from_after(head0)
    next(b_sum)
    dxc_keep, small_keep, sends, e0_mine, e0_other = call(
        k_end,
        [half_b, half_small, shape((2 * rows, width), BF16)] + [shape((own, width), BF16)] * 2,
        [
            core_s,
            small0,
            dconv0,
            after0,
            layer_of(cw_all, 0),
            dnz0,
            w_in(0, 0),
            x0,
            row(norm_gain, 0),
            e1,
        ],
        [
            pltpu.VMEM((n_small, inner), F32),
            pltpu.VMEM((rows, inner), BF16),
            pltpu.VMEM((rows + HALO, inner), F32),
            pltpu.VMEM((rows, width), F32),
        ],
        cost=LONG,
    )
    came = swap(sends)
    c_sum = summed(
        [(n0_pair, (dxc_keep, piece(came, 0)))], (small_keep, piece(came, 1))
    )
    sum_b = next(b_sum)
    next(c_sum)
    g_out = placed(sum_a, 0, g_out_shape, out_block, out_at(1), True, None)
    input_grad = done_by_now(from_runs(e0_mine, e0_other))
    next(c_sum)
    next(c_sum)
    g_in = placed(sum_a, 1, g_in_shape, in_block, in_at(1, 1), False, None)
    next(c_sum)
    next(c_sum)
    sum_c = next(c_sum)
    g_in = placed(sum_c, 0, g_in_shape, in_block, in_at(0, 0), False, g_in)
    g_in = placed(sum_b, 0, g_in_shape, in_block, in_at(1, 0), False, g_in)
    g_out = placed(sum_b, 1, g_out_shape, out_block, out_at(0), True, g_out)
    g_in = placed(sum_b, 2, g_in_shape, in_block, in_at(0, 1), False, g_in)
    g_norm, g_cw, g_cb, g_xw, g_dw, g_db, g_al, g_sk = placed_small([(sum_c, 1), (sum_b, 3)])
    return (
        hidden_out,
        input_grad,
        g_norm,
        g_in,
        jnp.swapaxes(g_cw, 1, 2),
        g_cb,
        jnp.swapaxes(g_xw, 1, 2),
        g_dw,
        g_db,
        jnp.swapaxes(g_al, 1, 2),
        g_sk,
        g_out.reshape(layers, inner, width),
    )


def solution(mesh):
    split = P(None, AXIS, None)
    return jax.shard_map(
        shards,
        mesh=mesh,
        in_specs=(split,) + (P(),) * 10 + (split,),
        out_specs=(split, split) + (P(),) * 10,
        check_vma=False,
    )
```

```python
import functools
import math

import jax
import jax.numpy as jnp
from jax import lax
from jax.experimental import pallas as pl
from jax.experimental.pallas import tpu as pltpu
from jax.sharding import PartitionSpec as P

BF16 = jnp.bfloat16
F32 = jnp.float32
LOG2E = 1.4426950408889634
LN2 = 0.6931471805599453
AXIS = "seq"
XD = 128
EXTRA = 256
CHUNK = 512
UNROLL = 8
HALO = 8
COST = pl.CostEstimate(flops=1, bytes_accessed=1, transcendentals=0)
LONG = pl.CostEstimate(flops=1, bytes_accessed=10**8, transcendentals=0)
SPARE = 4
BLOCKS = 16


def full(array):
    nd = len(array.shape)
    return pl.BlockSpec(array.shape, lambda i, nd=nd: (0,) * nd)


def part(shape, index):
    return pl.BlockSpec(shape, lambda i, index=index: index)


def room(specs, dtypes, out_specs, out_dtypes, scratch, spare):
    total = spare << 20
    for spec, dtype in list(zip(specs, dtypes)) + list(zip(out_specs, out_dtypes)):
        if spec.block_shape is not None:
            total += math.prod(d or 1 for d in spec.block_shape) * jnp.dtype(dtype).itemsize
    for item in scratch:
        if not hasattr(item, "shape"):
            continue
        total += math.prod(item.shape) * jnp.dtype(item.dtype).itemsize
    return min(total, 58 << 20)


class Late:
    def __init__(self, array, index, dims):
        self.array, self.index, self.dims = array, index, dims


class Fetched:
    def __init__(self, source, target, sem):
        self.copy, self.ref = pltpu.make_async_copy(source, target, sem), target
        self.copy.start()

    def __getitem__(self, where):
        if self.copy is not None:
            self.copy.wait()
            self.copy = None
        return self.ref[where]


class Row:
    def __init__(self, array, index):
        self.array, self.index = array, index


def run(kernel, outs, ins, scratch=(), turn=None, cost=COST, spare=SPARE):
    out_specs = [o[1] if isinstance(o, tuple) else full(o) for o in outs]
    outs = [o[0] if isinstance(o, tuple) else o for o in outs]
    arrays, specs, picks, late = [], [], {}, {}
    scratch = list(scratch)
    for item in ins:
        if isinstance(item, Late):
            late[len(arrays)] = item.index
            scratch += [pltpu.VMEM(item.dims, item.array.dtype), pltpu.SemaphoreType.DMA]
            item = (item.array, pl.BlockSpec(memory_space=pltpu.HBM))
        if isinstance(item, Row):
            picks[len(arrays)] = item.index
            item = item.array
        if isinstance(item, tuple):
            arrays.append(item[0])
            specs.append(item[1])
        else:
            arrays.append(item)
            specs.append(full(item))
    n = len(arrays)
    limit = room(specs, [a.dtype for a in arrays], out_specs, [o.dtype for o in outs], scratch, spare)
    if turn:
        arrays.append(turn[0])
        specs.append(pl.BlockSpec(memory_space=pl.ANY))
    after = len(arrays)

    def body(*refs):
        given = list(refs[:n])
        for k, index in picks.items():
            given[k] = given[k].at[index : index + 1, :]
        rest, buffers = refs[after:], ()
        if late:
            rest, buffers = rest[: -2 * len(late)], rest[-2 * len(late) :]
        for i, (k, index) in enumerate(late.items()):
            given[k] = Fetched(given[k].at[index], buffers[2 * i], buffers[2 * i + 1])
        kernel(*given, *rest)

    results = pl.pallas_call(
        body,
        grid=(1,),
        in_specs=specs,
        out_specs=out_specs,
        out_shape=outs,
        scratch_shapes=list(scratch),
        compiler_params=pltpu.CompilerParams(vmem_limit_bytes=limit),
        cost_estimate=cost,
    )(*arrays)
    if turn is not None:
        turn[:] = [results[-1]]
    return results


def shape(dims, dtype):
    return jax.ShapeDtypeStruct(dims, dtype)


def dot(a, b):
    return jnp.dot(a, b, preferred_element_type=F32)


def dot_t(a, b):
    return lax.dot_general(a, b, (((1,), (1,)), ((), ())), preferred_element_type=F32)


def dot_rows(a, b):
    return lax.dot_general(a, b, (((0,), (0,)), ((), ())), preferred_element_type=F32)


def sigmoid(v):
    return 1.0 / (1.0 + jnp.exp(-v))


def softplus(v):
    return jnp.maximum(v, 0.0) + jnp.log1p(jnp.exp(-jnp.abs(v)))


def slope(v):
    s = sigmoid(v)
    return s * (1.0 + v * (1.0 - s))


def wide(block, lanes):
    return jnp.concatenate([block] * (lanes // block.shape[1]), axis=1)


def rows_of_sums(parts):
    row = lax.broadcasted_iota(jnp.int32, parts[0].shape, 0)
    m4, m2, m1 = row < 4, (row & 2) == 0, (row & 1) == 0
    q = []
    for i in range(4):
        first = jnp.where(m4, parts[i], parts[i + 4])
        other = jnp.where(m4, parts[i + 4], parts[i])
        q.append(first + pltpu.roll(other, 4, 0))
    s = []
    for i in range(2):
        s.append(
            jnp.where(
                m2, q[i] + pltpu.roll(q[i], 6, 0), q[i + 2] + pltpu.roll(q[i + 2], 2, 0)
            )
        )
    return jnp.where(m1, s[0] + pltpu.roll(s[0], 7, 0), s[1] + pltpu.roll(s[1], 1, 0))


def fold(block):
    out = block[0:8]
    for k in range(8, block.shape[0], 8):
        out = out + block[k : k + 8]
    return out


def fold_lanes(block):
    out = block[:, 0:128]
    for k in range(128, block.shape[1], 128):
        out = out + block[:, k : k + 128]
    return out


def normed_of(x, gain):
    rinv = lax.rsqrt(jnp.mean(x * x, axis=-1, keepdims=True) + 1e-05)
    return (x * rinv * gain).astype(BF16)


def fill_table(xdf_ref, lhs_ref, bc_ref, rank, states):
    rows = xdf_ref.shape[0]
    n_i = lax.broadcasted_iota(jnp.int32, (states, XD), 0)
    lane = lax.broadcasted_iota(jnp.int32, (states, XD), 1)
    mask = ((lane == rank + n_i) | (lane == rank + states + n_i)).astype(F32)

    def body(i, carry):
        for j in range(UNROLL):
            t = i * UNROLL + j
            line = xdf_ref[pl.ds(t, 1), :]
            lhs_ref[pl.ds(pl.multiple_of(t * states, states), states), :] = (
                line * mask
            ).astype(BF16)
        return carry

    lax.fori_loop(0, rows // UNROLL, body, 0)
    k_i = lax.broadcasted_iota(jnp.int32, (XD, 256), 0)
    c_i = lax.broadcasted_iota(jnp.int32, (XD, 256), 1)
    low = rank + jnp.where(c_i >= 128, states, 0)
    pick = ((k_i >= low) & (k_i < low + states)).astype(BF16)
    bc_ref[...] = dot(lhs_ref[...], pick)


def state_rows(t, states):
    return pl.ds(pl.multiple_of(t * states, states), states)


def scan_ends(dt_ref, dtu_ref, bc_ref, a2_ref, end_ref):
    rows, inner = dt_ref.shape
    states = a2_ref.shape[0]

    def chunk(c, carry):
        lanes = pl.ds(pl.multiple_of(c * CHUNK, CHUNK), CHUNK)
        a2 = a2_ref[:, lanes]

        def body(i, h):
            for j in range(UNROLL):
                t = i * UNROLL + j
                a = jnp.exp2(dt_ref[pl.ds(t, 1), lanes] * a2)
                b = wide(bc_ref[state_rows(t, states), 0:128], CHUNK)
                h = a * h + dtu_ref[pl.ds(t, 1), lanes] * b
            return h

        end_ref[:, lanes] = lax.fori_loop(
            0, rows // UNROLL, body, jnp.zeros((states, CHUNK), F32)
        )
        return carry

    lax.fori_loop(0, inner // CHUNK, chunk, 0)


def scan_back_ends(dt_ref, dy_ref, bc_ref, a2_ref, end_ref):
    rows, inner = dt_ref.shape
    states = a2_ref.shape[0]

    def chunk(c, carry):
        lanes = pl.ds(pl.multiple_of(c * CHUNK, CHUNK), CHUNK)
        a2 = a2_ref[:, lanes]

        def body(i, back):
            for j in range(UNROLL):
                t = rows - 1 - (i * UNROLL + j)
                a = jnp.exp2(dt_ref[pl.ds(t, 1), lanes] * a2)
                c_row = wide(bc_ref[state_rows(t, states), 128:256], CHUNK)
                back = a * (dy_ref[pl.ds(t, 1), lanes] * c_row + back)
            return back

        end_ref[:, lanes] = lax.fori_loop(
            0, rows // UNROLL, body, jnp.zeros((states, CHUNK), F32)
        )
        return carry

    lax.fori_loop(0, inner // CHUNK, chunk, 0)


def scan_forward(dt_ref, dtu_ref, bc_ref, a2_ref, h_in_ref, y_ref):
    rows, inner = dt_ref.shape
    states = a2_ref.shape[0]

    def chunk(c, carry):
        lanes = pl.ds(pl.multiple_of(c * CHUNK, CHUNK), CHUNK)
        a2 = a2_ref[:, lanes]

        def body(i, h):
            parts = []
            for j in range(UNROLL):
                t = i * UNROLL + j
                a = jnp.exp2(dt_ref[pl.ds(t, 1), lanes] * a2)
                both = bc_ref[state_rows(t, states), :]
                h = a * h + dtu_ref[pl.ds(t, 1), lanes] * wide(both[:, 0:128], CHUNK)
                parts.append(fold(h * wide(both[:, 128:256], CHUNK)))
            y_ref[pl.ds(pl.multiple_of(i * UNROLL, UNROLL), UNROLL), lanes] = rows_of_sums(
                parts
            )
            return h

        lax.fori_loop(0, rows // UNROLL, body, h_in_ref[:, lanes])
        return carry

    lax.fori_loop(0, inner // CHUNK, chunk, 0)


def scan_both(
    dt_ref,
    dtu_ref,
    dy_ref,
    bc_ref,
    a2_ref,
    h_in_ref,
    g_in_ref,
    sgb_ref,
    sqa_ref,
    rate_ref,
    db_ref,
    dc_ref,
    a_s,
    ah_s,
):
    rows, inner = dt_ref.shape
    states = a2_ref.shape[0]
    db_ref[...] = jnp.zeros(db_ref.shape, F32)
    dc_ref[...] = jnp.zeros(dc_ref.shape, F32)

    def chunk(c, carry):
        lanes = pl.ds(pl.multiple_of(c * CHUNK, CHUNK), CHUNK)
        a2 = a2_ref[:, lanes]

        def ahead(i, h):
            for j in range(UNROLL):
                t = i * UNROLL + j
                at = state_rows(t, states)
                a = jnp.exp2(dt_ref[pl.ds(t, 1), lanes] * a2)
                b_row = wide(bc_ref[at, 0:128], CHUNK)
                ah = a * h
                a_s[at, :] = a
                ah_s[at, :] = ah
                h = ah + dtu_ref[pl.ds(t, 1), lanes] * b_row
                dc_ref[at, :] += fold_lanes(h * dy_ref[pl.ds(t, 1), lanes])
            return h

        lax.fori_loop(0, rows // UNROLL, ahead, h_in_ref[:, lanes])

        def retreat(i, carried):
            back, rate = carried
            block = rows // UNROLL - 1 - i
            gbs, qas = [None] * UNROLL, [None] * UNROLL
            for j in reversed(range(UNROLL)):
                t = block * UNROLL + j
                at = state_rows(t, states)
                both = bc_ref[at, :]
                g = dy_ref[pl.ds(t, 1), lanes] * wide(both[:, 128:256], CHUNK) + back
                q = g * ah_s[at, :]
                gbs[j] = fold(g * wide(both[:, 0:128], CHUNK))
                qas[j] = fold(q * a2)
                rate = rate + q * dt_ref[pl.ds(t, 1), lanes]
                db_ref[at, :] += fold_lanes(g * dtu_ref[pl.ds(t, 1), lanes])
                back = a_s[at, :] * g
            here = pl.ds(pl.multiple_of(block * UNROLL, UNROLL), UNROLL)
            sgb_ref[here, lanes] = rows_of_sums(gbs)
            sqa_ref[here, lanes] = rows_of_sums(qas)
            return back, rate

        _, rate = lax.fori_loop(
            0,
            rows // UNROLL,
            retreat,
            (g_in_ref[:, lanes], jnp.zeros((states, CHUNK), F32)),
        )
        rate_ref[:, lanes] = rate
        return carry

    lax.fori_loop(0, inner // CHUNK, chunk, 0)


def packed(state, total, wide_s):
    inner = total.shape[1]
    high = total.astype(BF16).astype(F32)
    rest = total - high
    wide_s[:, 0:inner] = state
    wide_s[:, inner:] = jnp.zeros((state.shape[0], EXTRA), F32)
    for k in range(inner // 128):
        wide_s[k : k + 1, inner : inner + 128] = high[:, k * 128 : (k + 1) * 128]
        wide_s[k : k + 1, inner + 128 : inner + 256] = rest[:, k * 128 : (k + 1) * 128]
    return wide_s[...].astype(BF16)


def unpack_total(wide_ref, m, total_ref, inner):
    for k in range(inner // 128):
        total_ref[m, 0:1, k * 128 : (k + 1) * 128] = (
            wide_ref[m, k : k + 1, inner : inner + 128]
            + wide_ref[m, k : k + 1, inner + 128 : inner + 256]
        )


def join_runs(states_ref, totals_ref, a2, digit, group, backward):
    inner = a2.shape[1]
    before = jnp.zeros(a2.shape, F32)
    entire = jnp.zeros(a2.shape, F32)
    sum_before = jnp.zeros((1, inner), F32)
    sum_entire = jnp.zeros((1, inner), F32)
    order = reversed(range(group)) if backward else range(group)
    for p in order:
        m = jnp.bitwise_xor(digit, p)
        state = states_ref[m, :, 0:inner]
        total = totals_ref[m, 0:1, :]
        through = jnp.exp2(total * a2)
        counts = (p > digit) if backward else (p < digit)
        before = jnp.where(counts, through * before + state, before)
        sum_before = jnp.where(counts, sum_before + total, sum_before)
        entire = through * entire + state
        sum_entire = sum_entire + total
    return before, sum_before, entire, sum_entire


def k_in(x_ref, g_ref, w_ref, n_ref, xc_ref, tail_ref):
    normed = normed_of(x_ref[...], g_ref[...])
    n_ref[...] = normed
    xc = dot(normed, w_ref[...]).astype(BF16)
    xc_ref[...] = xc
    tail_ref[...] = xc.astype(F32)[xc.shape[0] - HALO :, :]


def k_gate(n_ref, w_ref, z_ref):
    z_ref[...] = dot(n_ref[...], w_ref[...]).astype(BF16)


def k_dgated(e_ref, w_ref, out_ref):
    out_ref[...] = dot_t(e_ref[...], w_ref[...])


def conv_of(ext_s, halo_ref, xc_ref, cw_ref, cb_ref):
    rows = xc_ref.shape[0]
    taps = cw_ref.shape[0]
    ext_s[0:HALO, :] = halo_ref[...]
    ext_s[HALO:, :] = xc_ref[...].astype(F32)
    out = cb_ref[...]
    for k in range(taps):
        first = HALO - (taps - 1) + k
        out = out + cw_ref[k : k + 1, :] * ext_s[first : first + rows, :]
    return out


def k_local(
    rank, both, *refs
):
    refs = list(refs)
    halo, xc, cw, cb, xw, dw, db, a2 = refs[:8]
    refs = refs[8:]
    if both:
        dgated, z = refs[:2]
        refs = refs[2:]
    u_ref, xd_ref, v_ref, dt_s, pay_ref = refs[:5]
    refs = refs[5:]
    if both:
        dy_ref = refs[0]
        refs = refs[1:]
    ext_s, dtu_s, xdf_s, lhs_s, bc_s, end_s, wide_s = refs
    states = a2.shape[0]
    conv = conv_of(ext_s, halo, xc, cw, cb)
    u = (conv * sigmoid(conv)).astype(BF16)
    u_ref[...] = u
    xd = dot(u, xw[...]).astype(BF16)
    xd_ref[...] = xd
    xdf_s[...] = xd.astype(F32)
    v = dot(xd, dw[...]) + db[...]
    v_ref[...] = v
    dt = softplus(v)
    dt_s[...] = dt
    dtu_s[...] = dt * u.astype(F32)
    total = jnp.sum(dt, axis=0, keepdims=True)
    fill_table(xdf_s, lhs_s, bc_s, rank, states)
    scan_ends(dt_s, dtu_s, bc_s, a2, end_s)
    pay_ref[0:states, :] = packed(end_s[...], total, wide_s)
    if both:
        zf = z[...].astype(F32)
        dy_ref[...] = dgated[...] * (zf * sigmoid(zf))
        scan_back_ends(dt_s, dy_ref, bc_s, a2, end_s)
        pay_ref[states:, :] = packed(end_s[...], total, wide_s)


def k_join(group, nextgroup, mode, digits, *refs):
    refs = list(refs)
    received, refs = refs[:group], refs[group:]
    a2_ref, refs = refs[0], refs[1:]
    kinds = list(mode)
    n_pay = (nextgroup - 1) if (len(kinds) == 2 and nextgroup) else 1
    pays, refs = refs[:n_pay], refs[n_pay:]
    befores, refs = refs[: len(kinds)], refs[len(kinds) :]
    sums, refs = refs[: len(kinds)], refs[len(kinds) :]
    states_s, totals_s, wide_s = refs
    states, inner = a2_ref.shape
    digit = digits[0]
    nextdigit = digits[1]
    out = []
    for i in range(len(kinds)):
        for m in range(group):
            states_s[m] = received[m][i * states : (i + 1) * states, :].astype(F32)
            if i == 0:
                unpack_total(states_s, m, totals_s, inner)
        before, sum_before, entire, sum_entire = join_runs(
            states_s, totals_s, a2_ref[...], digit, group, kinds[i] == "b"
        )
        befores[i][...] = before
        sums[i][...] = sum_before
        out.append(packed(entire, sum_entire, wide_s))
    if len(kinds) == 2 and nextgroup:
        for m in range(1, nextgroup):
            ahead = jnp.bitwise_xor(nextdigit, m) > nextdigit
            pays[m - 1][...] = jnp.where(ahead, out[0].astype(F32), out[1].astype(F32)).astype(
                BF16
            )
    else:
        for i in range(len(kinds)):
            pays[0][i * states : (i + 1) * states, :] = out[i]


def entering(received, a2_ref, digit, befores, sums, states_s, totals_s, backward, lane0=0):
    lanes = a2_ref.shape[1]
    inner = received[0].shape[1] - EXTRA
    here = slice(lane0, lane0 + lanes)
    group = len(received) + 1
    states_s[0] = jnp.zeros(states_s.shape[1:], F32)
    totals_s[0] = jnp.zeros(totals_s.shape[1:], F32)
    for m in range(1, group):
        states_s[m] = received[m - 1][:, here].astype(F32)
        sums_m = received[m - 1][:, inner:].astype(F32)
        for k in range(lanes // 128):
            row = lane0 // 128 + k
            totals_s[m, 0:1, k * 128 : (k + 1) * 128] = (
                sums_m[row : row + 1, 0:128] + sums_m[row : row + 1, 128:256]
            )
    value, _, _, _ = join_runs(states_s, totals_s, a2_ref[...], digit, group, backward)
    for before, total in reversed(list(zip(befores, sums))):
        value = jnp.exp2(total[:, here] * a2_ref[...]) * value + before[:, here]
    return value


def k_mix(rank, last, n_recv, n_low, digits, core, *refs):
    refs = list(refs)
    received, refs = refs[:n_recv], refs[n_recv:]
    befores, refs = refs[:n_low], refs[n_low:]
    sums, refs = refs[:n_low], refs[n_low:]
    a2, u_ref, dt_ref, xd_ref, z_ref, x_ref, sk_ref, ow_ref = refs[:8]
    refs = refs[8:]
    if last:
        dgated_ref, hid_mine, hid_other, dz_ref, dz_keep, gated_keep, sends, h_in_ref = refs[:8]
        y_ref, hid_s, refs = refs[8], refs[9], refs[10:]
    else:
        g_ref, iw_ref, y_ref, x1_ref, n_ref, xc_ref, tail_ref = refs[:7]
        gated_keep, sends, h_in_ref = refs[7:10]
        refs = refs[10:]
    gated_s, dtu_s, xdf_s, lhs_s, bc_s, states_s, totals_s = refs
    h_in_ref[...] = entering(received, a2, digits[0], befores, sums, states_s, totals_s, False)
    uf = u_ref[...].astype(F32)
    dtu_s[...] = dt_ref[...] * uf
    xdf_s[...] = xd_ref[...].astype(F32)
    fill_table(xdf_s, lhs_s, bc_s, rank, a2.shape[0])
    scan_forward(dt_ref, dtu_s, bc_s, a2, h_in_ref, y_ref)
    y = y_ref[...] + sk_ref[...] * u_ref[...].astype(F32)
    zf = z_ref[...].astype(F32)
    s = sigmoid(zf)
    gated = (y * (zf * s)).astype(BF16)
    gated_s[...] = gated
    rows = gated.shape[0]
    gated_keep[...] = lane_half(gated_s, core[0])
    sends[0:rows, :] = lane_half(gated_s, 1 - core[0])
    x1 = x_ref[...] + dot(gated, ow_ref[...])
    if last:
        dz_ref[...] = (dgated_ref[...] * y * (s * (1.0 + zf * (1.0 - s)))).astype(BF16)
        dz_keep[...] = lane_half(dz_ref, core[0])
        sends[rows:, :] = lane_half(dz_ref, 1 - core[0])
        hid_s[...] = x1
        hid_mine[...] = row_half(hid_s, core[0]).astype(BF16)
        hid_other[...] = row_half(hid_s, 1 - core[0]).astype(BF16)
    else:
        y_ref[...] = y
        x1_ref[...] = x1
        normed = normed_of(x1, g_ref[...])
        n_ref[...] = normed
        sends[rows:, :] = normed
        xc = dot(normed, iw_ref[...]).astype(BF16)
        xc_ref[...] = xc
        tail_ref[...] = xc.astype(F32)[xc.shape[0] - HALO :, :]


def k_scan(rank, lane0, n_recv, n_low, digits, *refs):
    refs = list(refs)
    received, refs = refs[:n_recv], refs[n_recv:]
    befores, refs = refs[:n_low], refs[n_low:]
    sums, refs = refs[:n_low], refs[n_low:]
    a2, u_ref, dt_ref, dy_ref, h_in_ref, xd_ref = refs[:6]
    sgb_ref, sqa_ref, rate_ref, dbc_ref = refs[6:10]
    dtu_s, xdf_s, lhs_s, bc_s, states_s, totals_s, db_s, dc_s, a_s, ah_s, g_s = refs[10:]
    states = a2.shape[0]
    rows = u_ref.shape[0]
    g_s[...] = entering(
        received, a2, digits[0], befores, sums, states_s, totals_s, True, lane0
    )
    dtu_s[...] = dt_ref[...] * u_ref[...].astype(F32)
    xdf_s[...] = xd_ref[...].astype(F32)
    fill_table(xdf_s, lhs_s, bc_s, rank, states)
    scan_both(
        dt_ref, dtu_s, dy_ref, bc_s, a2, h_in_ref, g_s, sgb_ref, sqa_ref, rate_ref, db_s, dc_s, a_s, ah_s
    )
    rate_ref[...] = rate_ref[...] * (a2[...] * LN2)

    ones = jnp.ones((128, 128), BF16)

    def lane_sums(block):
        high = block.astype(BF16)
        rest = (block - high.astype(F32)).astype(BF16)
        return dot(high, ones) + dot(rest, ones)

    n_i = lax.broadcasted_iota(jnp.int32, (states, XD), 0)
    lane = lax.broadcasted_iota(jnp.int32, (states, XD), 1)
    mask_b = (lane == rank + n_i).astype(F32)
    mask_c = (lane == rank + states + n_i).astype(F32)
    db_s[...] = lane_sums(db_s[...])
    dc_s[...] = lane_sums(dc_s[...])

    def gather(i, carry):
        parts = []
        for j in range(UNROLL):
            at = state_rows(i * UNROLL + j, states)
            parts.append(fold(db_s[at, :] * mask_b + dc_s[at, :] * mask_c))
        dbc_ref[pl.ds(pl.multiple_of(i * UNROLL, UNROLL), UNROLL), :] = rows_of_sums(parts)
        return carry

    lax.fori_loop(0, rows // UNROLL, gather, 0)


def k_post(rank, n_parts, *refs):
    refs = list(refs)
    sgbs, refs = refs[:n_parts], refs[n_parts:]
    sqas, refs = refs[:n_parts], refs[n_parts:]
    rates, refs = refs[:n_parts], refs[n_parts:]
    dbcs, refs = refs[:n_parts], refs[n_parts:]
    u_ref, v_ref, dt_ref, xd_ref, dy_ref, halo, xc, cw, cb, xw, dw, sk_ref = refs[:12]
    dconv_ref, head_ref, small_ref, ext_s = refs[12:]
    states = rates[0].shape[0]
    rows, inner = u_ref.shape
    sgb = jnp.concatenate([ref[...] for ref in sgbs], axis=1)
    sqa = jnp.concatenate([ref[...] for ref in sqas], axis=1)
    dbc = dbcs[0][...]
    for ref in dbcs[1:]:
        dbc = dbc + ref[...]
    u = u_ref[...]
    uf = u.astype(F32)
    dy = dy_ref[...]
    v = v_ref[...]
    dpre = (LN2 * sqa + uf * sgb) * sigmoid(v)
    dpl = dpre.astype(BF16)
    dxd = (dot_t(dpl, dw[...]) + dbc).astype(BF16)
    du = dt_ref[...] * sgb + sk_ref[...] * dy + dot_t(dxd, xw[...])
    conv = conv_of(ext_s, halo, xc, cw, cb)
    dconv = du * slope(conv)
    dconv_ref[...] = dconv
    head_ref[...] = dconv[0:HALO, :]
    taps = cw.shape[0]
    width = rank + 2 * states
    g_x = dot_rows(dxd, u)
    g_dt = dot_rows(xd_ref[...], dpl)
    at = 0
    small_ref[at : at + width, :] = g_x[0:width]
    at += width
    small_ref[at : at + rank, :] = g_dt[0:rank]
    at += rank
    small_ref[at : at + states, :] = jnp.concatenate([ref[...] for ref in rates], axis=1)
    at += states
    for k in range(taps):
        first = HALO - (taps - 1) + k
        small_ref[at : at + 1, :] = jnp.sum(
            dconv * ext_s[first : first + rows, :], axis=0, keepdims=True
        )
        at += 1
    small_ref[at : at + 1, :] = jnp.sum(dconv, axis=0, keepdims=True)
    small_ref[at + 1 : at + 2, :] = jnp.sum(dpre, axis=0, keepdims=True)
    small_ref[at + 2 : at + 3, :] = jnp.sum(dy * uf, axis=0, keepdims=True)
    small_ref[at + 3 : at + 4, :] = jnp.zeros((1, inner), F32)


def row_half(ref, which):
    half = ref.shape[0] // 2
    return ref[pl.ds(pl.multiple_of(which * half, 16), half), :]


def lane_half(ref, which):
    half = ref.shape[1] // 2
    return ref[:, pl.ds(pl.multiple_of(which * half, 128), half)]


def conv_back(dce_s, dconv_ref, next_ref, cw_ref):
    rows = dconv_ref.shape[0]
    taps = cw_ref.shape[0]
    dce_s[0:rows, :] = dconv_ref[...]
    dce_s[rows:, :] = next_ref[...]
    out = cw_ref[taps - 1 : taps, :] * dce_s[0:rows, :]
    for k in range(taps - 1):
        first = taps - 1 - k
        out = out + cw_ref[k : k + 1, :] * dce_s[first : first + rows, :]
    return out.astype(BF16)


def norm_back(x, gain, e, dn):
    rinv = lax.rsqrt(jnp.mean(x * x, axis=-1, keepdims=True) + 1e-05)
    xhat = x * rinv
    dhat = dn * gain
    g_norm = jnp.sum(dn * xhat, axis=0, keepdims=True)
    return e + rinv * (dhat - xhat * jnp.mean(dhat * xhat, axis=-1, keepdims=True)), g_norm


def small_out(core, small_ref, g_norm, keep_ref, sends, at):
    rows, inner = small_ref.shape
    width = g_norm.shape[1]
    small_ref[rows - 1 : rows, 0:width] = g_norm
    pad = keep_ref.shape[0] - rows
    for which, ref, first in ((core[0], keep_ref, 0), (1 - core[0], sends, at)):
        block = lane_half(small_ref, which)
        block = jnp.concatenate([block, jnp.zeros((pad, block.shape[1]), F32)], axis=0)
        ref[first : first + rows + pad, :] = block.astype(ref.dtype)
    sends[at + rows + pad :, :] = jnp.zeros((sends.shape[0] - at - rows - pad, inner // 2), BF16)


def k_turn(
    rank,
    core,
    small_ref,
    dconv_ref,
    next_ref,
    cw_ref,
    dnz_ref,
    iw_ref,
    x_ref,
    g_ref,
    e_ref,
    ow_ref,
    y_ref,
    z_ref,
    dt_ref,
    xd_ref,
    a2,
    iz_ref,
    dxc_keep,
    small_keep,
    e1_ref,
    de_ref,
    dy_ref,
    dz_ref,
    dz_keep,
    sends,
    dnz0_ref,
    pay_ref,
    small_s,
    dxc_s,
    dce_s,
    xdf_s,
    lhs_s,
    bc_s,
    end_s,
    wide_s,
):
    dxc = conv_back(dce_s, dconv_ref, next_ref, cw_ref)
    rows = dxc.shape[0]
    dxc_s[...] = dxc
    dxc_keep[...] = lane_half(dxc_s, core[0])
    sends[0:rows, :] = lane_half(dxc_s, 1 - core[0])
    dn = dnz_ref[...] + dot_t(dxc, iw_ref[...])
    e1, g_norm = norm_back(x_ref[...], g_ref[...], e_ref[...].astype(F32), dn)
    small_s[...] = small_ref[...]
    small_out(core, small_s, g_norm, small_keep, sends, 3 * rows)
    e1_ref[...] = e1
    de = e1.astype(BF16)
    de_ref[...] = de
    sends[2 * rows : 3 * rows, :] = de
    dgated = dot_t(de, ow_ref[...])
    zf = z_ref[...].astype(F32)
    s = sigmoid(zf)
    dy_ref[...] = dgated * (zf * s)
    dz_ref[...] = (dgated * y_ref[...] * (s * (1.0 + zf * (1.0 - s)))).astype(BF16)
    dz_keep[...] = lane_half(dz_ref, core[0])
    sends[rows : 2 * rows, :] = lane_half(dz_ref, 1 - core[0])
    dnz0_ref[...] = dot_t(dz_ref[...], iz_ref[...])
    states = a2.shape[0]
    total = jnp.sum(dt_ref[...], axis=0, keepdims=True)
    xdf_s[...] = xd_ref[...].astype(F32)
    fill_table(xdf_s, lhs_s, bc_s, rank, states)
    scan_back_ends(dt_ref, dy_ref, bc_s, a2, end_s)
    pay_ref[...] = packed(end_s[...], total, wide_s)


def k_end(
    core,
    small_ref,
    dconv_ref,
    next_ref,
    cw_ref,
    dnz_ref,
    iw_ref,
    x_ref,
    g_ref,
    e_ref,
    dxc_keep,
    small_keep,
    sends,
    e0_mine,
    e0_other,
    small_s,
    dxc_s,
    dce_s,
    e0_s,
):
    dxc = conv_back(dce_s, dconv_ref, next_ref, cw_ref)
    rows = dxc.shape[0]
    dxc_s[...] = dxc
    dxc_keep[...] = lane_half(dxc_s, core[0])
    sends[0:rows, :] = lane_half(dxc_s, 1 - core[0])
    dn = dnz_ref[...] + dot_t(dxc, iw_ref[...])
    e0, g_norm = norm_back(x_ref[...], g_ref[...], e_ref[...], dn)
    small_s[...] = small_ref[...]
    small_out(core, small_s, g_norm, small_keep, sends, rows)
    e0_s[...] = e0
    e0_mine[...] = row_half(e0_s, core[0]).astype(BF16)
    e0_other[...] = row_half(e0_s, 1 - core[0]).astype(BF16)


def k_dnz(dz_ref, iw_ref, out_ref):
    out_ref[...] = dot_t(dz_ref[...], iw_ref[...])


def chip_sums(n_pairs, has_small, refs, s_ref):
    refs = list(refs)
    pairs, refs = [refs[4 * i : 4 * i + 4] for i in range(n_pairs)], refs[4 * n_pairs :]
    blocks = s_ref.shape[0]
    rows = pairs[0][0].shape[1] // blocks
    for i, (a, a_came, b, b_came) in enumerate(pairs):
        total = dot_rows(
            jnp.concatenate([a[...], a_came[...]], axis=0),
            jnp.concatenate([b[...], b_came[...]], axis=0),
        )
        s_ref[:, 0:rows, :] = total.reshape(blocks, rows, total.shape[1])
        yield i * rows, rows
    if has_small:
        small_a, small_b = refs
        n = small_a.shape[0] // blocks
        s_ref[:, 0:16, :] = jnp.zeros((blocks, 16, s_ref.shape[2]), F32)
        small = small_a[...] + small_b[...].astype(F32)[0 : small_a.shape[0]]
        for k in range(blocks):
            s_ref[k, 0:n, :] = small[k * n : (k + 1) * n]
        yield n_pairs * rows, 16


def k_chip_sum(n_pairs, has_small, *refs):
    out, s_ref = refs[-2:]
    for top, rows in chip_sums(n_pairs, has_small, refs[:-2], s_ref):
        out[:, top : top + rows, :] = s_ref[:, 0:rows, :]


def k_first(n_pairs, has_small, place, *refs):
    keep_a, keep_b, send_a, send_b, s_ref = refs[-5:]
    blocks = s_ref.shape[0]
    half = s_ref.shape[2] // 2
    x, y = place[0] & 1, (place[0] >> 1) & 1
    for top, rows in chip_sums(n_pairs, has_small, refs[:-5], s_ref):
        to, take = slice(top, top + rows), slice(0, rows)
        for i in range(blocks // 2):
            at = (i >> 1) * 4 + (i & 1) * 2
            keep_a[i, to, :] = s_ref[at + x, take, 0:half]
            send_a[i, to, :] = s_ref[at + 1 - x, take, 0:half].astype(BF16)
            at = (i >> 1) * 4 + (i & 1)
            keep_b[i, to, :] = s_ref[at + 2 * y, take, half:]
            send_b[i, to, :] = s_ref[at + 2 * (1 - y), take, half:].astype(BF16)


def k_second(place, keep_a, keep_b, came_a, came_b, stay_a, stay_b, send_a, send_b):
    x, y = place[0] & 1, (place[0] >> 1) & 1
    for i in range(stay_a.shape[0]):
        for keep, came, stay, send, bit in (
            (keep_a, came_a, stay_a, send_a, y),
            (keep_b, came_b, stay_b, send_b, x),
        ):
            at = 2 * i + bit
            stay[i] = keep[at] + came[at].astype(F32)
            at = 2 * i + 1 - bit
            send[i] = (keep[at] + came[at].astype(F32)).astype(BF16)


def k_third(place, stay_a, stay_b, came_a, came_b, keep, send1, send2, send3):
    z = (place[0] >> 2) & 3
    half = stay_a.shape[2]
    for m, ref in enumerate((keep, send1, send2, send3)):
        at = jnp.bitwise_xor(z, m)
        ref[:, 0:half] = (stay_a[at] + came_a[at].astype(F32)).astype(ref.dtype)
        ref[:, half:] = (stay_b[at] + came_b[at].astype(F32)).astype(ref.dtype)


def k_fourth(keep, came1, came2, came3, out):
    out[...] = (
        keep[...] + came1[...].astype(F32) + came2[...].astype(F32) + came3[...].astype(F32)
    ).astype(BF16)


def k_stack(mine, came1, came2, came3, out_a, out_b):
    half = out_a.shape[2]
    for m, ref in enumerate((mine, came1, came2, came3)):
        out_a[m] = ref[:, 0:half]
        out_b[m] = ref[:, half:]


def k_chip(place, *refs):
    left, right, out = refs[0:4], refs[4:8], refs[8]
    half = left[0].shape[2]
    xy, z = place[0] & 3, (place[0] >> 2) & 3
    for d in range(4):
        for m in range(4):
            at = jnp.bitwise_xor(z, m) * 4 + jnp.bitwise_xor(xy, d)
            out[at, :, 0:half] = left[d][m]
            out[at, :, half:] = right[d][m]


def in_order(core, sources):
    if len(sources) == 1:
        return sources[0][:, 0].astype(F32), sources[0][:, 1].astype(F32)
    own = core[0] == 0
    a, b = sources[0][...].astype(F32), sources[1][...].astype(F32)
    return jnp.where(own, a, b), jnp.where(own, b, a)


def k_place(n_sources, split_rows, core, *refs):
    out, done = refs[-2:]
    done[...] = jnp.zeros(done.shape, F32)
    low, high = in_order(core, refs[:n_sources])
    blocks, rows, lanes = low.shape
    low, high = low.reshape(blocks * rows, lanes), high.reshape(blocks * rows, lanes)
    if split_rows:
        out[0], out[1] = low, high
    else:
        out[:, 0:lanes] = low
        out[:, lanes:] = high


def k_place_small(rank, taps, counts, core, *refs):
    refs = list(refs)
    given, refs = refs[: sum(counts)], refs[sum(counts) :]
    norm, cw, cb, xw, dw, db, al, sk, all_s = refs
    states = al.shape[1]
    n_x = rank + 2 * states
    all_s[...] = jnp.zeros(all_s.shape, F32)
    at = 0
    for l, count in enumerate(counts):
        low, high = in_order(core, given[at : at + count])
        at += count
        blocks, _, lanes = low.shape
        n = -(-(n_x + rank + states + taps + 4) // blocks)
        for k in range(blocks):
            all_s[k * n : (k + 1) * n, 0:lanes] = low[k, 0:n]
            all_s[k * n : (k + 1) * n, lanes:] = high[k, 0:n]
        dw[l] = all_s[n_x : n_x + rank, :]
        first = n_x + rank
        xw[l] = all_s[0:n_x, :]
        al[l] = all_s[first : first + states, :]
        cw[l] = all_s[first + states : first + states + taps, :]
        first += states + taps
        cb[l : l + 1, :] = all_s[first : first + 1, :]
        db[l : l + 1, :] = all_s[first + 1 : first + 2, :]
        sk[l : l + 1, :] = all_s[first + 2 : first + 3, :]
        norm[l : l + 1, :] = all_s[first + 3 : first + 4, 0 : norm.shape[1]]


def shards(
    hidden_in,
    norm_gain,
    in_weight,
    conv_weight,
    conv_bias,
    xproj_weight,
    dtproj_weight,
    dt_bias,
    a_log,
    skip_gain,
    out_weight,
    hidden_grad,
):
    layers, width, _ = in_weight.shape
    inner, states = a_log.shape[1], a_log.shape[2]
    rank = dtproj_weight.shape[1]
    taps = conv_weight.shape[2]
    seqs, own, _ = hidden_in.shape
    ndev = lax.axis_size(AXIS)
    me = lax.axis_index(AXIS)
    core = me % 2
    chip = me // 2
    rows = seqs * own
    assert layers == 2 and seqs == 2 and ndev % 2 == 0
    assert inner % CHUNK == 0 and inner // 128 <= states and rank + 2 * states <= XD

    pairs = [(i, i ^ 1) for i in range(ndev)]
    turn = []
    call = functools.partial(run, turn=turn)

    def to_runs(block):
        mine = lax.dynamic_index_in_dim(block, core, 0, keepdims=False)
        other = lax.dynamic_index_in_dim(block, 1 - core, 0, keepdims=False)
        came = lax.ppermute(other, AXIS, pairs)
        first = jnp.where(core == 0, mine, came)
        second = jnp.where(core == 0, came, mine)
        return jnp.concatenate([first, second], axis=0)

    def from_runs(mine, other):
        came = lax.ppermute(other, AXIS, pairs)
        first = jnp.where(core == 0, mine, came)
        second = jnp.where(core == 0, came, mine)
        return jnp.stack([first, second], axis=0)

    def done_by_now(array):
        array, turn[0] = lax.optimization_barrier((array, turn[0]))
        return array

    def not_before(*arrays):
        return lax.optimization_barrier(arrays + (turn[0],))[:-1]

    def from_before(block):
        return lax.ppermute(block, AXIS, [(i, i + 2) for i in range(ndev - 2)])

    def from_after(block):
        return lax.ppermute(block, AXIS, [(i + 2, i) for i in range(ndev - 2)])

    bits = (ndev // 2).bit_length() - 1
    assert 2 << bits == ndev and bits > 2
    rounds = []
    low = 0
    while low < bits:
        n = 2 if bits - low >= 2 else 1
        rounds.append((low, 1 << n))
        low += n

    def digit_of(r):
        low, group = rounds[r]
        return (chip >> low) & (group - 1)

    def digits_of(r):
        nxt = digit_of(r + 1) if r + 1 < len(rounds) else jnp.zeros_like(chip)
        return jnp.stack([digit_of(r), nxt]).astype(jnp.int32)

    def send(block, r, m, which):
        low, group = rounds[r]
        flip = (m << low) << 1
        route = [(i, i ^ flip) for i in range(ndev)]
        if which == "up":
            route = [(i, j) for i, j in route if j > i]
        if which == "down":
            route = [(i, j) for i, j in route if j < i]
        return lax.ppermute(block, AXIS, route)

    smem = pl.BlockSpec(memory_space=pltpu.SMEM)
    core_s = (core[None].astype(jnp.int32), smem)

    def swap(block):
        return lax.ppermute(block, AXIS, pairs)

    pay = shape((states, inner + EXTRA), BF16)

    kept = {}

    def exchange(payload, a2, mode, meanwhile=()):
        meanwhile = dict(enumerate(meanwhile))
        befores = [[] for _ in mode]
        sums = [[] for _ in mode]
        for r, (low, group) in enumerate(rounds[:-1]):
            received = [payload] + [send(payload, r, m, "all") for m in range(1, group)]
            kept["first"] = received[1:]
            if r in meanwhile:
                meanwhile[r]()
            final = r + 2 == len(rounds)
            split = len(mode) == 2 and final
            nextgroup = rounds[r + 1][1] if split else 0
            pays = (
                [pay] * (nextgroup - 1)
                if split
                else [shape((states * len(mode), inner + EXTRA), BF16)]
            )
            outs = call(
                functools.partial(k_join, group, nextgroup, mode),
                pays
                + [shape((states, inner), F32)] * len(mode)
                + [shape((1, inner), F32)] * len(mode),
                [(digits_of(r), smem)] + received + [a2],
                [
                    pltpu.VMEM((group, states, inner + EXTRA), F32),
                    pltpu.VMEM((group, 8, inner), F32),
                    pltpu.VMEM((states, inner + EXTRA), F32),
                ],
            )
            sent, outs = outs[: len(pays)], outs[len(pays) :]
            for i in range(len(mode)):
                befores[i].append(outs[i])
                sums[i].append(outs[len(mode) + i])
            payload = sent if split else sent[0]
        r = len(rounds) - 1
        if len(mode) == 2:
            last = [send(payload[m - 1], r, m, "all") for m in range(1, rounds[r][1])]
        else:
            way = "all"
            last = [send(payload, r, m, way) for m in range(1, rounds[r][1])]
        for step in sorted(meanwhile):
            if step >= r:
                meanwhile[step]()
        return last, sum(befores, []), sum(sums, []), digits_of(r)

    def row(array, l):
        return Row(array, l)

    def layer_of(array, l):
        return array, part((None,) + array.shape[1:], (l, 0, 0))

    def w_in(l, half):
        columns = slice(half * inner, (half + 1) * inner)
        return Late(in_weight, (l, slice(None), columns), (width, inner))

    def w_out(l):
        return Late(out_weight, (l,), (inner, width))

    def table_scratch():
        return [
            pltpu.VMEM((rows, XD), F32),
            pltpu.VMEM((rows * states, XD), BF16),
            pltpu.VMEM((rows * states, 256), F32),
        ]

    act = shape((rows, inner), F32)
    act_b = shape((rows, inner), BF16)
    res = shape((rows, width), F32)
    res_b = shape((rows, width), BF16)
    edge = shape((HALO, inner), F32)
    mm = 2 * rows * width * inner

    x0 = to_runs(hidden_in).astype(F32)

    normed = [None, None]
    xc = [None, None]
    halo = [None, None]
    z = [None, None]
    u = [None, None]
    xd = [None, None]
    v = [None, None]
    step = [None, None]

    normed[0], xc[0], tail = call(
        k_in, [res_b, act_b, edge], [x0, row(norm_gain, 0), in_weight[0, :, 0:inner]]
    )

    a_log, conv_weight, xproj_weight, dtproj_weight, hidden_grad = not_before(
        a_log, conv_weight, xproj_weight, dtproj_weight, hidden_grad
    )
    a2_all = -jnp.exp(jnp.swapaxes(a_log, 1, 2)) * LOG2E
    cw_all = jnp.swapaxes(conv_weight, 1, 2)
    xw_all = jnp.pad(xproj_weight, ((0, 0), (0, 0), (0, XD - xproj_weight.shape[2])))
    dw_all = jnp.pad(dtproj_weight, ((0, 0), (0, XD - rank), (0, 0)))
    grad_out = to_runs(hidden_grad)

    def gate(l):
        (z[l],) = call(k_gate, [act_b], [normed[l], w_in(l, 1)], cost=LONG)

    def before_scan(l, tail, dgated=None):
        halo[l] = from_before(tail)
        if l:
            gate(l)
        both = dgated is not None
        outs = call(
            functools.partial(k_local, rank, both),
            [
                act_b,
                shape((rows, XD), BF16),
                act,
                act,
                shape((states * (2 if both else 1), inner + EXTRA), BF16),
            ]
            + ([act] if both else []),
            [
                halo[l],
                xc[l],
                layer_of(cw_all, l),
                row(conv_bias, l),
                layer_of(xw_all, l),
                layer_of(dw_all, l),
                row(dt_bias, l),
                layer_of(a2_all, l),
            ]
            + ([dgated, z[l]] if both else []),
            [pltpu.VMEM((rows + HALO, inner), F32)]
            + [pltpu.VMEM((rows, inner), F32)]
            + table_scratch()
            + [pltpu.VMEM((states, inner), F32), pltpu.VMEM((states, inner + EXTRA), F32)],
            cost=LONG,
        )
        u[l], xd[l], v[l], step[l] = outs[:4]
        return outs[4:]

    def join_scratch():
        group = rounds[-1][1]
        return [
            pltpu.VMEM((group, states, inner), F32),
            pltpu.VMEM((group, 8, inner), F32),
        ]

    def piece(array, i):
        return array, part((rows, array.shape[1]), (i, 0))

    def mix(l, parts, extra, outs):
        final = l == layers - 1
        last, befores, sums, digits = parts
        befores, sums = befores[: len(rounds) - 1], sums[: len(rounds) - 1]
        return call(
            functools.partial(k_mix, rank, final, len(last), len(befores)),
            outs,
            [(digits, smem), core_s]
            + last
            + befores
            + sums
            + [layer_of(a2_all, l), u[l], step[l], xd[l], z[l], residual[l], row(skip_gain, l), w_out(l)]
            + extra,
            ([act_scratch, pltpu.VMEM((rows, width), F32)] if final else [])
            + [pltpu.VMEM((rows, inner), BF16)]
            + [act_scratch]
            + table_scratch()
            + join_scratch(),
            cost=LONG,
        )

    half_b = shape((rows, width), BF16)
    entry = shape((states, inner), F32)
    act_scratch = pltpu.VMEM((rows, inner), F32)
    residual = [x0, None]
    def shadow_00():
        gate(0)

    def shadow_0():
        (kept["dgated1"],) = call(k_dgated, [act], [grad_out, w_out(1)], cost=LONG)

    (payload,) = before_scan(0, tail)
    parts = exchange(payload, layer_of(a2_all, 0), "f", (shadow_00, shadow_0))
    dgated1 = kept["dgated1"]
    y0, x1, normed[1], xc[1], tail, gated_keep, sends, h0 = mix(
        0,
        parts,
        [row(norm_gain, 1), w_in(1, 0)],
        [act, res, res_b, act_b, edge, half_b, shape((2 * rows, width), BF16), entry],
    )
    residual[1] = x1
    came = swap(sends)
    n1_pair = (normed[1], piece(came, 1))
    gated0_pair = (gated_keep, piece(came, 0))
    n0_pair = (normed[0], swap(normed[0]))
    e1_pair = (grad_out, swap(grad_out))
    payload, dy1 = before_scan(1, tail, dgated1)
    parts = exchange(payload, layer_of(a2_all, 1), "fb")
    n_small = rank + 2 * states + rank + states + taps + 4
    small = shape((n_small, inner), F32)
    small_pad = -(-n_small // (BLOCKS * 2)) * BLOCKS * 2 if n_small % BLOCKS else n_small

    n_chunks = inner // CHUNK
    cuts = [(0, (n_chunks + 1) // 2 * CHUNK), ((n_chunks + 1) // 2 * CHUNK, n_chunks // 2 * CHUNK)]
    n_parts = len(cuts)
    assert all(first % lanes == 0 for first, lanes in cuts)

    def scan(l, i, dy, parts, h_in):
        lane0, lanes = cuts[i]
        last, befores, sums, digits = parts
        n_low = len(rounds) - 1
        cut = part((rows, lanes), (0, lane0 // lanes))
        cut_s = part((states, lanes), (0, lane0 // lanes))
        cut_a = part((None, states, lanes), (l, 0, lane0 // lanes))
        return call(
            functools.partial(k_scan, rank, lane0, len(last), n_low),
            [shape((rows, lanes), F32)] * 2 + [shape((states, lanes), F32), shape((rows, XD), F32)],
            [(digits, smem)]
            + last
            + befores[-n_low:]
            + sums[-n_low:]
            + [(a2_all, cut_a), (u[l], cut), (step[l], cut), (dy, cut), (h_in, cut_s), xd[l]],
            [pltpu.VMEM((rows, lanes), F32)]
            + table_scratch()
            + [
                pltpu.VMEM((rounds[-1][1], states, lanes), F32),
                pltpu.VMEM((rounds[-1][1], 8, lanes), F32),
            ]
            + [pltpu.VMEM((rows * states, 128), F32)] * 2
            + [pltpu.VMEM((rows * states, CHUNK), F32)] * 2
            + [pltpu.VMEM((states, lanes), F32)],
            cost=LONG,
        )

    def post(l, scans, dy):
        return call(
            functools.partial(k_post, rank, n_parts),
            [act, edge, small],
            [outs[k] for k in range(4) for outs in scans]
            + [
                u[l],
                v[l],
                step[l],
                xd[l],
                dy,
                halo[l],
                xc[l],
                layer_of(cw_all, l),
                row(conv_bias, l),
                layer_of(xw_all, l),
                layer_of(dw_all, l),
                row(skip_gain, l),
            ],
            [pltpu.VMEM((rows + HALO, inner), F32)],
            cost=LONG,
        )


    def over(block, flip):
        return lax.ppermute(block, AXIS, [(i, i ^ (flip << 1)) for i in range(ndev)])

    place_s = (chip[None].astype(jnp.int32), smem)

    def held(arrays, gate):
        if gate is None:
            return arrays
        return lax.optimization_barrier(tuple(arrays) + tuple(gate()))[: len(arrays)]

    def summed(matrices, smalls, aside=False, gates=(None, None, None)):
        ins = []
        each = width // BLOCKS
        for (a, a_came), (b, b_came) in matrices:
            ins += [a, a_came, b, b_came]
        r = each * len(matrices)
        if smalls is not None:
            ins += list(smalls)
            r += 16
        has_small = smalls is not None
        half = width // 2
        if ndev != 2 * BLOCKS:
            (mine,) = call(
                functools.partial(k_chip_sum, len(matrices), has_small),
                [shape((BLOCKS, r, width), F32)],
                ins,
                [pltpu.VMEM((BLOCKS, each, width), F32)],
            )
            empty = jnp.zeros((2,) + mine.shape, F32)
            total = lax.psum(lax.dynamic_update_index_in_dim(empty, mine, core, 0), AXIS)
            total = total.astype(BF16)
            for _ in range(3 if aside else 5):
                yield None
            if aside:
                yield jnp.swapaxes(total, 0, 1)
                return
            yield (
                lax.dynamic_index_in_dim(total, core, 0, keepdims=False),
                lax.dynamic_index_in_dim(total, 1 - core, 0, keepdims=False),
            )
            return
        n = BLOCKS // 2
        keep_a, keep_b, send_a, send_b = call(
            functools.partial(k_first, len(matrices), has_small),
            [shape((n, r, half), F32)] * 2 + [shape((n, r, half), BF16)] * 2,
            [place_s] + ins,
            [pltpu.VMEM((BLOCKS, each, width), F32)],
            cost=LONG,
        )
        send_a, send_b = held([send_a, send_b], gates[0])
        came_a, came_b = over(send_a, 1), over(send_b, 2)
        yield None
        n = BLOCKS // 4
        stay_a, stay_b, send_a, send_b = call(
            k_second,
            [shape((n, r, half), F32)] * 2 + [shape((n, r, half), BF16)] * 2,
            [place_s, keep_a, keep_b, came_a, came_b],
        )
        send_a, send_b = held([send_a, send_b], gates[1])
        came_a, came_b = over(send_a, 2), over(send_b, 1)
        yield None
        keep, *sends = call(
            k_third,
            [shape((r, width), F32)] + [shape((r, width), BF16)] * 3,
            [place_s, stay_a, stay_b, came_a, came_b],
        )
        sends = held(sends, gates[2])
        came = [over(send_m, 4 * (m + 1)) for m, send_m in enumerate(sends)]
        yield None
        (done,) = call(k_fourth, [shape((r, width), BF16)], [keep] + came)
        if aside:
            every = lax.all_gather(done, AXIS)
            yield every.reshape(BLOCKS, 2, r, width)
            return
        came = [over(done, 4 * m) for m in (1, 2, 3)]
        yield None
        left, right = call(k_stack, [shape((4, r, half), BF16)] * 2, [done] + came)
        left_y, right_x = over(left, 2), over(right, 1)
        lefts = [left, over(left, 1), left_y, over(left_y, 1)]
        rights = [right, right_x, over(right, 2), over(right_x, 2)]
        yield None
        (mine,) = call(
            k_chip, [shape((BLOCKS, r, width), BF16)], [place_s] + lefts + rights
        )
        yield mine, swap(mine)

    def sources(halves, i, per, each, place):
        if not isinstance(halves, tuple):
            spec = pl.BlockSpec((per, 2, each, width), lambda g: (place(g), 0, i, 0))
            return [halves], [spec]
        spec = pl.BlockSpec((per, each, width), lambda g: (place(g), i, 0))
        return list(halves), [spec, spec]

    def placed(halves, i, whole, block, index, split_rows, before):
        each = width // BLOCKS
        steps = 2
        anywhere = pl.BlockSpec(memory_space=pl.ANY)
        arrays, specs = sources(halves, i, BLOCKS // steps, each, lambda g: g)
        ins = [core_s[0]] + arrays + [turn[0]]
        specs = [smem] + specs + [anywhere]
        aliases = {}
        if before is not None:
            aliases = {len(ins): 0}
            ins.append(before)
            specs.append(anywhere)
        out, turn[0] = pl.pallas_call(
            functools.partial(k_place, len(arrays), split_rows),
            grid=(steps,),
            in_specs=specs,
            out_specs=[pl.BlockSpec(block, index), pl.BlockSpec((8, 128), lambda g: (0, 0))],
            out_shape=[whole, shape((8, 128), F32)],
            input_output_aliases=aliases,
            compiler_params=pltpu.CompilerParams(vmem_limit_bytes=58 * 1024 * 1024),
            cost_estimate=COST,
        )(*ins)
        return out

    g_out_shape = shape((layers, 2, width, width), F32)
    g_in_shape = shape((layers, width, 2 * inner), F32)
    several = width // 2
    out_block = (None, 2, several, width)
    in_block = (None, several, inner)

    def out_at(l):
        return lambda g: (l, 0, g, 0)

    def in_at(l, half):
        return lambda g: (l, g, half)

    def placed_small(layer_sums):
        each = width // BLOCKS
        ins, counts = [core_s], []
        for halves, i in layer_sums:
            arrays, specs = sources(halves, i * each // 16, BLOCKS, 16, lambda g: 0)
            ins += list(zip(arrays, specs))
            counts.append(len(arrays))
        n_x = rank + 2 * states
        return call(
            functools.partial(k_place_small, rank, taps, tuple(counts)),
            [
                shape((layers, width), F32),
                shape((layers, taps, inner), F32),
                shape((layers, inner), F32),
                shape((layers, n_x, inner), F32),
                shape((layers, rank, inner), F32),
                shape((layers, inner), F32),
                shape((layers, states, inner), F32),
                shape((layers, inner), F32),
            ],
            ins,
            [pltpu.VMEM((small_pad, inner), F32)],
            spare=58,
        )

    half_small = shape((small_pad, width), F32)

    hid_mine, hid_other, dz1, dz_keep, gated_keep, sends, h1 = mix(
        1,
        parts,
        [dgated1],
        [shape((own, width), BF16)] * 2
        + [act_b, half_b, half_b, shape((2 * rows, width), BF16), entry],
    )
    came = swap(sends)
    hidden_out = from_runs(hid_mine, hid_other)
    a_sum = summed(
        [((gated_keep, piece(came, 0)), e1_pair), (n1_pair, (dz_keep, piece(came, 1)))],
        None,
        True,
        (None, None, lambda: [after1]),
    )
    scans = [scan(1, 0, dy1, parts, h1)]
    next(a_sum)
    scans.append(scan(1, 1, dy1, parts, h1))
    hidden_out = done_by_now(hidden_out)
    next(a_sum)
    dconv1, head1, small1 = post(1, scans, dy1)
    after1 = from_after(head1)
    (dnz1,) = call(k_dnz, [res], [dz1, w_in(1, 1)], cost=LONG)
    next(a_sum)
    turn_back = functools.partial(
        call,
        functools.partial(k_turn, rank),
        [half_b, half_small, res, res_b, act, act_b, half_b]
        + [shape((4 * rows, width), BF16), res, pay],
        [
            core_s,
            small1,
            dconv1,
            after1,
            layer_of(cw_all, 1),
            dnz1,
            w_in(1, 0),
            x1,
            row(norm_gain, 1),
            grad_out,
            w_out(0),
            y0,
            z[0],
            step[0],
            xd[0],
            layer_of(a2_all, 0),
            w_in(0, 1),
        ],
        [
            pltpu.VMEM((n_small, inner), F32),
            pltpu.VMEM((rows, inner), BF16),
            pltpu.VMEM((rows + HALO, inner), F32),
        ]
        + table_scratch()
        + [pltpu.VMEM((states, inner), F32), pltpu.VMEM((states, inner + EXTRA), F32)],
        cost=LONG,
    )
    dxc_keep, small_keep, e1, de0, dy0, _, dz_keep, sends, dnz0, payload = turn_back()
    came = swap(sends)
    b_sum = summed(
        [
            (n1_pair, (dxc_keep, piece(came, 0))),
            (gated0_pair, (de0, piece(came, 2))),
            (n0_pair, (dz_keep, piece(came, 1))),
        ],
        (small_keep, piece(came, 3)),
        True,
        (lambda: kept["first"], None, None),
    )

    def shadow_1():
        next(b_sum)

    def shadow_2():
        kept["sum_a"] = next(a_sum)

    parts = exchange(payload, layer_of(a2_all, 0), "b", (shadow_1, shadow_2))
    sum_a = kept["sum_a"]
    scans = [scan(0, 0, dy0, parts, h0)]
    next(b_sum)
    scans.append(scan(0, 1, dy0, parts, h0))
    dconv0, head0, small0 = post(0, scans, dy0)
    after0 = from_after(head0)
    next(b_sum)
    dxc_keep, small_keep, sends, e0_mine, e0_other = call(
        k_end,
        [half_b, half_small, shape((2 * rows, width), BF16)] + [shape((own, width), BF16)] * 2,
        [
            core_s,
            small0,
            dconv0,
            after0,
            layer_of(cw_all, 0),
            dnz0,
            w_in(0, 0),
            x0,
            row(norm_gain, 0),
            e1,
        ],
        [
            pltpu.VMEM((n_small, inner), F32),
            pltpu.VMEM((rows, inner), BF16),
            pltpu.VMEM((rows + HALO, inner), F32),
            pltpu.VMEM((rows, width), F32),
        ],
        cost=LONG,
    )
    came = swap(sends)
    c_sum = summed(
        [(n0_pair, (dxc_keep, piece(came, 0)))], (small_keep, piece(came, 1))
    )
    sum_b = next(b_sum)
    next(c_sum)
    g_out = placed(sum_a, 0, g_out_shape, out_block, out_at(1), True, None)
    input_grad = done_by_now(from_runs(e0_mine, e0_other))
    next(c_sum)
    next(c_sum)
    g_in = placed(sum_a, 1, g_in_shape, in_block, in_at(1, 1), False, None)
    next(c_sum)
    next(c_sum)
    sum_c = next(c_sum)
    g_in = placed(sum_c, 0, g_in_shape, in_block, in_at(0, 0), False, g_in)
    g_in = placed(sum_b, 0, g_in_shape, in_block, in_at(1, 0), False, g_in)
    g_out = placed(sum_b, 1, g_out_shape, out_block, out_at(0), True, g_out)
    g_in = placed(sum_b, 2, g_in_shape, in_block, in_at(0, 1), False, g_in)
    g_norm, g_cw, g_cb, g_xw, g_dw, g_db, g_al, g_sk = placed_small([(sum_c, 1), (sum_b, 3)])
    return (
        hidden_out,
        input_grad,
        g_norm,
        g_in,
        jnp.swapaxes(g_cw, 1, 2),
        g_cb,
        jnp.swapaxes(g_xw, 1, 2),
        g_dw,
        g_db,
        jnp.swapaxes(g_al, 1, 2),
        g_sk,
        g_out.reshape(layers, inner, width),
    )


def solution(mesh):
    split = P(None, AXIS, None)
    return jax.shard_map(
        shards,
        mesh=mesh,
        in_specs=(split,) + (P(),) * 10 + (split,),
        out_specs=(split, split) + (P(),) * 10,
        check_vma=False,
    )
```

```python
import functools
import math

import jax
import jax.numpy as jnp
from jax import lax
from jax.experimental import pallas as pl
from jax.experimental.pallas import tpu as pltpu
from jax.sharding import PartitionSpec as P

BF16 = jnp.bfloat16
F32 = jnp.float32
LOG2E = 1.4426950408889634
LN2 = 0.6931471805599453
AXIS = "seq"
XD = 128
EXTRA = 256
CHUNK = 512
UNROLL = 8
HALO = 8
COST = pl.CostEstimate(flops=1, bytes_accessed=1, transcendentals=0)
LONG = pl.CostEstimate(flops=1, bytes_accessed=10**8, transcendentals=0)
SPARE = 4
BLOCKS = 16


def full(array):
    nd = len(array.shape)
    return pl.BlockSpec(array.shape, lambda i, nd=nd: (0,) * nd)


def part(shape, index):
    return pl.BlockSpec(shape, lambda i, index=index: index)


def room(specs, dtypes, out_specs, out_dtypes, scratch, spare):
    total = spare << 20
    for spec, dtype in list(zip(specs, dtypes)) + list(zip(out_specs, out_dtypes)):
        if spec.block_shape is not None:
            total += math.prod(d or 1 for d in spec.block_shape) * jnp.dtype(dtype).itemsize
    for item in scratch:
        if not hasattr(item, "shape"):
            continue
        total += math.prod(item.shape) * jnp.dtype(item.dtype).itemsize
    return min(total, 58 << 20)


class Late:
    def __init__(self, array, index, dims):
        self.array, self.index, self.dims = array, index, dims


class Fetched:
    def __init__(self, source, target, sem):
        self.copy, self.ref = pltpu.make_async_copy(source, target, sem), target
        self.copy.start()

    def __getitem__(self, where):
        if self.copy is not None:
            self.copy.wait()
            self.copy = None
        return self.ref[where]


class Row:
    def __init__(self, array, index):
        self.array, self.index = array, index


def run(kernel, outs, ins, scratch=(), turn=None, cost=COST, spare=SPARE):
    out_specs = [o[1] if isinstance(o, tuple) else full(o) for o in outs]
    outs = [o[0] if isinstance(o, tuple) else o for o in outs]
    arrays, specs, picks, late = [], [], {}, {}
    scratch = list(scratch)
    for item in ins:
        if isinstance(item, Late):
            late[len(arrays)] = item.index
            scratch += [pltpu.VMEM(item.dims, item.array.dtype), pltpu.SemaphoreType.DMA]
            item = (item.array, pl.BlockSpec(memory_space=pltpu.HBM))
        if isinstance(item, Row):
            picks[len(arrays)] = item.index
            item = item.array
        if isinstance(item, tuple):
            arrays.append(item[0])
            specs.append(item[1])
        else:
            arrays.append(item)
            specs.append(full(item))
    n = len(arrays)
    limit = room(specs, [a.dtype for a in arrays], out_specs, [o.dtype for o in outs], scratch, spare)
    if turn:
        arrays.append(turn[0])
        specs.append(pl.BlockSpec(memory_space=pl.ANY))
    after = len(arrays)

    def body(*refs):
        given = list(refs[:n])
        for k, index in picks.items():
            given[k] = given[k].at[index : index + 1, :]
        rest, buffers = refs[after:], ()
        if late:
            rest, buffers = rest[: -2 * len(late)], rest[-2 * len(late) :]
        for i, (k, index) in enumerate(late.items()):
            given[k] = Fetched(given[k].at[index], buffers[2 * i], buffers[2 * i + 1])
        kernel(*given, *rest)

    results = pl.pallas_call(
        body,
        grid=(1,),
        in_specs=specs,
        out_specs=out_specs,
        out_shape=outs,
        scratch_shapes=list(scratch),
        compiler_params=pltpu.CompilerParams(vmem_limit_bytes=limit),
        cost_estimate=cost,
    )(*arrays)
    if turn is not None:
        turn[:] = [results[-1]]
    return results


def shape(dims, dtype):
    return jax.ShapeDtypeStruct(dims, dtype)


def dot(a, b):
    return jnp.dot(a, b, preferred_element_type=F32)


def dot_t(a, b):
    return lax.dot_general(a, b, (((1,), (1,)), ((), ())), preferred_element_type=F32)


def dot_rows(a, b):
    return lax.dot_general(a, b, (((0,), (0,)), ((), ())), preferred_element_type=F32)


def sigmoid(v):
    return 1.0 / (1.0 + jnp.exp(-v))


def softplus(v):
    return jnp.maximum(v, 0.0) + jnp.log1p(jnp.exp(-jnp.abs(v)))


def slope(v):
    s = sigmoid(v)
    return s * (1.0 + v * (1.0 - s))


def wide(block, lanes):
    return jnp.concatenate([block] * (lanes // block.shape[1]), axis=1)


def rows_of_sums(parts):
    row = lax.broadcasted_iota(jnp.int32, parts[0].shape, 0)
    m4, m2, m1 = row < 4, (row & 2) == 0, (row & 1) == 0
    q = []
    for i in range(4):
        first = jnp.where(m4, parts[i], parts[i + 4])
        other = jnp.where(m4, parts[i + 4], parts[i])
        q.append(first + pltpu.roll(other, 4, 0))
    s = []
    for i in range(2):
        s.append(
            jnp.where(
                m2, q[i] + pltpu.roll(q[i], 6, 0), q[i + 2] + pltpu.roll(q[i + 2], 2, 0)
            )
        )
    return jnp.where(m1, s[0] + pltpu.roll(s[0], 7, 0), s[1] + pltpu.roll(s[1], 1, 0))


def fold(block):
    out = block[0:8]
    for k in range(8, block.shape[0], 8):
        out = out + block[k : k + 8]
    return out


def fold_lanes(block):
    out = block[:, 0:128]
    for k in range(128, block.shape[1], 128):
        out = out + block[:, k : k + 128]
    return out


def normed_of(x, gain):
    rinv = lax.rsqrt(jnp.mean(x * x, axis=-1, keepdims=True) + 1e-05)
    return (x * rinv * gain).astype(BF16)


def fill_table(xdf_ref, lhs_ref, bc_ref, rank, states):
    rows = xdf_ref.shape[0]
    n_i = lax.broadcasted_iota(jnp.int32, (states, XD), 0)
    lane = lax.broadcasted_iota(jnp.int32, (states, XD), 1)
    mask = ((lane == rank + n_i) | (lane == rank + states + n_i)).astype(F32)

    def body(i, carry):
        for j in range(UNROLL):
            t = i * UNROLL + j
            line = xdf_ref[pl.ds(t, 1), :]
            lhs_ref[pl.ds(pl.multiple_of(t * states, states), states), :] = (
                line * mask
            ).astype(BF16)
        return carry

    lax.fori_loop(0, rows // UNROLL, body, 0)
    k_i = lax.broadcasted_iota(jnp.int32, (XD, 256), 0)
    c_i = lax.broadcasted_iota(jnp.int32, (XD, 256), 1)
    low = rank + jnp.where(c_i >= 128, states, 0)
    pick = ((k_i >= low) & (k_i < low + states)).astype(BF16)
    bc_ref[...] = dot(lhs_ref[...], pick)


def state_rows(t, states):
    return pl.ds(pl.multiple_of(t * states, states), states)


def scan_ends(dt_ref, dtu_ref, bc_ref, a2_ref, end_ref):
    rows, inner = dt_ref.shape
    states = a2_ref.shape[0]

    def chunk(c, carry):
        lanes = pl.ds(pl.multiple_of(c * CHUNK, CHUNK), CHUNK)
        a2 = a2_ref[:, lanes]

        def body(i, h):
            for j in range(UNROLL):
                t = i * UNROLL + j
                a = jnp.exp2(dt_ref[pl.ds(t, 1), lanes] * a2)
                b = wide(bc_ref[state_rows(t, states), 0:128], CHUNK)
                h = a * h + dtu_ref[pl.ds(t, 1), lanes] * b
            return h

        end_ref[:, lanes] = lax.fori_loop(
            0, rows // UNROLL, body, jnp.zeros((states, CHUNK), F32)
        )
        return carry

    lax.fori_loop(0, inner // CHUNK, chunk, 0)


def scan_back_ends(dt_ref, dy_ref, bc_ref, a2_ref, end_ref):
    rows, inner = dt_ref.shape
    states = a2_ref.shape[0]

    def chunk(c, carry):
        lanes = pl.ds(pl.multiple_of(c * CHUNK, CHUNK), CHUNK)
        a2 = a2_ref[:, lanes]

        def body(i, back):
            for j in range(UNROLL):
                t = rows - 1 - (i * UNROLL + j)
                a = jnp.exp2(dt_ref[pl.ds(t, 1), lanes] * a2)
                c_row = wide(bc_ref[state_rows(t, states), 128:256], CHUNK)
                back = a * (dy_ref[pl.ds(t, 1), lanes] * c_row + back)
            return back

        end_ref[:, lanes] = lax.fori_loop(
            0, rows // UNROLL, body, jnp.zeros((states, CHUNK), F32)
        )
        return carry

    lax.fori_loop(0, inner // CHUNK, chunk, 0)


def scan_forward(dt_ref, dtu_ref, bc_ref, a2_ref, h_in_ref, y_ref):
    rows, inner = dt_ref.shape
    states = a2_ref.shape[0]

    def chunk(c, carry):
        lanes = pl.ds(pl.multiple_of(c * CHUNK, CHUNK), CHUNK)
        a2 = a2_ref[:, lanes]

        def body(i, h):
            parts = []
            for j in range(UNROLL):
                t = i * UNROLL + j
                a = jnp.exp2(dt_ref[pl.ds(t, 1), lanes] * a2)
                both = bc_ref[state_rows(t, states), :]
                h = a * h + dtu_ref[pl.ds(t, 1), lanes] * wide(both[:, 0:128], CHUNK)
                parts.append(fold(h * wide(both[:, 128:256], CHUNK)))
            y_ref[pl.ds(pl.multiple_of(i * UNROLL, UNROLL), UNROLL), lanes] = rows_of_sums(
                parts
            )
            return h

        lax.fori_loop(0, rows // UNROLL, body, h_in_ref[:, lanes])
        return carry

    lax.fori_loop(0, inner // CHUNK, chunk, 0)


def scan_both(
    dt_ref,
    dtu_ref,
    dy_ref,
    bc_ref,
    a2_ref,
    h_in_ref,
    g_in_ref,
    sgb_ref,
    sqa_ref,
    rate_ref,
    db_ref,
    dc_ref,
    a_s,
    ah_s,
):
    rows, inner = dt_ref.shape
    states = a2_ref.shape[0]
    db_ref[...] = jnp.zeros(db_ref.shape, F32)
    dc_ref[...] = jnp.zeros(dc_ref.shape, F32)

    def chunk(c, carry):
        lanes = pl.ds(pl.multiple_of(c * CHUNK, CHUNK), CHUNK)
        a2 = a2_ref[:, lanes]

        def ahead(i, h):
            for j in range(UNROLL):
                t = i * UNROLL + j
                at = state_rows(t, states)
                a = jnp.exp2(dt_ref[pl.ds(t, 1), lanes] * a2)
                b_row = wide(bc_ref[at, 0:128], CHUNK)
                ah = a * h
                a_s[at, :] = a
                ah_s[at, :] = ah
                h = ah + dtu_ref[pl.ds(t, 1), lanes] * b_row
                dc_ref[at, :] += fold_lanes(h * dy_ref[pl.ds(t, 1), lanes])
            return h

        lax.fori_loop(0, rows // UNROLL, ahead, h_in_ref[:, lanes])

        def retreat(i, carried):
            back, rate = carried
            block = rows // UNROLL - 1 - i
            gbs, qas = [None] * UNROLL, [None] * UNROLL
            for j in reversed(range(UNROLL)):
                t = block * UNROLL + j
                at = state_rows(t, states)
                both = bc_ref[at, :]
                g = dy_ref[pl.ds(t, 1), lanes] * wide(both[:, 128:256], CHUNK) + back
                q = g * ah_s[at, :]
                gbs[j] = fold(g * wide(both[:, 0:128], CHUNK))
                qas[j] = fold(q * a2)
                rate = rate + q * dt_ref[pl.ds(t, 1), lanes]
                db_ref[at, :] += fold_lanes(g * dtu_ref[pl.ds(t, 1), lanes])
                back = a_s[at, :] * g
            here = pl.ds(pl.multiple_of(block * UNROLL, UNROLL), UNROLL)
            sgb_ref[here, lanes] = rows_of_sums(gbs)
            sqa_ref[here, lanes] = rows_of_sums(qas)
            return back, rate

        _, rate = lax.fori_loop(
            0,
            rows // UNROLL,
            retreat,
            (g_in_ref[:, lanes], jnp.zeros((states, CHUNK), F32)),
        )
        rate_ref[:, lanes] = rate
        return carry

    lax.fori_loop(0, inner // CHUNK, chunk, 0)


def packed(state, total, wide_s):
    inner = total.shape[1]
    high = total.astype(BF16).astype(F32)
    rest = total - high
    wide_s[:, 0:inner] = state
    wide_s[:, inner:] = jnp.zeros((state.shape[0], EXTRA), F32)
    for k in range(inner // 128):
        wide_s[k : k + 1, inner : inner + 128] = high[:, k * 128 : (k + 1) * 128]
        wide_s[k : k + 1, inner + 128 : inner + 256] = rest[:, k * 128 : (k + 1) * 128]
    return wide_s[...].astype(BF16)


def unpack_total(wide_ref, m, total_ref, inner):
    for k in range(inner // 128):
        total_ref[m, 0:1, k * 128 : (k + 1) * 128] = (
            wide_ref[m, k : k + 1, inner : inner + 128]
            + wide_ref[m, k : k + 1, inner + 128 : inner + 256]
        )


def join_runs(states_ref, totals_ref, a2, digit, group, backward):
    inner = a2.shape[1]
    before = jnp.zeros(a2.shape, F32)
    entire = jnp.zeros(a2.shape, F32)
    sum_before = jnp.zeros((1, inner), F32)
    sum_entire = jnp.zeros((1, inner), F32)
    order = reversed(range(group)) if backward else range(group)
    for p in order:
        m = jnp.bitwise_xor(digit, p)
        state = states_ref[m, :, 0:inner]
        total = totals_ref[m, 0:1, :]
        through = jnp.exp2(total * a2)
        counts = (p > digit) if backward else (p < digit)
        before = jnp.where(counts, through * before + state, before)
        sum_before = jnp.where(counts, sum_before + total, sum_before)
        entire = through * entire + state
        sum_entire = sum_entire + total
    return before, sum_before, entire, sum_entire


def k_in(x_ref, g_ref, w_ref, n_ref, xc_ref, tail_ref):
    normed = normed_of(x_ref[...], g_ref[...])
    n_ref[...] = normed
    xc = dot(normed, w_ref[...]).astype(BF16)
    xc_ref[...] = xc
    tail_ref[...] = xc.astype(F32)[xc.shape[0] - HALO :, :]


def k_gate(n_ref, w_ref, z_ref):
    z_ref[...] = dot(n_ref[...], w_ref[...]).astype(BF16)


def k_dgated(e_ref, w_ref, out_ref):
    out_ref[...] = dot_t(e_ref[...], w_ref[...])


def conv_of(ext_s, halo_ref, xc_ref, cw_ref, cb_ref):
    rows = xc_ref.shape[0]
    taps = cw_ref.shape[0]
    ext_s[0:HALO, :] = halo_ref[...]
    ext_s[HALO:, :] = xc_ref[...].astype(F32)
    out = cb_ref[...]
    for k in range(taps):
        first = HALO - (taps - 1) + k
        out = out + cw_ref[k : k + 1, :] * ext_s[first : first + rows, :]
    return out


def k_local(
    rank, both, *refs
):
    refs = list(refs)
    halo, xc, cw, cb, xw, dw, db, a2 = refs[:8]
    refs = refs[8:]
    if both:
        dgated, z = refs[:2]
        refs = refs[2:]
    u_ref, xd_ref, v_ref, dt_s, pay_ref = refs[:5]
    refs = refs[5:]
    if both:
        dy_ref = refs[0]
        refs = refs[1:]
    ext_s, dtu_s, xdf_s, lhs_s, bc_s, end_s, wide_s = refs
    states = a2.shape[0]
    conv = conv_of(ext_s, halo, xc, cw, cb)
    u = (conv * sigmoid(conv)).astype(BF16)
    u_ref[...] = u
    xd = dot(u, xw[...]).astype(BF16)
    xd_ref[...] = xd
    xdf_s[...] = xd.astype(F32)
    v = dot(xd, dw[...]) + db[...]
    v_ref[...] = v
    dt = softplus(v)
    dt_s[...] = dt
    dtu_s[...] = dt * u.astype(F32)
    total = jnp.sum(dt, axis=0, keepdims=True)
    fill_table(xdf_s, lhs_s, bc_s, rank, states)
    scan_ends(dt_s, dtu_s, bc_s, a2, end_s)
    pay_ref[0:states, :] = packed(end_s[...], total, wide_s)
    if both:
        zf = z[...].astype(F32)
        dy_ref[...] = dgated[...] * (zf * sigmoid(zf))
        scan_back_ends(dt_s, dy_ref, bc_s, a2, end_s)
        pay_ref[states:, :] = packed(end_s[...], total, wide_s)


def k_join(group, nextgroup, mode, digits, *refs):
    refs = list(refs)
    received, refs = refs[:group], refs[group:]
    a2_ref, refs = refs[0], refs[1:]
    kinds = list(mode)
    n_pay = (nextgroup - 1) if (len(kinds) == 2 and nextgroup) else 1
    pays, refs = refs[:n_pay], refs[n_pay:]
    befores, refs = refs[: len(kinds)], refs[len(kinds) :]
    sums, refs = refs[: len(kinds)], refs[len(kinds) :]
    states_s, totals_s, wide_s = refs
    states, inner = a2_ref.shape
    digit = digits[0]
    nextdigit = digits[1]
    out = []
    for i in range(len(kinds)):
        for m in range(group):
            states_s[m] = received[m][i * states : (i + 1) * states, :].astype(F32)
            if i == 0:
                unpack_total(states_s, m, totals_s, inner)
        before, sum_before, entire, sum_entire = join_runs(
            states_s, totals_s, a2_ref[...], digit, group, kinds[i] == "b"
        )
        befores[i][...] = before
        sums[i][...] = sum_before
        out.append(packed(entire, sum_entire, wide_s))
    if len(kinds) == 2 and nextgroup:
        for m in range(1, nextgroup):
            ahead = jnp.bitwise_xor(nextdigit, m) > nextdigit
            pays[m - 1][...] = jnp.where(ahead, out[0].astype(F32), out[1].astype(F32)).astype(
                BF16
            )
    else:
        for i in range(len(kinds)):
            pays[0][i * states : (i + 1) * states, :] = out[i]


def entering(received, a2_ref, digit, befores, sums, states_s, totals_s, backward, lane0=0):
    lanes = a2_ref.shape[1]
    inner = received[0].shape[1] - EXTRA
    here = slice(lane0, lane0 + lanes)
    group = len(received) + 1
    states_s[0] = jnp.zeros(states_s.shape[1:], F32)
    totals_s[0] = jnp.zeros(totals_s.shape[1:], F32)
    for m in range(1, group):
        states_s[m] = received[m - 1][:, here].astype(F32)
        sums_m = received[m - 1][:, inner:].astype(F32)
        for k in range(lanes // 128):
            row = lane0 // 128 + k
            totals_s[m, 0:1, k * 128 : (k + 1) * 128] = (
                sums_m[row : row + 1, 0:128] + sums_m[row : row + 1, 128:256]
            )
    value, _, _, _ = join_runs(states_s, totals_s, a2_ref[...], digit, group, backward)
    for before, total in reversed(list(zip(befores, sums))):
        value = jnp.exp2(total[:, here] * a2_ref[...]) * value + before[:, here]
    return value


def k_mix(rank, last, n_recv, n_low, digits, core, *refs):
    refs = list(refs)
    received, refs = refs[:n_recv], refs[n_recv:]
    befores, refs = refs[:n_low], refs[n_low:]
    sums, refs = refs[:n_low], refs[n_low:]
    a2, u_ref, dt_ref, xd_ref, z_ref, x_ref, sk_ref, ow_ref = refs[:8]
    refs = refs[8:]
    if last:
        dgated_ref, hid_mine, hid_other, dz_ref, dz_keep, gated_keep, sends, h_in_ref = refs[:8]
        y_ref, hid_s, refs = refs[8], refs[9], refs[10:]
    else:
        g_ref, iw_ref, y_ref, x1_ref, n_ref, xc_ref, tail_ref = refs[:7]
        gated_keep, sends, h_in_ref = refs[7:10]
        refs = refs[10:]
    gated_s, dtu_s, xdf_s, lhs_s, bc_s, states_s, totals_s = refs
    h_in_ref[...] = entering(received, a2, digits[0], befores, sums, states_s, totals_s, False)
    uf = u_ref[...].astype(F32)
    dtu_s[...] = dt_ref[...] * uf
    xdf_s[...] = xd_ref[...].astype(F32)
    fill_table(xdf_s, lhs_s, bc_s, rank, a2.shape[0])
    scan_forward(dt_ref, dtu_s, bc_s, a2, h_in_ref, y_ref)
    y = y_ref[...] + sk_ref[...] * u_ref[...].astype(F32)
    zf = z_ref[...].astype(F32)
    s = sigmoid(zf)
    gated = (y * (zf * s)).astype(BF16)
    gated_s[...] = gated
    rows = gated.shape[0]
    gated_keep[...] = lane_half(gated_s, core[0])
    sends[0:rows, :] = lane_half(gated_s, 1 - core[0])
    x1 = x_ref[...] + dot(gated, ow_ref[...])
    if last:
        dz_ref[...] = (dgated_ref[...] * y * (s * (1.0 + zf * (1.0 - s)))).astype(BF16)
        dz_keep[...] = lane_half(dz_ref, core[0])
        sends[rows:, :] = lane_half(dz_ref, 1 - core[0])
        hid_s[...] = x1
        hid_mine[...] = row_half(hid_s, core[0]).astype(BF16)
        hid_other[...] = row_half(hid_s, 1 - core[0]).astype(BF16)
    else:
        y_ref[...] = y
        x1_ref[...] = x1
        normed = normed_of(x1, g_ref[...])
        n_ref[...] = normed
        sends[rows:, :] = normed
        xc = dot(normed, iw_ref[...]).astype(BF16)
        xc_ref[...] = xc
        tail_ref[...] = xc.astype(F32)[xc.shape[0] - HALO :, :]


def k_scan(rank, lane0, n_recv, n_low, digits, *refs):
    refs = list(refs)
    received, refs = refs[:n_recv], refs[n_recv:]
    befores, refs = refs[:n_low], refs[n_low:]
    sums, refs = refs[:n_low], refs[n_low:]
    a2, u_ref, dt_ref, dy_ref, h_in_ref, xd_ref = refs[:6]
    sgb_ref, sqa_ref, rate_ref, dbc_ref = refs[6:10]
    dtu_s, xdf_s, lhs_s, bc_s, states_s, totals_s, db_s, dc_s, a_s, ah_s, g_s = refs[10:]
    states = a2.shape[0]
    rows = u_ref.shape[0]
    g_s[...] = entering(
        received, a2, digits[0], befores, sums, states_s, totals_s, True, lane0
    )
    dtu_s[...] = dt_ref[...] * u_ref[...].astype(F32)
    xdf_s[...] = xd_ref[...].astype(F32)
    fill_table(xdf_s, lhs_s, bc_s, rank, states)
    scan_both(
        dt_ref, dtu_s, dy_ref, bc_s, a2, h_in_ref, g_s, sgb_ref, sqa_ref, rate_ref, db_s, dc_s, a_s, ah_s
    )
    rate_ref[...] = rate_ref[...] * (a2[...] * LN2)

    ones = jnp.ones((128, 128), BF16)

    def lane_sums(block):
        high = block.astype(BF16)
        rest = (block - high.astype(F32)).astype(BF16)
        return dot(high, ones) + dot(rest, ones)

    n_i = lax.broadcasted_iota(jnp.int32, (states, XD), 0)
    lane = lax.broadcasted_iota(jnp.int32, (states, XD), 1)
    mask_b = (lane == rank + n_i).astype(F32)
    mask_c = (lane == rank + states + n_i).astype(F32)
    db_s[...] = lane_sums(db_s[...])
    dc_s[...] = lane_sums(dc_s[...])

    def gather(i, carry):
        parts = []
        for j in range(UNROLL):
            at = state_rows(i * UNROLL + j, states)
            parts.append(fold(db_s[at, :] * mask_b + dc_s[at, :] * mask_c))
        dbc_ref[pl.ds(pl.multiple_of(i * UNROLL, UNROLL), UNROLL), :] = rows_of_sums(parts)
        return carry

    lax.fori_loop(0, rows // UNROLL, gather, 0)


def k_post(rank, n_parts, *refs):
    refs = list(refs)
    sgbs, refs = refs[:n_parts], refs[n_parts:]
    sqas, refs = refs[:n_parts], refs[n_parts:]
    rates, refs = refs[:n_parts], refs[n_parts:]
    dbcs, refs = refs[:n_parts], refs[n_parts:]
    u_ref, v_ref, dt_ref, xd_ref, dy_ref, halo, xc, cw, cb, xw, dw, sk_ref = refs[:12]
    dconv_ref, head_ref, small_ref, ext_s = refs[12:]
    states = rates[0].shape[0]
    rows, inner = u_ref.shape
    sgb = jnp.concatenate([ref[...] for ref in sgbs], axis=1)
    sqa = jnp.concatenate([ref[...] for ref in sqas], axis=1)
    dbc = dbcs[0][...]
    for ref in dbcs[1:]:
        dbc = dbc + ref[...]
    u = u_ref[...]
    uf = u.astype(F32)
    dy = dy_ref[...]
    v = v_ref[...]
    dpre = (LN2 * sqa + uf * sgb) * sigmoid(v)
    dpl = dpre.astype(BF16)
    dxd = (dot_t(dpl, dw[...]) + dbc).astype(BF16)
    du = dt_ref[...] * sgb + sk_ref[...] * dy + dot_t(dxd, xw[...])
    conv = conv_of(ext_s, halo, xc, cw, cb)
    dconv = du * slope(conv)
    dconv_ref[...] = dconv
    head_ref[...] = dconv[0:HALO, :]
    taps = cw.shape[0]
    width = rank + 2 * states
    g_x = dot_rows(dxd, u)
    g_dt = dot_rows(xd_ref[...], dpl)
    at = 0
    small_ref[at : at + width, :] = g_x[0:width]
    at += width
    small_ref[at : at + rank, :] = g_dt[0:rank]
    at += rank
    small_ref[at : at + states, :] = jnp.concatenate([ref[...] for ref in rates], axis=1)
    at += states
    for k in range(taps):
        first = HALO - (taps - 1) + k
        small_ref[at : at + 1, :] = jnp.sum(
            dconv * ext_s[first : first + rows, :], axis=0, keepdims=True
        )
        at += 1
    small_ref[at : at + 1, :] = jnp.sum(dconv, axis=0, keepdims=True)
    small_ref[at + 1 : at + 2, :] = jnp.sum(dpre, axis=0, keepdims=True)
    small_ref[at + 2 : at + 3, :] = jnp.sum(dy * uf, axis=0, keepdims=True)
    small_ref[at + 3 : at + 4, :] = jnp.zeros((1, inner), F32)


def row_half(ref, which):
    half = ref.shape[0] // 2
    return ref[pl.ds(pl.multiple_of(which * half, 16), half), :]


def lane_half(ref, which):
    half = ref.shape[1] // 2
    return ref[:, pl.ds(pl.multiple_of(which * half, 128), half)]


def conv_back(dce_s, dconv_ref, next_ref, cw_ref):
    rows = dconv_ref.shape[0]
    taps = cw_ref.shape[0]
    dce_s[0:rows, :] = dconv_ref[...]
    dce_s[rows:, :] = next_ref[...]
    out = cw_ref[taps - 1 : taps, :] * dce_s[0:rows, :]
    for k in range(taps - 1):
        first = taps - 1 - k
        out = out + cw_ref[k : k + 1, :] * dce_s[first : first + rows, :]
    return out.astype(BF16)


def norm_back(x, gain, e, dn):
    rinv = lax.rsqrt(jnp.mean(x * x, axis=-1, keepdims=True) + 1e-05)
    xhat = x * rinv
    dhat = dn * gain
    g_norm = jnp.sum(dn * xhat, axis=0, keepdims=True)
    return e + rinv * (dhat - xhat * jnp.mean(dhat * xhat, axis=-1, keepdims=True)), g_norm


def small_out(core, small_ref, g_norm, keep_ref, sends, at):
    rows, inner = small_ref.shape
    width = g_norm.shape[1]
    small_ref[rows - 1 : rows, 0:width] = g_norm
    pad = keep_ref.shape[0] - rows
    for which, ref, first in ((core[0], keep_ref, 0), (1 - core[0], sends, at)):
        block = lane_half(small_ref, which)
        block = jnp.concatenate([block, jnp.zeros((pad, block.shape[1]), F32)], axis=0)
        ref[first : first + rows + pad, :] = block.astype(ref.dtype)
    sends[at + rows + pad :, :] = jnp.zeros((sends.shape[0] - at - rows - pad, inner // 2), BF16)


def k_turn(
    rank,
    core,
    small_ref,
    dconv_ref,
    next_ref,
    cw_ref,
    dnz_ref,
    iw_ref,
    x_ref,
    g_ref,
    e_ref,
    ow_ref,
    y_ref,
    z_ref,
    dt_ref,
    xd_ref,
    a2,
    iz_ref,
    dxc_keep,
    small_keep,
    e1_ref,
    de_ref,
    dy_ref,
    dz_ref,
    dz_keep,
    sends,
    dnz0_ref,
    pay_ref,
    small_s,
    dxc_s,
    dce_s,
    xdf_s,
    lhs_s,
    bc_s,
    end_s,
    wide_s,
):
    dxc = conv_back(dce_s, dconv_ref, next_ref, cw_ref)
    rows = dxc.shape[0]
    dxc_s[...] = dxc
    dxc_keep[...] = lane_half(dxc_s, core[0])
    sends[0:rows, :] = lane_half(dxc_s, 1 - core[0])
    dn = dnz_ref[...] + dot_t(dxc, iw_ref[...])
    e1, g_norm = norm_back(x_ref[...], g_ref[...], e_ref[...].astype(F32), dn)
    small_s[...] = small_ref[...]
    small_out(core, small_s, g_norm, small_keep, sends, 3 * rows)
    e1_ref[...] = e1
    de = e1.astype(BF16)
    de_ref[...] = de
    sends[2 * rows : 3 * rows, :] = de
    dgated = dot_t(de, ow_ref[...])
    zf = z_ref[...].astype(F32)
    s = sigmoid(zf)
    dy_ref[...] = dgated * (zf * s)
    dz_ref[...] = (dgated * y_ref[...] * (s * (1.0 + zf * (1.0 - s)))).astype(BF16)
    dz_keep[...] = lane_half(dz_ref, core[0])
    sends[rows : 2 * rows, :] = lane_half(dz_ref, 1 - core[0])
    dnz0_ref[...] = dot_t(dz_ref[...], iz_ref[...])
    states = a2.shape[0]
    total = jnp.sum(dt_ref[...], axis=0, keepdims=True)
    xdf_s[...] = xd_ref[...].astype(F32)
    fill_table(xdf_s, lhs_s, bc_s, rank, states)
    scan_back_ends(dt_ref, dy_ref, bc_s, a2, end_s)
    pay_ref[...] = packed(end_s[...], total, wide_s)


def k_end(
    core,
    small_ref,
    dconv_ref,
    next_ref,
    cw_ref,
    dnz_ref,
    iw_ref,
    x_ref,
    g_ref,
    e_ref,
    dxc_keep,
    small_keep,
    sends,
    e0_mine,
    e0_other,
    small_s,
    dxc_s,
    dce_s,
    e0_s,
):
    dxc = conv_back(dce_s, dconv_ref, next_ref, cw_ref)
    rows = dxc.shape[0]
    dxc_s[...] = dxc
    dxc_keep[...] = lane_half(dxc_s, core[0])
    sends[0:rows, :] = lane_half(dxc_s, 1 - core[0])
    dn = dnz_ref[...] + dot_t(dxc, iw_ref[...])
    e0, g_norm = norm_back(x_ref[...], g_ref[...], e_ref[...], dn)
    small_s[...] = small_ref[...]
    small_out(core, small_s, g_norm, small_keep, sends, rows)
    e0_s[...] = e0
    e0_mine[...] = row_half(e0_s, core[0]).astype(BF16)
    e0_other[...] = row_half(e0_s, 1 - core[0]).astype(BF16)


def k_dnz(dz_ref, iw_ref, out_ref):
    out_ref[...] = dot_t(dz_ref[...], iw_ref[...])


def chip_sums(n_pairs, n_small, refs, s_ref):
    refs = list(refs)
    pairs, refs = [refs[4 * i : 4 * i + 4] for i in range(n_pairs)], refs[4 * n_pairs :]
    blocks = s_ref.shape[0]
    rows = pairs[0][0].shape[1] // blocks
    for i, (a, a_came, b, b_came) in enumerate(pairs):
        total = dot_rows(
            jnp.concatenate([a[...], a_came[...]], axis=0),
            jnp.concatenate([b[...], b_came[...]], axis=0),
        )
        s_ref[:, 0:rows, :] = total.reshape(blocks, rows, total.shape[1])
        yield i * rows, rows
    for j in range(n_small):
        small_a, small_b = refs[2 * j : 2 * j + 2]
        n = small_a.shape[0] // blocks
        s_ref[:, 0:16, :] = jnp.zeros((blocks, 16, s_ref.shape[2]), F32)
        small = small_a[...] + small_b[...].astype(F32)[0 : small_a.shape[0]]
        for k in range(blocks):
            s_ref[k, 0:n, :] = small[k * n : (k + 1) * n]
        yield n_pairs * rows + 16 * j, 16


def k_chip_sum(n_pairs, n_small, *refs):
    out, s_ref = refs[-2:]
    for top, rows in chip_sums(n_pairs, n_small, refs[:-2], s_ref):
        out[:, top : top + rows, :] = s_ref[:, 0:rows, :]


def k_first(n_pairs, n_small, place, *refs):
    keep_a, keep_b, send_a, send_b, s_ref = refs[-5:]
    blocks = s_ref.shape[0]
    half = s_ref.shape[2] // 2
    x, y = place[0] & 1, (place[0] >> 1) & 1
    for top, rows in chip_sums(n_pairs, n_small, refs[:-5], s_ref):
        to, take = slice(top, top + rows), slice(0, rows)
        for i in range(blocks // 2):
            at = (i >> 1) * 4 + (i & 1) * 2
            keep_a[i, to, :] = s_ref[at + x, take, 0:half]
            send_a[i, to, :] = s_ref[at + 1 - x, take, 0:half].astype(BF16)
            at = (i >> 1) * 4 + (i & 1)
            keep_b[i, to, :] = s_ref[at + 2 * y, take, half:]
            send_b[i, to, :] = s_ref[at + 2 * (1 - y), take, half:].astype(BF16)


def k_second(place, keep_a, keep_b, came_a, came_b, stay_a, stay_b, send_a, send_b):
    x, y = place[0] & 1, (place[0] >> 1) & 1
    for i in range(stay_a.shape[0]):
        for keep, came, stay, send, bit in (
            (keep_a, came_a, stay_a, send_a, y),
            (keep_b, came_b, stay_b, send_b, x),
        ):
            at = 2 * i + bit
            stay[i] = keep[at] + came[at].astype(F32)
            at = 2 * i + 1 - bit
            send[i] = (keep[at] + came[at].astype(F32)).astype(BF16)


def k_third(place, stay_a, stay_b, came_a, came_b, keep, send1, send2, send3):
    z = (place[0] >> 2) & 3
    half = stay_a.shape[2]
    for m, ref in enumerate((keep, send1, send2, send3)):
        at = jnp.bitwise_xor(z, m)
        ref[:, 0:half] = (stay_a[at] + came_a[at].astype(F32)).astype(ref.dtype)
        ref[:, half:] = (stay_b[at] + came_b[at].astype(F32)).astype(ref.dtype)


def k_fourth(keep, came1, came2, came3, out):
    out[...] = (
        keep[...] + came1[...].astype(F32) + came2[...].astype(F32) + came3[...].astype(F32)
    ).astype(BF16)


def k_stack(mine, came1, came2, came3, out_a, out_b):
    half = out_a.shape[2]
    for m, ref in enumerate((mine, came1, came2, came3)):
        out_a[m] = ref[:, 0:half]
        out_b[m] = ref[:, half:]


def k_chip(place, *refs):
    left, right, out = refs[0:4], refs[4:8], refs[8]
    half = left[0].shape[2]
    xy, z = place[0] & 3, (place[0] >> 2) & 3
    for d in range(4):
        for m in range(4):
            at = jnp.bitwise_xor(z, m) * 4 + jnp.bitwise_xor(xy, d)
            out[at, :, 0:half] = left[d][m]
            out[at, :, half:] = right[d][m]


def in_order(core, sources):
    if len(sources) == 1:
        return sources[0][:, 0].astype(F32), sources[0][:, 1].astype(F32)
    own = core[0] == 0
    a, b = sources[0][...].astype(F32), sources[1][...].astype(F32)
    return jnp.where(own, a, b), jnp.where(own, b, a)


def k_place(n_sources, split_rows, core, *refs):
    out, done = refs[-2:]
    done[...] = jnp.zeros(done.shape, F32)
    low, high = in_order(core, refs[:n_sources])
    blocks, rows, lanes = low.shape
    low, high = low.reshape(blocks * rows, lanes), high.reshape(blocks * rows, lanes)
    if split_rows:
        out[0], out[1] = low, high
    else:
        out[:, 0:lanes] = low
        out[:, lanes:] = high


def k_place_small(rank, taps, counts, core, *refs):
    refs = list(refs)
    given, refs = refs[: sum(counts)], refs[sum(counts) :]
    norm, cw, cb, xw, dw, db, al, sk, all_s = refs
    states = al.shape[1]
    n_x = rank + 2 * states
    all_s[...] = jnp.zeros(all_s.shape, F32)
    at = 0
    for l, count in enumerate(counts):
        low, high = in_order(core, given[at : at + count])
        at += count
        blocks, _, lanes = low.shape
        n = -(-(n_x + rank + states + taps + 4) // blocks)
        for k in range(blocks):
            all_s[k * n : (k + 1) * n, 0:lanes] = low[k, 0:n]
            all_s[k * n : (k + 1) * n, lanes:] = high[k, 0:n]
        dw[l] = all_s[n_x : n_x + rank, :]
        first = n_x + rank
        xw[l] = all_s[0:n_x, :]
        al[l] = all_s[first : first + states, :]
        cw[l] = all_s[first + states : first + states + taps, :]
        first += states + taps
        cb[l : l + 1, :] = all_s[first : first + 1, :]
        db[l : l + 1, :] = all_s[first + 1 : first + 2, :]
        sk[l : l + 1, :] = all_s[first + 2 : first + 3, :]
        norm[l : l + 1, :] = all_s[first + 3 : first + 4, 0 : norm.shape[1]]


def shards(
    hidden_in,
    norm_gain,
    in_weight,
    conv_weight,
    conv_bias,
    xproj_weight,
    dtproj_weight,
    dt_bias,
    a_log,
    skip_gain,
    out_weight,
    hidden_grad,
):
    layers, width, _ = in_weight.shape
    inner, states = a_log.shape[1], a_log.shape[2]
    rank = dtproj_weight.shape[1]
    taps = conv_weight.shape[2]
    seqs, own, _ = hidden_in.shape
    ndev = lax.axis_size(AXIS)
    me = lax.axis_index(AXIS)
    core = me % 2
    chip = me // 2
    rows = seqs * own
    assert layers == 2 and seqs == 2 and ndev % 2 == 0
    assert inner % CHUNK == 0 and inner // 128 <= states and rank + 2 * states <= XD

    pairs = [(i, i ^ 1) for i in range(ndev)]
    turn = []
    call = functools.partial(run, turn=turn)

    def to_runs(block):
        mine = lax.dynamic_index_in_dim(block, core, 0, keepdims=False)
        other = lax.dynamic_index_in_dim(block, 1 - core, 0, keepdims=False)
        came = lax.ppermute(other, AXIS, pairs)
        first = jnp.where(core == 0, mine, came)
        second = jnp.where(core == 0, came, mine)
        return jnp.concatenate([first, second], axis=0)

    def from_runs(mine, other):
        came = lax.ppermute(other, AXIS, pairs)
        first = jnp.where(core == 0, mine, came)
        second = jnp.where(core == 0, came, mine)
        return jnp.stack([first, second], axis=0)

    def done_by_now(array):
        array, turn[0] = lax.optimization_barrier((array, turn[0]))
        return array

    def not_before(*arrays):
        return lax.optimization_barrier(arrays + (turn[0],))[:-1]

    def from_before(block):
        return lax.ppermute(block, AXIS, [(i, i + 2) for i in range(ndev - 2)])

    def from_after(block):
        return lax.ppermute(block, AXIS, [(i + 2, i) for i in range(ndev - 2)])

    bits = (ndev // 2).bit_length() - 1
    assert 2 << bits == ndev and bits > 2
    rounds = []
    low = 0
    while low < bits:
        n = 2 if bits - low >= 2 else 1
        rounds.append((low, 1 << n))
        low += n

    def digit_of(r):
        low, group = rounds[r]
        return (chip >> low) & (group - 1)

    def digits_of(r):
        nxt = digit_of(r + 1) if r + 1 < len(rounds) else jnp.zeros_like(chip)
        return jnp.stack([digit_of(r), nxt]).astype(jnp.int32)

    def send(block, r, m, which):
        low, group = rounds[r]
        flip = (m << low) << 1
        route = [(i, i ^ flip) for i in range(ndev)]
        if which == "up":
            route = [(i, j) for i, j in route if j > i]
        if which == "down":
            route = [(i, j) for i, j in route if j < i]
        return lax.ppermute(block, AXIS, route)

    smem = pl.BlockSpec(memory_space=pltpu.SMEM)
    core_s = (core[None].astype(jnp.int32), smem)

    def swap(block):
        return lax.ppermute(block, AXIS, pairs)

    pay = shape((states, inner + EXTRA), BF16)

    kept = {}

    def exchange(payload, a2, mode, meanwhile=()):
        meanwhile = dict(enumerate(meanwhile))
        befores = [[] for _ in mode]
        sums = [[] for _ in mode]
        for r, (low, group) in enumerate(rounds[:-1]):
            received = [payload] + [send(payload, r, m, "all") for m in range(1, group)]
            kept["first"] = received[1:]
            if r in meanwhile:
                meanwhile[r]()
            final = r + 2 == len(rounds)
            split = len(mode) == 2 and final
            nextgroup = rounds[r + 1][1] if split else 0
            pays = (
                [pay] * (nextgroup - 1)
                if split
                else [shape((states * len(mode), inner + EXTRA), BF16)]
            )
            outs = call(
                functools.partial(k_join, group, nextgroup, mode),
                pays
                + [shape((states, inner), F32)] * len(mode)
                + [shape((1, inner), F32)] * len(mode),
                [(digits_of(r), smem)] + received + [a2],
                [
                    pltpu.VMEM((group, states, inner + EXTRA), F32),
                    pltpu.VMEM((group, 8, inner), F32),
                    pltpu.VMEM((states, inner + EXTRA), F32),
                ],
            )
            sent, outs = outs[: len(pays)], outs[len(pays) :]
            for i in range(len(mode)):
                befores[i].append(outs[i])
                sums[i].append(outs[len(mode) + i])
            payload = sent if split else sent[0]
        r = len(rounds) - 1
        if len(mode) == 2:
            last = [send(payload[m - 1], r, m, "all") for m in range(1, rounds[r][1])]
        else:
            way = "all"
            last = [send(payload, r, m, way) for m in range(1, rounds[r][1])]
        for step in sorted(meanwhile):
            if step >= r:
                meanwhile[step]()
        return last, sum(befores, []), sum(sums, []), digits_of(r)

    def row(array, l):
        return Row(array, l)

    def layer_of(array, l):
        return array, part((None,) + array.shape[1:], (l, 0, 0))

    def w_in(l, half):
        columns = slice(half * inner, (half + 1) * inner)
        return Late(in_weight, (l, slice(None), columns), (width, inner))

    def w_out(l):
        return Late(out_weight, (l,), (inner, width))

    def table_scratch():
        return [
            pltpu.VMEM((rows, XD), F32),
            pltpu.VMEM((rows * states, XD), BF16),
            pltpu.VMEM((rows * states, 256), F32),
        ]

    act = shape((rows, inner), F32)
    act_b = shape((rows, inner), BF16)
    res = shape((rows, width), F32)
    res_b = shape((rows, width), BF16)
    edge = shape((HALO, inner), F32)
    mm = 2 * rows * width * inner

    x0 = to_runs(hidden_in).astype(F32)

    normed = [None, None]
    xc = [None, None]
    halo = [None, None]
    z = [None, None]
    u = [None, None]
    xd = [None, None]
    v = [None, None]
    step = [None, None]

    normed[0], xc[0], tail = call(
        k_in, [res_b, act_b, edge], [x0, row(norm_gain, 0), in_weight[0, :, 0:inner]]
    )

    a_log, conv_weight, xproj_weight, dtproj_weight, hidden_grad = not_before(
        a_log, conv_weight, xproj_weight, dtproj_weight, hidden_grad
    )
    a2_all = -jnp.exp(jnp.swapaxes(a_log, 1, 2)) * LOG2E
    cw_all = jnp.swapaxes(conv_weight, 1, 2)
    xw_all = jnp.pad(xproj_weight, ((0, 0), (0, 0), (0, XD - xproj_weight.shape[2])))
    dw_all = jnp.pad(dtproj_weight, ((0, 0), (0, XD - rank), (0, 0)))
    grad_out = to_runs(hidden_grad)

    def gate(l):
        (z[l],) = call(k_gate, [act_b], [normed[l], w_in(l, 1)], cost=LONG)

    def before_scan(l, tail, dgated=None):
        halo[l] = from_before(tail)
        if l:
            gate(l)
        both = dgated is not None
        outs = call(
            functools.partial(k_local, rank, both),
            [
                act_b,
                shape((rows, XD), BF16),
                act,
                act,
                shape((states * (2 if both else 1), inner + EXTRA), BF16),
            ]
            + ([act] if both else []),
            [
                halo[l],
                xc[l],
                layer_of(cw_all, l),
                row(conv_bias, l),
                layer_of(xw_all, l),
                layer_of(dw_all, l),
                row(dt_bias, l),
                layer_of(a2_all, l),
            ]
            + ([dgated, z[l]] if both else []),
            [pltpu.VMEM((rows + HALO, inner), F32)]
            + [pltpu.VMEM((rows, inner), F32)]
            + table_scratch()
            + [pltpu.VMEM((states, inner), F32), pltpu.VMEM((states, inner + EXTRA), F32)],
            cost=LONG,
        )
        u[l], xd[l], v[l], step[l] = outs[:4]
        return outs[4:]

    def join_scratch():
        group = rounds[-1][1]
        return [
            pltpu.VMEM((group, states, inner), F32),
            pltpu.VMEM((group, 8, inner), F32),
        ]

    def piece(array, i):
        return array, part((rows, array.shape[1]), (i, 0))

    def mix(l, parts, extra, outs):
        final = l == layers - 1
        last, befores, sums, digits = parts
        befores, sums = befores[: len(rounds) - 1], sums[: len(rounds) - 1]
        return call(
            functools.partial(k_mix, rank, final, len(last), len(befores)),
            outs,
            [(digits, smem), core_s]
            + last
            + befores
            + sums
            + [layer_of(a2_all, l), u[l], step[l], xd[l], z[l], residual[l], row(skip_gain, l), w_out(l)]
            + extra,
            ([act_scratch, pltpu.VMEM((rows, width), F32)] if final else [])
            + [pltpu.VMEM((rows, inner), BF16)]
            + [act_scratch]
            + table_scratch()
            + join_scratch(),
            cost=LONG,
        )

    half_b = shape((rows, width), BF16)
    entry = shape((states, inner), F32)
    act_scratch = pltpu.VMEM((rows, inner), F32)
    residual = [x0, None]
    def shadow_00():
        gate(0)

    def shadow_0():
        (kept["dgated1"],) = call(k_dgated, [act], [grad_out, w_out(1)], cost=LONG)

    (payload,) = before_scan(0, tail)
    parts = exchange(payload, layer_of(a2_all, 0), "f", (shadow_00, shadow_0))
    dgated1 = kept["dgated1"]
    y0, x1, normed[1], xc[1], tail, gated_keep, sends, h0 = mix(
        0,
        parts,
        [row(norm_gain, 1), w_in(1, 0)],
        [act, res, res_b, act_b, edge, half_b, shape((2 * rows, width), BF16), entry],
    )
    residual[1] = x1
    came = swap(sends)
    n1_pair = (normed[1], piece(came, 1))
    gated0_pair = (gated_keep, piece(came, 0))
    n0_pair = (normed[0], swap(normed[0]))
    e1_pair = (grad_out, swap(grad_out))
    payload, dy1 = before_scan(1, tail, dgated1)
    parts = exchange(payload, layer_of(a2_all, 1), "fb")
    n_small = rank + 2 * states + rank + states + taps + 4
    small = shape((n_small, inner), F32)
    small_pad = -(-n_small // (BLOCKS * 2)) * BLOCKS * 2 if n_small % BLOCKS else n_small

    n_chunks = inner // CHUNK
    cuts = [(0, (n_chunks + 1) // 2 * CHUNK), ((n_chunks + 1) // 2 * CHUNK, n_chunks // 2 * CHUNK)]
    n_parts = len(cuts)
    assert all(first % lanes == 0 for first, lanes in cuts)

    def scan(l, i, dy, parts, h_in):
        lane0, lanes = cuts[i]
        last, befores, sums, digits = parts
        n_low = len(rounds) - 1
        cut = part((rows, lanes), (0, lane0 // lanes))
        cut_s = part((states, lanes), (0, lane0 // lanes))
        cut_a = part((None, states, lanes), (l, 0, lane0 // lanes))
        return call(
            functools.partial(k_scan, rank, lane0, len(last), n_low),
            [shape((rows, lanes), F32)] * 2 + [shape((states, lanes), F32), shape((rows, XD), F32)],
            [(digits, smem)]
            + last
            + befores[-n_low:]
            + sums[-n_low:]
            + [(a2_all, cut_a), (u[l], cut), (step[l], cut), (dy, cut), (h_in, cut_s), xd[l]],
            [pltpu.VMEM((rows, lanes), F32)]
            + table_scratch()
            + [
                pltpu.VMEM((rounds[-1][1], states, lanes), F32),
                pltpu.VMEM((rounds[-1][1], 8, lanes), F32),
            ]
            + [pltpu.VMEM((rows * states, 128), F32)] * 2
            + [pltpu.VMEM((rows * states, CHUNK), F32)] * 2
            + [pltpu.VMEM((states, lanes), F32)],
            cost=LONG,
        )

    def post(l, scans, dy):
        return call(
            functools.partial(k_post, rank, n_parts),
            [act, edge, small],
            [outs[k] for k in range(4) for outs in scans]
            + [
                u[l],
                v[l],
                step[l],
                xd[l],
                dy,
                halo[l],
                xc[l],
                layer_of(cw_all, l),
                row(conv_bias, l),
                layer_of(xw_all, l),
                layer_of(dw_all, l),
                row(skip_gain, l),
            ],
            [pltpu.VMEM((rows + HALO, inner), F32)],
            cost=LONG,
        )


    def over(block, flip):
        return lax.ppermute(block, AXIS, [(i, i ^ (flip << 1)) for i in range(ndev)])

    place_s = (chip[None].astype(jnp.int32), smem)

    def held(arrays, gate):
        if gate is None:
            return arrays
        return lax.optimization_barrier(tuple(arrays) + tuple(gate()))[: len(arrays)]

    def summed(matrices, smalls, aside=False, gates=(None, None, None)):
        ins = []
        each = width // BLOCKS
        for (a, a_came), (b, b_came) in matrices:
            ins += [a, a_came, b, b_came]
        for pair in smalls:
            ins += list(pair)
        r = each * len(matrices) + 16 * len(smalls)
        half = width // 2
        if ndev != 2 * BLOCKS:
            (mine,) = call(
                functools.partial(k_chip_sum, len(matrices), len(smalls)),
                [shape((BLOCKS, r, width), F32)],
                ins,
                [pltpu.VMEM((BLOCKS, each, width), F32)],
            )
            empty = jnp.zeros((2,) + mine.shape, F32)
            total = lax.psum(lax.dynamic_update_index_in_dim(empty, mine, core, 0), AXIS)
            total = total.astype(BF16)
            for _ in range(3 if aside else 5):
                yield None
            if aside:
                yield jnp.swapaxes(total, 0, 1)
                return
            yield (
                lax.dynamic_index_in_dim(total, core, 0, keepdims=False),
                lax.dynamic_index_in_dim(total, 1 - core, 0, keepdims=False),
            )
            return
        n = BLOCKS // 2
        keep_a, keep_b, send_a, send_b = call(
            functools.partial(k_first, len(matrices), len(smalls)),
            [shape((n, r, half), F32)] * 2 + [shape((n, r, half), BF16)] * 2,
            [place_s] + ins,
            [pltpu.VMEM((BLOCKS, each, width), F32)],
            cost=LONG,
        )
        send_a, send_b = held([send_a, send_b], gates[0])
        came_a, came_b = over(send_a, 1), over(send_b, 2)
        yield None
        n = BLOCKS // 4
        stay_a, stay_b, send_a, send_b = call(
            k_second,
            [shape((n, r, half), F32)] * 2 + [shape((n, r, half), BF16)] * 2,
            [place_s, keep_a, keep_b, came_a, came_b],
        )
        send_a, send_b = held([send_a, send_b], gates[1])
        came_a, came_b = over(send_a, 2), over(send_b, 1)
        yield None
        keep, *sends = call(
            k_third,
            [shape((r, width), F32)] + [shape((r, width), BF16)] * 3,
            [place_s, stay_a, stay_b, came_a, came_b],
        )
        sends = held(sends, gates[2])
        came = [over(send_m, 4 * (m + 1)) for m, send_m in enumerate(sends)]
        yield None
        (done,) = call(k_fourth, [shape((r, width), BF16)], [keep] + came)
        if aside:
            every = lax.all_gather(done, AXIS)
            yield every.reshape(BLOCKS, 2, r, width)
            return
        came = [over(done, 4 * m) for m in (1, 2, 3)]
        yield None
        left, right = call(k_stack, [shape((4, r, half), BF16)] * 2, [done] + came)
        left_y, right_x = over(left, 2), over(right, 1)
        lefts = [left, over(left, 1), left_y, over(left_y, 1)]
        rights = [right, right_x, over(right, 2), over(right_x, 2)]
        yield None
        (mine,) = call(
            k_chip, [shape((BLOCKS, r, width), BF16)], [place_s] + lefts + rights
        )
        yield mine, swap(mine)

    def sources(halves, i, per, each, place):
        if not isinstance(halves, tuple):
            spec = pl.BlockSpec((per, 2, each, width), lambda g: (place(g), 0, i, 0))
            return [halves], [spec]
        spec = pl.BlockSpec((per, each, width), lambda g: (place(g), i, 0))
        return list(halves), [spec, spec]

    def placed(halves, i, whole, block, index, split_rows, before):
        each = width // BLOCKS
        steps = 2
        anywhere = pl.BlockSpec(memory_space=pl.ANY)
        arrays, specs = sources(halves, i, BLOCKS // steps, each, lambda g: g)
        ins = [core_s[0]] + arrays + [turn[0]]
        specs = [smem] + specs + [anywhere]
        aliases = {}
        if before is not None:
            aliases = {len(ins): 0}
            ins.append(before)
            specs.append(anywhere)
        out, turn[0] = pl.pallas_call(
            functools.partial(k_place, len(arrays), split_rows),
            grid=(steps,),
            in_specs=specs,
            out_specs=[pl.BlockSpec(block, index), pl.BlockSpec((8, 128), lambda g: (0, 0))],
            out_shape=[whole, shape((8, 128), F32)],
            input_output_aliases=aliases,
            compiler_params=pltpu.CompilerParams(vmem_limit_bytes=58 * 1024 * 1024),
            cost_estimate=COST,
        )(*ins)
        return out

    g_out_shape = shape((layers, 2, width, width), F32)
    g_in_shape = shape((layers, width, 2 * inner), F32)
    several = width // 2
    out_block = (None, 2, several, width)
    in_block = (None, several, inner)

    def out_at(l):
        return lambda g: (l, 0, g, 0)

    def in_at(l, half):
        return lambda g: (l, g, half)

    def placed_small(layer_sums):
        ins, counts = [core_s], []
        for halves, first in layer_sums:
            arrays, specs = sources(halves, first // 16, BLOCKS, 16, lambda g: 0)
            ins += list(zip(arrays, specs))
            counts.append(len(arrays))
        n_x = rank + 2 * states
        return call(
            functools.partial(k_place_small, rank, taps, tuple(counts)),
            [
                shape((layers, width), F32),
                shape((layers, taps, inner), F32),
                shape((layers, inner), F32),
                shape((layers, n_x, inner), F32),
                shape((layers, rank, inner), F32),
                shape((layers, inner), F32),
                shape((layers, states, inner), F32),
                shape((layers, inner), F32),
            ],
            ins,
            [pltpu.VMEM((small_pad, inner), F32)],
            spare=58,
        )

    half_small = shape((small_pad, width), F32)

    hid_mine, hid_other, dz1, dz_keep, gated_keep, sends, h1 = mix(
        1,
        parts,
        [dgated1],
        [shape((own, width), BF16)] * 2
        + [act_b, half_b, half_b, shape((2 * rows, width), BF16), entry],
    )
    came = swap(sends)
    hidden_out = from_runs(hid_mine, hid_other)
    a_sum = summed(
        [((gated_keep, piece(came, 0)), e1_pair), (n1_pair, (dz_keep, piece(came, 1)))],
        [],
        True,
        (None, None, lambda: [after1]),
    )
    scans = [scan(1, 0, dy1, parts, h1)]
    next(a_sum)
    scans.append(scan(1, 1, dy1, parts, h1))
    hidden_out = done_by_now(hidden_out)
    next(a_sum)
    dconv1, head1, small1 = post(1, scans, dy1)
    after1 = from_after(head1)
    (dnz1,) = call(k_dnz, [res], [dz1, w_in(1, 1)], cost=LONG)
    next(a_sum)
    turn_back = functools.partial(
        call,
        functools.partial(k_turn, rank),
        [half_b, half_small, res, res_b, act, act_b, half_b]
        + [shape((4 * rows, width), BF16), res, pay],
        [
            core_s,
            small1,
            dconv1,
            after1,
            layer_of(cw_all, 1),
            dnz1,
            w_in(1, 0),
            x1,
            row(norm_gain, 1),
            grad_out,
            w_out(0),
            y0,
            z[0],
            step[0],
            xd[0],
            layer_of(a2_all, 0),
            w_in(0, 1),
        ],
        [
            pltpu.VMEM((n_small, inner), F32),
            pltpu.VMEM((rows, inner), BF16),
            pltpu.VMEM((rows + HALO, inner), F32),
        ]
        + table_scratch()
        + [pltpu.VMEM((states, inner), F32), pltpu.VMEM((states, inner + EXTRA), F32)],
        cost=LONG,
    )
    dxc_keep, small_keep, e1, de0, dy0, _, dz_keep, sends, dnz0, payload = turn_back()
    came = swap(sends)
    small1_pair = (small_keep, piece(came, 3))
    b_sum = summed(
        [
            (n1_pair, (dxc_keep, piece(came, 0))),
            (gated0_pair, (de0, piece(came, 2))),
            (n0_pair, (dz_keep, piece(came, 1))),
        ],
        [],
        True,
        (lambda: kept["first"], None, None),
    )

    def shadow_1():
        next(b_sum)

    def shadow_2():
        kept["sum_a"] = next(a_sum)

    parts = exchange(payload, layer_of(a2_all, 0), "b", (shadow_1, shadow_2))
    sum_a = kept["sum_a"]
    scans = [scan(0, 0, dy0, parts, h0)]
    next(b_sum)
    scans.append(scan(0, 1, dy0, parts, h0))
    dconv0, head0, small0 = post(0, scans, dy0)
    after0 = from_after(head0)
    next(b_sum)
    dxc_keep, small_keep, sends, e0_mine, e0_other = call(
        k_end,
        [half_b, half_small, shape((2 * rows, width), BF16)] + [shape((own, width), BF16)] * 2,
        [
            core_s,
            small0,
            dconv0,
            after0,
            layer_of(cw_all, 0),
            dnz0,
            w_in(0, 0),
            x0,
            row(norm_gain, 0),
            e1,
        ],
        [
            pltpu.VMEM((n_small, inner), F32),
            pltpu.VMEM((rows, inner), BF16),
            pltpu.VMEM((rows + HALO, inner), F32),
            pltpu.VMEM((rows, width), F32),
        ],
        cost=LONG,
    )
    came = swap(sends)
    c_sum = summed(
        [(n0_pair, (dxc_keep, piece(came, 0)))], [(small_keep, piece(came, 1)), small1_pair]
    )
    sum_b = next(b_sum)
    next(c_sum)
    input_grad = done_by_now(from_runs(e0_mine, e0_other))
    next(c_sum)
    next(c_sum)
    g_out = placed(sum_a, 0, g_out_shape, out_block, out_at(1), True, None)
    g_in = placed(sum_a, 1, g_in_shape, in_block, in_at(1, 1), False, None)
    next(c_sum)
    next(c_sum)
    g_in = placed(sum_b, 0, g_in_shape, in_block, in_at(1, 0), False, g_in)
    g_out = placed(sum_b, 1, g_out_shape, out_block, out_at(0), True, g_out)
    sum_c = next(c_sum)
    g_in = placed(sum_b, 2, g_in_shape, in_block, in_at(0, 1), False, g_in)
    g_in = placed(sum_c, 0, g_in_shape, in_block, in_at(0, 0), False, g_in)
    g_norm, g_cw, g_cb, g_xw, g_dw, g_db, g_al, g_sk = placed_small(
        [(sum_c, width // BLOCKS), (sum_c, width // BLOCKS + 16)]
    )
    return (
        hidden_out,
        input_grad,
        g_norm,
        g_in,
        jnp.swapaxes(g_cw, 1, 2),
        g_cb,
        jnp.swapaxes(g_xw, 1, 2),
        g_dw,
        g_db,
        jnp.swapaxes(g_al, 1, 2),
        g_sk,
        g_out.reshape(layers, inner, width),
    )


def solution(mesh):
    split = P(None, AXIS, None)
    return jax.shard_map(
        shards,
        mesh=mesh,
        in_specs=(split,) + (P(),) * 10 + (split,),
        out_specs=(split, split) + (P(),) * 10,
        check_vma=False,
    )
```
